32 devices in a mesh: batch: 2 (over x), seq: 16 (over z, y, core).
Axes of the slice: x: 2, y: 2, z: 4, core: 2. Of those that a mesh axis runs over, the one named last changes fastest.
Arguments:
- tokens: bfloat16 [2, 16384, 768], P('batch', 'seq'), may hold values from -6 to 6
- global_states: bfloat16 [2, 1024, 768], P('batch', 'seq'), may hold values from -6 to 6
- lengths: int32 [2, 8], replicated, may hold values from 0 to 16384, as said below
- bucket_of: int32 [2], replicated, may hold values from 0 to 1, each once
- query_weight: bfloat16 [768, 768], replicated, may hold values from -0.5 to 0.5
- key_weight: bfloat16 [768, 768], replicated, may hold values from -0.21875 to 0.21875
- value_weight: bfloat16 [768, 768], replicated, may hold values from -0.21875 to 0.21875
- output_weight: bfloat16 [768, 768], replicated, may hold values from -2.5 to 2.5
- expand_weight: bfloat16 [768, 3072], replicated, may hold values from -0.21875 to 0.21875
- hidden_bias: float32 [3072], replicated, may hold values from -3 to 3
- contract_weight: bfloat16 [3072, 768], replicated, may hold values from -0.109375 to 0.109375
- output_bias: float32 [768], replicated, may hold values from -2 to 2
- norm_params: float32 [6, 768], replicated
- cotangent: bfloat16 [2, 16384, 768], P('batch', 'seq'), may hold values from -6 to 6
- global_cotangent: bfloat16 [2, 1024, 768], P('batch', 'seq'), may hold values from -12 to 12
Outputs:
- layer_out: bfloat16 [2, 16384, 768], P('batch', 'seq')
- global_out: bfloat16 [2, 1024, 768], P('batch', 'seq')
- token_grad: float32 [2, 16384, 768], P('batch', 'seq')
- global_grad: float32 [2, 1024, 768], P('batch', 'seq')
- query_weight_grad: float32 [768, 768], P('batch', 'seq')
- key_weight_grad: float32 [768, 768], P('batch', 'seq')
- value_weight_grad: float32 [768, 768], P('batch', 'seq')
- output_weight_grad: float32 [768, 768], P('batch', 'seq')
- expand_weight_grad: float32 [768, 3072], P('batch', 'seq')
- contract_weight_grad: float32 [3072, 768], P('batch', 'seq')
- hidden_bias_grad: float32 [3072], replicated
- output_bias_grad: float32 [768], replicated
- norm_params_grad: float32 [6, 768], replicated
The draws below stay inside these ranges and needn't reach their ends.
Inputs may be any that keep to these rules, and one draw needn't show every extreme that they name: Row j holds the lengths of bucket j: its first 1, 4 or 8 entries are positive and sum to 16384, the rest are 0; a bucket whose index is 0 modulo 4 holds one sequence of 16384 tokens. bucket_of names each bucket once.
All inputs are finite; a program needn't handle non-finite values.
Results may differ from the reference program's by a relative error of at most 0.023.
Values may be sent and summed in bfloat16 or wider, within the bound.
A program may use at most 384 MiB of HBM per device.

```python
import jax
import jax.numpy as jnp
from jax import lax

D = 768
HEADS = 12
HEAD_DIM = 64
FF = 3072
BLOCK = 512
HALF = 256
GLOBALS = 128
SLOTS = 8
GROUP = 16384
N_BATCH = 2


def draw_lengths(key, part):
    key = jax.random.fold_in(key, 11)
    bucket = jnp.arange(N_BATCH, dtype=jnp.int32)
    counts = jnp.array([1, 8, 4, 8], dtype=jnp.int32)[bucket % 4]
    base = GROUP // counts
    spread = base // 16
    offsets = jax.random.randint(key, (N_BATCH, SLOTS), -spread[:, None], spread[:, None] + 1, dtype=jnp.int32)
    slot = jnp.arange(SLOTS, dtype=jnp.int32)[None, :]
    leading = jnp.where(slot < counts[:, None] - 1, base[:, None] + offsets, 0)
    closing = GROUP - jnp.sum(leading, axis=1, keepdims=True)
    return jnp.where(slot == counts[:, None] - 1, closing, leading).astype(jnp.int32)


def draw_norm_params(key, part):
    key = jax.random.fold_in(key, 23)
    row = jnp.arange(6)[:, None]
    noise = jax.random.uniform(key, (6, D), jnp.float32, -1.0, 1.0)
    return jnp.where(row % 2 == 0, 1.0 + 0.3 * noise, 0.5 * noise).astype(jnp.float32)


def block_levels(key, shape, split, least, top_value):
    loudness = 1.0
    for dim, blocks in split:
        draws = jax.random.uniform(jax.random.fold_in(jax.random.fold_in(key, 6), dim), (blocks,), jnp.float32, least / len(split), top_value / len(split))
        loudness = loudness * jnp.repeat(jnp.exp(draws), shape[dim] // blocks).reshape((-1,) + (1,) * (len(shape) - 1 - dim))
    return loudness


def scatter_about(stream_key, shape, width, bound, cuts=(), kind=jnp.bfloat16):
    values = jax.random.normal(stream_key, shape, jnp.float32) * width
    if len(cuts) > 0:
        values = block_levels(stream_key, shape, cuts, -0.22, 0.18) * values
    return jnp.clip(values, min=-bound, max=bound).astype(kind)


def setup_inputs(seed: int = 0) -> dict:
    splits = jax.random.split(jax.random.key(seed), 16)
    return {
        "tokens": scatter_about(splits[0], (N_BATCH, GROUP, D), 1.0, 6.0, ((0, 2), (1, 16))),
        "global_states": scatter_about(splits[1], (N_BATCH, SLOTS * GLOBALS, D), 1.0, 6.0, ((0, 2), (1, 16))),
        "lengths": draw_lengths(jax.random.fold_in(splits[15], 71), 0),
        "bucket_of": jax.random.permutation(splits[3], N_BATCH).astype(jnp.int32),
        "query_weight": scatter_about(splits[4], (D, D), (max(HEAD_DIM * D // 400, 1)) ** -0.5, 0.5),
        "key_weight": scatter_about(splits[5], (D, D), D ** -0.5, 0.21875),
        "value_weight": scatter_about(splits[6], (D, D), D ** -0.5, 0.21875),
        "output_weight": scatter_about(splits[7], (D, D), (max(D // 128, 1)) ** -0.5, 2.5),
        "expand_weight": scatter_about(splits[8], (D, FF), D ** -0.5, 0.21875),
        "hidden_bias": scatter_about(splits[9], (FF,), 0.5, 3.0, (), jnp.float32),
        "contract_weight": scatter_about(splits[10], (FF, D), FF ** -0.5, 0.109375),
        "output_bias": scatter_about(splits[11], (D,), 0.3, 2.0, (), jnp.float32),
        "norm_params": draw_norm_params(jax.random.fold_in(splits[15], 71), 0),
        "cotangent": scatter_about(splits[13], (N_BATCH, GROUP, D), 1.0, 6.0, ((0, 2), (1, 16))),
        "global_cotangent": scatter_about(splits[14], (N_BATCH, SLOTS * GLOBALS, D), 2.0, 12.0, ((0, 2), (1, 16))),
    }


@jax.custom_vjp
def low(v):
    return lax.optimization_barrier(v.astype(jnp.bfloat16)).astype(jnp.float32)

@jax.custom_vjp
def low_back(v):
    return v

def low_keep(v):
    return (low(v), None)

def low_pass(kept, grad):
    return (grad,)

def back_keep(v):
    return (v, None)

def back_low(kept, grad):
    return (low(grad),)
low.defvjp(low_keep, low_pass)
low_back.defvjp(back_keep, back_low)
norm_eps = 1e-05
masked_score = -1e+30
query_scale = 0.125
highest = lax.Precision.HIGHEST

def both(values):
    return low(low_back(values))

def layer_norm(values, gain, offset):
    mean = lax.optimization_barrier(jnp.mean(values, axis=-1, keepdims=True))
    centered = values - mean
    variance = lax.optimization_barrier(jnp.mean(centered * centered, axis=-1, keepdims=True))
    return centered * lax.rsqrt(variance + norm_eps) * gain + offset

def product(left, right):
    return jnp.dot(left, right, precision=highest)

def split_heads(values):
    return values.reshape(values.shape[0], HEADS, values.shape[1] // HEADS)

def attend(queries, keys, values, allowed):
    score = low_back(jnp.einsum('qhd,khd->hqk', queries, keys, precision=highest))
    score = jnp.where(allowed[None], score, masked_score)
    weights = jnp.exp(score - lax.optimization_barrier(jnp.max(score, axis=-1, keepdims=True)))
    total = lax.optimization_barrier(jnp.sum(weights, axis=-1))
    summed = low_back(jnp.einsum('hqk,khd->qhd', low(weights), values, precision=highest))
    return summed / jnp.transpose(total)[:, :, None]

def local_attend(queries, keys, values, global_keys, global_values, block_ids, seq_ids, slot_ids):
    blocks = GROUP // BLOCK

    def one_block(piece):
        block_queries, block_keys, block_values, ids_here, seq_here = piece
        to_globals = slot_ids[None, :] == seq_here[:, None]
        to_block = (ids_here[None, :] == ids_here[:, None]) & (seq_here[None, :] == seq_here[:, None])
        allowed = jnp.concatenate([to_globals, to_block], 1)
        return attend(block_queries, jnp.concatenate([global_keys, block_keys], 0), jnp.concatenate([global_values, block_values], 0), allowed)
    stacked = (queries.reshape((blocks, BLOCK) + queries.shape[1:]), keys.reshape((blocks, BLOCK) + keys.shape[1:]), values.reshape((blocks, BLOCK) + values.shape[1:]), block_ids.reshape(blocks, BLOCK), seq_ids.reshape(blocks, BLOCK))
    result = lax.map(jax.checkpoint(one_block), stacked)
    return result.reshape(GROUP, queries.shape[1] * queries.shape[2])

def global_attend(queries, keys, values, allowed):

    def one_head(piece):
        head_queries, head_keys, head_values = piece
        return attend(head_queries[:, None], head_keys[:, None], head_values[:, None], allowed)[:, 0]
    result = lax.map(jax.checkpoint(one_head), (jnp.swapaxes(queries, 0, 1), jnp.swapaxes(keys, 0, 1), jnp.swapaxes(values, 0, 1)))
    result = jnp.swapaxes(result, 0, 1)
    return result.reshape(result.shape[0], result.shape[1] * result.shape[2])

def group_forward(params, tokens_group, globals_group, lens):
    query_w, key_w, value_w, output_w, expand_w, hidden_b, contract_w, output_b, norms = params
    order = (jnp.arange(GROUP, dtype=jnp.int32) - HALF) % GROUP
    staggered = jnp.roll(tokens_group, HALF, axis=0)
    block_ids = (order + HALF) // BLOCK
    bounds = jnp.cumsum(lens)
    seq_ids = lax.optimization_barrier(jnp.sum((bounds[None, :] <= order[:, None]).astype(jnp.int32), axis=1))
    slot_ids = jnp.arange(SLOTS * GLOBALS, dtype=jnp.int32) // GLOBALS
    normed = low(layer_norm(staggered, norms[0], norms[1]))
    normed_global = low(layer_norm(globals_group, norms[2], norms[3]))
    queries = split_heads(both(product(normed, query_w) * query_scale))
    keys = split_heads(both(product(normed, key_w)))
    values = split_heads(both(product(normed, value_w)))
    global_queries = split_heads(both(product(normed_global, query_w) * query_scale))
    global_keys = split_heads(both(product(normed_global, key_w)))
    global_values = split_heads(both(product(normed_global, value_w)))
    attended = low(local_attend(queries, keys, values, global_keys, global_values, block_ids, seq_ids, slot_ids))
    allowed_global = jnp.concatenate([slot_ids[:, None] == seq_ids[None, :], slot_ids[:, None] == slot_ids[None, :]], 1)
    global_attended = low(global_attend(global_queries, jnp.concatenate([keys, global_keys], 0), jnp.concatenate([values, global_values], 0), allowed_global))

    def branch(inputs, attended_rows):
        middle = inputs + low_back(product(attended_rows, output_w))
        normed_second = low(layer_norm(middle, norms[4], norms[5]))
        expanded = low_back(product(normed_second, expand_w) + hidden_b)
        activated = low(jax.nn.gelu(expanded, approximate=False))
        return middle + low_back(product(activated, contract_w) + output_b)
    result = branch(staggered, attended)
    global_result = branch(globals_group, global_attended)
    return (jnp.roll(result, -HALF, axis=0), global_result)

def reference(tokens, global_states, lengths, bucket_of, query_weight, key_weight, value_weight, output_weight, expand_weight, hidden_bias, contract_weight, output_bias, norm_params, cotangent, global_cotangent):
    params = tuple((item.astype(jnp.float32) for item in (query_weight, key_weight, value_weight, output_weight, expand_weight, hidden_bias, contract_weight, output_bias, norm_params)))
    outputs = []
    global_outputs = []
    token_grads = []
    global_grads = []
    totals = None
    for group in range(N_BATCH):
        lens = lengths[bucket_of[group]]

        def forward(prm, rows_in, globals_in):
            return group_forward(prm, rows_in, globals_in, lens)
        (result, global_result), pullback = jax.vjp(forward, params, tokens[group].astype(jnp.float32), global_states[group].astype(jnp.float32))
        param_grads, rows_grad, globals_grad = pullback((cotangent[group].astype(jnp.float32), global_cotangent[group].astype(jnp.float32)))
        totals = param_grads if totals is None else jax.tree.map(jnp.add, totals, param_grads)
        outputs.append(result.astype(jnp.bfloat16))
        global_outputs.append(global_result.astype(jnp.bfloat16))
        token_grads.append(rows_grad)
        global_grads.append(globals_grad)
    return (jnp.stack(outputs), jnp.stack(global_outputs), jnp.stack(token_grads), jnp.stack(global_grads), totals[0], totals[1], totals[2], totals[3], totals[4], totals[6], totals[5], totals[7], totals[8])
```

```python
import functools

import jax
import jax.numpy as jnp
from jax import lax
from jax.experimental import pallas as pl
from jax.experimental.pallas import tpu as pltpu
from jax.sharding import PartitionSpec as P

HEADS = 12
HEAD_DIM = 64
PAIRS = HEADS // 2
LANES = 128
BLOCK = 512
HALF = 256
GLOBALS = 128
SLOTS = 8
FF_CHUNK = 512

norm_eps = 1e-05
masked_score = -1e30
query_scale = 0.125

SEG_LANE = 0
SLOT_LANE = 16
STAT_LANE = 24
GLOBAL_LANE = 32

f32 = jnp.float32
bf16 = jnp.bfloat16
VMEM_LIMIT = 60 * 1024 * 1024


def nn(left, right):
    return jnp.dot(left, right, preferred_element_type=f32)


def nt(left, right):
    return lax.dot_general(left, right, (((1,), (1,)), ((), ())), preferred_element_type=f32)


def tn(left, right):
    return lax.dot_general(left, right, (((0,), (0,)), ((), ())), preferred_element_type=f32)


def iota(shape, dim):
    return lax.broadcasted_iota(jnp.int32, shape, dim)


def stack_pair(pair):
    lane = iota((1, LANES), 1)
    low = jnp.where(lane < HEAD_DIM, 1.0, 0.0).astype(bf16)
    high = jnp.where(lane < HEAD_DIM, 0.0, 1.0).astype(bf16)
    return jnp.concatenate([pair * low, pair * high], axis=0)


def split_three(value):
    first = value.astype(bf16)
    rest = value - first.astype(f32)
    second = rest.astype(bf16)
    third = (rest - second.astype(f32)).astype(bf16)
    return first.astype(f32), second.astype(f32), third.astype(f32)


def place_three(value, lane, start, other):
    first, second, third = split_three(value)
    return jnp.where(
        lane == start,
        first,
        jnp.where(lane == start + 1, second, jnp.where(lane == start + 2, third, other)),
    )


def read_edges(lengths, bucket_of, place, edges):
    bucket = bucket_of[place[0]]
    total = jnp.int32(0)
    edges[0] = total
    for slot in range(SLOTS):
        total = total + lengths[bucket, slot]
        edges[slot + 1] = total


def block_start(place, rows, block):
    return place[1] * rows + block * BLOCK - HALF


def slot_present(slot, place, edges, rows, group_rows, block):
    low = edges[slot]
    high = edges[slot + 1]
    found = jnp.bool_(False)
    for part in range(BLOCK // HALF):
        start = block_start(place, rows, block) + part * HALF
        start = jnp.where(start < 0, start + group_rows, start)
        found = found | ((high > low) & (low < start + HALF) & (high > start))
    return found


def row_numbers(place, edges, rows, group_rows, block):
    place_in = block_start(place, rows, block) + iota((BLOCK, LANES), 0)
    wrapped = place_in < 0
    token = jnp.where(wrapped, place_in + group_rows, place_in)
    slot = jnp.zeros((BLOCK, LANES), jnp.int32)
    for j in range(SLOTS):
        slot = slot + jnp.where(edges[j + 1] <= token, 1, 0)
    return slot, slot + jnp.where(wrapped, SLOTS, 0)


def key_extra(slot, segment):
    lane = iota((BLOCK, LANES), 1)
    extra = jnp.where((lane < SLOT_LANE) & (lane != segment), masked_score, 0.0)
    extra = jnp.where((lane >= STAT_LANE) & (lane < STAT_LANE + 3), -1.0, extra)
    return jnp.where(lane == GLOBAL_LANE + slot, 1.0, extra)


def query_extra(slot, segment):
    lane = iota((BLOCK, LANES), 1)
    return jnp.where((lane == segment) | (lane == SLOT_LANE + slot), 1.0, 0.0)


def global_key_extra(slot):
    lane = iota((GLOBALS, LANES), 1)
    inside = (lane >= SLOT_LANE) & (lane < SLOT_LANE + SLOTS)
    extra = jnp.where(inside & (lane != SLOT_LANE + slot), masked_score, 0.0)
    extra = jnp.where((lane >= STAT_LANE) & (lane < STAT_LANE + 3), -1.0, extra)
    return jnp.where(lane == GLOBAL_LANE + slot, 1.0, extra)


def global_query_extra(slot):
    lane = iota((GLOBALS, LANES), 1)
    inside = (lane >= GLOBAL_LANE) & (lane < GLOBAL_LANE + SLOTS)
    return jnp.where(inside & (lane != GLOBAL_LANE + slot), masked_score, 0.0)


def normalize_rows(values):
    mean = jnp.mean(values, axis=-1, keepdims=True)
    centered = values - mean
    variance = jnp.mean(centered * centered, axis=-1, keepdims=True)
    scale = lax.rsqrt(variance + norm_eps)
    return centered * scale, scale


def norm_back(unit, scale, gain, upstream):
    inner = upstream * gain
    along = jnp.mean(inner * unit, axis=-1, keepdims=True)
    return scale * (inner - jnp.mean(inner, axis=-1, keepdims=True) - unit * along)


def gelu_parts(value):
    decay = jnp.exp(-0.5 * value * value)
    step = 1.0 / (1.0 + (0.3275911 * 0.7071067811865476) * jnp.abs(value))
    series = 1.061405429 * step - 1.453152027
    series = series * step + 1.421413741
    series = series * step - 0.284496736
    series = series * step + 0.254829592
    tail = (0.5 * series) * step * decay
    area = jnp.where(value >= 0.0, 1.0 - tail, tail)
    return area, decay * 0.3989422804014327


def full(shape):
    return pl.BlockSpec(shape, lambda *unused: (0,) * len(shape))


def once(shape):
    return pl.BlockSpec(
        shape, lambda *unused: (0,) * len(shape), pipeline_mode=pl.Buffered(buffer_count=1)
    )


def params(**more):
    return pltpu.CompilerParams(vmem_limit_bytes=VMEM_LIMIT, **more)


def project_rows(rows_ref, gain_ref, offset_ref, wq_ref, wk_ref, wv_ref, outs):
    unit, unused = normalize_rows(rows_ref[...].astype(f32))
    normed = (unit * gain_ref[...] + offset_ref[...]).astype(bf16)
    outs[0][...] = normed
    outs[1][...] = (nn(normed, wq_ref[...]) * query_scale).astype(bf16)
    outs[2][...] = nn(normed, wk_ref[...]).astype(bf16)
    outs[3][...] = nn(normed, wv_ref[...]).astype(bf16)


def project_local_kernel(rows_ref, gain_ref, offset_ref, wq_ref, wk_ref, wv_ref, *outs):
    project_rows(rows_ref, gain_ref, offset_ref, wq_ref, wk_ref, wv_ref, outs)


def project_local(rows, gain, offset, wq, wk, wv):
    count, width = rows.shape
    tile = pl.BlockSpec((BLOCK, width), lambda i: (i, 0))
    return pl.pallas_call(
        project_local_kernel,
        grid=(count // BLOCK,),
        in_specs=[tile, full((1, width)), full((1, width))] + [once((width, width))] * 3,
        out_specs=[tile] * 4,
        out_shape=[jax.ShapeDtypeStruct((count, width), bf16)] * 4,
        compiler_params=params(),
        cost_estimate=pl.CostEstimate(
            flops=6 * count * width * width, bytes_accessed=12 * count * width, transcendentals=0
        ),
        name="project_local",
    )(rows, gain, offset, wq, wk, wv)


def project_global_kernel(
    rows_count,
    group_rows,
    lengths,
    bucket_of,
    place,
    rows_ref,
    gain_ref,
    offset_ref,
    wq_ref,
    wk_ref,
    wv_ref,
    h_ref,
    q_ref,
    k_ref,
    v_ref,
    edges,
):
    slot = pl.program_id(0)

    @pl.when(slot == 0)
    def _():
        read_edges(lengths, bucket_of, place, edges)

    needed = slot == place[2]
    for block in range(rows_count // BLOCK):
        needed = needed | slot_present(slot, place, edges, rows_count, group_rows, block)

    @pl.when(needed)
    def _():
        project_rows(
            rows_ref, gain_ref, offset_ref, wq_ref, wk_ref, wv_ref, (h_ref, q_ref, k_ref, v_ref)
        )


def project_global(scalars, rows_count, group_rows, rows, gain, offset, wq, wk, wv):
    count, width = rows.shape
    tile = pl.BlockSpec((GLOBALS, width), lambda i, *unused: (i, 0))
    return pl.pallas_call(
        functools.partial(project_global_kernel, rows_count, group_rows),
        grid_spec=pltpu.PrefetchScalarGridSpec(
            num_scalar_prefetch=3,
            grid=(SLOTS,),
            in_specs=[tile, full((1, width)), full((1, width))] + [once((width, width))] * 3,
            out_specs=[tile] * 4,
            scratch_shapes=[pltpu.SMEM((16,), jnp.int32)],
        ),
        out_shape=[jax.ShapeDtypeStruct((count, width), bf16)] * 4,
        compiler_params=params(),
        cost_estimate=pl.CostEstimate(
            flops=6 * 256 * width * width, bytes_accessed=12 * count * width, transcendentals=0
        ),
        name="project_global",
    )(*scalars, rows, gain, offset, wq, wk, wv)


def global_forward_kernel(
    rows_count,
    group_rows,
    lengths,
    bucket_of,
    place,
    k_ref,
    v_ref,
    gq_ref,
    gk_ref,
    gv_ref,
    sum_ref,
    peak_ref,
    total_ref,
    edges,
    keys_ref,
):
    pair = pl.program_id(0)
    block = pl.program_id(1)

    @pl.when((pair == 0) & (block == 0))
    def _():
        read_edges(lengths, bucket_of, place, edges)

    @pl.when(block == 0)
    def _():
        sum_ref[...] = jnp.zeros_like(sum_ref)
        total_ref[...] = jnp.zeros_like(total_ref)
        peak_ref[...] = jnp.full(peak_ref.shape, masked_score, f32)

    slot_of, segment = row_numbers(place, edges, rows_count, group_rows, block)
    keys_ref[:, :LANES] = k_ref[...]
    keys_ref[:, LANES:] = key_extra(slot_of, segment).astype(bf16)

    def add(slot, keys, values):
        at = pl.ds(pl.multiple_of(slot * GLOBALS, GLOBALS), GLOBALS)
        extra = global_query_extra(slot).astype(bf16)
        queries = jnp.concatenate(
            [stack_pair(gq_ref[at, :]), jnp.concatenate([extra, extra], 0)], axis=1
        )
        score = nt(keys, queries)
        old = peak_ref[0, pl.ds(slot, 1), :]
        peak = jnp.maximum(old, jnp.max(score, axis=0, keepdims=True))
        weights = jnp.exp(score - peak)
        keep = jnp.exp(old - peak)
        peak_ref[0, pl.ds(slot, 1), :] = peak
        total_ref[0, pl.ds(slot, 1), :] = total_ref[0, pl.ds(slot, 1), :] * keep + jnp.sum(
            weights, axis=0, keepdims=True
        )
        more = tn(values, weights.astype(bf16))
        sum_ref[:HEAD_DIM, at] = (
            sum_ref[:HEAD_DIM, at] * keep[:, :GLOBALS] + more[:HEAD_DIM, :GLOBALS]
        )
        sum_ref[HEAD_DIM:, at] = (
            sum_ref[HEAD_DIM:, at] * keep[:, GLOBALS:] + more[HEAD_DIM:, GLOBALS:]
        )

    def one_slot(slot, carry):
        @pl.when(slot_present(slot, place, edges, rows_count, group_rows, block))
        def _():
            add(slot, keys_ref[...], v_ref[...])

        return carry

    lax.fori_loop(0, SLOTS, one_slot, 0)

    @pl.when((block == pl.num_programs(1) - 1) & (place[2] >= 0))
    def _():
        slot = place[2]
        at = pl.ds(pl.multiple_of(slot * GLOBALS, GLOBALS), GLOBALS)
        keys = jnp.concatenate([gk_ref[at, :], global_key_extra(slot).astype(bf16)], axis=1)
        add(slot, keys, gv_ref[at, :])


def global_forward(scalars, rows_count, group_rows, k, v, gq, gk, gv):
    blocks = rows_count // BLOCK
    all_globals, width = gq.shape
    block_spec = pl.BlockSpec((BLOCK, LANES), lambda p, b, *unused: (b, p))
    pair_spec = pl.BlockSpec((all_globals, LANES), lambda p, b, *unused: (0, p))
    stat_spec = pl.BlockSpec((1, SLOTS, 2 * GLOBALS), lambda p, b, *unused: (p, 0, 0))
    return pl.pallas_call(
        functools.partial(global_forward_kernel, rows_count, group_rows),
        grid_spec=pltpu.PrefetchScalarGridSpec(
            num_scalar_prefetch=3,
            grid=(PAIRS, blocks),
            in_specs=[block_spec] * 2 + [pair_spec] * 3,
            out_specs=[
                pl.BlockSpec((LANES, all_globals), lambda p, b, *unused: (p, 0)),
                stat_spec,
                stat_spec,
            ],
            scratch_shapes=[pltpu.SMEM((16,), jnp.int32), pltpu.VMEM((BLOCK, 2 * LANES), bf16)],
        ),
        out_shape=[
            jax.ShapeDtypeStruct((width, all_globals), f32),
            jax.ShapeDtypeStruct((PAIRS, SLOTS, 2 * GLOBALS), f32),
            jax.ShapeDtypeStruct((PAIRS, SLOTS, 2 * GLOBALS), f32),
        ],
        compiler_params=params(),
        cost_estimate=pl.CostEstimate(
            flops=4 * 4 * rows_count * GLOBALS * width,
            bytes_accessed=10 * all_globals * width,
            transcendentals=HEADS * rows_count * GLOBALS,
        ),
        name="global_forward",
    )(*scalars, k, v, gq, gk, gv)


def local_forward_kernel(
    rows_count,
    group_rows,
    lengths,
    bucket_of,
    place,
    q_ref,
    k_ref,
    v_ref,
    gk_ref,
    gv_ref,
    o_ref,
    extra_ref,
    edges,
    queries_ref,
    score_ref,
    sum_ref,
):
    pair = pl.program_id(0)
    block = pl.program_id(1)

    @pl.when((pair == 0) & (block == 0))
    def _():
        read_edges(lengths, bucket_of, place, edges)

    slot_of, segment = row_numbers(place, edges, rows_count, group_rows, block)
    extra = query_extra(slot_of, segment)
    extra = jnp.concatenate([extra, extra], 0)
    slot_both = jnp.concatenate([slot_of, slot_of], 0)
    queries_ref[:, :LANES] = stack_pair(q_ref[...])
    queries_ref[:, LANES:] = extra.astype(bf16)
    queries = queries_ref[...]
    keys = jnp.concatenate([k_ref[...], key_extra(slot_of, segment).astype(bf16)], axis=1)
    score = nt(queries, keys)
    score_ref[...] = jnp.full(score_ref.shape, masked_score, f32)

    def score_slot(slot, carry):
        @pl.when(slot_present(slot, place, edges, rows_count, group_rows, block))
        def _():
            at = pl.ds(pl.multiple_of(slot * GLOBALS, GLOBALS), GLOBALS)
            slot_keys = jnp.concatenate([gk_ref[at, :], global_key_extra(slot).astype(bf16)], 1)
            score_ref[...] = jnp.maximum(score_ref[...], nt(queries_ref[...], slot_keys))

        return carry

    lax.fori_loop(0, SLOTS, score_slot, 0)
    far_score = score_ref[...]
    peak = jnp.maximum(
        jnp.max(score, axis=1, keepdims=True), jnp.max(far_score, axis=1, keepdims=True)
    )
    weights = jnp.exp(score - peak)
    far_weights = jnp.exp(far_score - peak)
    total = jnp.sum(weights, axis=1, keepdims=True) + jnp.sum(far_weights, axis=1, keepdims=True)
    sum_ref[...] = nn(weights.astype(bf16), v_ref[...])
    score_ref[...] = far_weights

    def add_slot(slot, carry):
        @pl.when(slot_present(slot, place, edges, rows_count, group_rows, block))
        def _():
            at = pl.ds(pl.multiple_of(slot * GLOBALS, GLOBALS), GLOBALS)
            chosen = jnp.where(slot_both == slot, score_ref[...], 0.0).astype(bf16)
            sum_ref[...] = sum_ref[...] + nn(chosen, gv_ref[at, :])

        return carry

    lax.fori_loop(0, SLOTS, add_slot, 0)
    mean = sum_ref[...] / total
    lane = iota((BLOCK, LANES), 1)
    o_ref[...] = jnp.where(lane < HEAD_DIM, mean[:BLOCK], mean[BLOCK:]).astype(bf16)
    stat = peak + jnp.log(total)
    lane = iota((2 * BLOCK, LANES), 1)
    extra_ref[...] = (
        place_three(stat, lane, STAT_LANE, extra).astype(bf16).reshape(2, BLOCK, LANES)
    )


def local_forward(scalars, rows_count, group_rows, q, k, v, gk, gv):
    blocks = rows_count // BLOCK
    all_globals, width = gk.shape
    block_spec = pl.BlockSpec((BLOCK, LANES), lambda p, b, *unused: (b, p))
    pair_spec = pl.BlockSpec((all_globals, LANES), lambda p, b, *unused: (0, p))
    return pl.pallas_call(
        functools.partial(local_forward_kernel, rows_count, group_rows),
        grid_spec=pltpu.PrefetchScalarGridSpec(
            num_scalar_prefetch=3,
            grid=(PAIRS, blocks),
            in_specs=[block_spec] * 3 + [pair_spec] * 2,
            out_specs=[
                block_spec,
                pl.BlockSpec((2, BLOCK, LANES), lambda p, b, *unused: (p, b, 0)),
            ],
            scratch_shapes=[
                pltpu.SMEM((16,), jnp.int32),
                pltpu.VMEM((2 * BLOCK, 2 * LANES), bf16),
                pltpu.VMEM((2 * BLOCK, LANES), f32),
                pltpu.VMEM((2 * BLOCK, LANES), f32),
            ],
        ),
        out_shape=[
            jax.ShapeDtypeStruct((rows_count, width), bf16),
            jax.ShapeDtypeStruct((HEADS, rows_count, LANES), bf16),
        ],
        compiler_params=params(),
        cost_estimate=pl.CostEstimate(
            flops=16 * rows_count * (BLOCK + GLOBALS) * width,
            bytes_accessed=16 * rows_count * width,
            transcendentals=HEADS * rows_count * (BLOCK + GLOBALS),
        ),
        name="local_forward",
    )(*scalars, q, k, v, gk, gv)


def branch_kernel(
    tile,
    x_ref,
    o_ref,
    ct_ref,
    wo_ref,
    w1_ref,
    b1_ref,
    w2_ref,
    b2_ref,
    gain_ref,
    offset_ref,
    z_ref,
    dy_ref,
    do_ref,
    dw1_ref,
    dw2_ref,
    dwo_ref,
    db1_ref,
    db2_ref,
    dgain_ref,
    doffset_ref,
    y_ref,
    h_ref,
    dh_ref,
    dft_ref,
    a_ref,
    du_ref,
):
    step = pl.program_id(0)
    count, width = x_ref.shape
    tiles = count // tile

    def rows_at(i):
        return pl.ds(pl.multiple_of(i * tile, tile), tile)

    @pl.when(step == 0)
    def _():
        dft_ref[...] = ct_ref[...].T

        def start(i, carry):
            at = rows_at(i)
            y = x_ref[at, :].astype(f32) + nn(o_ref[at, :], wo_ref[...])
            unit, unused = normalize_rows(y)
            h_ref[at, :] = (unit * gain_ref[...] + offset_ref[...]).astype(bf16)
            y_ref[at, :] = y
            dh_ref[at, :] = jnp.zeros((tile, width), f32)
            return carry

        lax.fori_loop(0, tiles, start, 0)

    db1_ref[...] = jnp.zeros_like(db1_ref)

    def chunk(i, carry):
        at = rows_at(i)
        u = nn(h_ref[at, :], w1_ref[...]) + b1_ref[...]
        da = nt(ct_ref[at, :], w2_ref[...])
        area, density = gelu_parts(u)
        a = (u * area).astype(bf16)
        du = (da * (area + u * density)).astype(bf16)
        a_ref[at, :] = a
        du_ref[at, :] = du
        db1_ref[...] += jnp.sum(du.astype(f32), axis=0, keepdims=True)
        more = nn(a, w2_ref[...])

        @pl.when(step == 0)
        def _():
            dy_ref[at, :] = y_ref[at, :] + b2_ref[...] + more

        @pl.when(step > 0)
        def _():
            dy_ref[at, :] = dy_ref[at, :] + more

        dh_ref[at, :] = dh_ref[at, :] + nt(du, w1_ref[...])
        return carry

    lax.fori_loop(0, tiles, chunk, 0)
    dw1_ref[...] = tn(du_ref[...], h_ref[...]).astype(bf16)
    dw2_ref[...] = nn(dft_ref[...], a_ref[...]).astype(bf16)

    @pl.when(step == pl.num_programs(0) - 1)
    def _():
        db2_ref[...] = jnp.zeros_like(db2_ref)
        dgain_ref[...] = jnp.zeros_like(dgain_ref)
        doffset_ref[...] = jnp.zeros_like(doffset_ref)

        def finish(i, carry):
            at = rows_at(i)
            z_ref[at, :] = dy_ref[at, :].astype(bf16)
            unit, scale = normalize_rows(y_ref[at, :])
            dh = dh_ref[at, :]
            ct = ct_ref[at, :].astype(f32)
            dy = ct + norm_back(unit, scale, gain_ref[...], dh)
            dy_ref[at, :] = dy
            db2_ref[...] += jnp.sum(ct, axis=0, keepdims=True)
            doffset_ref[...] += jnp.sum(dh, axis=0, keepdims=True)
            dgain_ref[...] += jnp.sum(dh * unit, axis=0, keepdims=True)
            low = dy.astype(bf16)
            h_ref[at, :] = low
            do_ref[at, :] = nt(low, wo_ref[...]).astype(bf16)
            return carry

        lax.fori_loop(0, tiles, finish, 0)
        dwo_ref[...] = tn(h_ref[...], o_ref[...]).astype(bf16)


def branch(x, o, ct, wo, w1, b1, w2, b2, gain, offset, name):
    count, width = x.shape
    hidden = w1.shape[1]
    chunk = FF_CHUNK
    tile = min(count, 512)
    row = once((count, width))
    line = full((1, width))
    return pl.pallas_call(
        functools.partial(branch_kernel, tile),
        grid=(hidden // chunk,),
        in_specs=[
            row,
            row,
            row,
            once((width, width)),
            pl.BlockSpec((width, chunk), lambda j: (0, j)),
            pl.BlockSpec((1, chunk), lambda j: (0, j)),
            pl.BlockSpec((chunk, width), lambda j: (j, 0)),
            line,
            line,
            line,
        ],
        out_specs=[
            row,
            row,
            row,
            pl.BlockSpec((chunk, width), lambda j: (j, 0)),
            pl.BlockSpec((width, chunk), lambda j: (0, j)),
            full((width, width)),
            pl.BlockSpec((1, chunk), lambda j: (0, j)),
            line,
            line,
            line,
        ],
        out_shape=[
            jax.ShapeDtypeStruct((count, width), bf16),
            jax.ShapeDtypeStruct((count, width), f32),
            jax.ShapeDtypeStruct((count, width), bf16),
            jax.ShapeDtypeStruct((hidden, width), bf16),
            jax.ShapeDtypeStruct((width, hidden), bf16),
            jax.ShapeDtypeStruct((width, width), bf16),
            jax.ShapeDtypeStruct((1, hidden), f32),
            jax.ShapeDtypeStruct((1, width), f32),
            jax.ShapeDtypeStruct((1, width), f32),
            jax.ShapeDtypeStruct((1, width), f32),
        ],
        scratch_shapes=[
            pltpu.VMEM((count, width), f32),
            pltpu.VMEM((count, width), bf16),
            pltpu.VMEM((count, width), f32),
            pltpu.VMEM((width, count), bf16),
            pltpu.VMEM((count, chunk), bf16),
            pltpu.VMEM((count, chunk), bf16),
        ],
        compiler_params=params(),
        cost_estimate=pl.CostEstimate(
            flops=6 * count * width * (2 * hidden + width),
            bytes_accessed=8 * width * hidden + 16 * count * width,
            transcendentals=2 * count * hidden,
        ),
        name=name,
    )(x, o, ct, wo, w1, b1, w2, b2, gain, offset)


def local_backward_kernel(
    rows_count,
    group_rows,
    lengths,
    bucket_of,
    place,
    q_ref,
    k_ref,
    v_ref,
    do_ref,
    o_ref,
    extra_ref,
    gk_ref,
    gv_ref,
    dq_ref,
    dk_ref,
    dv_ref,
    dgk_ref,
    dgv_ref,
    edges,
    queries_ref,
    grads_ref,
    turned_ref,
):
    pair = pl.program_id(0)
    block = pl.program_id(1)

    @pl.when((pair == 0) & (block == 0))
    def _():
        read_edges(lengths, bucket_of, place, edges)

    @pl.when(block == 0)
    def _():
        dgk_ref[...] = jnp.zeros_like(dgk_ref)
        dgv_ref[...] = jnp.zeros_like(dgv_ref)

    slot_of, segment = row_numbers(place, edges, rows_count, group_rows, block)
    queries_ref[:, :LANES] = stack_pair(q_ref[...])
    queries_ref[:, LANES:] = extra_ref[...].reshape(2 * BLOCK, LANES)
    upstream = stack_pair(do_ref[...])
    attended = jnp.concatenate([o_ref[...], o_ref[...]], 0)
    centre = jnp.sum(upstream.astype(f32) * attended.astype(f32), axis=1, keepdims=True)
    lane = iota((2 * BLOCK, LANES), 1)
    grads_ref[:, :LANES] = upstream
    grads_ref[:, LANES:] = place_three(
        centre, lane, STAT_LANE, jnp.zeros((2 * BLOCK, LANES), f32)
    ).astype(bf16)

    def gradients(keys, key_columns, values):
        columns = iota(values.shape, 1)
        minus = jnp.where((columns >= STAT_LANE) & (columns < STAT_LANE + 3), -1.0, 0.0)
        weights = jnp.exp(nt(jnp.concatenate([keys, key_columns], 1), queries_ref[...]))
        along = nt(jnp.concatenate([values, minus.astype(bf16)], 1), grads_ref[...])
        score_grad = (weights * along).astype(bf16)
        value_grad = nn(weights.astype(bf16), grads_ref[:, :LANES])
        key_grad = nn(score_grad, queries_ref[:, :LANES])
        return key_grad, value_grad, tn(keys, score_grad)

    key_grad, value_grad, turned = gradients(
        k_ref[...], key_extra(slot_of, segment).astype(bf16), v_ref[...]
    )
    dk_ref[...] = key_grad
    dv_ref[...] = value_grad
    turned_ref[...] = turned

    def one_slot(slot, carry):
        @pl.when(slot_present(slot, place, edges, rows_count, group_rows, block))
        def _():
            at = pl.ds(pl.multiple_of(slot * GLOBALS, GLOBALS), GLOBALS)
            key_grad, value_grad, turned = gradients(
                gk_ref[at, :], global_key_extra(slot).astype(bf16), gv_ref[at, :]
            )
            dgk_ref[at, :] = dgk_ref[at, :] + key_grad
            dgv_ref[at, :] = dgv_ref[at, :] + value_grad
            turned_ref[...] = turned_ref[...] + turned

        return carry

    lax.fori_loop(0, SLOTS, one_slot, 0)
    both = jnp.concatenate([turned_ref[:HEAD_DIM, :BLOCK], turned_ref[HEAD_DIM:, BLOCK:]], 0)
    dq_ref[...] = both.T.astype(bf16)


def local_backward(scalars, rows_count, group_rows, q, k, v, do, o, extra, gk, gv):
    blocks = rows_count // BLOCK
    all_globals, width = gk.shape
    block_spec = pl.BlockSpec((BLOCK, LANES), lambda p, b, *unused: (b, p))
    pair_spec = pl.BlockSpec((all_globals, LANES), lambda p, b, *unused: (0, p))
    return pl.pallas_call(
        functools.partial(local_backward_kernel, rows_count, group_rows),
        grid_spec=pltpu.PrefetchScalarGridSpec(
            num_scalar_prefetch=3,
            grid=(PAIRS, blocks),
            in_specs=[block_spec] * 5
            + [pl.BlockSpec((2, BLOCK, LANES), lambda p, b, *unused: (p, b, 0))]
            + [pair_spec] * 2,
            out_specs=[block_spec] * 3 + [pair_spec] * 2,
            scratch_shapes=[
                pltpu.SMEM((16,), jnp.int32),
                pltpu.VMEM((2 * BLOCK, 2 * LANES), bf16),
                pltpu.VMEM((2 * BLOCK, 2 * LANES), bf16),
                pltpu.VMEM((LANES, 2 * BLOCK), f32),
            ],
        ),
        out_shape=[
            jax.ShapeDtypeStruct((rows_count, width), bf16),
            jax.ShapeDtypeStruct((rows_count, width), f32),
            jax.ShapeDtypeStruct((rows_count, width), f32),
            jax.ShapeDtypeStruct((all_globals, width), f32),
            jax.ShapeDtypeStruct((all_globals, width), f32),
        ],
        compiler_params=params(),
        cost_estimate=pl.CostEstimate(
            flops=40 * rows_count * (BLOCK + GLOBALS) * width,
            bytes_accessed=30 * rows_count * width,
            transcendentals=HEADS * rows_count * (BLOCK + GLOBALS),
        ),
        name="local_backward",
    )(*scalars, q, k, v, do, o, extra, gk, gv)


def global_backward_kernel(
    rows_count,
    group_rows,
    lengths,
    bucket_of,
    place,
    k_ref,
    v_ref,
    dk_ref,
    dv_ref,
    gq_ref,
    gk_ref,
    gv_ref,
    gdo_ref,
    gstat_ref,
    dgk_in_ref,
    dgv_in_ref,
    dk_out_ref,
    dv_out_ref,
    dgq_ref,
    dgk_ref,
    dgv_ref,
    edges,
    keys_ref,
    values_ref,
    dk_sum_ref,
    dv_sum_ref,
):
    pair = pl.program_id(0)
    block = pl.program_id(1)

    @pl.when((pair == 0) & (block == 0))
    def _():
        read_edges(lengths, bucket_of, place, edges)

    @pl.when(block == 0)
    def _():
        dgq_ref[...] = jnp.zeros_like(dgq_ref)
        dgk_ref[...] = dgk_in_ref[...].astype(bf16)
        dgv_ref[...] = dgv_in_ref[...].astype(bf16)

    slot_of, segment = row_numbers(place, edges, rows_count, group_rows, block)
    column = iota((BLOCK, LANES), 1)
    minus = jnp.where((column >= STAT_LANE) & (column < STAT_LANE + 3), -1.0, 0.0).astype(bf16)
    keys_ref[:, :LANES] = k_ref[...]
    keys_ref[:, LANES:] = key_extra(slot_of, segment).astype(bf16)
    values_ref[:, :LANES] = v_ref[...]
    values_ref[:, LANES:] = minus
    dk_sum_ref[...] = dk_ref[...]
    dv_sum_ref[...] = dv_ref[...]

    def gradients(slot, keys, values):
        at = pl.ds(pl.multiple_of(slot * GLOBALS, GLOBALS), GLOBALS)
        source = iota((LANES, LANES), 0)
        target = iota((LANES, LANES), 1)
        stats = gstat_ref[at, :]

        def moved(head, first):
            match = jnp.zeros((LANES, LANES), jnp.bool_)
            for piece in range(3):
                match = match | (
                    (target == STAT_LANE + piece) & (source == first + piece * HEADS + head)
                )
            return nn(stats, jnp.where(match, 1.0, 0.0).astype(bf16))

        extra = global_query_extra(slot)
        query_columns = jnp.concatenate(
            [moved(2 * pair, 0) + extra, moved(2 * pair + 1, 0) + extra], 0
        ).astype(bf16)
        grad_columns = jnp.concatenate(
            [moved(2 * pair, 3 * HEADS), moved(2 * pair + 1, 3 * HEADS)], 0
        ).astype(bf16)
        queries = stack_pair(gq_ref[at, :])
        upstream = stack_pair(gdo_ref[at, :])
        weights = jnp.exp(nt(keys, jnp.concatenate([queries, query_columns], 1)))
        along = nt(values, jnp.concatenate([upstream, grad_columns], 1))
        score_grad = (weights * along).astype(bf16)
        key_grad = nn(score_grad, queries)
        value_grad = nn(weights.astype(bf16), upstream)
        turned = tn(keys[:, :LANES], score_grad)
        turned = jnp.concatenate([turned[:HEAD_DIM, :GLOBALS], turned[HEAD_DIM:, GLOBALS:]], 0)
        dgq_ref[at, :] = dgq_ref[at, :] + turned.T
        return key_grad, value_grad

    def one_slot(slot, carry):
        @pl.when(slot_present(slot, place, edges, rows_count, group_rows, block))
        def _():
            key_grad, value_grad = gradients(slot, keys_ref[...], values_ref[...])
            dk_sum_ref[...] = dk_sum_ref[...] + key_grad
            dv_sum_ref[...] = dv_sum_ref[...] + value_grad

        return carry

    lax.fori_loop(0, SLOTS, one_slot, 0)
    dk_out_ref[...] = dk_sum_ref[...].astype(bf16)
    dv_out_ref[...] = dv_sum_ref[...].astype(bf16)

    @pl.when((block == pl.num_programs(1) - 1) & (place[2] >= 0))
    def _():
        slot = place[2]
        at = pl.ds(pl.multiple_of(slot * GLOBALS, GLOBALS), GLOBALS)
        keys = jnp.concatenate([gk_ref[at, :], global_key_extra(slot).astype(bf16)], axis=1)
        values = jnp.concatenate([gv_ref[at, :], minus[:GLOBALS]], axis=1)
        key_grad, value_grad = gradients(slot, keys, values)
        dgk_ref[at, :] = (dgk_in_ref[at, :] + key_grad).astype(bf16)
        dgv_ref[at, :] = (dgv_in_ref[at, :] + value_grad).astype(bf16)


def global_backward(scalars, rows_count, group_rows, k, v, dk, dv, gq, gk, gv, gdo, gstat, dgk, dgv):
    blocks = rows_count // BLOCK
    all_globals, width = gk.shape
    block_spec = pl.BlockSpec((BLOCK, LANES), lambda p, b, *unused: (b, p))
    pair_spec = pl.BlockSpec((all_globals, LANES), lambda p, b, *unused: (0, p))
    return pl.pallas_call(
        functools.partial(global_backward_kernel, rows_count, group_rows),
        grid_spec=pltpu.PrefetchScalarGridSpec(
            num_scalar_prefetch=3,
            grid=(PAIRS, blocks),
            in_specs=[block_spec] * 4
            + [pair_spec] * 4
            + [pl.BlockSpec((all_globals, LANES), lambda p, b, *unused: (0, 0))]
            + [pair_spec] * 2,
            out_specs=[block_spec] * 2 + [pair_spec] * 3,
            scratch_shapes=[
                pltpu.SMEM((16,), jnp.int32),
                pltpu.VMEM((BLOCK, 2 * LANES), bf16),
                pltpu.VMEM((BLOCK, 2 * LANES), bf16),
                pltpu.VMEM((BLOCK, LANES), f32),
                pltpu.VMEM((BLOCK, LANES), f32),
            ],
        ),
        out_shape=[
            jax.ShapeDtypeStruct((rows_count, width), bf16),
            jax.ShapeDtypeStruct((rows_count, width), bf16),
            jax.ShapeDtypeStruct((all_globals, width), f32),
            jax.ShapeDtypeStruct((all_globals, width), bf16),
            jax.ShapeDtypeStruct((all_globals, width), bf16),
        ],
        compiler_params=params(),
        cost_estimate=pl.CostEstimate(
            flops=40 * rows_count * GLOBALS * width,
            bytes_accessed=30 * rows_count * width,
            transcendentals=HEADS * rows_count * GLOBALS,
        ),
        name="global_backward",
    )(*scalars, k, v, dk, dv, gq, gk, gv, gdo, gstat, dgk, dgv)


def project_back_kernel(
    rows_count,
    group_rows,
    tile,
    lengths,
    bucket_of,
    place,
    x_ref,
    dy_ref,
    h_ref,
    dq_ref,
    dk_ref,
    dv_ref,
    gh_ref,
    dgq_ref,
    dgk_ref,
    dgv_ref,
    wq_ref,
    wk_ref,
    wv_ref,
    gain_ref,
    dx_ref,
    dgh_ref,
    dwq_ref,
    dwk_ref,
    dwv_ref,
    dgain_ref,
    doffset_ref,
    edges,
    sq_ref,
    sk_ref,
    sv_ref,
):
    read_edges(lengths, bucket_of, place, edges)
    count, width = x_ref.shape
    dgain_ref[...] = jnp.zeros_like(dgain_ref)
    doffset_ref[...] = jnp.zeros_like(doffset_ref)

    def back(dq, dk, dv):
        return nt(dq, wq_ref[...]) * query_scale + nt(dk, wk_ref[...]) + nt(dv, wv_ref[...])

    def one_tile(i, carry):
        at = pl.ds(pl.multiple_of(i * tile, tile), tile)
        dh = back(dq_ref[at, :], dk_ref[at, :], dv_ref[at, :])
        unit, scale = normalize_rows(x_ref[at, :].astype(f32))
        doffset_ref[...] += jnp.sum(dh, axis=0, keepdims=True)
        dgain_ref[...] += jnp.sum(dh * unit, axis=0, keepdims=True)
        dx_ref[at, :] = dy_ref[at, :] + norm_back(unit, scale, gain_ref[...], dh)
        return carry

    lax.fori_loop(0, count // tile, one_tile, 0)
    sums = (sq_ref, sk_ref, sv_ref)
    for target, source in zip(sums, (dq_ref, dk_ref, dv_ref)):
        target[...] = tn(source[...], h_ref[...])
    dgh_ref[...] = jnp.zeros_like(dgh_ref)

    def one_slot(slot, carry):
        needed = slot == place[2]
        for block in range(rows_count // BLOCK):
            needed = needed | slot_present(slot, place, edges, rows_count, group_rows, block)

        @pl.when(needed)
        def _():
            at = pl.ds(pl.multiple_of(slot * GLOBALS, GLOBALS), GLOBALS)
            grads = (dgq_ref[at, :].astype(bf16), dgk_ref[at, :], dgv_ref[at, :])
            for target, grad in zip(sums, grads):
                target[...] = target[...] + tn(grad, gh_ref[at, :])
            dgh_ref[at, :] = back(*grads).astype(bf16)

        return carry

    lax.fori_loop(0, SLOTS, one_slot, 0)
    dwq_ref[...] = (sq_ref[...] * query_scale).astype(bf16)
    dwk_ref[...] = sk_ref[...].astype(bf16)
    dwv_ref[...] = sv_ref[...].astype(bf16)


def project_back(scalars, group_rows, x, dy, h, dq, dk, dv, gh, dgq, dgk, dgv, wq, wk, wv, gain):
    count, width = x.shape
    all_globals = gh.shape[0]
    vmem = pl.BlockSpec(memory_space=pltpu.VMEM)
    smem = pl.BlockSpec(memory_space=pltpu.SMEM)
    return pl.pallas_call(
        functools.partial(project_back_kernel, count, group_rows, 512),
        in_specs=[smem] * 3 + [vmem] * 14,
        out_specs=[vmem] * 7,
        scratch_shapes=[pltpu.SMEM((16,), jnp.int32)] + [pltpu.VMEM((width, width), f32)] * 3,
        out_shape=[
            jax.ShapeDtypeStruct((count, width), f32),
            jax.ShapeDtypeStruct((all_globals, width), bf16),
            jax.ShapeDtypeStruct((width, width), bf16),
            jax.ShapeDtypeStruct((width, width), bf16),
            jax.ShapeDtypeStruct((width, width), bf16),
            jax.ShapeDtypeStruct((1, width), f32),
            jax.ShapeDtypeStruct((1, width), f32),
        ],
        compiler_params=params(),
        cost_estimate=pl.CostEstimate(
            flops=12 * count * width * width, bytes_accessed=30 * count * width, transcendentals=0
        ),
        name="project_back",
    )(*scalars, x, dy, h, dq, dk, dv, gh, dgq, dgk, dgv, wq, wk, wv, gain)


def from_behind(value, axis, steps):
    count = lax.axis_size(axis)
    pairs = [(source, (source + steps) % count) for source in range(count)]
    return lax.ppermute(value, axis, pairs)


def pieces(value):
    first = lax.reduce_precision(value, 8, 7)
    second = lax.reduce_precision(value - first, 8, 7)
    return [first.astype(bf16), second.astype(bf16), (value - first - second).astype(bf16)]


def scatter_sum(value):
    half = lax.psum_scatter(value, "batch", scatter_dimension=1, tiled=True)
    part = lax.psum_scatter(half, "seq", scatter_dimension=0, tiled=True)
    return part.T.astype(f32)


def on_device(
    tokens,
    global_states,
    lengths,
    bucket_of,
    wq,
    wk,
    wv,
    wo,
    w1,
    b1,
    w2,
    b2,
    norm_params,
    cotangent,
    global_cotangent,
):
    rows = tokens.shape[1]
    width = tokens.shape[2]
    own = global_states.shape[1]
    seq_count = lax.axis_size("seq")
    seq_place = lax.axis_index("seq")
    group_rows = rows * seq_count
    own_start = seq_place * own
    first_of_slot = own_start % GLOBALS == 0
    place = jnp.stack(
        [
            lax.axis_index("batch"),
            seq_place,
            jnp.where(first_of_slot, own_start // GLOBALS, -1),
        ]
    ).astype(jnp.int32)
    scalars = (lengths, bucket_of, place)
    norms = [norm_params[i : i + 1] for i in range(6)]
    b1_line = b1[None]
    b2_line = b2[None]

    arrived_tokens, arrived_grads = from_behind(
        (tokens[0, rows - HALF :], cotangent[0, rows - HALF :]), "seq", 1
    )
    x = jnp.concatenate([arrived_tokens, tokens[0, : rows - HALF]], 0)
    ct = jnp.concatenate([arrived_grads, cotangent[0, : rows - HALF]], 0)
    all_states = lax.all_gather(global_states[0], "seq", axis=0, tiled=True)

    h, q, k, v = project_local(x, norms[0], norms[1], wq, wk, wv)
    gh, gq, gk, gv = project_global(
        scalars, rows, group_rows, all_states, norms[2], norms[3], wq, wk, wv
    )
    part_sum, part_peak, part_total = global_forward(scalars, rows, group_rows, k, v, gq, gk, gv)

    def by_head(value):
        value = value.reshape(PAIRS, SLOTS, 2, GLOBALS).transpose(0, 2, 1, 3)
        return value.reshape(HEADS, SLOTS * GLOBALS)

    part_peak = by_head(part_peak)
    peak = jnp.max(lax.all_gather(part_peak, "seq"), axis=0)
    o, extra = local_forward(scalars, rows, group_rows, q, k, v, gk, gv)
    factor = jnp.exp(part_peak - peak)
    scaled = (part_sum.reshape(HEADS, HEAD_DIM, -1) * factor[:, None, :]).reshape(width, -1)
    payload = jnp.concatenate([scaled, by_head(part_total) * factor, jnp.zeros((4, scaled.shape[1]), f32)], 0)
    sums = lax.psum_scatter(
        payload.astype(bf16).T, "seq", scatter_dimension=0, tiled=True
    ).astype(f32)
    own_total = sums[:, width : width + HEADS]
    own_peak = lax.dynamic_slice_in_dim(peak, own_start, own, 1).T
    go = (
        (sums[:, :width].reshape(own, HEADS, HEAD_DIM) / own_total[:, :, None])
        .reshape(own, width)
        .astype(bf16)
    )
    gstat = own_peak + jnp.log(own_total)

    z, dy, do, dw1, dw2, dwo, db1, db2, dgain2, doffset2 = branch(
        x, o, ct, wo, w1, b1_line, w2, b2_line, norms[4], norms[5], "branch_local"
    )
    gz, gdy, gdo, gdw1, gdw2, gdwo, gdb1, gdb2, gdgain2, gdoffset2 = branch(
        global_states[0],
        go,
        global_cotangent[0],
        wo,
        w1,
        b1_line,
        w2,
        b2_line,
        norms[4],
        norms[5],
        "branch_global",
    )
    gcentre = jnp.sum(
        (gdo.astype(f32) * go.astype(f32)).reshape(own, HEADS, HEAD_DIM), axis=-1
    )
    message = jnp.concatenate(
        [gdo]
        + pieces(gstat)
        + pieces(gcentre)
        + [jnp.zeros((own, LANES - 6 * HEADS), bf16)],
        axis=1,
    )
    everyone = lax.all_gather(message, "seq", axis=0, tiled=True)
    dq, dk, dv, dgk, dgv = local_backward(
        scalars, rows, group_rows, q, k, v, do, o, extra, gk, gv
    )
    dk, dv, dgq, dgk, dgv = global_backward(
        scalars,
        rows,
        group_rows,
        k,
        v,
        dk,
        dv,
        gq,
        gk,
        gv,
        everyone[:, :width],
        everyone[:, width:],
        dgk,
        dgv,
    )
    dx, dgh, dwq, dwk, dwv, dgain1, doffset1 = project_back(
        scalars, group_rows, x, dy, h, dq, dk, dv, gh, dgq, dgk, dgv, wq, wk, wv, norms[0]
    )
    dgh = lax.psum_scatter(dgh, "seq", scatter_dimension=0, tiled=True).astype(f32)
    gunit, gscale = normalize_rows(global_states[0].astype(f32))
    global_grad = gdy + norm_back(gunit, gscale, norms[2], dgh)
    norm_grad = jnp.concatenate(
        [
            dgain1,
            doffset1,
            jnp.sum(dgh * gunit, axis=0, keepdims=True),
            jnp.sum(dgh, axis=0, keepdims=True),
            dgain2 + gdgain2,
            doffset2 + gdoffset2,
        ],
        0,
    )
    back_z, back_grad = from_behind((z[:HALF], dx[:HALF].astype(bf16)), "seq", -1)
    layer_out = jnp.concatenate([z[HALF:], back_z], 0)
    token_grad = jnp.concatenate([dx[HALF:], back_grad.astype(f32)], 0)
    small = lax.psum((db1[0] + gdb1[0], db2[0] + gdb2[0], norm_grad), ("batch", "seq"))
    return (
        layer_out[None],
        gz[None],
        token_grad[None],
        global_grad[None],
        scatter_sum(dwq),
        scatter_sum(dwk),
        scatter_sum(dwv),
        scatter_sum(dwo + gdwo),
        scatter_sum(dw1 + gdw1),
        scatter_sum(dw2 + gdw2),
        small[0],
        small[1],
        small[2],
    )


def solution(mesh):
    split = P("batch", "seq", None)
    return jax.shard_map(
        on_device,
        mesh=mesh,
        in_specs=(split, split) + (P(),) * 11 + (split, split),
        out_specs=(split,) * 4 + (P("batch", "seq"),) * 6 + (P(),) * 3,
        check_vma=False,
    )
```

```python
import functools

import jax
import jax.numpy as jnp
from jax import lax
from jax.experimental import pallas as pl
from jax.experimental.pallas import tpu as pltpu
from jax.sharding import PartitionSpec as P

HEADS = 12
HEAD_DIM = 64
PAIRS = HEADS // 2
LANES = 128
BLOCK = 512
HALF = 256
GLOBALS = 128
SLOTS = 8
FF_CHUNK = 768

norm_eps = 1e-05
masked_score = -1e30
query_scale = 0.125

SLOT_LANE = 16
GLOBAL_LANE = 32

f32 = jnp.float32
bf16 = jnp.bfloat16
VMEM_LIMIT = 60 * 1024 * 1024


def nn(left, right):
    return jnp.dot(left, right, preferred_element_type=f32)


def nt(left, right):
    return lax.dot_general(left, right, (((1,), (1,)), ((), ())), preferred_element_type=f32)


def tn(left, right):
    return lax.dot_general(left, right, (((0,), (0,)), ((), ())), preferred_element_type=f32)


def iota(shape, dim):
    return lax.broadcasted_iota(jnp.int32, shape, dim)


def stack_pair(pair):
    lane = iota((1, LANES), 1)
    low = jnp.where(lane < HEAD_DIM, 1.0, 0.0).astype(bf16)
    high = jnp.where(lane < HEAD_DIM, 0.0, 1.0).astype(bf16)
    return jnp.concatenate([pair * low, pair * high], axis=0)


def read_edges(lengths, bucket_of, place, edges):
    bucket = bucket_of[place[0]]
    total = jnp.int32(0)
    edges[0] = total
    for slot in range(SLOTS):
        total = total + lengths[bucket, slot]
        edges[slot + 1] = total


def block_start(place, rows, block):
    return place[1] * rows + block * BLOCK - HALF


def slot_present(slot, place, edges, rows, group_rows, block):
    low = edges[slot]
    high = edges[slot + 1]
    found = jnp.bool_(False)
    for part in range(BLOCK // HALF):
        start = block_start(place, rows, block) + part * HALF
        start = jnp.where(start < 0, start + group_rows, start)
        found = found | ((high > low) & (low < start + HALF) & (high > start))
    return found


def row_numbers(place, edges, rows, group_rows, block):
    place_in = block_start(place, rows, block) + iota((BLOCK, LANES), 0)
    wrapped = place_in < 0
    token = jnp.where(wrapped, place_in + group_rows, place_in)
    slot = jnp.zeros((BLOCK, LANES), jnp.int32)
    for j in range(SLOTS):
        slot = slot + jnp.where(edges[j + 1] <= token, 1, 0)
    return slot, slot + jnp.where(wrapped, SLOTS, 0)


def key_extra(slot, segment):
    lane = iota((BLOCK, LANES), 1)
    extra = jnp.where((lane < SLOT_LANE) & (lane != segment), masked_score, 0.0)
    return jnp.where(lane == GLOBAL_LANE + slot, 1.0, extra)


def query_extra(slot, segment):
    lane = iota((BLOCK, LANES), 1)
    return jnp.where((lane == segment) | (lane == SLOT_LANE + slot), 1.0, 0.0)


def global_key_extra(slot):
    lane = iota((GLOBALS, LANES), 1)
    inside = (lane >= SLOT_LANE) & (lane < SLOT_LANE + SLOTS)
    extra = jnp.where(inside & (lane != SLOT_LANE + slot), masked_score, 0.0)
    return jnp.where(lane == GLOBAL_LANE + slot, 1.0, extra)


def global_query_extra(slot):
    lane = iota((GLOBALS, LANES), 1)
    inside = (lane >= GLOBAL_LANE) & (lane < GLOBAL_LANE + SLOTS)
    return jnp.where(inside & (lane != GLOBAL_LANE + slot), masked_score, 0.0)


def normalize_rows(values):
    mean = jnp.mean(values, axis=-1, keepdims=True)
    centered = values - mean
    variance = jnp.mean(centered * centered, axis=-1, keepdims=True)
    scale = lax.rsqrt(variance + norm_eps)
    return centered * scale, scale


def norm_back(unit, scale, gain, upstream):
    inner = upstream * gain
    along = jnp.mean(inner * unit, axis=-1, keepdims=True)
    return scale * (inner - jnp.mean(inner, axis=-1, keepdims=True) - unit * along)


def gelu_parts(value):
    decay = jnp.exp(-0.5 * value * value)
    step = 1.0 / (1.0 + (0.3275911 * 0.7071067811865476) * jnp.abs(value))
    series = 1.061405429 * step - 1.453152027
    series = series * step + 1.421413741
    series = series * step - 0.284496736
    series = series * step + 0.254829592
    tail = (0.5 * series) * step * decay
    area = jnp.where(value >= 0.0, 1.0 - tail, tail)
    return area, decay * 0.3989422804014327


def full(shape):
    return pl.BlockSpec(shape, lambda *unused: (0,) * len(shape))


def once(shape):
    return pl.BlockSpec(
        shape, lambda *unused: (0,) * len(shape), pipeline_mode=pl.Buffered(buffer_count=1)
    )


def params(**more):
    return pltpu.CompilerParams(vmem_limit_bytes=VMEM_LIMIT, **more)


STAGES = 5
MESH = pl.DeviceIdType.MESH
WEIGHTS = (("core", 1), ("y", 2), ("z0", 4), ("z1", 8))


def my_place():
    batch = lax.axis_index("batch")
    seq = lax.axis_index("seq")
    bits = {"x": batch}
    partners = {"x": (1 - batch, seq)}
    for name, weight in WEIGHTS:
        bits[name] = (seq // weight) % 2
        partners[name] = (batch, seq + weight - 2 * weight * bits[name])
    return bits, partners


def meet(devices):
    barrier = pltpu.get_barrier_semaphore()
    for device in devices:
        pl.semaphore_signal(barrier, inc=1, device_id=device, device_id_type=MESH)
    pl.semaphore_wait(barrier, len(devices))


def remote(source, target, send, recv, device):
    return pltpu.make_async_remote_copy(
        src_ref=source,
        dst_ref=target,
        send_sem=send,
        recv_sem=recv,
        device_id=device,
        device_id_type=MESH,
    )


class RowGather:
    def __init__(self, ref, cut, send_sem, recv_sem, bits, partners):
        self.ref = ref
        self.cut = cut
        self.send_sem = send_sem
        self.recv_sem = recv_sem
        self.bits = bits
        self.partners = partners

    def copies(self, number):
        core, y, z0, z1 = (self.bits[name] for name in ("core", "y", "z0", "z1"))
        ref = self.ref
        rows = pl.ds(0, ref.shape[4])
        left = pl.ds(0, self.cut)
        right = pl.ds(self.cut, ref.shape[5] - self.cut)
        if number == 0:
            moves = [
                (ref.at[z1, z0, y, core, rows, left], "z1"),
                (ref.at[z1, z0, y, core, rows, right], "y"),
            ]
        elif number == 1:
            moves = [
                (ref.at[:, z0, y, core, rows, left], "z0"),
                (ref.at[z1, z0, :, core, rows, right], "z1"),
            ]
        elif number == 2:
            moves = [
                (ref.at[:, :, y, core, rows, left], "y"),
                (ref.at[:, z0, :, core, rows, right], "z0"),
            ]
        else:
            moves = [
                (ref.at[:, :, :, core, rows, left], "core"),
                (ref.at[:, :, :, core, rows, right], "core"),
            ]
        return [
            remote(
                part,
                part,
                self.send_sem.at[number, side],
                self.recv_sem.at[number, side],
                self.partners[name],
            )
            for side, (part, name) in enumerate(moves)
        ]

    def begin(self):
        for copy in self.copies(0):
            copy.start()

    def advance(self, number):
        for copy in self.copies(number):
            copy.wait_recv()
        if number < 3:
            for copy in self.copies(number + 1):
                copy.start()

    def end(self):
        for number in range(4):
            for copy in self.copies(number):
                copy.wait_send()


ORDERS = (("core", "x", "y", "z0", "z1"), ("core", "y", "x", "z0", "z1"))


class WeightSum:
    def __init__(self, sources, landings, own, send_sem, recv_sem, own_sem, out, bits, partners):
        self.sources = sources
        self.landings = landings
        self.own = own
        self.send_sem = send_sem
        self.recv_sem = recv_sem
        self.own_sem = own_sem
        self.out = out
        self.bits = bits
        self.partners = partners

    def part(self, unit, stage, other):
        name = ORDERS[unit % 2][stage]
        side = 1 - self.bits[name] if other else self.bits[name]
        if stage == 0:
            if not other and self.own is not None:
                return self.own.at[unit]
            return self.sources[unit](side)
        ref = self.landings[stage - 1].at[unit]
        if stage == 1:
            return ref.at[:, :, :, side] if name == "x" else ref.at[:, :, side]
        if stage == 2:
            return ref.at[:, :, side]
        if stage == 3:
            return ref.at[:, side]
        return ref.at[side]

    def copy(self, unit, stage):
        return remote(
            self.part(unit, stage, True),
            self.landings[stage].at[unit],
            self.send_sem.at[unit, stage],
            self.recv_sem.at[unit, stage],
            self.partners[ORDERS[unit % 2][stage]],
        )

    def own_copy(self, unit):
        return pltpu.make_async_copy(
            self.sources[unit](self.bits["core"]), self.own.at[unit], self.own_sem.at[unit]
        )

    def begin(self, unit):
        if self.own is not None:
            self.own_copy(unit).start()
        self.copy(unit, 0).start()

    def advance(self, unit, stage, stop=False):
        if stage == 0 and self.own is not None:
            self.own_copy(unit).wait()
        self.copy(unit, stage).wait_recv()
        landing = self.landings[stage].at[unit]
        kept = self.part(unit, stage, False)
        if stage < STAGES - 1:
            add_into(landing, kept)
            if not stop:
                self.copy(unit, stage + 1).start()
        else:
            rows = landing.shape[0]
            self.out[unit * rows : (unit + 1) * rows] = landing[...].astype(f32) + kept[
                ...
            ].astype(f32)

    def sent(self, unit, stage):
        self.copy(unit, stage).wait_send()


def add_into(target, more):
    def one(i, carry):
        target[i] = target[i] + more[i]
        return carry

    lax.fori_loop(0, target.shape[0], one, 0)


def sum_scratch(units, rows, lanes, with_own):
    piece = (rows, lanes)
    dma = pltpu.SemaphoreType.DMA
    shapes = [pltpu.VMEM((units, 2, 2, 2, 2) + piece, bf16)] if with_own else []
    shapes += [
        pltpu.VMEM((units, 2, 2, 2, 2) + piece, bf16),
        pltpu.VMEM((units, 2, 2, 2) + piece, bf16),
        pltpu.VMEM((units, 2, 2) + piece, bf16),
        pltpu.VMEM((units, 2) + piece, bf16),
        pltpu.VMEM((units,) + piece, bf16),
        dma((units, STAGES)),
        dma((units, STAGES)),
    ]
    return shapes + ([dma((units,))] if with_own else [])


def project_rows(rows_ref, gain_ref, offset_ref, wq_ref, wk_ref, wv_ref, outs):
    unit, unused = normalize_rows(rows_ref[...].astype(f32))
    normed = (unit * gain_ref[...] + offset_ref[...]).astype(bf16)
    outs[0][...] = normed
    outs[1][...] = (nn(normed, wq_ref[...]) * query_scale).astype(bf16)
    outs[2][...] = nn(normed, wk_ref[...]).astype(bf16)
    outs[3][...] = nn(normed, wv_ref[...]).astype(bf16)


def project_local_kernel(rows_ref, gain_ref, offset_ref, wq_ref, wk_ref, wv_ref, *outs):
    project_rows(rows_ref, gain_ref, offset_ref, wq_ref, wk_ref, wv_ref, outs)


def project_local(rows, gain, offset, wq, wk, wv):
    count, width = rows.shape
    tile = pl.BlockSpec((BLOCK, width), lambda i: (i, 0))
    return pl.pallas_call(
        project_local_kernel,
        grid=(count // BLOCK,),
        in_specs=[tile, full((1, width)), full((1, width))] + [once((width, width))] * 3,
        out_specs=[tile] * 4,
        out_shape=[jax.ShapeDtypeStruct((count, width), bf16)] * 4,
        compiler_params=params(),
        cost_estimate=pl.CostEstimate(
            flops=6 * count * width * width, bytes_accessed=12 * count * width, transcendentals=0
        ),
        name="project_local",
    )(rows, gain, offset, wq, wk, wv)


def gather_project_kernel(
    tokens_ref,
    ct_ref,
    states_ref,
    w1_ref,
    norms_ref,
    wq_ref,
    wk_ref,
    wv_ref,
    h_ref,
    q_ref,
    k_ref,
    v_ref,
    x_ref,
    ct_out_ref,
    all_ref,
    gh_ref,
    gq_ref,
    gk_ref,
    gv_ref,
    w1t_ref,
    w1s_ref,
    halo_send,
    halo_recv,
    move_sem,
    w1_sem,
    send_sem,
    recv_sem,
):
    bits, partners = my_place()
    batch = lax.axis_index("batch")
    seq = lax.axis_index("seq")
    count = lax.axis_size("seq")
    after = (batch, lax.rem(seq + 1, count))
    before = (batch, lax.rem(seq + count - 1, count))
    rows, width = tokens_ref.shape
    own = states_ref.shape[0]
    core, y, z0, z1 = (bits[name] for name in ("core", "y", "z0", "z1"))
    w1_copy = pltpu.make_async_copy(w1_ref, w1s_ref, w1_sem)
    w1_copy.start()
    ct_copy = pltpu.make_async_copy(
        ct_ref.at[pl.ds(0, rows - HALF)], ct_out_ref.at[pl.ds(HALF, rows - HALF)], move_sem
    )
    ct_copy.start()
    all_ref[z1, z0, y, core] = states_ref[...]
    meet([partners[name] for name, unused in WEIGHTS] + [before, after])
    end = pl.ds(rows - HALF, HALF)
    start = pl.ds(0, HALF)
    halo = [
        remote(
            tokens_ref.at[end], x_ref.at[start], halo_send.at[0], halo_recv.at[0], after
        ),
        remote(
            ct_ref.at[end], ct_out_ref.at[start], halo_send.at[1], halo_recv.at[1], after
        ),
    ]
    halo[0].start()

    gather = RowGather(all_ref, width // 2, send_sem, recv_sem, bits, partners)

    def project(at):
        project_rows(
            x_ref.at[at],
            norms_ref.at[0:1],
            norms_ref.at[1:2],
            wq_ref,
            wk_ref,
            wv_ref,
            [ref.at[at] for ref in (h_ref, q_ref, k_ref, v_ref)],
        )

    gather.begin()
    halo[1].start()
    x_ref[HALF:] = tokens_ref[: rows - HALF]
    project(pl.ds(HALF, HALF))
    gather.advance(0)
    project(pl.ds(2 * HALF, HALF))
    for index in range(3, rows // HALF):
        project(pl.ds(index * HALF, HALF))
    gather.advance(1)
    halo[0].wait_recv()
    project(start)
    w1_copy.wait()

    def turn(i, carry):
        at = pl.ds(pl.multiple_of(i * HALF, HALF), HALF)
        w1t_ref[at, :] = w1s_ref[:, at].T
        return carry

    lax.fori_loop(0, w1t_ref.shape[0] // HALF, turn, 0)
    gather.advance(2)
    gather.advance(3)

    def project_states(i, carry):
        at = pl.ds(pl.multiple_of(i * HALF, HALF), HALF)
        piece = all_ref[i // 2, i % 2].reshape(HALF, width)
        unit, unused = normalize_rows(piece.astype(f32))
        normed = (unit * norms_ref[2:3] + norms_ref[3:4]).astype(bf16)
        gh_ref[at, :] = normed
        gq_ref[at, :] = (nn(normed, wq_ref[...]) * query_scale).astype(bf16)
        gk_ref[at, :] = nn(normed, wk_ref[...]).astype(bf16)
        gv_ref[at, :] = nn(normed, wv_ref[...]).astype(bf16)
        return carry

    lax.fori_loop(0, 4, project_states, 0)
    ct_copy.wait()
    halo[1].wait_recv()
    for copy in halo:
        copy.wait_send()
    gather.end()


def gather_project(tokens, ct, states, w1, norms, wq, wk, wv):
    rows, width = tokens.shape
    own = states.shape[0]
    all_globals = 16 * own
    vmem = pl.BlockSpec(memory_space=pltpu.VMEM)
    anywhere = pl.BlockSpec(memory_space=pl.ANY)
    dma = pltpu.SemaphoreType.DMA
    local = jax.ShapeDtypeStruct((rows, width), bf16)
    glob = jax.ShapeDtypeStruct((all_globals, width), bf16)
    return pl.pallas_call(
        gather_project_kernel,
        in_specs=[vmem, anywhere, vmem, anywhere] + [vmem] * 4,
        out_specs=[vmem] * 5 + [anywhere] + [vmem] * 6,
        out_shape=[local] * 6
        + [jax.ShapeDtypeStruct((2, 2, 2, 2, own, width), bf16)]
        + [glob] * 4
        + [jax.ShapeDtypeStruct((w1.shape[1], width), bf16)],
        scratch_shapes=[
            pltpu.VMEM(w1.shape, bf16),
            dma((2,)),
            dma((2,)),
            dma,
            dma,
            dma((4, 2)),
            dma((4, 2)),
        ],
        compiler_params=params(collective_id=1, has_side_effects=True),
        cost_estimate=pl.CostEstimate(
            flops=6 * (rows + all_globals) * width * width,
            bytes_accessed=24 * rows * width,
            transcendentals=0,
        ),
        name="gather_project",
    )(tokens, ct, states, w1, norms, wq, wk, wv)


def project_global_kernel(
    rows_count,
    group_rows,
    lengths,
    bucket_of,
    place,
    rows_ref,
    gain_ref,
    offset_ref,
    wq_ref,
    wk_ref,
    wv_ref,
    h_ref,
    q_ref,
    k_ref,
    v_ref,
    edges,
):
    slot = pl.program_id(0)

    @pl.when(slot == 0)
    def _():
        read_edges(lengths, bucket_of, place, edges)

    needed = slot == place[2]
    for block in range(rows_count // BLOCK):
        needed = needed | slot_present(slot, place, edges, rows_count, group_rows, block)

    @pl.when(needed)
    def _():
        project_rows(
            rows_ref, gain_ref, offset_ref, wq_ref, wk_ref, wv_ref, (h_ref, q_ref, k_ref, v_ref)
        )


def project_global(scalars, rows_count, group_rows, rows, gain, offset, wq, wk, wv):
    count, width = rows.shape
    tile = pl.BlockSpec((GLOBALS, width), lambda i, *unused: (i, 0))
    return pl.pallas_call(
        functools.partial(project_global_kernel, rows_count, group_rows),
        grid_spec=pltpu.PrefetchScalarGridSpec(
            num_scalar_prefetch=3,
            grid=(SLOTS,),
            in_specs=[tile, full((1, width)), full((1, width))] + [once((width, width))] * 3,
            out_specs=[tile] * 4,
            scratch_shapes=[pltpu.SMEM((16,), jnp.int32)],
        ),
        out_shape=[jax.ShapeDtypeStruct((count, width), bf16)] * 4,
        compiler_params=params(),
        cost_estimate=pl.CostEstimate(
            flops=6 * 256 * width * width, bytes_accessed=12 * count * width, transcendentals=0
        ),
        name="project_global",
    )(*scalars, rows, gain, offset, wq, wk, wv)


def block_columns(place, edges, rows, group_rows, block, step, blocks, query_columns, key_columns):
    @pl.when(step < blocks)
    def _():
        slot_of, segment = row_numbers(place, edges, rows, group_rows, block)
        query_columns[block] = query_extra(slot_of, segment).astype(bf16)
        key_columns[block] = key_extra(slot_of, segment).astype(bf16)


def slot_line(place, edges, rows, group_rows, block):
    token = block_start(place, rows, block) + iota((1, BLOCK), 1)
    token = jnp.where(token < 0, token + group_rows, token)
    slot = jnp.zeros((1, BLOCK), jnp.int32)
    for j in range(SLOTS):
        slot = slot + jnp.where(edges[j + 1] <= token, 1, 0)
    return slot


def side_by_side(stacked):
    return stacked[:HEAD_DIM, : stacked.shape[1] // 2], stacked[HEAD_DIM:, stacked.shape[1] // 2 :]


def slot_forward_kernel(
    rows_count,
    group_rows,
    lengths,
    bucket_of,
    place,
    q_ref,
    k_ref,
    v_ref,
    gq_ref,
    gk_ref,
    gv_ref,
    far_ref,
    far_stat_ref,
    part_ref,
    part_stat_ref,
    edges,
    query_columns,
    key_columns,
    keys_ref,
    queries_ref,
    sum_ref,
):
    pair = pl.program_id(0)
    block = pl.program_id(1)
    blocks = rows_count // BLOCK
    step = pair * blocks + block

    @pl.when(step == 0)
    def _():
        read_edges(lengths, bucket_of, place, edges)

    @pl.when(block == 0)
    def _():
        sum_ref[...] = jnp.zeros_like(sum_ref)
        part_stat_ref[...] = jnp.broadcast_to(
            jnp.where(iota((8, GLOBALS), 0) < 2, masked_score, 0.0), part_stat_ref.shape
        )

    block_columns(
        place, edges, rows_count, group_rows, block, step, blocks, query_columns, key_columns
    )
    extra = query_columns[block]
    keys_ref[:, :LANES] = k_ref[...]
    keys_ref[:, LANES:] = key_columns[block]
    queries_ref[:, :LANES] = stack_pair(q_ref[...])
    queries_ref[:BLOCK, LANES:] = extra
    queries_ref[BLOCK:, LANES:] = extra
    line = slot_line(place, edges, rows_count, group_rows, block)
    both_lines = jnp.concatenate([line, line], 1)

    def add(slot, keys, values):
        at = pl.ds(pl.multiple_of(slot * GLOBALS, GLOBALS), GLOBALS)
        extra = global_query_extra(slot).astype(bf16)
        queries = jnp.concatenate(
            [stack_pair(gq_ref[at, :]), jnp.concatenate([extra, extra], 0)], axis=1
        )
        score = nt(keys, queries)
        stat = part_stat_ref[slot, 0]
        old = jnp.concatenate([stat[0:1], stat[1:2]], axis=1)
        peak = jnp.maximum(old, jnp.max(score, axis=0, keepdims=True))
        weights = jnp.exp(score - peak)
        keep = jnp.exp(old - peak)
        total = jnp.concatenate([stat[2:3], stat[3:4]], axis=1) * keep + jnp.sum(
            weights, axis=0, keepdims=True
        )
        part_stat_ref[slot, 0] = jnp.concatenate(
            [
                peak[:, :GLOBALS],
                peak[:, GLOBALS:],
                total[:, :GLOBALS],
                total[:, GLOBALS:],
                jnp.zeros((4, GLOBALS), f32),
            ],
            axis=0,
        )
        low, high = side_by_side(tn(values, weights.astype(bf16)))
        sum_ref[slot, :HEAD_DIM] = sum_ref[slot, :HEAD_DIM] * keep[:, :GLOBALS] + low
        sum_ref[slot, HEAD_DIM:] = sum_ref[slot, HEAD_DIM:] * keep[:, GLOBALS:] + high

    far_ref[...] = jnp.zeros_like(far_ref)
    far_stat_ref[...] = jnp.zeros_like(far_stat_ref)

    def one_slot(slot, carry):
        @pl.when(slot_present(slot, place, edges, rows_count, group_rows, block))
        def _():
            add(slot, keys_ref[...], v_ref[...])
            at = pl.ds(pl.multiple_of(slot * GLOBALS, GLOBALS), GLOBALS)
            slot_keys = jnp.concatenate([gk_ref[at, :], global_key_extra(slot).astype(bf16)], 1)
            score = nt(slot_keys, queries_ref[...])
            peak = jnp.max(score, axis=0, keepdims=True)
            weights = jnp.exp(score - peak)
            total = jnp.sum(weights, axis=0, keepdims=True)
            mine = both_lines == slot
            far_stat_ref[0, 0, 0:1] = jnp.where(mine, peak, far_stat_ref[0, 0, 0:1])
            far_stat_ref[0, 0, 1:2] = jnp.where(mine, total, far_stat_ref[0, 0, 1:2])
            low, high = side_by_side(tn(gv_ref[at, :], weights.astype(bf16)))
            here = line == slot
            far_ref[:HEAD_DIM] = jnp.where(here, low, far_ref[:HEAD_DIM])
            far_ref[HEAD_DIM:] = jnp.where(here, high, far_ref[HEAD_DIM:])

        return carry

    lax.fori_loop(0, SLOTS, one_slot, 0)

    @pl.when((block == blocks - 1) & (place[2] >= 0))
    def _():
        slot = place[2]
        at = pl.ds(pl.multiple_of(slot * GLOBALS, GLOBALS), GLOBALS)
        keys = jnp.concatenate([gk_ref[at, :], global_key_extra(slot).astype(bf16)], axis=1)
        add(slot, keys, gv_ref[at, :])

    @pl.when(block == blocks - 1)
    def _():
        part_ref[:, 0] = sum_ref[...].astype(bf16)


def line_spec():
    return pl.BlockSpec((1, 1, 8, 2 * BLOCK), lambda p, b, *unused: (p, b, 0, 0))


def column_scratch(blocks):
    return [pltpu.SMEM((16,), jnp.int32)] + [pltpu.VMEM((blocks, BLOCK, LANES), bf16)] * 2


def slot_forward(scalars, rows_count, group_rows, q, k, v, gq, gk, gv):
    blocks = rows_count // BLOCK
    all_globals, width = gq.shape
    block_spec = pl.BlockSpec((BLOCK, LANES), lambda p, b, *unused: (b, p))
    pair_spec = pl.BlockSpec((all_globals, LANES), lambda p, b, *unused: (0, p))
    return pl.pallas_call(
        functools.partial(slot_forward_kernel, rows_count, group_rows),
        grid_spec=pltpu.PrefetchScalarGridSpec(
            num_scalar_prefetch=3,
            grid=(PAIRS, blocks),
            in_specs=[block_spec] * 3 + [pair_spec] * 3,
            out_specs=[
                pl.BlockSpec((LANES, BLOCK), lambda p, b, *unused: (p, b)),
                line_spec(),
                pl.BlockSpec((SLOTS, 1, LANES, GLOBALS), lambda p, b, *unused: (0, p, 0, 0)),
                pl.BlockSpec((SLOTS, 1, 8, GLOBALS), lambda p, b, *unused: (0, p, 0, 0)),
            ],
            scratch_shapes=column_scratch(blocks)
            + [
                pltpu.VMEM((BLOCK, 2 * LANES), bf16),
                pltpu.VMEM((2 * BLOCK, 2 * LANES), bf16),
                pltpu.VMEM((SLOTS, LANES, GLOBALS), f32),
            ],
        ),
        out_shape=[
            jax.ShapeDtypeStruct((width, rows_count), f32),
            jax.ShapeDtypeStruct((PAIRS, blocks, 8, 2 * BLOCK), f32),
            jax.ShapeDtypeStruct((SLOTS, PAIRS, LANES, GLOBALS), bf16),
            jax.ShapeDtypeStruct((SLOTS, PAIRS, 8, GLOBALS), f32),
        ],
        compiler_params=params(),
        cost_estimate=pl.CostEstimate(
            flops=8 * 4 * rows_count * GLOBALS * width,
            bytes_accessed=20 * all_globals * width,
            transcendentals=2 * HEADS * rows_count * GLOBALS,
        ),
        name="slot_forward",
    )(*scalars, q, k, v, gq, gk, gv)


def merge_parts(stat, sums, more_stat, more_sums):
    peak = jnp.maximum(stat[0:2], more_stat[0:2])
    keep = jnp.exp(stat[0:2] - peak)
    take = jnp.exp(more_stat[0:2] - peak)
    total = stat[2:4] * keep + more_stat[2:4] * take
    low = sums[:HEAD_DIM].astype(f32) * keep[0:1] + more_sums[:HEAD_DIM].astype(f32) * take[0:1]
    high = sums[HEAD_DIM:].astype(f32) * keep[1:2] + more_sums[HEAD_DIM:].astype(f32) * take[1:2]
    return (
        jnp.concatenate([peak, total, jnp.zeros((4, GLOBALS), f32)], 0),
        jnp.concatenate([low, high], 0),
    )


class SlotSum:
    ORDER = ("core", "y", "z0", "z1")

    def __init__(self, source, sums, stats, send_sem, recv_sem, bits, partners):
        self.source = source
        self.sums = sums
        self.stats = stats
        self.send_sem = send_sem
        self.recv_sem = recv_sem
        self.bits = bits
        self.partners = partners

    def held(self, stage, other):
        bit = self.bits[self.ORDER[stage]]
        side = 1 - bit if other else bit
        if stage == 0:
            return self.source(side)
        index = ((), (slice(None), slice(None)), (slice(None),), ())[stage] + (side,)
        return self.sums[stage - 1].at[index], self.stats[stage - 1].at[index]

    def copies(self, stage):
        partner = self.partners[self.ORDER[stage]]
        sums, stat = self.held(stage, True)
        return (
            remote(
                sums,
                self.sums[stage],
                self.send_sem.at[stage, 0],
                self.recv_sem.at[stage, 0],
                partner,
            ),
            remote(
                stat,
                self.stats[stage],
                self.send_sem.at[stage, 1],
                self.recv_sem.at[stage, 1],
                partner,
            ),
        )

    def begin(self, stage):
        for copy in self.copies(stage):
            copy.start()

    def merge(self, stage, kept=None):
        for copy in self.copies(stage):
            copy.wait_recv()
        sums, stat = self.held(stage, False) if kept is None else kept
        lead = self.sums[stage].shape[:-3]
        total = 1
        for size in lead:
            total = total * size

        def one(number, carry):
            index = []
            left = number
            for size in reversed(lead):
                index.append(left % size)
                left = left // size
            index = tuple(reversed(index))
            for which in range(PAIRS // 2):
                spot = index + (which,)
                new_stat, new_sums = merge_parts(
                    self.stats[stage][spot], self.sums[stage][spot], stat[spot], sums[spot]
                )
                self.stats[stage][spot] = new_stat
                self.sums[stage][spot] = new_sums.astype(bf16)
            return carry

        lax.fori_loop(0, total, one, 0)

    def sent(self, stage):
        for copy in self.copies(stage):
            copy.wait_send()


def local_forward_kernel(
    talk,
    rows_count,
    group_rows,
    lengths,
    bucket_of,
    place,
    q_ref,
    k_ref,
    v_ref,
    far_ref,
    far_stat_ref,
    *refs,
):
    if talk:
        part_ref, part_stat_ref, o_ref, line_ref, half_ref, half_stat_ref = refs[:6]
        own_ref, own_stat_ref = refs[6:8]
        sums_refs = refs[8:10]
        stat_refs = refs[10:12]
        edges, query_columns, key_columns, send_sem, recv_sem, own_sem = refs[12:]
    else:
        o_ref, line_ref, edges, query_columns, key_columns = refs
    pair = pl.program_id(0)
    block = pl.program_id(1)
    blocks = rows_count // BLOCK
    step = pair * blocks + block

    @pl.when(step == 0)
    def _():
        read_edges(lengths, bucket_of, place, edges)

    if talk:
        bits, partners = my_place()
        slot_sum = SlotSum(
            lambda side: (part_ref.at[:, :, :, side], part_stat_ref.at[:, :, :, side]),
            sums_refs,
            stat_refs,
            send_sem,
            recv_sem,
            bits,
            partners,
        )
        own_parts = slot_sum.held(0, False)
        own_copies = [
            pltpu.make_async_copy(own_parts[0], own_ref, own_sem.at[0]),
            pltpu.make_async_copy(own_parts[1], own_stat_ref, own_sem.at[1]),
        ]

        @pl.when(step == 0)
        def _():
            meet([partners["core"], partners["y"]])
            for copy in own_copies:
                copy.start()
            slot_sum.begin(0)

        @pl.when(step == 3)
        def _():
            for copy in own_copies:
                copy.wait()
            slot_sum.merge(0, (own_ref, own_stat_ref))
            slot_sum.begin(1)

        @pl.when(step == PAIRS * blocks - 1)
        def _():
            slot_sum.merge(1)
            half_ref[...] = sums_refs[1][...]
            half_stat_ref[...] = stat_refs[1][...]
            slot_sum.sent(0)
            slot_sum.sent(1)

    block_columns(
        place, edges, rows_count, group_rows, block, step, blocks, query_columns, key_columns
    )
    extra = query_columns[block]
    queries = jnp.concatenate(
        [stack_pair(q_ref[...]), jnp.concatenate([extra, extra], 0)], axis=1
    )
    keys = jnp.concatenate([k_ref[...], key_columns[block]], axis=1)
    score = nt(keys, queries)
    far_peak = far_stat_ref[0, 0, 0:1]
    peak = jnp.maximum(jnp.max(score, axis=0, keepdims=True), far_peak)
    weights = jnp.exp(score - peak)
    far_keep = jnp.exp(far_peak - peak)
    total = jnp.sum(weights, axis=0, keepdims=True) + far_stat_ref[0, 0, 1:2] * far_keep
    low, high = side_by_side(tn(v_ref[...], weights.astype(bf16)))
    low = (low + far_ref[:HEAD_DIM] * far_keep[:, :BLOCK]) / total[:, :BLOCK]
    high = (high + far_ref[HEAD_DIM:] * far_keep[:, BLOCK:]) / total[:, BLOCK:]
    o_ref[...] = jnp.concatenate([low, high], 0).T.astype(bf16)
    line_ref[0, 0] = jnp.broadcast_to(peak + jnp.log(total), (8, 2 * BLOCK))


def local_forward(talk, scalars, rows_count, group_rows, q, k, v, far, far_stat, part, part_stat):
    blocks = rows_count // BLOCK
    width = q.shape[1]
    block_spec = pl.BlockSpec((BLOCK, LANES), lambda p, b, *unused: (b, p))
    operands = [q, k, v, far, far_stat]
    in_specs = [block_spec] * 3 + [
        pl.BlockSpec((LANES, BLOCK), lambda p, b, *unused: (p, b)),
        line_spec(),
    ]
    out_specs = [block_spec, line_spec()]
    out_shape = [
        jax.ShapeDtypeStruct((rows_count, width), bf16),
        jax.ShapeDtypeStruct((PAIRS, blocks, 8, 2 * BLOCK), f32),
    ]
    scratch = []
    more = {}
    edges = column_scratch(blocks)
    if talk:
        cut = (2, 2, 2, 2, PAIRS // 2)
        operands += [part.reshape(cut + part.shape[2:]), part_stat.reshape(cut + part_stat.shape[2:])]
        in_specs += [pl.BlockSpec(memory_space=pl.ANY)] * 2
        shapes = [
            (2, 2, PAIRS // 2, LANES, GLOBALS),
            (2, 2, PAIRS // 2, 8, GLOBALS),
        ]
        out_specs += [full(shape) for shape in shapes]
        out_shape += [
            jax.ShapeDtypeStruct(shapes[0], bf16),
            jax.ShapeDtypeStruct(shapes[1], f32),
        ]
        leads = [(2, 2, 2), (2, 2, 2), (2, 2)]
        sums = [pltpu.VMEM(lead + shapes[0][2:], bf16) for lead in leads]
        stats = [pltpu.VMEM(lead + shapes[1][2:], f32) for lead in leads]
        dma = pltpu.SemaphoreType.DMA
        scratch = [sums[0], stats[0]] + sums[1:] + stats[1:]
        edges += [dma((2, 2)), dma((2, 2)), dma((2,))]
        more = {"collective_id": 2, "has_side_effects": True}
    return pl.pallas_call(
        functools.partial(local_forward_kernel, talk, rows_count, group_rows),
        grid_spec=pltpu.PrefetchScalarGridSpec(
            num_scalar_prefetch=3,
            grid=(PAIRS, blocks),
            in_specs=in_specs,
            out_specs=out_specs,
            scratch_shapes=scratch + edges,
        ),
        out_shape=out_shape,
        compiler_params=params(**more),
        cost_estimate=pl.CostEstimate(
            flops=16 * rows_count * BLOCK * width,
            bytes_accessed=16 * rows_count * width,
            transcendentals=HEADS * rows_count * BLOCK,
        ),
        name="local_forward",
    )(*scalars, *operands)


def put_grouped(ref, value):
    seq, batch, rows, lanes = ref.shape
    for part in range(batch):
        piece = value[:, part * lanes : (part + 1) * lanes].astype(bf16)
        ref[:, part] = piece.reshape(seq, rows, lanes)


def put_unit(ref, value):
    batch, rows, lanes = ref.shape[4:]
    for part in range(batch):
        piece = value[:, part * lanes : (part + 1) * lanes].astype(bf16)
        ref[:, :, :, :, part] = piece.reshape(ref.shape[:4] + (rows, lanes))


TICKS = 3
DELAYS = (0, 2, 3, 4, 6)


def branch_kernel(
    tile,
    talk,
    x_ref,
    o_ref,
    ct_ref,
    gx_ref,
    go_in_ref,
    gstat_in_ref,
    gct_ref,
    wo_ref,
    w1_ref,
    b1_ref,
    w2_ref,
    b2_ref,
    norms_ref,
    z_ref,
    dy_ref,
    do_ref,
    gz_ref,
    gdy_ref,
    gdo_ref,
    dwo_ref,
    db1_ref,
    db2_ref,
    dgain_ref,
    doffset_ref,
    first_ref,
    second_ref,
    *refs,
):
    if talk:
        message_ref, rest_ref = refs[:2]
        refs = refs[2:]
    os_ref, cts_ref, y_ref, h_ref, z_sum_ref, dh_ref, dft_ref, a_ref, du_ref, load_sem = refs[:10]
    refs = refs[10:]
    step = pl.program_id(0)
    steps = pl.num_programs(0)
    count, width = x_ref.shape
    own = gx_ref.shape[0]
    extra = os_ref.shape[0] - count
    tiles = count // tile
    tail = pl.ds(count, extra)

    def rows_at(i):
        return pl.ds(i * tile, tile)

    def padded(value):
        return jnp.concatenate([value, jnp.zeros((extra - own, width), value.dtype)], axis=0)

    if talk:
        units_ref = refs[0]
        landings = refs[1:6]
        send_sem, recv_sem = refs[6:8]
        half_ref, half_stat_ref = refs[8:10]
        slot_sums = refs[10:12]
        slot_stats = refs[12:14]
        turned_ref, go_land, gstat_land, stat_ref, slot_send, slot_recv = refs[14:]
        last_step = 4
        bits, partners = my_place()
        core = bits["core"]
        chunks = last_step - 1
        slots = units_ref.shape[0]
        plan = [
            (TICKS * chunk + DELAYS[stage], chunk, stage)
            for chunk in range(chunks)
            for stage in range(STAGES if chunk < chunks - 1 else 2)
        ]

        def source(unit):
            return lambda side: units_ref.at[unit % slots, :, :, :, side]

        engine = WeightSum(
            [source(unit) for unit in range(2 * chunks)],
            landings,
            None,
            send_sem,
            recv_sem,
            None,
            first_ref,
            bits,
            partners,
        )

        def advance(tick):
            for when, chunk, stage in sorted(plan, key=lambda entry: -entry[2]):
                if when == tick:
                    for unit in (2 * chunk, 2 * chunk + 1):
                        engine.advance(unit, stage, stop=chunk == chunks - 1 and stage == 1)

        def tick_at(position):
            for number in range(1, last_step):
                tick = TICKS * (number - 1) + position

                @pl.when(step == number)
                def _():
                    advance(tick)

        slot_sum = SlotSum(
            None,
            (None, half_ref) + tuple(slot_sums),
            (None, half_stat_ref) + tuple(slot_stats),
            slot_send,
            slot_recv,
            bits,
            partners,
        )
        half_pairs = PAIRS // 2
        lanes = half_pairs * LANES
        my_lanes = pl.ds(pl.multiple_of(core * lanes, LANES), lanes)

        def final_copies():
            theirs = pl.ds(pl.multiple_of((1 - core) * own, own), own)
            return (
                remote(
                    turned_ref.at[theirs],
                    go_land.at[:, my_lanes],
                    slot_send.at[4, 0],
                    slot_recv.at[4, 0],
                    partners["core"],
                ),
                remote(
                    gstat_land.at[core],
                    gstat_land.at[core],
                    slot_send.at[4, 1],
                    slot_recv.at[4, 1],
                    partners["core"],
                ),
            )

        def finish_slots():
            slot_sum.merge(3)
            for which in range(half_pairs):
                stat = slot_stats[1][which]
                total = stat[2:4]
                sums = slot_sums[1][which].astype(f32)
                mean = jnp.concatenate(
                    [sums[:HEAD_DIM] / total[0:1], sums[HEAD_DIM:] / total[1:2]], 0
                )
                turned_ref[:, which * LANES : (which + 1) * LANES] = mean.T.astype(bf16)
                whole = stat[0:2] + jnp.log(total)
                gstat_land[core, which] = jnp.concatenate(
                    [whole, jnp.zeros((6, GLOBALS), f32)], 0
                )
            mine = pl.ds(pl.multiple_of(core * own, own), own)
            go_land[:, my_lanes] = turned_ref[mine, :]
            for copy in final_copies():
                copy.start()

        def put_message():
            product = gdo_ref[...].astype(f32) * go_land[...].astype(f32)
            head_of = iota((width, LANES), 0) // HEAD_DIM == iota((width, LANES), 1)
            head_of = jnp.where(head_of, 1.0, 0.0).astype(bf16)
            first = product.astype(bf16)
            second = (product - first.astype(f32)).astype(bf16)
            centre = nn(first, head_of) + nn(second, head_of)
            lines = [gstat_land[half, which, 0:2] for half in (0, 1) for which in range(half_pairs)]
            lines = jnp.concatenate(lines + [jnp.zeros((LANES - HEADS, GLOBALS), f32)], 0)
            stat_ref[...] = lines.T
            total = stat_ref[pl.ds(pl.multiple_of(core * own, own), own), :]
            spread = jnp.zeros((own, LANES), f32)
            for number, value in enumerate((total, centre)):
                for piece in range(3):
                    low = value.astype(bf16)
                    value = value - low.astype(f32)
                    start_lane = (3 * number + piece) * HEADS
                    source_lane = iota((LANES, LANES), 0)
                    moved = iota((LANES, LANES), 1) == source_lane + start_lane
                    moved = jnp.where(moved & (source_lane < HEADS), 1.0, 0.0).astype(bf16)
                    spread = spread + nn(low, moved)
            message_ref[:, :width] = gdo_ref[...]
            message_ref[:, width:] = spread.astype(bf16)

    else:

        def tick_at(position):
            pass

    loads = [
        pltpu.make_async_copy(o_ref, os_ref.at[pl.ds(0, count)], load_sem.at[0]),
        pltpu.make_async_copy(ct_ref, cts_ref.at[pl.ds(0, count)], load_sem.at[1]),
    ]

    def start(at, size, x, sums):
        y = x.astype(f32) + nn(os_ref[at, :], wo_ref[...])
        unit, unused = normalize_rows(y)
        h_ref[at, :] = (unit * norms_ref[4:5] + norms_ref[5:6]).astype(bf16)
        y_ref[at, :] = y
        sums[...] = y + b2_ref[...]
        dh_ref[at, :] = jnp.zeros((size, width), f32)

    @pl.when(step == 0)
    def _():
        for load in loads:
            load.start()
        if talk:
            half_ref[...] = go_in_ref[...]
            half_stat_ref[...] = gstat_in_ref[...]
            meet([partners[name] for name in ORDERS[0]])
            slot_sum.begin(2)
        cts_ref[count:] = padded(gct_ref[...])
        loads[0].wait()

        def start_tile(i, carry):
            at = pl.ds(pl.multiple_of(i * tile, tile), tile)
            start(at, tile, x_ref[at, :], dy_ref.at[at])
            return carry

        lax.fori_loop(0, tiles, start_tile, 0)
        loads[1].wait()
        dft_ref[...] = cts_ref[...].T
        if talk:
            slot_sum.merge(2)
            slot_sum.begin(3)

    db1_ref[...] = jnp.zeros_like(db1_ref)
    w1 = w1_ref[...].reshape(width, width)
    w2 = w2_ref[...].reshape(width, width)

    def chunk_of(at, sums):
        u = nt(h_ref[at, :], w1) + b1_ref[0]
        da = nt(cts_ref[at, :], w2)
        area, density = gelu_parts(u)
        a = (u * area).astype(bf16)
        du = (da * (area + u * density)).astype(bf16)
        a_ref[at, :] = a
        du_ref[at, :] = du
        db1_ref[0] += jnp.sum(du.astype(f32), axis=0, keepdims=True)
        sums[...] = sums[...] + nn(a, w2)
        dh_ref[at, :] = dh_ref[at, :] + nn(du, w1)

    chunk_of(rows_at(0), dy_ref.at[rows_at(0)])
    if talk:

        @pl.when(step == 0)
        def _():
            finish_slots()

    tick_at(0)
    for i in range(1, tiles):
        chunk_of(rows_at(i), dy_ref.at[rows_at(i)])

    @pl.when(step == 0)
    def _():
        if talk:
            for copy in final_copies():
                copy.wait_recv()
            os_ref[count:] = padded(go_land[...])
        else:
            os_ref[count:] = padded(go_in_ref[...])
        start(tail, extra, padded(gx_ref[...]), z_sum_ref)

    chunk_of(tail, z_sum_ref)
    tick_at(1)
    dw1 = tn(du_ref[...], h_ref[...])
    dw2 = nn(dft_ref[...], a_ref[...])
    if talk:
        for number in range(chunks):

            @pl.when(step == number)
            def _():
                for which, value in ((0, dw1), (1, dw2)):
                    unit = 2 * number + which
                    if unit >= slots:
                        engine.sent(unit - slots, 0)
                    put_unit(units_ref.at[unit % slots], value)

        @pl.when(step == chunks)
        def _():
            put_unit(second_ref.at[0], dw1)
            put_unit(second_ref.at[1], dw2)

        tick_at(2)
        for number in range(chunks):

            @pl.when(step == number)
            def _():
                engine.begin(2 * number)
                engine.begin(2 * number + 1)

    else:
        first_ref[...] = dw1.astype(bf16)
        second_ref[...] = dw2.astype(bf16)

    @pl.when(step == steps - 1)
    def _():
        db2_ref[...] = jnp.zeros_like(db2_ref)
        dgain_ref[...] = jnp.zeros_like(dgain_ref)
        doffset_ref[...] = jnp.zeros_like(doffset_ref)

        def finish(at, size, sums, put):
            z = sums[...].astype(bf16)
            unit, scale = normalize_rows(y_ref[at, :])
            dh = dh_ref[at, :]
            ct = cts_ref[at, :].astype(f32)
            dy = ct + norm_back(unit, scale, norms_ref[4:5], dh)
            db2_ref[...] += jnp.sum(ct, axis=0, keepdims=True)
            doffset_ref[...] += jnp.sum(dh, axis=0, keepdims=True)
            dgain_ref[...] += jnp.sum(dh * unit, axis=0, keepdims=True)
            low = dy.astype(bf16)
            h_ref[at, :] = low
            put(z, dy, nt(low, wo_ref[...]).astype(bf16))

        def finish_tile(i, carry):
            at = pl.ds(pl.multiple_of(i * tile, tile), tile)

            def put(z, dy, do):
                z_ref[at, :] = z
                dy_ref[at, :] = dy
                do_ref[at, :] = do

            finish(at, tile, dy_ref.at[at], put)
            return carry

        lax.fori_loop(0, tiles, finish_tile, 0)

        def put_tail(z, dy, do):
            gz_ref[...] = z[:own]
            gdy_ref[...] = dy[:own]
            gdo_ref[...] = do[:own]

        finish(tail, extra, z_sum_ref, put_tail)
        if talk:
            put_message()
        dwo = tn(h_ref[...], os_ref[...])
        if talk:
            put_grouped(dwo_ref, dwo)
            advance(TICKS * chunks)
            rest_ref[...] = landings[1][2 * chunks - 2 :]
            for when, chunk, stage in plan:
                for unit in (2 * chunk, 2 * chunk + 1):
                    if stage > 0 or unit + slots >= 2 * chunks:
                        engine.sent(unit, stage)
            slot_sum.sent(2)
            slot_sum.sent(3)
            for copy in final_copies():
                copy.wait_send()
        else:
            dwo_ref[...] = dwo.astype(bf16)


def branch(grid_of, x, o, ct, gx, go, gstat, gct, wo, w1t, b1, w2, b2, norms):
    count, width = x.shape
    own = gx.shape[0]
    hidden = w2.shape[0]
    steps = hidden // FF_CHUNK
    total = count + -(-own // LANES) * LANES
    row = once((count, width))
    few = once((own, width))
    line = full((1, width))
    anywhere = pl.BlockSpec(memory_space=pl.ANY)
    scratch = []
    more = {}
    if grid_of is None:
        weight_spec = pl.BlockSpec((FF_CHUNK, width), lambda j: (j, 0))
        b1 = b1.reshape(steps, 1, FF_CHUNK)
        dw_shapes = [(hidden, width), (width, hidden)]
        dw_types = [bf16, bf16]
        dw_specs = [weight_spec, pl.BlockSpec((width, FF_CHUNK), lambda j: (0, j))]
        dwo_shape = (width, width)
    else:
        seq, batch = grid_of
        rows, lanes = width // seq, width // batch
        weight_spec = pl.BlockSpec((seq, 1, rows, width), lambda j: (0, j, 0, 0))
        w1t = w1t.reshape(seq, steps, rows, width)
        w2 = w2.reshape(seq, steps, rows, width)
        b1 = b1.reshape(seq, steps, rows).transpose(1, 0, 2).reshape(steps, 1, FF_CHUNK)
        units = 2 * (steps - 1)
        sums, stats = go.shape[2:], gstat.shape[2:]
        dw_shapes = [
            ((units - 2) * rows, lanes),
            (2, 2, 2, 2, 2, batch, rows, lanes),
            (own, width + LANES),
            (2, 2, 2, 2, rows, lanes),
        ]
        dw_types = [f32, bf16, bf16, bf16]
        dw_specs = [once(shape) for shape in dw_shapes]
        dwo_shape = (seq, batch, rows, lanes)
        dma = pltpu.SemaphoreType.DMA
        scratch = (
            [pltpu.VMEM((4,) + dw_shapes[1][1:], bf16)]
            + sum_scratch(units, rows, lanes, False)
            + [
                pltpu.VMEM(go.shape, bf16),
                pltpu.VMEM(gstat.shape, f32),
                pltpu.VMEM((2,) + sums, bf16),
                pltpu.VMEM(sums, bf16),
                pltpu.VMEM((2,) + stats, f32),
                pltpu.VMEM(stats, f32),
                pltpu.VMEM((GLOBALS, PAIRS // 2 * LANES), bf16),
                pltpu.VMEM((own, width), bf16),
                pltpu.VMEM((2,) + stats, f32),
                pltpu.VMEM((GLOBALS, LANES), f32),
                dma((5, 2)),
                dma((5, 2)),
            ]
        )
        more = {"collective_id": 3, "has_side_effects": True}
    out = pl.pallas_call(
        functools.partial(branch_kernel, BLOCK, grid_of is not None),
        grid=(steps,),
        in_specs=[
            row,
            anywhere,
            anywhere,
            few,
            once(go.shape),
            once(gstat.shape),
            few,
            once((width, width)),
            weight_spec,
            pl.BlockSpec((1, 1, FF_CHUNK), lambda j: (j, 0, 0)),
            weight_spec,
            line,
            full(norms.shape),
        ],
        out_specs=[row, row, row, few, few, few]
        + [once(dwo_shape), pl.BlockSpec((1, 1, FF_CHUNK), lambda j: (j, 0, 0)), line, line, line]
        + dw_specs,
        out_shape=[
            jax.ShapeDtypeStruct((count, width), bf16),
            jax.ShapeDtypeStruct((count, width), f32),
            jax.ShapeDtypeStruct((count, width), bf16),
            jax.ShapeDtypeStruct((own, width), bf16),
            jax.ShapeDtypeStruct((own, width), f32),
            jax.ShapeDtypeStruct((own, width), bf16),
            jax.ShapeDtypeStruct(dwo_shape, bf16),
            jax.ShapeDtypeStruct((steps, 1, FF_CHUNK), f32),
            jax.ShapeDtypeStruct((1, width), f32),
            jax.ShapeDtypeStruct((1, width), f32),
            jax.ShapeDtypeStruct((1, width), f32),
        ]
        + [jax.ShapeDtypeStruct(shape, kind) for shape, kind in zip(dw_shapes, dw_types)],
        scratch_shapes=[
            pltpu.VMEM((total, width), bf16),
            pltpu.VMEM((total, width), bf16),
            pltpu.VMEM((total, width), f32),
            pltpu.VMEM((total, width), bf16),
            pltpu.VMEM((total - count, width), f32),
            pltpu.VMEM((total, width), f32),
            pltpu.VMEM((width, total), bf16),
            pltpu.VMEM((total, FF_CHUNK), bf16),
            pltpu.VMEM((total, FF_CHUNK), bf16),
            pltpu.SemaphoreType.DMA((2,)),
        ]
        + scratch,
        compiler_params=params(**more),
        cost_estimate=pl.CostEstimate(
            flops=6 * total * width * (2 * hidden + width),
            bytes_accessed=8 * width * hidden + 16 * total * width,
            transcendentals=2 * total * hidden,
        ),
        name="branch",
    )(x, o, ct, gx, go, gstat, gct, wo, w1t, b1, w2, b2, norms)
    db1 = out[7].reshape(steps, FF_CHUNK)
    if grid_of is not None:
        db1 = db1.reshape(steps, seq, rows).transpose(1, 0, 2).reshape(-1, width)
    return [*out[:7], db1, *out[8:]]


def local_backward_kernel(
    talk,
    rows_count,
    group_rows,
    lengths,
    bucket_of,
    place,
    q_ref,
    k_ref,
    v_ref,
    do_ref,
    o_ref,
    line_ref,
    *refs,
):
    if talk:
        message_ref, rest_ref, last_ref, dwo_ref = refs[:4]
        refs = refs[4:]
    dq_ref, dk_ref, dv_ref, centre_ref = refs[:4]
    refs = refs[4:]
    if talk:
        everyone_ref, sums_ref, rest_out_ref = refs[:3]
        refs = refs[3:]
    edges, query_columns, key_columns = refs[:3]
    pair = pl.program_id(0)
    block = pl.program_id(1)
    blocks = rows_count // BLOCK
    step = pair * blocks + block

    @pl.when(step == 0)
    def _():
        read_edges(lengths, bucket_of, place, edges)

    if talk:
        all_ref, gather_send, gather_recv, own_ref = refs[3:7]
        landings = refs[7:12]
        send_sem, recv_sem, own_sem = refs[12:]
        bits, partners = my_place()
        gather = RowGather(all_ref, 3 * LANES, gather_send, gather_recv, bits, partners)
        engine = WeightSum(
            [
                None,
                None,
                lambda side: last_ref.at[0, :, :, :, side],
                lambda side: last_ref.at[1, :, :, :, side],
                lambda side: dwo_ref.at[:, :, :, side],
            ],
            landings,
            own_ref,
            send_sem,
            recv_sem,
            own_sem,
            sums_ref,
            bits,
            partners,
        )
        plan = {
            1: [(2, 0), (3, 0), (4, 0)],
            3: [(0, 2), (1, 2)],
            6: [(0, 3), (1, 3)],
            11: [(0, 4), (1, 4), (2, 1), (3, 1), (4, 1)],
        }
        gather_plan = {2: 0, 5: 1, 8: 2, 11: 3}

        @pl.when(step == 0)
        def _():
            all_ref[bits["z1"], bits["z0"], bits["y"], bits["core"]] = message_ref[...]
            landings[1][:2] = rest_ref[...]
            meet([partners[name] for name in ORDERS[0]])
            gather.begin()
            for unit in (2, 3, 4):
                engine.begin(unit)
            for unit in (0, 1):
                engine.copy(unit, 2).start()

        for number in range(PAIRS * blocks):
            if number in plan or number in gather_plan:

                @pl.when(step == number)
                def _():
                    if number in gather_plan:
                        gather.advance(gather_plan[number])
                    for unit, stage in plan.get(number, ()):
                        engine.advance(unit, stage, stop=unit > 1 and stage == 1)

    block_columns(
        place, edges, rows_count, group_rows, block, step, blocks, query_columns, key_columns
    )
    extra = query_columns[block]
    upstream = do_ref[...]
    product = upstream.astype(f32) * o_ref[...].astype(f32)
    first = product.astype(bf16)
    second = (product - first.astype(f32)).astype(bf16)
    head = jnp.where(iota((8, LANES), 1) // HEAD_DIM == iota((8, LANES), 0), 1.0, 0.0).astype(bf16)
    by_head = nt(head, first) + nt(head, second)
    centre = jnp.concatenate([by_head[0:1], by_head[1:2]], axis=1)
    centre_ref[0, 0] = jnp.broadcast_to(centre, (8, 2 * BLOCK))
    queries = stack_pair(q_ref[...])
    grads = stack_pair(upstream)
    keys = k_ref[...]
    score = nt(
        jnp.concatenate([keys, key_columns[block]], 1),
        jnp.concatenate([queries, jnp.concatenate([extra, extra], 0)], 1),
    )
    weights = jnp.exp(score - line_ref[0, 0, 0:1])
    along = nt(v_ref[...], grads) - centre
    score_grad = (weights * along).astype(bf16)
    dv_ref[...] = nn(weights.astype(bf16), grads)
    dk_ref[...] = nn(score_grad, queries)
    low, high = side_by_side(tn(keys, score_grad))
    dq_ref[:HEAD_DIM] = low
    dq_ref[HEAD_DIM:] = high

    if talk:

        @pl.when(step == PAIRS * blocks - 1)
        def _():
            everyone_ref[...] = all_ref[...].reshape(everyone_ref.shape)
            gather.end()
            rest_out_ref[...] = landings[1][2:]
            for entries in plan.values():
                for unit, stage in entries:
                    engine.sent(unit, stage)


def local_backward(
    talk, scalars, rows_count, group_rows, q, k, v, do, o, line, message, rest, last, dwo
):
    blocks = rows_count // BLOCK
    width = q.shape[1]
    block_spec = pl.BlockSpec((BLOCK, LANES), lambda p, b, *unused: (b, p))
    operands = [q, k, v, do, o, line]
    in_specs = [block_spec] * 5 + [line_spec()]
    out_specs = (
        [pl.BlockSpec((LANES, BLOCK), lambda p, b, *unused: (p, b))]
        + [block_spec] * 2
        + [line_spec()]
    )
    out_shape = [
        jax.ShapeDtypeStruct((width, rows_count), f32),
        jax.ShapeDtypeStruct((rows_count, width), f32),
        jax.ShapeDtypeStruct((rows_count, width), f32),
        jax.ShapeDtypeStruct((PAIRS, blocks, 8, 2 * BLOCK), f32),
    ]
    scratch = column_scratch(blocks)
    more = {}
    if talk:
        own, wide = message.shape
        rows, lanes = last.shape[-2:]
        units = 5
        operands += [message, rest, last, dwo.reshape(last.shape[1:])]
        in_specs += [full(message.shape), once(rest.shape)]
        in_specs += [pl.BlockSpec(memory_space=pl.ANY)] * 2
        everyone = (16 * own, wide)
        rest_out = (units - 2,) + rest.shape[1:]
        out_specs += [once(everyone), once((2 * rows, lanes)), once(rest_out)]
        out_shape += [
            jax.ShapeDtypeStruct(everyone, bf16),
            jax.ShapeDtypeStruct((2 * rows, lanes), f32),
            jax.ShapeDtypeStruct(rest_out, bf16),
        ]
        dma = pltpu.SemaphoreType.DMA
        scratch += [pltpu.VMEM((2, 2, 2, 2, own, wide), bf16), dma((4, 2)), dma((4, 2))]
        scratch += sum_scratch(units, rows, lanes, True)
        more = {"collective_id": 4, "has_side_effects": True}
    return pl.pallas_call(
        functools.partial(local_backward_kernel, talk, rows_count, group_rows),
        grid_spec=pltpu.PrefetchScalarGridSpec(
            num_scalar_prefetch=3,
            grid=(PAIRS, blocks),
            in_specs=in_specs,
            out_specs=out_specs,
            scratch_shapes=scratch,
        ),
        out_shape=out_shape,
        compiler_params=params(**more),
        cost_estimate=pl.CostEstimate(
            flops=40 * rows_count * BLOCK * width,
            bytes_accessed=30 * rows_count * width,
            transcendentals=HEADS * rows_count * BLOCK,
        ),
        name="local_backward",
    )(*scalars, *operands)


def slot_backward_kernel(
    rows_count,
    group_rows,
    lengths,
    bucket_of,
    place,
    q_ref,
    k_ref,
    v_ref,
    do_ref,
    line_ref,
    centre_ref,
    dqt_ref,
    dk_in_ref,
    dv_in_ref,
    gq_ref,
    gk_ref,
    gv_ref,
    gdo_ref,
    gstat_ref,
    gx_ref,
    gh_ref,
    wq_ref,
    wk_ref,
    wv_ref,
    dq_ref,
    dk_ref,
    dv_ref,
    dw_ref,
    dgh_ref,
    dnorm_ref,
    edges,
    query_columns,
    key_columns,
    keys_ref,
    queries_ref,
    grads_ref,
    dqt_sum,
    dk_sum,
    dv_sum,
    dgqt_sum,
    dgk_sum,
    dgv_sum,
    lines_ref,
    dw_sum,
    dgh_sum,
):
    pair = pl.program_id(0)
    block = pl.program_id(1)
    blocks = rows_count // BLOCK
    step = pair * blocks + block

    @pl.when(step == 0)
    def _():
        read_edges(lengths, bucket_of, place, edges)

        def turn(slot, carry):
            at = pl.ds(pl.multiple_of(slot * GLOBALS, GLOBALS), GLOBALS)
            lines_ref[slot] = gstat_ref[at, :].astype(f32).T
            return carry

        lax.fori_loop(0, SLOTS, turn, 0)
        dgh_sum[...] = jnp.zeros_like(dgh_sum)
        dnorm_ref[...] = jnp.zeros_like(dnorm_ref)

    @pl.when(block == 0)
    def _():
        dgqt_sum[...] = jnp.zeros_like(dgqt_sum)
        dgk_sum[...] = jnp.zeros_like(dgk_sum)
        dgv_sum[...] = jnp.zeros_like(dgv_sum)

    block_columns(
        place, edges, rows_count, group_rows, block, step, blocks, query_columns, key_columns
    )
    extra = query_columns[block]
    keys_ref[:, :LANES] = k_ref[...]
    keys_ref[:, LANES:] = key_columns[block]
    queries_ref[:, :LANES] = stack_pair(q_ref[...])
    queries_ref[:BLOCK, LANES:] = extra
    queries_ref[BLOCK:, LANES:] = extra
    grads_ref[...] = stack_pair(do_ref[...])
    dqt_sum[...] = dqt_ref[...]
    dk_sum[...] = dk_in_ref[...]
    dv_sum[...] = dv_in_ref[...]

    def line_of(slot, first):
        halves = []
        for which in range(2):
            spot = first + 2 * pair + which
            halves.append(
                lines_ref[slot, pl.ds(spot, 1)]
                + lines_ref[slot, pl.ds(spot + HEADS, 1)]
                + lines_ref[slot, pl.ds(spot + 2 * HEADS, 1)]
            )
        return jnp.concatenate(halves, axis=1)

    def from_global(slot, keys, values):
        at = pl.ds(pl.multiple_of(slot * GLOBALS, GLOBALS), GLOBALS)
        extra = global_query_extra(slot).astype(bf16)
        queries = stack_pair(gq_ref[at, :])
        grads = stack_pair(gdo_ref[at, :])
        score = nt(keys, jnp.concatenate([queries, jnp.concatenate([extra, extra], 0)], 1))
        weights = jnp.exp(score - line_of(slot, 0))
        along = nt(values, grads) - line_of(slot, 3 * HEADS)
        score_grad = (weights * along).astype(bf16)
        low, high = side_by_side(tn(keys[:, :LANES], score_grad))
        dgqt_sum[slot, :HEAD_DIM] += low
        dgqt_sum[slot, HEAD_DIM:] += high
        return nn(score_grad, queries), nn(weights.astype(bf16), grads)

    def one_slot(slot, carry):
        @pl.when(slot_present(slot, place, edges, rows_count, group_rows, block))
        def _():
            key_grad, value_grad = from_global(slot, keys_ref[...], v_ref[...])
            dk_sum[...] += key_grad
            dv_sum[...] += value_grad
            at = pl.ds(pl.multiple_of(slot * GLOBALS, GLOBALS), GLOBALS)
            slot_keys = jnp.concatenate([gk_ref[at, :], global_key_extra(slot).astype(bf16)], 1)
            weights = jnp.exp(nt(slot_keys, queries_ref[...]) - line_ref[0, 0, 0:1])
            along = nt(gv_ref[at, :], grads_ref[...]) - centre_ref[0, 0, 0:1]
            score_grad = (weights * along).astype(bf16)
            dgv_sum[at, :] += nn(weights.astype(bf16), grads_ref[...])
            dgk_sum[at, :] += nn(score_grad, queries_ref[:, :LANES])
            low, high = side_by_side(tn(gk_ref[at, :], score_grad))
            dqt_sum[:HEAD_DIM] += low
            dqt_sum[HEAD_DIM:] += high

        return carry

    lax.fori_loop(0, SLOTS, one_slot, 0)
    dq_ref[...] = dqt_sum[...].T.astype(bf16)
    dk_ref[...] = dk_sum[...].astype(bf16)
    dv_ref[...] = dv_sum[...].astype(bf16)

    @pl.when((block == blocks - 1) & (place[2] >= 0))
    def _():
        slot = place[2]
        at = pl.ds(pl.multiple_of(slot * GLOBALS, GLOBALS), GLOBALS)
        keys = jnp.concatenate([gk_ref[at, :], global_key_extra(slot).astype(bf16)], axis=1)
        key_grad, value_grad = from_global(slot, keys, gv_ref[at, :])
        dgk_sum[at, :] += key_grad
        dgv_sum[at, :] += value_grad

    @pl.when(block == blocks - 1)
    def _():
        dw_sum[...] = jnp.zeros_like(dw_sum)

        def through(slot, carry):
            needed = slot == place[2]
            for number in range(blocks):
                needed = needed | slot_present(
                    slot, place, edges, rows_count, group_rows, number
                )

            @pl.when(needed)
            def _():
                at = pl.ds(pl.multiple_of(slot * GLOBALS, GLOBALS), GLOBALS)
                grads = (
                    (dgqt_sum[slot].T * query_scale).astype(bf16),
                    dgk_sum[at, :].astype(bf16),
                    dgv_sum[at, :].astype(bf16),
                )
                rows = gh_ref[at, :]
                total = dgh_sum[at, :]
                for index, weight in enumerate((wq_ref, wk_ref, wv_ref)):
                    dw_sum[index] += tn(grads[index], rows)
                    total = total + nt(grads[index], weight[...])
                dgh_sum[at, :] = total

                @pl.when(pair == PAIRS - 1)
                def _():
                    unit, unused = normalize_rows(gx_ref[at, :].astype(f32))
                    dnorm_ref[0:1] += jnp.sum(total * unit, axis=0, keepdims=True)
                    dnorm_ref[1:2] += jnp.sum(total, axis=0, keepdims=True)

            return carry

        lax.fori_loop(0, SLOTS, through, 0)
        dw_ref[...] = dw_sum[...].astype(bf16)

    @pl.when(step == PAIRS * blocks - 1)
    def _():
        dgh_ref[...] = dgh_sum[...].astype(bf16)


def slot_backward(
    scalars,
    rows_count,
    group_rows,
    q,
    k,
    v,
    do,
    line,
    centre,
    dqt,
    dk,
    dv,
    gq,
    gk,
    gv,
    everyone,
    gx,
    gh,
    wq,
    wk,
    wv,
):
    blocks = rows_count // BLOCK
    all_globals, width = gk.shape
    block_spec = pl.BlockSpec((BLOCK, LANES), lambda p, b, *unused: (b, p))
    pair_spec = pl.BlockSpec((all_globals, LANES), lambda p, b, *unused: (0, p))
    local = jax.ShapeDtypeStruct((rows_count, width), bf16)
    glob = jax.ShapeDtypeStruct((all_globals, width), bf16)
    return pl.pallas_call(
        functools.partial(slot_backward_kernel, rows_count, group_rows),
        grid_spec=pltpu.PrefetchScalarGridSpec(
            num_scalar_prefetch=3,
            grid=(PAIRS, blocks),
            in_specs=[block_spec] * 4
            + [line_spec()] * 2
            + [pl.BlockSpec((LANES, BLOCK), lambda p, b, *unused: (p, b))]
            + [block_spec] * 2
            + [pair_spec] * 4
            + [pl.BlockSpec((all_globals, LANES), lambda p, b, *unused: (0, PAIRS))]
            + [once((all_globals, width))] * 2
            + [pl.BlockSpec((width, LANES), lambda p, b, *unused: (0, p))] * 3,
            out_specs=[block_spec] * 3
            + [
                pl.BlockSpec((3, LANES, width), lambda p, b, *unused: (0, p, 0)),
                once((all_globals, width)),
                full((8, width)),
            ],
            scratch_shapes=column_scratch(blocks)
            + [
                pltpu.VMEM((BLOCK, 2 * LANES), bf16),
                pltpu.VMEM((2 * BLOCK, 2 * LANES), bf16),
                pltpu.VMEM((2 * BLOCK, LANES), bf16),
                pltpu.VMEM((LANES, BLOCK), f32),
                pltpu.VMEM((BLOCK, LANES), f32),
                pltpu.VMEM((BLOCK, LANES), f32),
                pltpu.VMEM((SLOTS, LANES, GLOBALS), f32),
                pltpu.VMEM((all_globals, LANES), f32),
                pltpu.VMEM((all_globals, LANES), f32),
                pltpu.VMEM((SLOTS, LANES, GLOBALS), f32),
                pltpu.VMEM((3, LANES, width), f32),
                pltpu.VMEM((all_globals, width), f32),
            ],
        ),
        out_shape=[local] * 3
        + [
            jax.ShapeDtypeStruct((3, width, width), bf16),
            glob,
            jax.ShapeDtypeStruct((8, width), f32),
        ],
        compiler_params=params(),
        cost_estimate=pl.CostEstimate(
            flops=80 * rows_count * GLOBALS * width,
            bytes_accessed=40 * rows_count * width,
            transcendentals=2 * HEADS * rows_count * GLOBALS,
        ),
        name="slot_backward",
    )(
        *scalars,
        q,
        k,
        v,
        do,
        line,
        centre,
        dqt,
        dk,
        dv,
        gq,
        gk,
        gv,
        everyone,
        everyone,
        gx,
        gh,
        wq,
        wk,
        wv,
    )


def project_back_kernel(
    tile,
    x_ref,
    dy_ref,
    h_ref,
    dq_ref,
    dk_ref,
    dv_ref,
    dwg_ref,
    wq_ref,
    wk_ref,
    wv_ref,
    gain_ref,
    dx_ref,
    dw_ref,
    dnorm_ref,
):
    count, width = x_ref.shape
    dnorm_ref[...] = jnp.zeros_like(dnorm_ref)

    def one_tile(i, carry):
        at = pl.ds(pl.multiple_of(i * tile, tile), tile)
        dh = (
            nt(dq_ref[at, :], wq_ref[...]) * query_scale
            + nt(dk_ref[at, :], wk_ref[...])
            + nt(dv_ref[at, :], wv_ref[...])
        )
        unit, scale = normalize_rows(x_ref[at, :].astype(f32))
        dnorm_ref[0:1] += jnp.sum(dh * unit, axis=0, keepdims=True)
        dnorm_ref[1:2] += jnp.sum(dh, axis=0, keepdims=True)
        dx_ref[at, :] = dy_ref[at, :] + norm_back(unit, scale, gain_ref[...], dh)
        return carry

    lax.fori_loop(0, count // tile, one_tile, 0)
    for index, source in enumerate((dq_ref, dk_ref, dv_ref)):
        value = tn(source[...], h_ref[...])
        if index == 0:
            value = value * query_scale
        dw_ref[index] = (value + dwg_ref[index].astype(f32)).astype(bf16)


def project_back(x, dy, h, dq, dk, dv, dwg, wq, wk, wv, gain):
    count, width = x.shape
    vmem = pl.BlockSpec(memory_space=pltpu.VMEM)
    return pl.pallas_call(
        functools.partial(project_back_kernel, BLOCK),
        in_specs=[vmem] * 11,
        out_specs=[vmem] * 3,
        out_shape=[
            jax.ShapeDtypeStruct((count, width), f32),
            jax.ShapeDtypeStruct((3, width, width), bf16),
            jax.ShapeDtypeStruct((8, width), f32),
        ],
        compiler_params=params(),
        cost_estimate=pl.CostEstimate(
            flops=12 * count * width * width, bytes_accessed=30 * count * width, transcendentals=0
        ),
        name="project_back",
    )(x, dy, h, dq, dk, dv, dwg, wq, wk, wv, gain)


class RowSum:
    ORDER = ("core", "y", "z0", "z1")

    def __init__(self, source, own, landings, send_sem, recv_sem, own_sem, bits, partners):
        self.source = source
        self.own = own
        self.landings = landings
        self.send_sem = send_sem
        self.recv_sem = recv_sem
        self.own_sem = own_sem
        self.bits = bits
        self.partners = partners

    def part(self, stage, other):
        bit = self.bits[self.ORDER[stage]]
        side = 1 - bit if other else bit
        if stage == 0:
            return self.source.at[:, :, :, side] if other else self.own
        ref = self.landings[stage - 1]
        if stage == 1:
            return ref.at[:, :, side]
        if stage == 2:
            return ref.at[:, side]
        return ref.at[side]

    def copy(self, stage):
        return remote(
            self.part(stage, True),
            self.landings[stage],
            self.send_sem.at[stage],
            self.recv_sem.at[stage],
            self.partners[self.ORDER[stage]],
        )

    def own_copy(self):
        return pltpu.make_async_copy(
            self.source.at[:, :, :, self.bits["core"]], self.own, self.own_sem
        )

    def begin(self):
        self.own_copy().start()
        self.copy(0).start()

    def advance(self, stage):
        if stage == 0:
            self.own_copy().wait()
        self.copy(stage).wait_recv()
        if stage < 3:
            add_into(self.landings[stage], self.part(stage, False))
            self.copy(stage + 1).start()
            return None
        return self.landings[3][...].astype(f32) + self.part(3, False)[...].astype(f32)

    def end(self):
        for stage in range(4):
            self.copy(stage).wait_send()


def finish_kernel(
    rest_ref,
    x_in,
    dy_in,
    h_in,
    dq_in,
    dk_in,
    dv_in,
    dwg_in,
    dgh_ref,
    z_in,
    wq_in,
    wk_in,
    wv_in,
    db1_ref,
    db2_ref,
    dnorm_global_ref,
    dgain2_ref,
    doffset2_ref,
    gx_ref,
    gdy_ref,
    norms_ref,
    out_ref,
    small_out_ref,
    grad_out_ref,
    layer_ref,
    token_ref,
    x_ref,
    dy_ref,
    h_ref,
    dq_ref,
    dk_ref,
    dv_ref,
    dwg_ref,
    wq_ref,
    wk_ref,
    wv_ref,
    load_sem,
    units_ref,
    one_ref,
    two_ref,
    three_ref,
    four_ref,
    five_ref,
    send_sem,
    recv_sem,
    gown_ref,
    gone_ref,
    gtwo_ref,
    gthree_ref,
    gfour_ref,
    gsend_sem,
    grecv_sem,
    gown_sem,
    sums_ref,
    here_ref,
    ssend_sem,
    srecv_sem,
    halo_out,
    halo_z,
    halo_dx,
    halo_send,
    halo_recv,
    dnorm_ref,
):
    bits, partners = my_place()
    count, width = x_ref.shape
    came = rest_ref.shape[0]
    units = came + 3
    batch = lax.axis_index("batch")
    seq = lax.axis_index("seq")
    places = lax.axis_size("seq")
    after = (batch, lax.rem(seq + 1, places))
    before = (batch, lax.rem(seq + places - 1, places))

    pairs = [
        (dq_in, dq_ref),
        (h_in, h_ref),
        (dwg_in, dwg_ref),
        (dk_in, dk_ref),
        (dv_in, dv_ref),
        (wq_in, wq_ref),
        (wk_in, wk_ref),
        (wv_in, wv_ref),
        (x_in, x_ref),
        (dy_in, dy_ref),
        (z_in.at[pl.ds(HALF, count - HALF)], layer_ref.at[pl.ds(0, count - HALF)]),
    ]
    loads = [
        pltpu.make_async_copy(source, target, load_sem.at[number])
        for number, (source, target) in enumerate(pairs)
    ]
    for load in loads:
        load.start()

    def source(unit):
        return lambda side: units_ref.at[unit - came, :, :, :, side]

    engine = WeightSum(
        [source(unit) for unit in range(units)],
        (one_ref, two_ref, three_ref, four_ref, five_ref),
        None,
        send_sem,
        recv_sem,
        None,
        out_ref,
        bits,
        partners,
    )
    row_sum = RowSum(
        dgh_ref,
        gown_ref,
        (gone_ref, gtwo_ref, gthree_ref, gfour_ref),
        gsend_sem,
        grecv_sem,
        gown_sem,
        bits,
        partners,
    )

    def scopy(stage):
        return remote(
            sums_ref.at[stage],
            here_ref.at[stage],
            ssend_sem.at[stage],
            srecv_sem.at[stage],
            partners[ORDERS[0][stage]],
        )

    def small_advance(stage):
        scopy(stage).wait_recv()
        total = sums_ref[stage] + here_ref[stage]
        if stage < STAGES - 1:
            sums_ref[stage + 1] = total
            scopy(stage + 1).start()
        else:
            small_out_ref[...] = total

    head = pl.ds(0, HALF)
    halos = [
        remote(z_in.at[head], halo_z, halo_send.at[0], halo_recv.at[0], before),
        remote(halo_out, halo_dx, halo_send.at[1], halo_recv.at[1], before),
    ]
    two_ref[:came] = rest_ref[...]
    meet([partners[name] for name in ORDERS[0]] + [before, after])
    for unit in range(came):
        engine.copy(unit, 2).start()
    row_sum.begin()
    halos[0].start()

    def weight_gradient(index, grads_ref):
        value = tn(grads_ref[...], h_ref[...])
        if index == 0:
            value = value * query_scale
        put_unit(units_ref.at[index], value + dwg_ref[index].astype(f32))
        engine.begin(came + index)

    for number in range(3):
        loads[number].wait()
    weight_gradient(0, dq_ref)
    row_sum.advance(0)
    loads[3].wait()
    weight_gradient(1, dk_ref)
    loads[4].wait()
    weight_gradient(2, dv_ref)
    for unit in range(came):
        engine.advance(unit, 2)
    for number in range(5, 10):
        loads[number].wait()
    dnorm_ref[...] = jnp.zeros_like(dnorm_ref)

    def back(index):
        at = pl.ds(index * HALF, HALF)
        dh = (
            nt(dq_ref[at, :], wq_ref[...]) * query_scale
            + nt(dk_ref[at, :], wk_ref[...])
            + nt(dv_ref[at, :], wv_ref[...])
        )
        unit, scale = normalize_rows(x_ref[at, :].astype(f32))
        dnorm_ref[0:1] += jnp.sum(dh * unit, axis=0, keepdims=True)
        dnorm_ref[1:2] += jnp.sum(dh, axis=0, keepdims=True)
        dx = dy_ref[at, :] + norm_back(unit, scale, norms_ref[0:1], dh)
        if index == 0:
            halo_out[...] = dx.astype(bf16)
        else:
            token_ref[pl.ds((index - 1) * HALF, HALF), :] = dx

    for index in range(count // HALF):
        back(index)
        if index == 0:
            halos[1].start()
            for unit in range(came, units):
                engine.advance(unit, 0)
        if index == 1:
            row_sum.advance(1)
        if index == 2:
            for unit in range(came):
                engine.advance(unit, 3)

    hidden_rows = db1_ref.shape[0]
    parts = [
        db1_ref[...],
        db2_ref[...],
        dnorm_ref[0:2],
        dnorm_global_ref[0:2],
        dgain2_ref[...],
        doffset2_ref[...],
    ]
    filled = hidden_rows + 7
    parts.append(jnp.zeros((sums_ref.shape[1] - filled, width), f32))
    sums_ref[0] = jnp.concatenate(parts, 0)
    scopy(0).start()
    row_sum.advance(2)
    for unit in range(came, units):
        engine.advance(unit, 1)
    small_advance(0)
    dgh = row_sum.advance(3)
    unit_rows, scale = normalize_rows(gx_ref[...].astype(f32))
    grad_out_ref[...] = gdy_ref[...] + norm_back(unit_rows, scale, norms_ref[2:3], dgh)
    small_advance(1)
    for unit in range(came):
        engine.advance(unit, 4)
    for unit in range(came, units):
        engine.advance(unit, 2)
    small_advance(2)
    halos[0].wait_recv()
    halos[1].wait_recv()
    loads[10].wait()
    layer_ref[count - HALF :, :] = halo_z[...]
    token_ref[count - HALF :, :] = halo_dx[...].astype(f32)
    for unit in range(came, units):
        engine.advance(unit, 3)
    small_advance(3)
    for unit in range(came, units):
        engine.advance(unit, 4)
    small_advance(4)

    for unit in range(units):
        for stage in range(2 if unit < came else 0, STAGES):
            engine.sent(unit, stage)
    for stage in range(STAGES):
        scopy(stage).wait_send()
    row_sum.end()
    for halo in halos:
        halo.wait_send()


def finish_all(rest, x, dy, h, dq, dk, dv, dwg, dgh, z, wq, wk, wv, small, gx, gdy, norms):
    count, width = x.shape
    rows, lanes = rest.shape[-2:]
    units = rest.shape[0] + 3
    own = gx.shape[0]
    place = (2, 2, 2, 2)
    small_rows = small[0].shape[0] + 7
    small_rows += -small_rows % 8
    anywhere = pl.BlockSpec(memory_space=pl.ANY)
    vmem = pl.BlockSpec(memory_space=pltpu.VMEM)
    dma = pltpu.SemaphoreType.DMA
    row = pltpu.VMEM((count, width), bf16)
    weight = pltpu.VMEM((width, width), bf16)
    half = pltpu.VMEM((HALF, width), bf16)
    return pl.pallas_call(
        finish_kernel,
        in_specs=[vmem] + [anywhere] * 12 + [vmem] * 8,
        out_specs=[vmem] * 5,
        out_shape=[
            jax.ShapeDtypeStruct((units * rows, lanes), f32),
            jax.ShapeDtypeStruct((small_rows, width), f32),
            jax.ShapeDtypeStruct((own, width), f32),
            jax.ShapeDtypeStruct((count, width), bf16),
            jax.ShapeDtypeStruct((count, width), f32),
        ],
        scratch_shapes=[
            row,
            pltpu.VMEM((count, width), f32),
            row,
            row,
            row,
            row,
            pltpu.VMEM((3, width, width), bf16),
            weight,
            weight,
            weight,
            dma((11,)),
            pltpu.VMEM((3, 2, 2, 2, 2, 2, rows, lanes), bf16),
        ]
        + sum_scratch(units, rows, lanes, False)
        + [
            pltpu.VMEM((2, 2, 2, own, width), bf16),
            pltpu.VMEM((2, 2, 2, own, width), bf16),
            pltpu.VMEM((2, 2, own, width), bf16),
            pltpu.VMEM((2, own, width), bf16),
            pltpu.VMEM((own, width), bf16),
            dma((4,)),
            dma((4,)),
            dma,
            pltpu.VMEM((STAGES, small_rows, width), f32),
            pltpu.VMEM((STAGES, small_rows, width), f32),
            dma((STAGES,)),
            dma((STAGES,)),
            half,
            half,
            half,
            dma((2,)),
            dma((2,)),
            pltpu.VMEM((8, width), f32),
        ],
        compiler_params=params(collective_id=0, has_side_effects=True),
        cost_estimate=pl.CostEstimate(
            flops=12 * count * width * width, bytes_accessed=30 * count * width, transcendentals=0
        ),
        name="finish_all",
    )(
        rest,
        x,
        dy,
        h,
        dq,
        dk,
        dv,
        dwg,
        dgh.reshape(place + (own, width)),
        z,
        wq,
        wk,
        wv,
        *small,
        gx,
        gdy,
        norms,
    )


def from_behind(value, axis, steps):
    count = lax.axis_size(axis)
    pairs = [(source, (source + steps) % count) for source in range(count)]
    return lax.ppermute(value, axis, pairs)


def pieces(value):
    first = lax.reduce_precision(value, 8, 7)
    second = lax.reduce_precision(value - first, 8, 7)
    return [first.astype(bf16), second.astype(bf16), (value - first - second).astype(bf16)]


def scatter_sum(value):
    half = lax.psum_scatter(value, "batch", scatter_dimension=1, tiled=True)
    part = lax.psum_scatter(half, "seq", scatter_dimension=0, tiled=True)
    return part.T.astype(f32)


def on_device(
    tokens,
    global_states,
    lengths,
    bucket_of,
    wq,
    wk,
    wv,
    wo,
    w1,
    b1,
    w2,
    b2,
    norm_params,
    cotangent,
    global_cotangent,
):
    rows = tokens.shape[1]
    width = tokens.shape[2]
    own = global_states.shape[1]
    seq_count = lax.axis_size("seq")
    seq_place = lax.axis_index("seq")
    group_rows = rows * seq_count
    own_start = seq_place * own
    first_of_slot = own_start % GLOBALS == 0
    place = jnp.stack(
        [
            lax.axis_index("batch"),
            seq_place,
            jnp.where(first_of_slot, own_start // GLOBALS, -1),
        ]
    ).astype(jnp.int32)
    scalars = (lengths, bucket_of, place)
    norms = [norm_params[i : i + 1] for i in range(6)]
    b2_line = b2[None]

    batch_count = lax.axis_size("batch")
    grid_of = None
    if seq_count == 16 and batch_count == 2 and 2 * own == GLOBALS and rows == 2 * BLOCK:
        grid_of = (seq_count, batch_count)

    if grid_of is None:
        arrived_tokens, arrived_grads = from_behind(
            (tokens[0, rows - HALF :], cotangent[0, rows - HALF :]), "seq", 1
        )
        x = jnp.concatenate([arrived_tokens, tokens[0, : rows - HALF]], 0)
        ct = jnp.concatenate([arrived_grads, cotangent[0, : rows - HALF]], 0)
        all_states = lax.all_gather(global_states[0], "seq", axis=0, tiled=True)
        w1t = w1.T
        h, q, k, v = project_local(x, norms[0], norms[1], wq, wk, wv)
        gh, gq, gk, gv = project_global(
            scalars, rows, group_rows, all_states, norms[2], norms[3], wq, wk, wv
        )
    else:
        h, q, k, v, x, ct, all_states, gh, gq, gk, gv, w1t = gather_project(
            tokens[0], cotangent[0], global_states[0], w1, norm_params, wq, wk, wv
        )
        all_states = all_states.reshape(-1, width)
    far, far_stat, part, part_stat = slot_forward(scalars, rows, group_rows, q, k, v, gq, gk, gv)
    if grid_of is None:
        o, line = local_forward(
            False, scalars, rows, group_rows, q, k, v, far, far_stat, None, None
        )
        part_peak = part_stat[:, :, 0:2]
        peak = jnp.max(lax.all_gather(part_peak, "seq"), axis=0)
        factor = jnp.exp(part_peak - peak)
        scaled = part.reshape(SLOTS, PAIRS, 2, HEAD_DIM, GLOBALS).astype(f32) * factor[:, :, :, None]
        scaled = scaled.reshape(SLOTS, width, GLOBALS)
        scaled_total = (part_stat[:, :, 2:4] * factor).reshape(SLOTS, HEADS, GLOBALS)
        payload = jnp.concatenate(
            [scaled, scaled_total, jnp.zeros((SLOTS, 4, GLOBALS), f32)], 1
        ).transpose(0, 2, 1)
        sums = lax.psum_scatter(
            payload.astype(bf16).reshape(SLOTS * GLOBALS, -1), "seq", scatter_dimension=0, tiled=True
        ).astype(f32)
        own_total = sums[:, width : width + HEADS]
        all_peak = peak.reshape(SLOTS, HEADS, GLOBALS).transpose(0, 2, 1).reshape(-1, HEADS)
        own_peak = lax.dynamic_slice_in_dim(all_peak, own_start, own, 0)
        go = (
            (sums[:, :width].reshape(own, HEADS, HEAD_DIM) / own_total[:, :, None])
            .reshape(own, width)
            .astype(bf16)
        )
        gstat = own_peak + jnp.log(own_total)
    else:
        o, line, half_sum, half_stat = local_forward(
            True, scalars, rows, group_rows, q, k, v, far, far_stat, part, part_stat
        )

    z, dy, do, gz, gdy, gdo, dwo, db1, db2, dgain2, doffset2, *dws = branch(
        grid_of,
        x,
        o,
        ct,
        global_states[0],
        go if grid_of is None else half_sum,
        gstat if grid_of is None else half_stat,
        global_cotangent[0],
        wo,
        w1t,
        b1,
        w2,
        b2_line,
        norm_params,
    )
    if grid_of is None:
        gcentre = jnp.sum(
            (gdo.astype(f32) * go.astype(f32)).reshape(own, HEADS, HEAD_DIM), axis=-1
        )
        message = jnp.concatenate(
            [gdo]
            + pieces(gstat)
            + pieces(gcentre)
            + [jnp.zeros((own, LANES - 6 * HEADS), bf16)],
            axis=1,
        )
        everyone = lax.all_gather(message, "seq", axis=0, tiled=True)
        dqt, dk, dv, centre = local_backward(
            False, scalars, rows, group_rows, q, k, v, do, o, line, None, None, None, None
        )
    else:
        sum_first, last, message, rest = dws
        dqt, dk, dv, centre, everyone, sum_second, rest = local_backward(
            True, scalars, rows, group_rows, q, k, v, do, o, line, message, rest, last, dwo
        )
    dq, dk, dv, dwg, dgh, dnorm_global = slot_backward(
        scalars,
        rows,
        group_rows,
        q,
        k,
        v,
        do,
        line,
        centre,
        dqt,
        dk,
        dv,
        gq,
        gk,
        gv,
        everyone,
        all_states,
        gh,
        wq,
        wk,
        wv,
    )
    if grid_of is None:
        dx, dqkv, dnorm = project_back(x, dy, h, dq, dk, dv, dwg, wq, wk, wv, norms[0])
        back_z, back_grad = from_behind((z[:HALF], dx[:HALF].astype(bf16)), "seq", -1)
        layer_out = jnp.concatenate([z[HALF:], back_z], 0)
        token_grad = jnp.concatenate([dx[HALF:], back_grad.astype(f32)], 0)
        small = jnp.concatenate([db1, db2, dnorm[:2], dnorm_global[:2], dgain2, doffset2], 0)
        dgh = lax.psum_scatter(dgh, "seq", scatter_dimension=0, tiled=True).astype(f32)
        gunit, gscale = normalize_rows(global_states[0].astype(f32))
        global_grad = gdy + norm_back(gunit, gscale, norms[2], dgh)
        small = lax.psum(small, ("batch", "seq"))
        dw1, dw2 = dws
        weights = [scatter_sum(value) for value in (dqkv[0], dqkv[1], dqkv[2], dwo, dw1, dw2)]
    else:
        sum_third, small, global_grad, layer_out, token_grad = finish_all(
            rest,
            x,
            dy,
            h,
            dq,
            dk,
            dv,
            dwg,
            dgh,
            z,
            wq,
            wk,
            wv,
            (db1, db2, dnorm_global, dgain2, doffset2),
            global_states[0],
            gdy,
            norm_params,
        )
        piece = width // seq_count
        lanes = width // batch_count
        steps = w1.shape[1] // FF_CHUNK
        chunks = jnp.concatenate([sum_first, sum_second, sum_third[: 2 * piece]], 0)
        chunks = chunks.reshape(steps, 2, piece, lanes)
        part1 = chunks[:, 0].reshape(steps * piece, lanes)
        part2 = chunks[:, 1].reshape(steps, piece, lanes // piece, piece)
        part2 = part2.transpose(1, 2, 0, 3).reshape(piece, -1)
        parts = [sum_third[i * piece : (i + 1) * piece] for i in (3, 4, 5, 2)] + [part1, part2]
        weights = [value.T for value in parts]
    hidden_rows = w1.shape[1] // width
    return (
        layer_out[None],
        gz[None],
        token_grad[None],
        global_grad[None],
        *weights,
        small[:hidden_rows].reshape(-1),
        small[hidden_rows],
        small[hidden_rows + 1 : hidden_rows + 7],
    )


def solution(mesh):
    split = P("batch", "seq", None)
    return jax.shard_map(
        on_device,
        mesh=mesh,
        in_specs=(split, split) + (P(),) * 11 + (split, split),
        out_specs=(split,) * 4 + (P("batch", "seq"),) * 6 + (P(),) * 3,
        check_vma=False,
    )
```

```python
import functools

import jax
import jax.numpy as jnp
from jax import lax
from jax.experimental import pallas as pl
from jax.experimental.pallas import tpu as pltpu
from jax.sharding import PartitionSpec as P

HEADS = 12
HEAD_DIM = 64
PAIRS = HEADS // 2
LANES = 128
BLOCK = 512
HALF = 256
GLOBALS = 128
SLOTS = 8
FF_CHUNK = 768
TOGETHER = 3

norm_eps = 1e-05
masked_score = -1e30
query_scale = 0.125

SLOT_LANE = 16
GLOBAL_LANE = 32

f32 = jnp.float32
bf16 = jnp.bfloat16
VMEM_LIMIT = 60 * 1024 * 1024


def nn(left, right):
    return jnp.dot(left, right, preferred_element_type=f32)


def nt(left, right):
    return lax.dot_general(left, right, (((1,), (1,)), ((), ())), preferred_element_type=f32)


def tn(left, right):
    return lax.dot_general(left, right, (((0,), (0,)), ((), ())), preferred_element_type=f32)


def iota(shape, dim):
    return lax.broadcasted_iota(jnp.int32, shape, dim)


def stack_pair(pair):
    lane = iota((1, LANES), 1)
    low = jnp.where(lane < HEAD_DIM, 1.0, 0.0).astype(bf16)
    high = jnp.where(lane < HEAD_DIM, 0.0, 1.0).astype(bf16)
    return jnp.concatenate([pair * low, pair * high], axis=0)


def read_edges(lengths, bucket_of, place, edges):
    bucket = bucket_of[place[0]]
    total = jnp.int32(0)
    edges[0] = total
    for slot in range(SLOTS):
        total = total + lengths[bucket, slot]
        edges[slot + 1] = total


def block_start(place, rows, block):
    return place[1] * rows + block * BLOCK - HALF


def slot_present(slot, place, edges, rows, group_rows, block):
    low = edges[slot]
    high = edges[slot + 1]
    found = jnp.bool_(False)
    for part in range(BLOCK // HALF):
        start = block_start(place, rows, block) + part * HALF
        start = jnp.where(start < 0, start + group_rows, start)
        found = found | ((high > low) & (low < start + HALF) & (high > start))
    return found


def row_numbers(place, edges, rows, group_rows, block):
    place_in = block_start(place, rows, block) + iota((BLOCK, LANES), 0)
    wrapped = place_in < 0
    token = jnp.where(wrapped, place_in + group_rows, place_in)
    slot = jnp.zeros((BLOCK, LANES), jnp.int32)
    for j in range(SLOTS):
        slot = slot + jnp.where(edges[j + 1] <= token, 1, 0)
    return slot, slot + jnp.where(wrapped, SLOTS, 0)


def key_extra(slot, segment):
    lane = iota((BLOCK, LANES), 1)
    extra = jnp.where((lane < SLOT_LANE) & (lane != segment), masked_score, 0.0)
    return jnp.where(lane == GLOBAL_LANE + slot, 1.0, extra)


def query_extra(slot, segment):
    lane = iota((BLOCK, LANES), 1)
    return jnp.where((lane == segment) | (lane == SLOT_LANE + slot), 1.0, 0.0)


def global_key_extra(slot):
    lane = iota((GLOBALS, LANES), 1)
    inside = (lane >= SLOT_LANE) & (lane < SLOT_LANE + SLOTS)
    extra = jnp.where(inside & (lane != SLOT_LANE + slot), masked_score, 0.0)
    return jnp.where(lane == GLOBAL_LANE + slot, 1.0, extra)


def global_query_extra(slot):
    lane = iota((GLOBALS, LANES), 1)
    inside = (lane >= GLOBAL_LANE) & (lane < GLOBAL_LANE + SLOTS)
    return jnp.where(inside & (lane != GLOBAL_LANE + slot), masked_score, 0.0)


def normalize_rows(values):
    mean = jnp.mean(values, axis=-1, keepdims=True)
    centered = values - mean
    variance = jnp.mean(centered * centered, axis=-1, keepdims=True)
    scale = lax.rsqrt(variance + norm_eps)
    return centered * scale, scale


def norm_back(unit, scale, gain, upstream):
    inner = upstream * gain
    along = jnp.mean(inner * unit, axis=-1, keepdims=True)
    return scale * (inner - jnp.mean(inner, axis=-1, keepdims=True) - unit * along)


def gelu_parts(value):
    decay = jnp.exp(-0.5 * value * value)
    step = 1.0 / (1.0 + (0.3275911 * 0.7071067811865476) * jnp.abs(value))
    series = 1.061405429 * step - 1.453152027
    series = series * step + 1.421413741
    series = series * step - 0.284496736
    series = series * step + 0.254829592
    tail = (0.5 * series) * step * decay
    area = jnp.where(value >= 0.0, 1.0 - tail, tail)
    return area, decay * 0.3989422804014327


def full(shape):
    return pl.BlockSpec(shape, lambda *unused: (0,) * len(shape))


def once(shape):
    return pl.BlockSpec(
        shape, lambda *unused: (0,) * len(shape), pipeline_mode=pl.Buffered(buffer_count=1)
    )


def params(**more):
    return pltpu.CompilerParams(vmem_limit_bytes=VMEM_LIMIT, **more)


STAGES = 5
MESH = pl.DeviceIdType.MESH
WEIGHTS = (("core", 1), ("y", 2), ("z0", 4), ("z1", 8))


def my_place():
    batch = lax.axis_index("batch")
    seq = lax.axis_index("seq")
    bits = {"x": batch}
    partners = {"x": (1 - batch, seq)}
    for name, weight in WEIGHTS:
        bits[name] = (seq // weight) % 2
        partners[name] = (batch, seq + weight - 2 * weight * bits[name])
    return bits, partners


def meet(devices):
    barrier = pltpu.get_barrier_semaphore()
    for device in devices:
        pl.semaphore_signal(barrier, inc=1, device_id=device, device_id_type=MESH)
    pl.semaphore_wait(barrier, len(devices))


def remote(source, target, send, recv, device):
    return pltpu.make_async_remote_copy(
        src_ref=source,
        dst_ref=target,
        send_sem=send,
        recv_sem=recv,
        device_id=device,
        device_id_type=MESH,
    )


class RowGather:
    def __init__(self, ref, cut, send_sem, recv_sem, bits, partners):
        self.ref = ref
        self.cut = cut
        self.send_sem = send_sem
        self.recv_sem = recv_sem
        self.bits = bits
        self.partners = partners

    def copies(self, number):
        core, y, z0, z1 = (self.bits[name] for name in ("core", "y", "z0", "z1"))
        ref = self.ref
        rows = pl.ds(0, ref.shape[4])
        left = pl.ds(0, self.cut)
        right = pl.ds(self.cut, ref.shape[5] - self.cut)
        if number == 0:
            moves = [
                (ref.at[z1, z0, y, core, rows, left], "z1"),
                (ref.at[z1, z0, y, core, rows, right], "y"),
            ]
        elif number == 1:
            moves = [
                (ref.at[:, z0, y, core, rows, left], "z0"),
                (ref.at[z1, z0, :, core, rows, right], "z1"),
            ]
        elif number == 2:
            moves = [
                (ref.at[:, :, y, core, rows, left], "y"),
                (ref.at[:, z0, :, core, rows, right], "z0"),
            ]
        else:
            moves = [
                (ref.at[:, :, :, core, rows, left], "core"),
                (ref.at[:, :, :, core, rows, right], "core"),
            ]
        return [
            remote(
                part,
                part,
                self.send_sem.at[number, side],
                self.recv_sem.at[number, side],
                self.partners[name],
            )
            for side, (part, name) in enumerate(moves)
        ]

    def begin(self):
        for copy in self.copies(0):
            copy.start()

    def advance(self, number):
        for copy in self.copies(number):
            copy.wait_recv()
        if number < 3:
            for copy in self.copies(number + 1):
                copy.start()

    def end(self):
        for number in range(4):
            for copy in self.copies(number):
                copy.wait_send()


X_FIRST = ("core", "x", "y", "z0", "z1")
Y_FIRST = ("core", "y", "x", "z0", "z1")
Z_FIRST = ("core", "z0", "x", "z1", "y")
AXES = ("z1", "z0", "y", "core", "x")


class HalvingSum:
    def __init__(
        self, orders, sources, landings, own, send_sem, recv_sem, own_sem, put, bits, partners
    ):
        self.orders = orders
        self.sources = sources
        self.landings = landings
        self.own = own
        self.send_sem = send_sem
        self.recv_sem = recv_sem
        self.own_sem = own_sem
        self.put = put
        self.bits = bits
        self.partners = partners

    def part(self, unit, stage, other):
        order = self.orders[unit]
        name = order[stage]
        side = 1 - self.bits[name] if other else self.bits[name]
        if stage == 0:
            if not other and self.own is not None:
                return self.own.at[unit]
            return self.sources[unit](side)
        left = [axis for axis in AXES if axis in order[stage:]]
        index = (slice(None),) * left.index(name) + (side,)
        return self.landings[stage - 1].at[unit].at[index]

    def copy(self, unit, stage):
        return remote(
            self.part(unit, stage, True),
            self.landings[stage].at[unit],
            self.send_sem.at[unit, stage],
            self.recv_sem.at[unit, stage],
            self.partners[self.orders[unit][stage]],
        )

    def own_copy(self, unit):
        return pltpu.make_async_copy(
            self.sources[unit](self.bits["core"]), self.own.at[unit], self.own_sem.at[unit]
        )

    def begin(self, unit):
        if self.own is not None:
            self.own_copy(unit).start()
        self.copy(unit, 0).start()

    def advance(self, unit, stage, stop=False):
        if stage == 0 and self.own is not None:
            self.own_copy(unit).wait()
        self.copy(unit, stage).wait_recv()
        landing = self.landings[stage].at[unit]
        kept = self.part(unit, stage, False)
        if stage < len(self.orders[unit]) - 1:
            add_into(landing, kept)
            if not stop:
                self.copy(unit, stage + 1).start()
        else:
            self.put(unit, landing[...].astype(f32) + kept[...].astype(f32))

    def sent(self, unit, stage):
        self.copy(unit, stage).wait_send()


def put_rows(ref, rows):
    def put(unit, value):
        ref[unit * rows : (unit + 1) * rows] = value

    return put


def add_into(target, more):
    def one(i, carry):
        target[i] = target[i] + more[i]
        return carry

    lax.fori_loop(0, target.shape[0], one, 0)


def sum_scratch(units, rows, lanes, with_own):
    piece = (rows, lanes)
    dma = pltpu.SemaphoreType.DMA
    shapes = [pltpu.VMEM((units, 2, 2, 2, 2) + piece, bf16)] if with_own else []
    shapes += [
        pltpu.VMEM((units, 2, 2, 2, 2) + piece, bf16),
        pltpu.VMEM((units, 2, 2, 2) + piece, bf16),
        pltpu.VMEM((units, 2, 2) + piece, bf16),
        pltpu.VMEM((units, 2) + piece, bf16),
        pltpu.VMEM((units,) + piece, bf16),
        dma((units, STAGES)),
        dma((units, STAGES)),
    ]
    return shapes + ([dma((units,))] if with_own else [])


def project_rows(rows_ref, gain_ref, offset_ref, wq_ref, wk_ref, wv_ref, outs):
    unit, unused = normalize_rows(rows_ref[...].astype(f32))
    normed = (unit * gain_ref[...] + offset_ref[...]).astype(bf16)
    outs[0][...] = normed
    outs[1][...] = (nn(normed, wq_ref[...]) * query_scale).astype(bf16)
    outs[2][...] = nn(normed, wk_ref[...]).astype(bf16)
    outs[3][...] = nn(normed, wv_ref[...]).astype(bf16)


def project_local_kernel(rows_ref, gain_ref, offset_ref, wq_ref, wk_ref, wv_ref, *outs):
    project_rows(rows_ref, gain_ref, offset_ref, wq_ref, wk_ref, wv_ref, outs)


def project_local(rows, gain, offset, wq, wk, wv):
    count, width = rows.shape
    tile = pl.BlockSpec((BLOCK, width), lambda i: (i, 0))
    return pl.pallas_call(
        project_local_kernel,
        grid=(count // BLOCK,),
        in_specs=[tile, full((1, width)), full((1, width))] + [once((width, width))] * 3,
        out_specs=[tile] * 4,
        out_shape=[jax.ShapeDtypeStruct((count, width), bf16)] * 4,
        compiler_params=params(),
        cost_estimate=pl.CostEstimate(
            flops=6 * count * width * width, bytes_accessed=12 * count * width, transcendentals=0
        ),
        name="project_local",
    )(rows, gain, offset, wq, wk, wv)


def gather_project_kernel(
    tokens_ref,
    ct_ref,
    states_ref,
    w1_ref,
    norms_ref,
    wq_in,
    wk_in,
    wv_in,
    h_out,
    q_out,
    k_out,
    v_out,
    x_out,
    ct_out,
    all_out,
    gh_out,
    gq_out,
    gk_out,
    gv_out,
    w1t_out,
    wq_ref,
    wk_ref,
    wv_ref,
    x_ref,
    all_ref,
    local_ref,
    global_ref,
    w1s_ref,
    w1t_ref,
    halo_send,
    halo_recv,
    load_sem,
    store_sem,
    gstore_sem,
    more_sem,
    send_sem,
    recv_sem,
):
    bits, partners = my_place()
    batch = lax.axis_index("batch")
    seq = lax.axis_index("seq")
    places = lax.axis_size("seq")
    after = (batch, lax.rem(seq + 1, places))
    before = (batch, lax.rem(seq + places - 1, places))
    rows, width = tokens_ref.shape
    own = states_ref.shape[0]
    core, y, z0, z1 = (bits[name] for name in ("core", "y", "z0", "z1"))
    start = pl.ds(0, HALF)
    most = pl.ds(0, rows - HALF)
    end = pl.ds(rows - HALF, HALF)
    shifted = pl.ds(HALF, rows - HALF)
    loads = [
        pltpu.make_async_copy(source, target, load_sem.at[number])
        for number, (source, target) in enumerate(
            (
                (tokens_ref.at[most], x_ref.at[shifted]),
                (wq_in, wq_ref),
                (wk_in, wk_ref),
                (wv_in, wv_ref),
                (w1_ref, w1s_ref),
                (ct_ref.at[most], ct_out.at[shifted]),
            )
        )
    ]
    for load in loads:
        load.start()
    all_ref[z1, z0, y, core] = states_ref[...]
    meet([partners[name] for name, unused in WEIGHTS] + [before, after])
    halo = [
        remote(tokens_ref.at[end], x_ref.at[start], halo_send.at[0], halo_recv.at[0], after),
        remote(ct_ref.at[end], ct_out.at[start], halo_send.at[1], halo_recv.at[1], after),
    ]
    gather = RowGather(all_ref, width // 2, send_sem, recv_sem, bits, partners)
    gather.begin()
    halo[0].start()

    outs = (h_out, q_out, k_out, v_out)

    def stores(index):
        at = pl.ds(index * HALF, HALF)
        return [
            pltpu.make_async_copy(local_ref.at[which, at], out.at[at], store_sem.at[which, index])
            for which, out in enumerate(outs)
        ]

    def project(index):
        at = pl.ds(index * HALF, HALF)
        project_rows(
            x_ref.at[at],
            norms_ref.at[0:1],
            norms_ref.at[1:2],
            wq_ref,
            wk_ref,
            wv_ref,
            [local_ref.at[which, at] for which in range(4)],
        )
        for store in stores(index):
            store.start()

    for number in range(4):
        loads[number].wait()
    tiles = rows // HALF
    project(1)
    gather.advance(0)
    for index in range(2, tiles):
        project(index)
    gather.advance(1)
    halo[0].wait_recv()
    x_store = pltpu.make_async_copy(x_ref, x_out, more_sem.at[0])
    x_store.start()
    project(0)
    loads[4].wait()

    def turn(i, carry):
        at = pl.ds(pl.multiple_of(i * HALF, HALF), HALF)
        w1t_ref[at, :] = w1s_ref[:, at].T
        return carry

    lax.fori_loop(0, w1t_ref.shape[0] // HALF, turn, 0)
    w1t_store = pltpu.make_async_copy(w1t_ref, w1t_out, more_sem.at[1])
    w1t_store.start()
    gather.advance(2)
    halo[1].start()

    gouts = (gh_out, gq_out, gk_out, gv_out)

    def gstores(first, side):
        return [
            pltpu.make_async_copy(
                global_ref.at[which, first, :, :, side],
                out.at[first, :, :, side],
                gstore_sem.at[which, first, number],
            )
            for which, out in enumerate(gouts)
            for number in ((0 if side is core else 1),)
        ]

    def project_states(side):
        for first in range(2):
            piece = all_ref[first, :, :, side].reshape(4 * own, width)
            unit, unused = normalize_rows(piece.astype(f32))
            normed = (unit * norms_ref[2:3] + norms_ref[3:4]).astype(bf16)
            values = (
                normed,
                (nn(normed, wq_ref[...]) * query_scale).astype(bf16),
                nn(normed, wk_ref[...]).astype(bf16),
                nn(normed, wv_ref[...]).astype(bf16),
            )
            for which, value in enumerate(values):
                global_ref[which, first, :, :, side] = value.reshape(2, 2, own, width)
            for store in gstores(first, side):
                store.start()

    other = 1 - core
    project_states(core)
    gather.advance(3)
    all_store = pltpu.make_async_copy(all_ref, all_out, more_sem.at[2])
    all_store.start()
    project_states(other)

    for index in range(tiles):
        for store in stores(index):
            store.wait()
    for side in (core, other):
        for first in range(2):
            for store in gstores(first, side):
                store.wait()
    x_store.wait()
    w1t_store.wait()
    all_store.wait()
    loads[5].wait()
    halo[1].wait_recv()
    for copy in halo:
        copy.wait_send()
    gather.end()


def gather_project(tokens, ct, states, w1, norms, wq, wk, wv):
    rows, width = tokens.shape
    own = states.shape[0]
    vmem = pl.BlockSpec(memory_space=pltpu.VMEM)
    anywhere = pl.BlockSpec(memory_space=pl.ANY)
    dma = pltpu.SemaphoreType.DMA
    local = jax.ShapeDtypeStruct((rows, width), bf16)
    glob = jax.ShapeDtypeStruct((2, 2, 2, 2, own, width), bf16)
    turned = (w1.shape[1], width)
    weight = pltpu.VMEM((width, width), bf16)
    return pl.pallas_call(
        gather_project_kernel,
        in_specs=[anywhere, anywhere, vmem, anywhere, vmem] + [anywhere] * 3,
        out_specs=[anywhere] * 12,
        out_shape=[local] * 6 + [glob] * 5 + [jax.ShapeDtypeStruct(turned, bf16)],
        scratch_shapes=[
            weight,
            weight,
            weight,
            pltpu.VMEM((rows, width), bf16),
            pltpu.VMEM(glob.shape, bf16),
            pltpu.VMEM((4, rows, width), bf16),
            pltpu.VMEM((4,) + glob.shape, bf16),
            pltpu.VMEM(w1.shape, bf16),
            pltpu.VMEM(turned, bf16),
            dma((2,)),
            dma((2,)),
            dma((6,)),
            dma((4, rows // HALF)),
            dma((4, 2, 2)),
            dma((3,)),
            dma((4, 2)),
            dma((4, 2)),
        ],
        compiler_params=params(collective_id=1, has_side_effects=True),
        cost_estimate=pl.CostEstimate(
            flops=6 * (rows + 16 * own) * width * width,
            bytes_accessed=24 * rows * width,
            transcendentals=0,
        ),
        name="gather_project",
    )(tokens, ct, states, w1, norms, wq, wk, wv)


def project_global_kernel(
    rows_count,
    group_rows,
    lengths,
    bucket_of,
    place,
    rows_ref,
    gain_ref,
    offset_ref,
    wq_ref,
    wk_ref,
    wv_ref,
    h_ref,
    q_ref,
    k_ref,
    v_ref,
    edges,
):
    slot = pl.program_id(0)

    @pl.when(slot == 0)
    def _():
        read_edges(lengths, bucket_of, place, edges)

    needed = slot == place[2]
    for block in range(rows_count // BLOCK):
        needed = needed | slot_present(slot, place, edges, rows_count, group_rows, block)

    @pl.when(needed)
    def _():
        project_rows(
            rows_ref, gain_ref, offset_ref, wq_ref, wk_ref, wv_ref, (h_ref, q_ref, k_ref, v_ref)
        )


def project_global(scalars, rows_count, group_rows, rows, gain, offset, wq, wk, wv):
    count, width = rows.shape
    tile = pl.BlockSpec((GLOBALS, width), lambda i, *unused: (i, 0))
    return pl.pallas_call(
        functools.partial(project_global_kernel, rows_count, group_rows),
        grid_spec=pltpu.PrefetchScalarGridSpec(
            num_scalar_prefetch=3,
            grid=(SLOTS,),
            in_specs=[tile, full((1, width)), full((1, width))] + [once((width, width))] * 3,
            out_specs=[tile] * 4,
            scratch_shapes=[pltpu.SMEM((16,), jnp.int32)],
        ),
        out_shape=[jax.ShapeDtypeStruct((count, width), bf16)] * 4,
        compiler_params=params(),
        cost_estimate=pl.CostEstimate(
            flops=6 * 256 * width * width, bytes_accessed=12 * count * width, transcendentals=0
        ),
        name="project_global",
    )(*scalars, rows, gain, offset, wq, wk, wv)


def block_columns(place, edges, rows, group_rows, block, step, blocks, query_columns, key_columns):
    @pl.when(step < blocks)
    def _():
        slot_of, segment = row_numbers(place, edges, rows, group_rows, block)
        query_columns[block] = query_extra(slot_of, segment).astype(bf16)
        key_columns[block] = key_extra(slot_of, segment).astype(bf16)


def slot_line(place, edges, rows, group_rows, block):
    token = block_start(place, rows, block) + iota((1, BLOCK), 1)
    token = jnp.where(token < 0, token + group_rows, token)
    slot = jnp.zeros((1, BLOCK), jnp.int32)
    for j in range(SLOTS):
        slot = slot + jnp.where(edges[j + 1] <= token, 1, 0)
    return slot


def side_by_side(stacked):
    return stacked[:HEAD_DIM, : stacked.shape[1] // 2], stacked[HEAD_DIM:, stacked.shape[1] // 2 :]


def slot_forward_kernel(
    rows_count,
    group_rows,
    lengths,
    bucket_of,
    place,
    q_ref,
    k_ref,
    v_ref,
    gq_ref,
    gk_ref,
    gv_ref,
    far_ref,
    far_stat_ref,
    part_ref,
    part_stat_ref,
    edges,
    query_columns,
    key_columns,
    keys_ref,
    queries_ref,
    sum_ref,
    far_sum,
):
    group = pl.program_id(0)
    block = pl.program_id(1)
    blocks = rows_count // BLOCK
    step = group * blocks + block
    together = range(TOGETHER)

    @pl.when(step == 0)
    def _():
        read_edges(lengths, bucket_of, place, edges)

    @pl.when(block == 0)
    def _():
        sum_ref[...] = jnp.zeros_like(sum_ref)
        part_stat_ref[...] = jnp.broadcast_to(
            jnp.where(iota((8, GLOBALS), 0) < 2, masked_score, 0.0), part_stat_ref.shape
        )

    block_columns(
        place, edges, rows_count, group_rows, block, step, blocks, query_columns, key_columns
    )
    extra = query_columns[block]
    for which in together:
        lanes = pl.ds(which * LANES, LANES)
        keys_ref[which, :, :LANES] = k_ref[:, lanes]
        keys_ref[which, :, LANES:] = key_columns[block]
        queries_ref[which, :, :LANES] = stack_pair(q_ref[:, lanes])
        queries_ref[which, :BLOCK, LANES:] = extra
        queries_ref[which, BLOCK:, LANES:] = extra
    line = slot_line(place, edges, rows_count, group_rows, block)
    both_lines = jnp.concatenate([line, line], 1)

    def add(slot, keys_of, values_of):
        at = pl.ds(pl.multiple_of(slot * GLOBALS, GLOBALS), GLOBALS)
        extra = global_query_extra(slot).astype(bf16)
        for which in together:
            lanes = pl.ds(which * LANES, LANES)
            queries = jnp.concatenate(
                [stack_pair(gq_ref[at, lanes]), jnp.concatenate([extra, extra], 0)], axis=1
            )
            score = nt(keys_of(which), queries)
            stat = part_stat_ref[slot, which]
            old = jnp.concatenate([stat[0:1], stat[1:2]], axis=1)
            peak = jnp.maximum(old, jnp.max(score, axis=0, keepdims=True))
            weights = jnp.exp(score - peak)
            keep = jnp.exp(old - peak)
            total = jnp.concatenate([stat[2:3], stat[3:4]], axis=1) * keep + jnp.sum(
                weights, axis=0, keepdims=True
            )
            part_stat_ref[slot, which] = jnp.concatenate(
                [
                    peak[:, :GLOBALS],
                    peak[:, GLOBALS:],
                    total[:, :GLOBALS],
                    total[:, GLOBALS:],
                    jnp.zeros((4, GLOBALS), f32),
                ],
                axis=0,
            )
            low, high = side_by_side(tn(values_of(which), weights.astype(bf16)))
            sums = sum_ref.at[which, slot]
            sums[:HEAD_DIM] = sums[:HEAD_DIM] * keep[:, :GLOBALS] + low
            sums[HEAD_DIM:] = sums[HEAD_DIM:] * keep[:, GLOBALS:] + high

    far_sum[...] = jnp.zeros_like(far_sum)
    far_stat_ref[...] = jnp.zeros_like(far_stat_ref)

    def one_slot(slot, carry):
        @pl.when(slot_present(slot, place, edges, rows_count, group_rows, block))
        def _():
            add(
                slot,
                lambda which: keys_ref[which],
                lambda which: v_ref[:, pl.ds(which * LANES, LANES)],
            )
            at = pl.ds(pl.multiple_of(slot * GLOBALS, GLOBALS), GLOBALS)
            columns = global_key_extra(slot).astype(bf16)
            mine = both_lines == slot
            here = line == slot
            for which in together:
                lanes = pl.ds(which * LANES, LANES)
                slot_keys = jnp.concatenate([gk_ref[at, lanes], columns], 1)
                score = nt(slot_keys, queries_ref[which])
                peak = jnp.max(score, axis=0, keepdims=True)
                weights = jnp.exp(score - peak)
                total = jnp.sum(weights, axis=0, keepdims=True)
                stat = far_stat_ref.at[which, 0]
                stat[0:1] = jnp.where(mine, peak, stat[0:1])
                stat[1:2] = jnp.where(mine, total, stat[1:2])
                low, high = side_by_side(tn(gv_ref[at, lanes], weights.astype(bf16)))
                first = pl.ds(which * LANES, HEAD_DIM)
                second = pl.ds(which * LANES + HEAD_DIM, HEAD_DIM)
                far_sum[first] = jnp.where(here, low, far_sum[first])
                far_sum[second] = jnp.where(here, high, far_sum[second])

        return carry

    lax.fori_loop(0, SLOTS, one_slot, 0)
    far_ref[...] = far_sum[...].astype(bf16)

    @pl.when((block == blocks - 1) & (place[2] >= 0))
    def _():
        slot = place[2]
        at = pl.ds(pl.multiple_of(slot * GLOBALS, GLOBALS), GLOBALS)
        columns = global_key_extra(slot).astype(bf16)
        add(
            slot,
            lambda which: jnp.concatenate(
                [gk_ref[at, pl.ds(which * LANES, LANES)], columns], axis=1
            ),
            lambda which: gv_ref[at, pl.ds(which * LANES, LANES)],
        )

    @pl.when(block == blocks - 1)
    def _():
        for which in together:
            part_ref[:, which] = sum_ref[which].astype(bf16)


def line_spec(pairs=1):
    return pl.BlockSpec((pairs, 1, 8, 2 * BLOCK), lambda p, b, *unused: (p, b, 0, 0))


def column_scratch(blocks):
    return [pltpu.SMEM((16,), jnp.int32)] + [pltpu.VMEM((blocks, BLOCK, LANES), bf16)] * 2


def slot_forward(scalars, rows_count, group_rows, q, k, v, gq, gk, gv):
    blocks = rows_count // BLOCK
    all_globals, width = gq.shape
    block_spec = pl.BlockSpec((BLOCK, TOGETHER * LANES), lambda p, b, *unused: (b, p))
    pair_spec = pl.BlockSpec((all_globals, TOGETHER * LANES), lambda p, b, *unused: (0, p))
    return pl.pallas_call(
        functools.partial(slot_forward_kernel, rows_count, group_rows),
        grid_spec=pltpu.PrefetchScalarGridSpec(
            num_scalar_prefetch=3,
            grid=(PAIRS // TOGETHER, blocks),
            in_specs=[block_spec] * 3 + [pair_spec] * 3,
            out_specs=[
                pl.BlockSpec((TOGETHER * LANES, BLOCK), lambda p, b, *unused: (p, b)),
                line_spec(TOGETHER),
                pl.BlockSpec((SLOTS, TOGETHER, LANES, GLOBALS), lambda p, b, *unused: (0, p, 0, 0)),
                pl.BlockSpec((SLOTS, TOGETHER, 8, GLOBALS), lambda p, b, *unused: (0, p, 0, 0)),
            ],
            scratch_shapes=column_scratch(blocks)
            + [
                pltpu.VMEM((TOGETHER, BLOCK, 2 * LANES), bf16),
                pltpu.VMEM((TOGETHER, 2 * BLOCK, 2 * LANES), bf16),
                pltpu.VMEM((TOGETHER, SLOTS, LANES, GLOBALS), f32),
                pltpu.VMEM((TOGETHER * LANES, BLOCK), f32),
            ],
        ),
        out_shape=[
            jax.ShapeDtypeStruct((width, rows_count), bf16),
            jax.ShapeDtypeStruct((PAIRS, blocks, 8, 2 * BLOCK), f32),
            jax.ShapeDtypeStruct((SLOTS, PAIRS, LANES, GLOBALS), bf16),
            jax.ShapeDtypeStruct((SLOTS, PAIRS, 8, GLOBALS), f32),
        ],
        compiler_params=params(),
        cost_estimate=pl.CostEstimate(
            flops=8 * 4 * rows_count * GLOBALS * width,
            bytes_accessed=20 * all_globals * width,
            transcendentals=2 * HEADS * rows_count * GLOBALS,
        ),
        name="slot_forward",
    )(*scalars, q, k, v, gq, gk, gv)


def merge_parts(stat, sums, more_stat, more_sums):
    peak = jnp.maximum(stat[0:2], more_stat[0:2])
    keep = jnp.exp(stat[0:2] - peak)
    take = jnp.exp(more_stat[0:2] - peak)
    total = stat[2:4] * keep + more_stat[2:4] * take
    low = sums[:HEAD_DIM].astype(f32) * keep[0:1] + more_sums[:HEAD_DIM].astype(f32) * take[0:1]
    high = sums[HEAD_DIM:].astype(f32) * keep[1:2] + more_sums[HEAD_DIM:].astype(f32) * take[1:2]
    return (
        jnp.concatenate([peak, total, jnp.zeros((4, GLOBALS), f32)], 0),
        jnp.concatenate([low, high], 0),
    )


class SlotSum:
    ORDER = ("core", "y", "z0", "z1")

    def __init__(self, source, sums, stats, send_sem, recv_sem, bits, partners):
        self.source = source
        self.sums = sums
        self.stats = stats
        self.send_sem = send_sem
        self.recv_sem = recv_sem
        self.bits = bits
        self.partners = partners

    def held(self, stage, other):
        bit = self.bits[self.ORDER[stage]]
        side = 1 - bit if other else bit
        if stage == 0:
            return self.source(side)
        index = ((), (slice(None), slice(None)), (slice(None),), ())[stage] + (side,)
        return self.sums[stage - 1].at[index], self.stats[stage - 1].at[index]

    def copies(self, stage):
        partner = self.partners[self.ORDER[stage]]
        sums, stat = self.held(stage, True)
        return (
            remote(
                sums,
                self.sums[stage],
                self.send_sem.at[stage, 0],
                self.recv_sem.at[stage, 0],
                partner,
            ),
            remote(
                stat,
                self.stats[stage],
                self.send_sem.at[stage, 1],
                self.recv_sem.at[stage, 1],
                partner,
            ),
        )

    def begin(self, stage):
        for copy in self.copies(stage):
            copy.start()

    def merge(self, stage, kept=None):
        for copy in self.copies(stage):
            copy.wait_recv()
        sums, stat = self.held(stage, False) if kept is None else kept
        lead = self.sums[stage].shape[:-3]
        total = 1
        for size in lead:
            total = total * size

        def one(number, carry):
            index = []
            left = number
            for size in reversed(lead):
                index.append(left % size)
                left = left // size
            index = tuple(reversed(index))
            for which in range(PAIRS // 2):
                spot = index + (which,)
                new_stat, new_sums = merge_parts(
                    self.stats[stage][spot], self.sums[stage][spot], stat[spot], sums[spot]
                )
                self.stats[stage][spot] = new_stat
                self.sums[stage][spot] = new_sums.astype(bf16)
            return carry

        lax.fori_loop(0, total, one, 0)

    def sent(self, stage):
        for copy in self.copies(stage):
            copy.wait_send()


def local_forward_kernel(
    talk,
    rows_count,
    group_rows,
    lengths,
    bucket_of,
    place,
    q_ref,
    k_ref,
    v_ref,
    far_ref,
    far_stat_ref,
    *refs,
):
    if talk:
        part_ref, part_stat_ref, o_ref, line_ref, half_ref, half_stat_ref = refs[:6]
        own_ref, own_stat_ref = refs[6:8]
        sums_refs = refs[8:10]
        stat_refs = refs[10:12]
        edges, query_columns, key_columns, send_sem, recv_sem, own_sem = refs[12:]
    else:
        o_ref, line_ref, edges, query_columns, key_columns = refs
    pair = pl.program_id(0)
    block = pl.program_id(1)
    blocks = rows_count // BLOCK
    step = pair * blocks + block

    @pl.when(step == 0)
    def _():
        read_edges(lengths, bucket_of, place, edges)

    if talk:
        bits, partners = my_place()
        slot_sum = SlotSum(
            lambda side: (part_ref.at[:, :, :, side], part_stat_ref.at[:, :, :, side]),
            sums_refs,
            stat_refs,
            send_sem,
            recv_sem,
            bits,
            partners,
        )
        own_parts = slot_sum.held(0, False)
        own_copies = [
            pltpu.make_async_copy(own_parts[0], own_ref, own_sem.at[0]),
            pltpu.make_async_copy(own_parts[1], own_stat_ref, own_sem.at[1]),
        ]

        @pl.when(step == 0)
        def _():
            meet([partners["core"], partners["y"]])
            for copy in own_copies:
                copy.start()
            slot_sum.begin(0)

        @pl.when(step == 3)
        def _():
            for copy in own_copies:
                copy.wait()
            slot_sum.merge(0, (own_ref, own_stat_ref))
            slot_sum.begin(1)

        @pl.when(step == PAIRS * blocks - 1)
        def _():
            slot_sum.merge(1)
            half_ref[...] = sums_refs[1][...]
            half_stat_ref[...] = stat_refs[1][...]
            slot_sum.sent(0)
            slot_sum.sent(1)

    block_columns(
        place, edges, rows_count, group_rows, block, step, blocks, query_columns, key_columns
    )
    extra = query_columns[block]
    queries = jnp.concatenate(
        [stack_pair(q_ref[...]), jnp.concatenate([extra, extra], 0)], axis=1
    )
    keys = jnp.concatenate([k_ref[...], key_columns[block]], axis=1)
    score = nt(keys, queries)
    far_peak = far_stat_ref[0, 0, 0:1]
    peak = jnp.maximum(jnp.max(score, axis=0, keepdims=True), far_peak)
    weights = jnp.exp(score - peak)
    far_keep = jnp.exp(far_peak - peak)
    total = jnp.sum(weights, axis=0, keepdims=True) + far_stat_ref[0, 0, 1:2] * far_keep
    low, high = side_by_side(tn(v_ref[...], weights.astype(bf16)))
    low = (low + far_ref[:HEAD_DIM] * far_keep[:, :BLOCK]) / total[:, :BLOCK]
    high = (high + far_ref[HEAD_DIM:] * far_keep[:, BLOCK:]) / total[:, BLOCK:]
    o_ref[...] = jnp.concatenate([low, high], 0).T.astype(bf16)
    line_ref[0, 0] = jnp.broadcast_to(peak + jnp.log(total), (8, 2 * BLOCK))


def local_forward(talk, scalars, rows_count, group_rows, q, k, v, far, far_stat, part, part_stat):
    blocks = rows_count // BLOCK
    width = q.shape[1]
    block_spec = pl.BlockSpec((BLOCK, LANES), lambda p, b, *unused: (b, p))
    operands = [q, k, v, far, far_stat]
    in_specs = [block_spec] * 3 + [
        pl.BlockSpec((LANES, BLOCK), lambda p, b, *unused: (p, b)),
        line_spec(),
    ]
    out_specs = [block_spec, line_spec()]
    out_shape = [
        jax.ShapeDtypeStruct((rows_count, width), bf16),
        jax.ShapeDtypeStruct((PAIRS, blocks, 8, 2 * BLOCK), f32),
    ]
    scratch = []
    more = {}
    edges = column_scratch(blocks)
    if talk:
        cut = (2, 2, 2, 2, PAIRS // 2)
        operands += [part.reshape(cut + part.shape[2:]), part_stat.reshape(cut + part_stat.shape[2:])]
        in_specs += [pl.BlockSpec(memory_space=pl.ANY)] * 2
        shapes = [
            (2, 2, PAIRS // 2, LANES, GLOBALS),
            (2, 2, PAIRS // 2, 8, GLOBALS),
        ]
        out_specs += [full(shape) for shape in shapes]
        out_shape += [
            jax.ShapeDtypeStruct(shapes[0], bf16),
            jax.ShapeDtypeStruct(shapes[1], f32),
        ]
        leads = [(2, 2, 2), (2, 2, 2), (2, 2)]
        sums = [pltpu.VMEM(lead + shapes[0][2:], bf16) for lead in leads]
        stats = [pltpu.VMEM(lead + shapes[1][2:], f32) for lead in leads]
        dma = pltpu.SemaphoreType.DMA
        scratch = [sums[0], stats[0]] + sums[1:] + stats[1:]
        edges += [dma((2, 2)), dma((2, 2)), dma((2,))]
        more = {"collective_id": 2, "has_side_effects": True}
    return pl.pallas_call(
        functools.partial(local_forward_kernel, talk, rows_count, group_rows),
        grid_spec=pltpu.PrefetchScalarGridSpec(
            num_scalar_prefetch=3,
            grid=(PAIRS, blocks),
            in_specs=in_specs,
            out_specs=out_specs,
            scratch_shapes=scratch + edges,
        ),
        out_shape=out_shape,
        compiler_params=params(**more),
        cost_estimate=pl.CostEstimate(
            flops=16 * rows_count * BLOCK * width,
            bytes_accessed=16 * rows_count * width,
            transcendentals=HEADS * rows_count * BLOCK,
        ),
        name="local_forward",
    )(*scalars, *operands)


def put_grouped(ref, value):
    seq, batch, rows, lanes = ref.shape
    for part in range(batch):
        piece = value[:, part * lanes : (part + 1) * lanes].astype(bf16)
        ref[:, part] = piece.reshape(seq, rows, lanes)


def put_unit(ref, value):
    batch, rows, lanes = ref.shape[4:]
    for part in range(batch):
        piece = value[:, part * lanes : (part + 1) * lanes].astype(bf16)
        ref[:, :, :, :, part] = piece.reshape(ref.shape[:4] + (rows, lanes))


TICKS = 3
DELAYS = (0, 2, 3, 4, 6)


def branch_kernel(
    tile,
    talk,
    x_ref,
    o_ref,
    ct_ref,
    gx_ref,
    go_in_ref,
    gstat_in_ref,
    gct_ref,
    wo_ref,
    w1_ref,
    b1_ref,
    w2_ref,
    b2_ref,
    norms_ref,
    z_ref,
    dy_ref,
    do_ref,
    gz_ref,
    gdy_ref,
    gdo_ref,
    dwo_ref,
    db1_ref,
    db2_ref,
    dgain_ref,
    doffset_ref,
    first_ref,
    second_ref,
    *refs,
):
    if talk:
        message_ref, rest_ref = refs[:2]
        refs = refs[2:]
    os_ref, cts_ref, y_ref, h_ref, z_sum_ref, dh_ref, dft_ref, a_ref, du_ref, load_sem = refs[:10]
    refs = refs[10:]
    step = pl.program_id(0)
    steps = pl.num_programs(0)
    count, width = x_ref.shape
    own = gx_ref.shape[0]
    extra = os_ref.shape[0] - count
    tiles = count // tile
    tail = pl.ds(count, extra)

    def rows_at(i):
        return pl.ds(i * tile, tile)

    def padded(value):
        return jnp.concatenate([value, jnp.zeros((extra - own, width), value.dtype)], axis=0)

    if talk:
        units_ref = refs[0]
        landings = refs[1:6]
        send_sem, recv_sem = refs[6:8]
        half_ref, half_stat_ref = refs[8:10]
        slot_sums = refs[10:12]
        slot_stats = refs[12:14]
        turned_ref, go_land, gstat_land, stat_ref, slot_send, slot_recv = refs[14:]
        last_step = 4
        bits, partners = my_place()
        core = bits["core"]
        chunks = last_step - 1
        slots = units_ref.shape[0]
        plan = [
            (TICKS * chunk + DELAYS[stage], chunk, stage)
            for chunk in range(chunks)
            for stage in range(STAGES if chunk < chunks - 1 else 2)
        ]

        def source(unit):
            return lambda side: units_ref.at[unit % slots, :, :, :, side]

        engine = HalvingSum(
            (X_FIRST, Y_FIRST) * chunks,
            [source(unit) for unit in range(2 * chunks)],
            landings,
            None,
            send_sem,
            recv_sem,
            None,
            put_rows(first_ref, landings[4].shape[1]),
            bits,
            partners,
        )

        def advance(tick):
            for when, chunk, stage in sorted(plan, key=lambda entry: -entry[2]):
                if when == tick:
                    for unit in (2 * chunk, 2 * chunk + 1):
                        engine.advance(unit, stage, stop=chunk == chunks - 1 and stage == 1)

        def tick_at(position):
            for number in range(1, last_step):
                tick = TICKS * (number - 1) + position

                @pl.when(step == number)
                def _():
                    advance(tick)

        slot_sum = SlotSum(
            None,
            (None, half_ref) + tuple(slot_sums),
            (None, half_stat_ref) + tuple(slot_stats),
            slot_send,
            slot_recv,
            bits,
            partners,
        )
        half_pairs = PAIRS // 2
        lanes = half_pairs * LANES
        my_lanes = pl.ds(pl.multiple_of(core * lanes, LANES), lanes)

        def final_copies():
            theirs = pl.ds(pl.multiple_of((1 - core) * own, own), own)
            return (
                remote(
                    turned_ref.at[theirs],
                    go_land.at[:, my_lanes],
                    slot_send.at[4, 0],
                    slot_recv.at[4, 0],
                    partners["core"],
                ),
                remote(
                    gstat_land.at[core],
                    gstat_land.at[core],
                    slot_send.at[4, 1],
                    slot_recv.at[4, 1],
                    partners["core"],
                ),
            )

        def finish_slots():
            slot_sum.merge(3)
            for which in range(half_pairs):
                stat = slot_stats[1][which]
                total = stat[2:4]
                sums = slot_sums[1][which].astype(f32)
                mean = jnp.concatenate(
                    [sums[:HEAD_DIM] / total[0:1], sums[HEAD_DIM:] / total[1:2]], 0
                )
                turned_ref[:, which * LANES : (which + 1) * LANES] = mean.T.astype(bf16)
                whole = stat[0:2] + jnp.log(total)
                gstat_land[core, which] = jnp.concatenate(
                    [whole, jnp.zeros((6, GLOBALS), f32)], 0
                )
            mine = pl.ds(pl.multiple_of(core * own, own), own)
            go_land[:, my_lanes] = turned_ref[mine, :]
            for copy in final_copies():
                copy.start()

        def put_message():
            product = gdo_ref[...].astype(f32) * go_land[...].astype(f32)
            head_of = iota((width, LANES), 0) // HEAD_DIM == iota((width, LANES), 1)
            head_of = jnp.where(head_of, 1.0, 0.0).astype(bf16)
            first = product.astype(bf16)
            second = (product - first.astype(f32)).astype(bf16)
            centre = nn(first, head_of) + nn(second, head_of)
            lines = [gstat_land[half, which, 0:2] for half in (0, 1) for which in range(half_pairs)]
            lines = jnp.concatenate(lines + [jnp.zeros((LANES - HEADS, GLOBALS), f32)], 0)
            stat_ref[...] = lines.T
            total = stat_ref[pl.ds(pl.multiple_of(core * own, own), own), :]
            spread = jnp.zeros((own, LANES), f32)
            for number, value in enumerate((total, centre)):
                for piece in range(3):
                    low = value.astype(bf16)
                    value = value - low.astype(f32)
                    start_lane = (3 * number + piece) * HEADS
                    source_lane = iota((LANES, LANES), 0)
                    moved = iota((LANES, LANES), 1) == source_lane + start_lane
                    moved = jnp.where(moved & (source_lane < HEADS), 1.0, 0.0).astype(bf16)
                    spread = spread + nn(low, moved)
            message_ref[:, :width] = gdo_ref[...]
            message_ref[:, width:] = spread.astype(bf16)

    else:

        def tick_at(position):
            pass

    loads = [
        pltpu.make_async_copy(o_ref, os_ref.at[pl.ds(0, count)], load_sem.at[0]),
        pltpu.make_async_copy(ct_ref, cts_ref.at[pl.ds(0, count)], load_sem.at[1]),
    ]

    def start(at, size, x, sums):
        y = x.astype(f32) + nn(os_ref[at, :], wo_ref[...])
        unit, unused = normalize_rows(y)
        h_ref[at, :] = (unit * norms_ref[4:5] + norms_ref[5:6]).astype(bf16)
        y_ref[at, :] = y
        sums[...] = y + b2_ref[...]
        dh_ref[at, :] = jnp.zeros((size, width), f32)

    @pl.when(step == 0)
    def _():
        for load in loads:
            load.start()
        if talk:
            half_ref[...] = go_in_ref[...]
            half_stat_ref[...] = gstat_in_ref[...]
            meet([partners[name] for name in AXES])
            slot_sum.begin(2)
        cts_ref[count:] = padded(gct_ref[...])
        loads[0].wait()

        def start_tile(i, carry):
            at = pl.ds(pl.multiple_of(i * tile, tile), tile)
            start(at, tile, x_ref[at, :], dy_ref.at[at])
            return carry

        lax.fori_loop(0, tiles, start_tile, 0)
        loads[1].wait()
        dft_ref[...] = cts_ref[...].T
        if talk:
            slot_sum.merge(2)
            slot_sum.begin(3)

    db1_ref[...] = jnp.zeros_like(db1_ref)
    w1 = w1_ref[...].reshape(width, width)
    w2 = w2_ref[...].reshape(width, width)

    def chunk_of(at, sums):
        u = nt(h_ref[at, :], w1) + b1_ref[0]
        da = nt(cts_ref[at, :], w2)
        area, density = gelu_parts(u)
        a = (u * area).astype(bf16)
        du = (da * (area + u * density)).astype(bf16)
        a_ref[at, :] = a
        du_ref[at, :] = du
        db1_ref[0] += jnp.sum(du.astype(f32), axis=0, keepdims=True)
        sums[...] = sums[...] + nn(a, w2)
        dh_ref[at, :] = dh_ref[at, :] + nn(du, w1)

    chunk_of(rows_at(0), dy_ref.at[rows_at(0)])
    if talk:

        @pl.when(step == 0)
        def _():
            finish_slots()

    tick_at(0)
    for i in range(1, tiles):
        chunk_of(rows_at(i), dy_ref.at[rows_at(i)])

    @pl.when(step == 0)
    def _():
        if talk:
            for copy in final_copies():
                copy.wait_recv()
            os_ref[count:] = padded(go_land[...])
        else:
            os_ref[count:] = padded(go_in_ref[...])
        start(tail, extra, padded(gx_ref[...]), z_sum_ref)

    chunk_of(tail, z_sum_ref)
    tick_at(1)
    dw1 = tn(du_ref[...], h_ref[...])
    dw2 = nn(dft_ref[...], a_ref[...])
    if talk:
        for number in range(chunks):

            @pl.when(step == number)
            def _():
                for which, value in ((0, dw1), (1, dw2)):
                    unit = 2 * number + which
                    if unit >= slots:
                        engine.sent(unit - slots, 0)
                    put_unit(units_ref.at[unit % slots], value)

        @pl.when(step == chunks)
        def _():
            put_unit(second_ref.at[0], dw1)
            put_unit(second_ref.at[1], dw2)

        tick_at(2)
        for number in range(chunks):

            @pl.when(step == number)
            def _():
                engine.begin(2 * number)
                engine.begin(2 * number + 1)

    else:
        first_ref[...] = dw1.astype(bf16)
        second_ref[...] = dw2.astype(bf16)

    @pl.when(step == steps - 1)
    def _():
        db2_ref[...] = jnp.zeros_like(db2_ref)
        dgain_ref[...] = jnp.zeros_like(dgain_ref)
        doffset_ref[...] = jnp.zeros_like(doffset_ref)

        def finish(at, size, sums, put):
            z = sums[...].astype(bf16)
            unit, scale = normalize_rows(y_ref[at, :])
            dh = dh_ref[at, :]
            ct = cts_ref[at, :].astype(f32)
            dy = ct + norm_back(unit, scale, norms_ref[4:5], dh)
            db2_ref[...] += jnp.sum(ct, axis=0, keepdims=True)
            doffset_ref[...] += jnp.sum(dh, axis=0, keepdims=True)
            dgain_ref[...] += jnp.sum(dh * unit, axis=0, keepdims=True)
            low = dy.astype(bf16)
            h_ref[at, :] = low
            put(z, dy, nt(low, wo_ref[...]).astype(bf16))

        def finish_tile(i, carry):
            at = pl.ds(pl.multiple_of(i * tile, tile), tile)

            def put(z, dy, do):
                z_ref[at, :] = z
                dy_ref[at, :] = dy
                do_ref[at, :] = do

            finish(at, tile, dy_ref.at[at], put)
            return carry

        lax.fori_loop(0, tiles, finish_tile, 0)

        def put_tail(z, dy, do):
            gz_ref[...] = z[:own]
            gdy_ref[...] = dy[:own]
            gdo_ref[...] = do[:own]

        finish(tail, extra, z_sum_ref, put_tail)
        if talk:
            put_message()
        dwo = tn(h_ref[...], os_ref[...])
        if talk:
            put_grouped(dwo_ref, dwo)
            advance(TICKS * chunks)
            rest_ref[...] = landings[1][2 * chunks - 2 :]
            for when, chunk, stage in plan:
                for unit in (2 * chunk, 2 * chunk + 1):
                    if stage > 0 or unit + slots >= 2 * chunks:
                        engine.sent(unit, stage)
            slot_sum.sent(2)
            slot_sum.sent(3)
            for copy in final_copies():
                copy.wait_send()
        else:
            dwo_ref[...] = dwo.astype(bf16)


def branch(grid_of, x, o, ct, gx, go, gstat, gct, wo, w1t, b1, w2, b2, norms):
    count, width = x.shape
    own = gx.shape[0]
    hidden = w2.shape[0]
    steps = hidden // FF_CHUNK
    total = count + -(-own // LANES) * LANES
    row = once((count, width))
    few = once((own, width))
    line = full((1, width))
    anywhere = pl.BlockSpec(memory_space=pl.ANY)
    scratch = []
    more = {}
    if grid_of is None:
        weight_spec = pl.BlockSpec((FF_CHUNK, width), lambda j: (j, 0))
        b1 = b1.reshape(steps, 1, FF_CHUNK)
        dw_shapes = [(hidden, width), (width, hidden)]
        dw_types = [bf16, bf16]
        dw_specs = [weight_spec, pl.BlockSpec((width, FF_CHUNK), lambda j: (0, j))]
        dwo_shape = (width, width)
    else:
        seq, batch = grid_of
        rows, lanes = width // seq, width // batch
        weight_spec = pl.BlockSpec((seq, 1, rows, width), lambda j: (0, j, 0, 0))
        w1t = w1t.reshape(seq, steps, rows, width)
        w2 = w2.reshape(seq, steps, rows, width)
        b1 = b1.reshape(seq, steps, rows).transpose(1, 0, 2).reshape(steps, 1, FF_CHUNK)
        units = 2 * (steps - 1)
        sums, stats = go.shape[2:], gstat.shape[2:]
        dw_shapes = [
            ((units - 2) * rows, lanes),
            (2, 2, 2, 2, 2, batch, rows, lanes),
            (own, width + LANES),
            (2, 2, 2, 2, rows, lanes),
        ]
        dw_types = [f32, bf16, bf16, bf16]
        dw_specs = [once(shape) for shape in dw_shapes]
        dwo_shape = (seq, batch, rows, lanes)
        dma = pltpu.SemaphoreType.DMA
        scratch = (
            [pltpu.VMEM((4,) + dw_shapes[1][1:], bf16)]
            + sum_scratch(units, rows, lanes, False)
            + [
                pltpu.VMEM(go.shape, bf16),
                pltpu.VMEM(gstat.shape, f32),
                pltpu.VMEM((2,) + sums, bf16),
                pltpu.VMEM(sums, bf16),
                pltpu.VMEM((2,) + stats, f32),
                pltpu.VMEM(stats, f32),
                pltpu.VMEM((GLOBALS, PAIRS // 2 * LANES), bf16),
                pltpu.VMEM((own, width), bf16),
                pltpu.VMEM((2,) + stats, f32),
                pltpu.VMEM((GLOBALS, LANES), f32),
                dma((5, 2)),
                dma((5, 2)),
            ]
        )
        more = {"collective_id": 3, "has_side_effects": True}
    out = pl.pallas_call(
        functools.partial(branch_kernel, BLOCK, grid_of is not None),
        grid=(steps,),
        in_specs=[
            row,
            anywhere,
            anywhere,
            few,
            once(go.shape),
            once(gstat.shape),
            few,
            once((width, width)),
            weight_spec,
            pl.BlockSpec((1, 1, FF_CHUNK), lambda j: (j, 0, 0)),
            weight_spec,
            line,
            full(norms.shape),
        ],
        out_specs=[row, row, row, few, few, few]
        + [once(dwo_shape), pl.BlockSpec((1, 1, FF_CHUNK), lambda j: (j, 0, 0)), line, line, line]
        + dw_specs,
        out_shape=[
            jax.ShapeDtypeStruct((count, width), bf16),
            jax.ShapeDtypeStruct((count, width), f32),
            jax.ShapeDtypeStruct((count, width), bf16),
            jax.ShapeDtypeStruct((own, width), bf16),
            jax.ShapeDtypeStruct((own, width), f32),
            jax.ShapeDtypeStruct((own, width), bf16),
            jax.ShapeDtypeStruct(dwo_shape, bf16),
            jax.ShapeDtypeStruct((steps, 1, FF_CHUNK), f32),
            jax.ShapeDtypeStruct((1, width), f32),
            jax.ShapeDtypeStruct((1, width), f32),
            jax.ShapeDtypeStruct((1, width), f32),
        ]
        + [jax.ShapeDtypeStruct(shape, kind) for shape, kind in zip(dw_shapes, dw_types)],
        scratch_shapes=[
            pltpu.VMEM((total, width), bf16),
            pltpu.VMEM((total, width), bf16),
            pltpu.VMEM((total, width), f32),
            pltpu.VMEM((total, width), bf16),
            pltpu.VMEM((total - count, width), f32),
            pltpu.VMEM((total, width), f32),
            pltpu.VMEM((width, total), bf16),
            pltpu.VMEM((total, FF_CHUNK), bf16),
            pltpu.VMEM((total, FF_CHUNK), bf16),
            pltpu.SemaphoreType.DMA((2,)),
        ]
        + scratch,
        compiler_params=params(**more),
        cost_estimate=pl.CostEstimate(
            flops=6 * total * width * (2 * hidden + width),
            bytes_accessed=8 * width * hidden + 16 * total * width,
            transcendentals=2 * total * hidden,
        ),
        name="branch",
    )(x, o, ct, gx, go, gstat, gct, wo, w1t, b1, w2, b2, norms)
    db1 = out[7].reshape(steps, FF_CHUNK)
    if grid_of is not None:
        db1 = db1.reshape(steps, seq, rows).transpose(1, 0, 2).reshape(-1, width)
    return [*out[:7], db1, *out[8:]]


def local_backward_kernel(
    talk,
    rows_count,
    group_rows,
    lengths,
    bucket_of,
    place,
    q_ref,
    k_ref,
    v_ref,
    do_ref,
    o_ref,
    line_ref,
    *refs,
):
    if talk:
        message_ref, rest_ref, last_ref, dwo_ref = refs[:4]
        refs = refs[4:]
    dq_ref, dk_ref, dv_ref, centre_ref = refs[:4]
    refs = refs[4:]
    if talk:
        everyone_ref, sums_ref, rest_out_ref = refs[:3]
        refs = refs[3:]
    edges, query_columns, key_columns = refs[:3]
    pair = pl.program_id(0)
    block = pl.program_id(1)
    blocks = rows_count // BLOCK
    step = pair * blocks + block

    @pl.when(step == 0)
    def _():
        read_edges(lengths, bucket_of, place, edges)

    if talk:
        all_ref, gather_send, gather_recv, own_ref = refs[3:7]
        landings = refs[7:12]
        send_sem, recv_sem, own_sem = refs[12:]
        bits, partners = my_place()
        gather = RowGather(all_ref, 3 * LANES, gather_send, gather_recv, bits, partners)
        engine = HalvingSum(
            (X_FIRST, Y_FIRST) * 2 + (X_FIRST,),
            [
                None,
                None,
                lambda side: last_ref.at[0, :, :, :, side],
                lambda side: last_ref.at[1, :, :, :, side],
                lambda side: dwo_ref.at[:, :, :, side],
            ],
            landings,
            own_ref,
            send_sem,
            recv_sem,
            own_sem,
            put_rows(sums_ref, landings[4].shape[1]),
            bits,
            partners,
        )
        plan = {
            3: [(2, 0), (3, 0), (4, 0)],
            4: [(0, 2), (1, 2)],
            7: [(0, 3), (1, 3)],
            11: [(0, 4), (1, 4), (2, 1), (3, 1), (4, 1)],
        }
        gather_plan = {2: 0, 5: 1, 8: 2, 10: 3}

        @pl.when(step == 0)
        def _():
            all_ref[bits["z1"], bits["z0"], bits["y"], bits["core"]] = message_ref[...]
            landings[1][:2] = rest_ref[...]
            meet([partners[name] for name in AXES])
            gather.begin()
            for unit in (0, 1):
                engine.copy(unit, 2).start()
            for unit in (2, 3, 4):
                engine.begin(unit)

        for number in range(PAIRS * blocks):
            if number in plan or number in gather_plan:

                @pl.when(step == number)
                def _():
                    if number in gather_plan:
                        gather.advance(gather_plan[number])
                    for unit, stage in plan.get(number, ()):
                        engine.advance(unit, stage, stop=unit > 1 and stage == 1)

    block_columns(
        place, edges, rows_count, group_rows, block, step, blocks, query_columns, key_columns
    )
    extra = query_columns[block]
    upstream = do_ref[...]
    product = upstream.astype(f32) * o_ref[...].astype(f32)
    first = product.astype(bf16)
    second = (product - first.astype(f32)).astype(bf16)
    head = jnp.where(iota((8, LANES), 1) // HEAD_DIM == iota((8, LANES), 0), 1.0, 0.0).astype(bf16)
    by_head = nt(head, first) + nt(head, second)
    centre = jnp.concatenate([by_head[0:1], by_head[1:2]], axis=1)
    centre_ref[0, 0] = jnp.broadcast_to(centre, (8, 2 * BLOCK))
    queries = stack_pair(q_ref[...])
    grads = stack_pair(upstream)
    keys = k_ref[...]
    score = nt(
        jnp.concatenate([keys, key_columns[block]], 1),
        jnp.concatenate([queries, jnp.concatenate([extra, extra], 0)], 1),
    )
    weights = jnp.exp(score - line_ref[0, 0, 0:1])
    along = nt(v_ref[...], grads) - centre
    score_grad = (weights * along).astype(bf16)
    dv_ref[...] = nn(weights.astype(bf16), grads).astype(bf16)
    dk_ref[...] = nn(score_grad, queries).astype(bf16)
    low, high = side_by_side(tn(keys, score_grad))
    dq_ref[:HEAD_DIM] = low.astype(bf16)
    dq_ref[HEAD_DIM:] = high.astype(bf16)

    if talk:

        @pl.when(step == PAIRS * blocks - 1)
        def _():
            everyone_ref[...] = all_ref[...].reshape(everyone_ref.shape)
            gather.end()
            rest_out_ref[...] = landings[1][2:]
            for entries in plan.values():
                for unit, stage in entries:
                    engine.sent(unit, stage)


def local_backward(
    talk, scalars, rows_count, group_rows, q, k, v, do, o, line, message, rest, last, dwo
):
    blocks = rows_count // BLOCK
    width = q.shape[1]
    block_spec = pl.BlockSpec((BLOCK, LANES), lambda p, b, *unused: (b, p))
    operands = [q, k, v, do, o, line]
    in_specs = [block_spec] * 5 + [line_spec()]
    out_specs = (
        [pl.BlockSpec((LANES, BLOCK), lambda p, b, *unused: (p, b))]
        + [block_spec] * 2
        + [line_spec()]
    )
    out_shape = [
        jax.ShapeDtypeStruct((width, rows_count), bf16),
        jax.ShapeDtypeStruct((rows_count, width), bf16),
        jax.ShapeDtypeStruct((rows_count, width), bf16),
        jax.ShapeDtypeStruct((PAIRS, blocks, 8, 2 * BLOCK), f32),
    ]
    scratch = column_scratch(blocks)
    more = {}
    if talk:
        own, wide = message.shape
        rows, lanes = last.shape[-2:]
        units = 5
        operands += [message, rest, last, dwo.reshape(last.shape[1:])]
        in_specs += [full(message.shape), once(rest.shape)]
        in_specs += [pl.BlockSpec(memory_space=pl.ANY)] * 2
        everyone = (16 * own, wide)
        rest_out = (units - 2,) + rest.shape[1:]
        out_specs += [once(everyone), once((2 * rows, lanes)), once(rest_out)]
        out_shape += [
            jax.ShapeDtypeStruct(everyone, bf16),
            jax.ShapeDtypeStruct((2 * rows, lanes), f32),
            jax.ShapeDtypeStruct(rest_out, bf16),
        ]
        dma = pltpu.SemaphoreType.DMA
        scratch += [pltpu.VMEM((2, 2, 2, 2, own, wide), bf16), dma((4, 2)), dma((4, 2))]
        scratch += sum_scratch(units, rows, lanes, True)
        more = {"collective_id": 4, "has_side_effects": True}
    return pl.pallas_call(
        functools.partial(local_backward_kernel, talk, rows_count, group_rows),
        grid_spec=pltpu.PrefetchScalarGridSpec(
            num_scalar_prefetch=3,
            grid=(PAIRS, blocks),
            in_specs=in_specs,
            out_specs=out_specs,
            scratch_shapes=scratch,
        ),
        out_shape=out_shape,
        compiler_params=params(**more),
        cost_estimate=pl.CostEstimate(
            flops=40 * rows_count * BLOCK * width,
            bytes_accessed=30 * rows_count * width,
            transcendentals=HEADS * rows_count * BLOCK,
        ),
        name="local_backward",
    )(*scalars, *operands)


def slot_backward_kernel(
    rows_count,
    group_rows,
    lengths,
    bucket_of,
    place,
    q_ref,
    k_ref,
    v_ref,
    do_ref,
    line_ref,
    centre_ref,
    dqt_ref,
    dk_in_ref,
    dv_in_ref,
    gq_ref,
    gk_ref,
    gv_ref,
    gdo_ref,
    gstat_ref,
    gx_ref,
    gh_ref,
    wq_ref,
    wk_ref,
    wv_ref,
    dq_ref,
    dk_ref,
    dv_ref,
    dw_ref,
    dgh_ref,
    dnorm_ref,
    edges,
    query_columns,
    key_columns,
    keys_ref,
    queries_ref,
    grads_ref,
    dqt_sum,
    dk_sum,
    dv_sum,
    dgqt_sum,
    dgk_sum,
    dgv_sum,
    lines_ref,
    dw_sum,
    dgh_sum,
):
    group = pl.program_id(0)
    block = pl.program_id(1)
    blocks = rows_count // BLOCK
    step = group * blocks + block
    together = range(TOGETHER)

    def lanes_of(which):
        return pl.ds(which * LANES, LANES)

    @pl.when(step == 0)
    def _():
        read_edges(lengths, bucket_of, place, edges)

        def turn(slot, carry):
            at = pl.ds(pl.multiple_of(slot * GLOBALS, GLOBALS), GLOBALS)
            lines_ref[slot] = gstat_ref[at, :].astype(f32).T
            return carry

        lax.fori_loop(0, SLOTS, turn, 0)
        dgh_sum[...] = jnp.zeros_like(dgh_sum)
        dnorm_ref[...] = jnp.zeros_like(dnorm_ref)

    @pl.when(block == 0)
    def _():
        dgqt_sum[...] = jnp.zeros_like(dgqt_sum)
        dgk_sum[...] = jnp.zeros_like(dgk_sum)
        dgv_sum[...] = jnp.zeros_like(dgv_sum)

    block_columns(
        place, edges, rows_count, group_rows, block, step, blocks, query_columns, key_columns
    )
    extra = query_columns[block]
    for which in together:
        lanes = lanes_of(which)
        keys_ref[which, :, :LANES] = k_ref[:, lanes]
        keys_ref[which, :, LANES:] = key_columns[block]
        queries_ref[which, :, :LANES] = stack_pair(q_ref[:, lanes])
        queries_ref[which, :BLOCK, LANES:] = extra
        queries_ref[which, BLOCK:, LANES:] = extra
        grads_ref[which] = stack_pair(do_ref[:, lanes])
    dqt_sum[...] = dqt_ref[...].astype(f32)
    dk_sum[...] = dk_in_ref[...].astype(f32)
    dv_sum[...] = dv_in_ref[...].astype(f32)

    def line_of(slot, which, first):
        halves = []
        for head in range(2):
            spot = first + 2 * (group * TOGETHER + which) + head
            halves.append(
                lines_ref[slot, pl.ds(spot, 1)]
                + lines_ref[slot, pl.ds(spot + HEADS, 1)]
                + lines_ref[slot, pl.ds(spot + 2 * HEADS, 1)]
            )
        return jnp.concatenate(halves, axis=1)

    def from_global(slot, which, keys, values):
        at = pl.ds(pl.multiple_of(slot * GLOBALS, GLOBALS), GLOBALS)
        extra = global_query_extra(slot).astype(bf16)
        queries = stack_pair(gq_ref[at, lanes_of(which)])
        grads = stack_pair(gdo_ref[at, lanes_of(which)])
        score = nt(keys, jnp.concatenate([queries, jnp.concatenate([extra, extra], 0)], 1))
        weights = jnp.exp(score - line_of(slot, which, 0))
        along = nt(values, grads) - line_of(slot, which, 3 * HEADS)
        score_grad = (weights * along).astype(bf16)
        low, high = side_by_side(tn(keys[:, :LANES], score_grad))
        dgqt_sum[which, slot, :HEAD_DIM] += low
        dgqt_sum[which, slot, HEAD_DIM:] += high
        return nn(score_grad, queries), nn(weights.astype(bf16), grads)

    def one_slot(slot, carry):
        @pl.when(slot_present(slot, place, edges, rows_count, group_rows, block))
        def _():
            at = pl.ds(pl.multiple_of(slot * GLOBALS, GLOBALS), GLOBALS)
            columns = global_key_extra(slot).astype(bf16)
            for which in together:
                lanes = lanes_of(which)
                key_grad, value_grad = from_global(slot, which, keys_ref[which], v_ref[:, lanes])
                dk_sum[:, lanes] += key_grad
                dv_sum[:, lanes] += value_grad
                keys = gk_ref[at, lanes]
                grads = grads_ref[which]
                score = nt(jnp.concatenate([keys, columns], 1), queries_ref[which])
                weights = jnp.exp(score - line_ref[which, 0, 0:1])
                along = nt(gv_ref[at, lanes], grads) - centre_ref[which, 0, 0:1]
                score_grad = (weights * along).astype(bf16)
                dgv_sum[at, lanes] += nn(weights.astype(bf16), grads)
                dgk_sum[at, lanes] += nn(score_grad, queries_ref[which, :, :LANES])
                low, high = side_by_side(tn(keys, score_grad))
                dqt_sum[pl.ds(which * LANES, HEAD_DIM)] += low
                dqt_sum[pl.ds(which * LANES + HEAD_DIM, HEAD_DIM)] += high

        return carry

    lax.fori_loop(0, SLOTS, one_slot, 0)
    dq_ref[...] = dqt_sum[...].T.astype(bf16)
    dk_ref[...] = dk_sum[...].astype(bf16)
    dv_ref[...] = dv_sum[...].astype(bf16)

    @pl.when((block == blocks - 1) & (place[2] >= 0))
    def _():
        slot = place[2]
        at = pl.ds(pl.multiple_of(slot * GLOBALS, GLOBALS), GLOBALS)
        columns = global_key_extra(slot).astype(bf16)
        for which in together:
            lanes = lanes_of(which)
            keys = jnp.concatenate([gk_ref[at, lanes], columns], axis=1)
            key_grad, value_grad = from_global(slot, which, keys, gv_ref[at, lanes])
            dgk_sum[at, lanes] += key_grad
            dgv_sum[at, lanes] += value_grad

    @pl.when(block == blocks - 1)
    def _():
        dw_sum[...] = jnp.zeros_like(dw_sum)

        def through(slot, carry):
            needed = slot == place[2]
            for number in range(blocks):
                needed = needed | slot_present(
                    slot, place, edges, rows_count, group_rows, number
                )

            @pl.when(needed)
            def _():
                at = pl.ds(pl.multiple_of(slot * GLOBALS, GLOBALS), GLOBALS)
                grads = (
                    (
                        jnp.concatenate([dgqt_sum[which, slot].T for which in together], 1)
                        * query_scale
                    ).astype(bf16),
                    dgk_sum[at, :].astype(bf16),
                    dgv_sum[at, :].astype(bf16),
                )
                rows = gh_ref[at, :]
                total = dgh_sum[at, :]
                for index, weight in enumerate((wq_ref, wk_ref, wv_ref)):
                    dw_sum[index] += tn(grads[index], rows)
                    total = total + nt(grads[index], weight[...])
                dgh_sum[at, :] = total

                @pl.when(group == PAIRS // TOGETHER - 1)
                def _():
                    unit, unused = normalize_rows(gx_ref[at, :].astype(f32))
                    dnorm_ref[0:1] += jnp.sum(total * unit, axis=0, keepdims=True)
                    dnorm_ref[1:2] += jnp.sum(total, axis=0, keepdims=True)

            return carry

        lax.fori_loop(0, SLOTS, through, 0)
        dw_ref[...] = dw_sum[...].astype(bf16)

    @pl.when(step == PAIRS // TOGETHER * blocks - 1)
    def _():
        dgh_ref[...] = dgh_sum[...].astype(bf16)


def slot_backward(
    scalars,
    rows_count,
    group_rows,
    q,
    k,
    v,
    do,
    line,
    centre,
    dqt,
    dk,
    dv,
    gq,
    gk,
    gv,
    everyone,
    gx,
    gh,
    wq,
    wk,
    wv,
):
    blocks = rows_count // BLOCK
    all_globals, width = gk.shape
    block_spec = pl.BlockSpec((BLOCK, TOGETHER * LANES), lambda p, b, *unused: (b, p))
    pair_spec = pl.BlockSpec((all_globals, TOGETHER * LANES), lambda p, b, *unused: (0, p))
    local = jax.ShapeDtypeStruct((rows_count, width), bf16)
    glob = jax.ShapeDtypeStruct((all_globals, width), bf16)
    return pl.pallas_call(
        functools.partial(slot_backward_kernel, rows_count, group_rows),
        grid_spec=pltpu.PrefetchScalarGridSpec(
            num_scalar_prefetch=3,
            grid=(PAIRS // TOGETHER, blocks),
            in_specs=[block_spec] * 4
            + [line_spec(TOGETHER)] * 2
            + [pl.BlockSpec((TOGETHER * LANES, BLOCK), lambda p, b, *unused: (p, b))]
            + [block_spec] * 2
            + [pair_spec] * 4
            + [pl.BlockSpec((all_globals, LANES), lambda p, b, *unused: (0, PAIRS))]
            + [once((all_globals, width))] * 2
            + [pl.BlockSpec((width, TOGETHER * LANES), lambda p, b, *unused: (0, p))] * 3,
            out_specs=[block_spec] * 3
            + [
                pl.BlockSpec((3, TOGETHER * LANES, width), lambda p, b, *unused: (0, p, 0)),
                once((all_globals, width)),
                full((8, width)),
            ],
            scratch_shapes=column_scratch(blocks)
            + [
                pltpu.VMEM((TOGETHER, BLOCK, 2 * LANES), bf16),
                pltpu.VMEM((TOGETHER, 2 * BLOCK, 2 * LANES), bf16),
                pltpu.VMEM((TOGETHER, 2 * BLOCK, LANES), bf16),
                pltpu.VMEM((TOGETHER * LANES, BLOCK), f32),
                pltpu.VMEM((BLOCK, TOGETHER * LANES), f32),
                pltpu.VMEM((BLOCK, TOGETHER * LANES), f32),
                pltpu.VMEM((TOGETHER, SLOTS, LANES, GLOBALS), f32),
                pltpu.VMEM((all_globals, TOGETHER * LANES), f32),
                pltpu.VMEM((all_globals, TOGETHER * LANES), f32),
                pltpu.VMEM((SLOTS, LANES, GLOBALS), f32),
                pltpu.VMEM((3, TOGETHER * LANES, width), f32),
                pltpu.VMEM((all_globals, width), f32),
            ],
        ),
        out_shape=[local] * 3
        + [
            jax.ShapeDtypeStruct((3, width, width), bf16),
            glob,
            jax.ShapeDtypeStruct((8, width), f32),
        ],
        compiler_params=params(),
        cost_estimate=pl.CostEstimate(
            flops=80 * rows_count * GLOBALS * width,
            bytes_accessed=40 * rows_count * width,
            transcendentals=2 * HEADS * rows_count * GLOBALS,
        ),
        name="slot_backward",
    )(
        *scalars,
        q,
        k,
        v,
        do,
        line,
        centre,
        dqt,
        dk,
        dv,
        gq,
        gk,
        gv,
        everyone,
        everyone,
        gx,
        gh,
        wq,
        wk,
        wv,
    )


def project_back_kernel(
    tile,
    x_ref,
    dy_ref,
    h_ref,
    dq_ref,
    dk_ref,
    dv_ref,
    dwg_ref,
    wq_ref,
    wk_ref,
    wv_ref,
    gain_ref,
    dx_ref,
    dw_ref,
    dnorm_ref,
):
    count, width = x_ref.shape
    dnorm_ref[...] = jnp.zeros_like(dnorm_ref)

    def one_tile(i, carry):
        at = pl.ds(pl.multiple_of(i * tile, tile), tile)
        dh = (
            nt(dq_ref[at, :], wq_ref[...]) * query_scale
            + nt(dk_ref[at, :], wk_ref[...])
            + nt(dv_ref[at, :], wv_ref[...])
        )
        unit, scale = normalize_rows(x_ref[at, :].astype(f32))
        dnorm_ref[0:1] += jnp.sum(dh * unit, axis=0, keepdims=True)
        dnorm_ref[1:2] += jnp.sum(dh, axis=0, keepdims=True)
        dx_ref[at, :] = dy_ref[at, :] + norm_back(unit, scale, gain_ref[...], dh)
        return carry

    lax.fori_loop(0, count // tile, one_tile, 0)
    for index, source in enumerate((dq_ref, dk_ref, dv_ref)):
        value = tn(source[...], h_ref[...])
        if index == 0:
            value = value * query_scale
        dw_ref[index] = (value + dwg_ref[index].astype(f32)).astype(bf16)


def project_back(x, dy, h, dq, dk, dv, dwg, wq, wk, wv, gain):
    count, width = x.shape
    vmem = pl.BlockSpec(memory_space=pltpu.VMEM)
    return pl.pallas_call(
        functools.partial(project_back_kernel, BLOCK),
        in_specs=[vmem] * 11,
        out_specs=[vmem] * 3,
        out_shape=[
            jax.ShapeDtypeStruct((count, width), f32),
            jax.ShapeDtypeStruct((3, width, width), bf16),
            jax.ShapeDtypeStruct((8, width), f32),
        ],
        compiler_params=params(),
        cost_estimate=pl.CostEstimate(
            flops=12 * count * width * width, bytes_accessed=30 * count * width, transcendentals=0
        ),
        name="project_back",
    )(x, dy, h, dq, dk, dv, dwg, wq, wk, wv, gain)


def finish_kernel(
    rest_ref,
    x_in,
    dy_in,
    h_in,
    dq_in,
    dk_in,
    dv_in,
    dwg_in,
    dgh_ref,
    z_in,
    wq_in,
    wk_in,
    wv_in,
    db1_ref,
    db2_ref,
    dnorm_global_ref,
    dgain2_ref,
    doffset2_ref,
    gx_ref,
    gdy_ref,
    norms_ref,
    out_ref,
    small_out_ref,
    grad_out_ref,
    layer_ref,
    token_ref,
    x_ref,
    dy_ref,
    h_ref,
    dq_ref,
    dk_ref,
    dv_ref,
    dwg_ref,
    wq_ref,
    wk_ref,
    wv_ref,
    load_sem,
    units_ref,
    one_ref,
    two_ref,
    three_ref,
    four_ref,
    five_ref,
    send_sem,
    recv_sem,
    gown_ref,
    gone_ref,
    gtwo_ref,
    gthree_ref,
    gfour_ref,
    gsend_sem,
    grecv_sem,
    gown_sem,
    sums_ref,
    here_ref,
    ssend_sem,
    srecv_sem,
    halo_out,
    halo_z,
    halo_dx,
    halo_send,
    halo_recv,
    dnorm_ref,
    dgh_sum_ref,
):
    bits, partners = my_place()
    count, width = x_ref.shape
    came = rest_ref.shape[0]
    units = came + 3
    batch = lax.axis_index("batch")
    seq = lax.axis_index("seq")
    places = lax.axis_size("seq")
    after = (batch, lax.rem(seq + 1, places))
    before = (batch, lax.rem(seq + places - 1, places))

    pairs = [
        (dq_in, dq_ref),
        (h_in, h_ref),
        (dwg_in, dwg_ref),
        (dk_in, dk_ref),
        (dv_in, dv_ref),
        (wq_in, wq_ref),
        (wk_in, wk_ref),
        (wv_in, wv_ref),
        (x_in, x_ref),
        (dy_in, dy_ref),
        (z_in.at[pl.ds(HALF, count - HALF)], layer_ref.at[pl.ds(0, count - HALF)]),
    ]
    loads = [
        pltpu.make_async_copy(source, target, load_sem.at[number])
        for number, (source, target) in enumerate(pairs)
    ]
    for load in loads:
        load.start()

    def source(unit):
        return lambda side: units_ref.at[unit - came, :, :, :, side]

    engine = HalvingSum(
        (X_FIRST, Y_FIRST, X_FIRST, X_FIRST, Y_FIRST, Z_FIRST),
        [source(unit) for unit in range(units)],
        (one_ref, two_ref, three_ref, four_ref, five_ref),
        None,
        send_sem,
        recv_sem,
        None,
        put_rows(out_ref, five_ref.shape[1]),
        bits,
        partners,
    )
    wide = gone_ref.shape[-1]

    def row_source(unit):
        lanes = pl.ds(unit * wide, wide)
        return lambda side: dgh_ref.at[:, :, :, side, :, lanes]

    def put_dgh(unit, value):
        dgh_sum_ref[:, unit * wide : (unit + 1) * wide] = value

    row_sum = HalvingSum(
        (("core", "y", "z0", "z1"), ("core", "z0", "y", "z1")),
        [row_source(unit) for unit in range(2)],
        (gone_ref, gtwo_ref, gthree_ref, gfour_ref),
        gown_ref,
        gsend_sem,
        grecv_sem,
        gown_sem,
        put_dgh,
        bits,
        partners,
    )

    def rows_advance(stage):
        for unit in range(2):
            row_sum.advance(unit, stage)

    def scopy(stage):
        return remote(
            sums_ref.at[stage],
            here_ref.at[stage],
            ssend_sem.at[stage],
            srecv_sem.at[stage],
            partners[X_FIRST[stage]],
        )

    def small_advance(stage):
        scopy(stage).wait_recv()
        total = sums_ref[stage] + here_ref[stage]
        if stage < STAGES - 1:
            sums_ref[stage + 1] = total
            scopy(stage + 1).start()
        else:
            small_out_ref[...] = total

    head = pl.ds(0, HALF)
    halos = [
        remote(z_in.at[head], halo_z, halo_send.at[0], halo_recv.at[0], before),
        remote(halo_out, halo_dx, halo_send.at[1], halo_recv.at[1], before),
    ]
    two_ref[:came] = rest_ref[...]
    meet([partners[name] for name in AXES] + [before, after])
    for unit in range(came):
        engine.copy(unit, 2).start()
    for unit in range(2):
        row_sum.begin(unit)
    halos[0].start()

    def weight_gradient(index, grads_ref):
        value = tn(grads_ref[...], h_ref[...])
        if index == 0:
            value = value * query_scale
        put_unit(units_ref.at[index], value + dwg_ref[index].astype(f32))
        engine.begin(came + index)

    for number in range(3):
        loads[number].wait()
    weight_gradient(0, dq_ref)
    rows_advance(0)
    loads[3].wait()
    weight_gradient(1, dk_ref)
    loads[4].wait()
    weight_gradient(2, dv_ref)
    for unit in range(came):
        engine.advance(unit, 2)
    for number in range(5, 10):
        loads[number].wait()
    dnorm_ref[...] = jnp.zeros_like(dnorm_ref)

    def back(index):
        at = pl.ds(index * HALF, HALF)
        dh = (
            nt(dq_ref[at, :], wq_ref[...]) * query_scale
            + nt(dk_ref[at, :], wk_ref[...])
            + nt(dv_ref[at, :], wv_ref[...])
        )
        unit, scale = normalize_rows(x_ref[at, :].astype(f32))
        dnorm_ref[0:1] += jnp.sum(dh * unit, axis=0, keepdims=True)
        dnorm_ref[1:2] += jnp.sum(dh, axis=0, keepdims=True)
        dx = dy_ref[at, :] + norm_back(unit, scale, norms_ref[0:1], dh)
        if index == 0:
            halo_out[...] = dx.astype(bf16)
        else:
            token_ref[pl.ds((index - 1) * HALF, HALF), :] = dx

    for index in range(count // HALF):
        back(index)
        if index == 0:
            halos[1].start()
            for unit in range(came, units):
                engine.advance(unit, 0)
        if index == 1:
            rows_advance(1)
        if index == 2:
            for unit in range(came):
                engine.advance(unit, 3)

    hidden_rows = db1_ref.shape[0]
    parts = [
        db1_ref[...],
        db2_ref[...],
        dnorm_ref[0:2],
        dnorm_global_ref[0:2],
        dgain2_ref[...],
        doffset2_ref[...],
    ]
    filled = hidden_rows + 7
    parts.append(jnp.zeros((sums_ref.shape[1] - filled, width), f32))
    sums_ref[0] = jnp.concatenate(parts, 0)
    scopy(0).start()
    rows_advance(2)
    for unit in range(came, units):
        engine.advance(unit, 1)
    small_advance(0)
    rows_advance(3)
    dgh = dgh_sum_ref[...]
    unit_rows, scale = normalize_rows(gx_ref[...].astype(f32))
    grad_out_ref[...] = gdy_ref[...] + norm_back(unit_rows, scale, norms_ref[2:3], dgh)
    small_advance(1)
    for unit in range(came):
        engine.advance(unit, 4)
    for unit in range(came, units):
        engine.advance(unit, 2)
    small_advance(2)
    halos[0].wait_recv()
    halos[1].wait_recv()
    loads[10].wait()
    layer_ref[count - HALF :, :] = halo_z[...]
    token_ref[count - HALF :, :] = halo_dx[...].astype(f32)
    for unit in range(came, units):
        engine.advance(unit, 3)
    small_advance(3)
    for unit in range(came, units):
        engine.advance(unit, 4)
    small_advance(4)

    for unit in range(units):
        for stage in range(2 if unit < came else 0, STAGES):
            engine.sent(unit, stage)
    for stage in range(STAGES):
        scopy(stage).wait_send()
    for unit in range(2):
        for stage in range(4):
            row_sum.sent(unit, stage)
    for halo in halos:
        halo.wait_send()


def finish_all(rest, x, dy, h, dq, dk, dv, dwg, dgh, z, wq, wk, wv, small, gx, gdy, norms):
    count, width = x.shape
    rows, lanes = rest.shape[-2:]
    units = rest.shape[0] + 3
    own = gx.shape[0]
    place = (2, 2, 2, 2)
    small_rows = small[0].shape[0] + 7
    small_rows += -small_rows % 8
    anywhere = pl.BlockSpec(memory_space=pl.ANY)
    vmem = pl.BlockSpec(memory_space=pltpu.VMEM)
    dma = pltpu.SemaphoreType.DMA
    row = pltpu.VMEM((count, width), bf16)
    weight = pltpu.VMEM((width, width), bf16)
    half = pltpu.VMEM((HALF, width), bf16)
    return pl.pallas_call(
        finish_kernel,
        in_specs=[vmem] + [anywhere] * 12 + [vmem] * 8,
        out_specs=[vmem] * 5,
        out_shape=[
            jax.ShapeDtypeStruct((units * rows, lanes), f32),
            jax.ShapeDtypeStruct((small_rows, width), f32),
            jax.ShapeDtypeStruct((own, width), f32),
            jax.ShapeDtypeStruct((count, width), bf16),
            jax.ShapeDtypeStruct((count, width), f32),
        ],
        scratch_shapes=[
            row,
            pltpu.VMEM((count, width), f32),
            row,
            row,
            row,
            row,
            pltpu.VMEM((3, width, width), bf16),
            weight,
            weight,
            weight,
            dma((11,)),
            pltpu.VMEM((3, 2, 2, 2, 2, 2, rows, lanes), bf16),
        ]
        + sum_scratch(units, rows, lanes, False)
        + [
            pltpu.VMEM((2, 2, 2, 2, own, width // 2), bf16),
            pltpu.VMEM((2, 2, 2, 2, own, width // 2), bf16),
            pltpu.VMEM((2, 2, 2, own, width // 2), bf16),
            pltpu.VMEM((2, 2, own, width // 2), bf16),
            pltpu.VMEM((2, own, width // 2), bf16),
            dma((2, 4)),
            dma((2, 4)),
            dma((2,)),
            pltpu.VMEM((STAGES, small_rows, width), f32),
            pltpu.VMEM((STAGES, small_rows, width), f32),
            dma((STAGES,)),
            dma((STAGES,)),
            half,
            half,
            half,
            dma((2,)),
            dma((2,)),
            pltpu.VMEM((8, width), f32),
            pltpu.VMEM((own, width), f32),
        ],
        compiler_params=params(collective_id=0, has_side_effects=True),
        cost_estimate=pl.CostEstimate(
            flops=12 * count * width * width, bytes_accessed=30 * count * width, transcendentals=0
        ),
        name="finish_all",
    )(
        rest,
        x,
        dy,
        h,
        dq,
        dk,
        dv,
        dwg,
        dgh.reshape(place + (own, width)),
        z,
        wq,
        wk,
        wv,
        *small,
        gx,
        gdy,
        norms,
    )


def from_behind(value, axis, steps):
    count = lax.axis_size(axis)
    pairs = [(source, (source + steps) % count) for source in range(count)]
    return lax.ppermute(value, axis, pairs)


def pieces(value):
    first = lax.reduce_precision(value, 8, 7)
    second = lax.reduce_precision(value - first, 8, 7)
    return [first.astype(bf16), second.astype(bf16), (value - first - second).astype(bf16)]


def scatter_sum(value):
    half = lax.psum_scatter(value, "batch", scatter_dimension=1, tiled=True)
    part = lax.psum_scatter(half, "seq", scatter_dimension=0, tiled=True)
    return part.T.astype(f32)


def on_device(
    tokens,
    global_states,
    lengths,
    bucket_of,
    wq,
    wk,
    wv,
    wo,
    w1,
    b1,
    w2,
    b2,
    norm_params,
    cotangent,
    global_cotangent,
):
    rows = tokens.shape[1]
    width = tokens.shape[2]
    own = global_states.shape[1]
    seq_count = lax.axis_size("seq")
    seq_place = lax.axis_index("seq")
    group_rows = rows * seq_count
    own_start = seq_place * own
    first_of_slot = own_start % GLOBALS == 0
    place = jnp.stack(
        [
            lax.axis_index("batch"),
            seq_place,
            jnp.where(first_of_slot, own_start // GLOBALS, -1),
        ]
    ).astype(jnp.int32)
    scalars = (lengths, bucket_of, place)
    norms = [norm_params[i : i + 1] for i in range(6)]
    b2_line = b2[None]

    batch_count = lax.axis_size("batch")
    grid_of = None
    if seq_count == 16 and batch_count == 2 and 2 * own == GLOBALS and rows == 2 * BLOCK:
        grid_of = (seq_count, batch_count)

    if grid_of is None:
        arrived_tokens, arrived_grads = from_behind(
            (tokens[0, rows - HALF :], cotangent[0, rows - HALF :]), "seq", 1
        )
        x = jnp.concatenate([arrived_tokens, tokens[0, : rows - HALF]], 0)
        ct = jnp.concatenate([arrived_grads, cotangent[0, : rows - HALF]], 0)
        all_states = lax.all_gather(global_states[0], "seq", axis=0, tiled=True)
        w1t = w1.T
        h, q, k, v = project_local(x, norms[0], norms[1], wq, wk, wv)
        gh, gq, gk, gv = project_global(
            scalars, rows, group_rows, all_states, norms[2], norms[3], wq, wk, wv
        )
    else:
        h, q, k, v, x, ct, all_states, gh, gq, gk, gv, w1t = gather_project(
            tokens[0], cotangent[0], global_states[0], w1, norm_params, wq, wk, wv
        )
        all_states, gh, gq, gk, gv = (
            value.reshape(-1, width) for value in (all_states, gh, gq, gk, gv)
        )
    far, far_stat, part, part_stat = slot_forward(scalars, rows, group_rows, q, k, v, gq, gk, gv)
    if grid_of is None:
        o, line = local_forward(
            False, scalars, rows, group_rows, q, k, v, far, far_stat, None, None
        )
        part_peak = part_stat[:, :, 0:2]
        peak = jnp.max(lax.all_gather(part_peak, "seq"), axis=0)
        factor = jnp.exp(part_peak - peak)
        scaled = part.reshape(SLOTS, PAIRS, 2, HEAD_DIM, GLOBALS).astype(f32) * factor[:, :, :, None]
        scaled = scaled.reshape(SLOTS, width, GLOBALS)
        scaled_total = (part_stat[:, :, 2:4] * factor).reshape(SLOTS, HEADS, GLOBALS)
        payload = jnp.concatenate(
            [scaled, scaled_total, jnp.zeros((SLOTS, 4, GLOBALS), f32)], 1
        ).transpose(0, 2, 1)
        sums = lax.psum_scatter(
            payload.astype(bf16).reshape(SLOTS * GLOBALS, -1), "seq", scatter_dimension=0, tiled=True
        ).astype(f32)
        own_total = sums[:, width : width + HEADS]
        all_peak = peak.reshape(SLOTS, HEADS, GLOBALS).transpose(0, 2, 1).reshape(-1, HEADS)
        own_peak = lax.dynamic_slice_in_dim(all_peak, own_start, own, 0)
        go = (
            (sums[:, :width].reshape(own, HEADS, HEAD_DIM) / own_total[:, :, None])
            .reshape(own, width)
            .astype(bf16)
        )
        gstat = own_peak + jnp.log(own_total)
    else:
        o, line, half_sum, half_stat = local_forward(
            True, scalars, rows, group_rows, q, k, v, far, far_stat, part, part_stat
        )

    z, dy, do, gz, gdy, gdo, dwo, db1, db2, dgain2, doffset2, *dws = branch(
        grid_of,
        x,
        o,
        ct,
        global_states[0],
        go if grid_of is None else half_sum,
        gstat if grid_of is None else half_stat,
        global_cotangent[0],
        wo,
        w1t,
        b1,
        w2,
        b2_line,
        norm_params,
    )
    if grid_of is None:
        gcentre = jnp.sum(
            (gdo.astype(f32) * go.astype(f32)).reshape(own, HEADS, HEAD_DIM), axis=-1
        )
        message = jnp.concatenate(
            [gdo]
            + pieces(gstat)
            + pieces(gcentre)
            + [jnp.zeros((own, LANES - 6 * HEADS), bf16)],
            axis=1,
        )
        everyone = lax.all_gather(message, "seq", axis=0, tiled=True)
        dqt, dk, dv, centre = local_backward(
            False, scalars, rows, group_rows, q, k, v, do, o, line, None, None, None, None
        )
    else:
        sum_first, last, message, rest = dws
        dqt, dk, dv, centre, everyone, sum_second, rest = local_backward(
            True, scalars, rows, group_rows, q, k, v, do, o, line, message, rest, last, dwo
        )
    dq, dk, dv, dwg, dgh, dnorm_global = slot_backward(
        scalars,
        rows,
        group_rows,
        q,
        k,
        v,
        do,
        line,
        centre,
        dqt,
        dk,
        dv,
        gq,
        gk,
        gv,
        everyone,
        all_states,
        gh,
        wq,
        wk,
        wv,
    )
    if grid_of is None:
        dx, dqkv, dnorm = project_back(x, dy, h, dq, dk, dv, dwg, wq, wk, wv, norms[0])
        back_z, back_grad = from_behind((z[:HALF], dx[:HALF].astype(bf16)), "seq", -1)
        layer_out = jnp.concatenate([z[HALF:], back_z], 0)
        token_grad = jnp.concatenate([dx[HALF:], back_grad.astype(f32)], 0)
        small = jnp.concatenate([db1, db2, dnorm[:2], dnorm_global[:2], dgain2, doffset2], 0)
        dgh = lax.psum_scatter(dgh, "seq", scatter_dimension=0, tiled=True).astype(f32)
        gunit, gscale = normalize_rows(global_states[0].astype(f32))
        global_grad = gdy + norm_back(gunit, gscale, norms[2], dgh)
        small = lax.psum(small, ("batch", "seq"))
        dw1, dw2 = dws
        weights = [scatter_sum(value) for value in (dqkv[0], dqkv[1], dqkv[2], dwo, dw1, dw2)]
    else:
        sum_third, small, global_grad, layer_out, token_grad = finish_all(
            rest,
            x,
            dy,
            h,
            dq,
            dk,
            dv,
            dwg,
            dgh,
            z,
            wq,
            wk,
            wv,
            (db1, db2, dnorm_global, dgain2, doffset2),
            global_states[0],
            gdy,
            norm_params,
        )
        piece = width // seq_count
        lanes = width // batch_count
        steps = w1.shape[1] // FF_CHUNK
        chunks = jnp.concatenate([sum_first, sum_second, sum_third[: 2 * piece]], 0)
        chunks = chunks.reshape(steps, 2, piece, lanes)
        part1 = chunks[:, 0].reshape(steps * piece, lanes)
        part2 = chunks[:, 1].reshape(steps, piece, lanes // piece, piece)
        part2 = part2.transpose(1, 2, 0, 3).reshape(piece, -1)
        parts = [sum_third[i * piece : (i + 1) * piece] for i in (3, 4, 5, 2)] + [part1, part2]
        weights = [value.T for value in parts]
    hidden_rows = w1.shape[1] // width
    return (
        layer_out[None],
        gz[None],
        token_grad[None],
        global_grad[None],
        *weights,
        small[:hidden_rows].reshape(-1),
        small[hidden_rows],
        small[hidden_rows + 1 : hidden_rows + 7],
    )


def solution(mesh):
    split = P("batch", "seq", None)
    return jax.shard_map(
        on_device,
        mesh=mesh,
        in_specs=(split, split) + (P(),) * 11 + (split, split),
        out_specs=(split,) * 4 + (P("batch", "seq"),) * 6 + (P(),) * 3,
        check_vma=False,
    )
```

```python
import functools

import jax
import jax.numpy as jnp
from jax import lax
from jax.experimental import pallas as pl
from jax.experimental.pallas import tpu as pltpu
from jax.sharding import PartitionSpec as P

HEADS = 12
HEAD_DIM = 64
PAIRS = HEADS // 2
LANES = 128
BLOCK = 512
HALF = 256
GLOBALS = 128
SLOTS = 8
FF_CHUNK = 768
TOGETHER = 3

norm_eps = 1e-05
masked_score = -1e30
query_scale = 0.125

SLOT_LANE = 16
GLOBAL_LANE = 32

f32 = jnp.float32
bf16 = jnp.bfloat16
VMEM_LIMIT = 60 * 1024 * 1024


def nn(left, right):
    return jnp.dot(left, right, preferred_element_type=f32)


def nt(left, right):
    return lax.dot_general(left, right, (((1,), (1,)), ((), ())), preferred_element_type=f32)


def tn(left, right):
    return lax.dot_general(left, right, (((0,), (0,)), ((), ())), preferred_element_type=f32)


def iota(shape, dim):
    return lax.broadcasted_iota(jnp.int32, shape, dim)


def stack_pair(pair):
    lane = iota((1, LANES), 1)
    low = jnp.where(lane < HEAD_DIM, 1.0, 0.0).astype(bf16)
    high = jnp.where(lane < HEAD_DIM, 0.0, 1.0).astype(bf16)
    return jnp.concatenate([pair * low, pair * high], axis=0)


def read_edges(lengths, bucket_of, place, edges):
    bucket = bucket_of[place[0]]
    total = jnp.int32(0)
    edges[0] = total
    for slot in range(SLOTS):
        total = total + lengths[bucket, slot]
        edges[slot + 1] = total


def block_start(place, rows, block):
    return place[1] * rows + block * BLOCK - HALF


def slot_present(slot, place, edges, rows, group_rows, block):
    low = edges[slot]
    high = edges[slot + 1]
    found = jnp.bool_(False)
    for part in range(BLOCK // HALF):
        start = block_start(place, rows, block) + part * HALF
        start = jnp.where(start < 0, start + group_rows, start)
        found = found | ((high > low) & (low < start + HALF) & (high > start))
    return found


def row_numbers(place, edges, rows, group_rows, block):
    place_in = block_start(place, rows, block) + iota((BLOCK, LANES), 0)
    wrapped = place_in < 0
    token = jnp.where(wrapped, place_in + group_rows, place_in)
    slot = jnp.zeros((BLOCK, LANES), jnp.int32)
    for j in range(SLOTS):
        slot = slot + jnp.where(edges[j + 1] <= token, 1, 0)
    return slot, slot + jnp.where(wrapped, SLOTS, 0)


def key_extra(slot, segment):
    lane = iota((BLOCK, LANES), 1)
    extra = jnp.where((lane < SLOT_LANE) & (lane != segment), masked_score, 0.0)
    return jnp.where(lane == GLOBAL_LANE + slot, 1.0, extra)


def query_extra(slot, segment):
    lane = iota((BLOCK, LANES), 1)
    return jnp.where((lane == segment) | (lane == SLOT_LANE + slot), 1.0, 0.0)


def global_key_extra(slot):
    lane = iota((GLOBALS, LANES), 1)
    inside = (lane >= SLOT_LANE) & (lane < SLOT_LANE + SLOTS)
    extra = jnp.where(inside & (lane != SLOT_LANE + slot), masked_score, 0.0)
    return jnp.where(lane == GLOBAL_LANE + slot, 1.0, extra)


def global_query_extra(slot):
    lane = iota((GLOBALS, LANES), 1)
    inside = (lane >= GLOBAL_LANE) & (lane < GLOBAL_LANE + SLOTS)
    return jnp.where(inside & (lane != GLOBAL_LANE + slot), masked_score, 0.0)


def normalize_rows(values):
    mean = jnp.mean(values, axis=-1, keepdims=True)
    centered = values - mean
    variance = jnp.mean(centered * centered, axis=-1, keepdims=True)
    scale = lax.rsqrt(variance + norm_eps)
    return centered * scale, scale


def norm_back(unit, scale, gain, upstream):
    inner = upstream * gain
    along = jnp.mean(inner * unit, axis=-1, keepdims=True)
    return scale * (inner - jnp.mean(inner, axis=-1, keepdims=True) - unit * along)


def gelu_parts(value):
    decay = jnp.exp(-0.5 * value * value)
    step = 1.0 / (1.0 + (0.3275911 * 0.7071067811865476) * jnp.abs(value))
    series = 1.061405429 * step - 1.453152027
    series = series * step + 1.421413741
    series = series * step - 0.284496736
    series = series * step + 0.254829592
    tail = (0.5 * series) * step * decay
    area = jnp.where(value >= 0.0, 1.0 - tail, tail)
    return area, decay * 0.3989422804014327


def full(shape):
    return pl.BlockSpec(shape, lambda *unused: (0,) * len(shape))


def once(shape):
    return pl.BlockSpec(
        shape, lambda *unused: (0,) * len(shape), pipeline_mode=pl.Buffered(buffer_count=1)
    )


def params(**more):
    return pltpu.CompilerParams(vmem_limit_bytes=VMEM_LIMIT, **more)


STAGES = 5
MESH = pl.DeviceIdType.MESH
WEIGHTS = (("core", 1), ("y", 2), ("z0", 4), ("z1", 8))


def my_place():
    batch = lax.axis_index("batch")
    seq = lax.axis_index("seq")
    bits = {"x": batch}
    partners = {"x": (1 - batch, seq)}
    for name, weight in WEIGHTS:
        bits[name] = (seq // weight) % 2
        partners[name] = (batch, seq + weight - 2 * weight * bits[name])
    return bits, partners


def meet(devices):
    barrier = pltpu.get_barrier_semaphore()
    for device in devices:
        pl.semaphore_signal(barrier, inc=1, device_id=device, device_id_type=MESH)
    pl.semaphore_wait(barrier, len(devices))


def remote(source, target, send, recv, device):
    return pltpu.make_async_remote_copy(
        src_ref=source,
        dst_ref=target,
        send_sem=send,
        recv_sem=recv,
        device_id=device,
        device_id_type=MESH,
    )


class RowGather:
    def __init__(self, ref, cut, send_sem, recv_sem, bits, partners):
        self.ref = ref
        self.cut = cut
        self.send_sem = send_sem
        self.recv_sem = recv_sem
        self.bits = bits
        self.partners = partners

    def copies(self, number):
        core, y, z0, z1 = (self.bits[name] for name in ("core", "y", "z0", "z1"))
        ref = self.ref
        rows = pl.ds(0, ref.shape[4])
        left = pl.ds(0, self.cut)
        right = pl.ds(self.cut, ref.shape[5] - self.cut)
        if number == 0:
            moves = [
                (ref.at[z1, z0, y, core, rows, left], "z1"),
                (ref.at[z1, z0, y, core, rows, right], "z1"),
            ]
        elif number == 1:
            moves = [
                (ref.at[:, z0, y, core, rows, left], "z0"),
                (ref.at[:, z0, y, core, rows, right], "y"),
            ]
        elif number == 2:
            moves = [
                (ref.at[:, :, y, core, rows, left], "y"),
                (ref.at[:, z0, :, core, rows, right], "z0"),
            ]
        else:
            moves = [
                (ref.at[:, :, :, core, rows, left], "core"),
                (ref.at[:, :, :, core, rows, right], "core"),
            ]
        return [
            remote(
                part,
                part,
                self.send_sem.at[number, side],
                self.recv_sem.at[number, side],
                self.partners[name],
            )
            for side, (part, name) in enumerate(moves)
        ]

    def begin(self):
        for copy in self.copies(0):
            copy.start()

    def advance(self, number):
        for copy in self.copies(number):
            copy.wait_recv()
        if number < 3:
            for copy in self.copies(number + 1):
                copy.start()

    def end(self):
        for number in range(4):
            for copy in self.copies(number):
                copy.wait_send()


X_FIRST = ("core", "x", "y", "z0", "z1")
Y_FIRST = ("core", "y", "x", "z0", "z1")
Z_FIRST = ("core", "z0", "x", "z1", "y")
AXES = ("z1", "z0", "y", "core", "x")


class HalvingSum:
    def __init__(
        self, orders, sources, landings, own, send_sem, recv_sem, own_sem, put, bits, partners
    ):
        self.orders = orders
        self.sources = sources
        self.landings = landings
        self.own = own
        self.send_sem = send_sem
        self.recv_sem = recv_sem
        self.own_sem = own_sem
        self.put = put
        self.bits = bits
        self.partners = partners

    def part(self, unit, stage, other):
        order = self.orders[unit]
        name = order[stage]
        side = 1 - self.bits[name] if other else self.bits[name]
        if stage == 0:
            if not other and self.own is not None:
                return self.own.at[unit]
            return self.sources[unit](side)
        left = [axis for axis in AXES if axis in order[stage:]]
        index = (slice(None),) * left.index(name) + (side,)
        return self.landings[stage - 1].at[unit].at[index]

    def copy(self, unit, stage):
        return remote(
            self.part(unit, stage, True),
            self.landings[stage].at[unit],
            self.send_sem.at[unit, stage],
            self.recv_sem.at[unit, stage],
            self.partners[self.orders[unit][stage]],
        )

    def own_copy(self, unit):
        return pltpu.make_async_copy(
            self.sources[unit](self.bits["core"]), self.own.at[unit], self.own_sem.at[unit]
        )

    def begin(self, unit):
        if self.own is not None:
            self.own_copy(unit).start()
        self.copy(unit, 0).start()

    def advance(self, unit, stage, stop=False):
        if stage == 0 and self.own is not None:
            self.own_copy(unit).wait()
        self.copy(unit, stage).wait_recv()
        landing = self.landings[stage].at[unit]
        kept = self.part(unit, stage, False)
        if stage < len(self.orders[unit]) - 1:
            add_into(landing, kept)
            if not stop:
                self.copy(unit, stage + 1).start()
        else:
            self.put(unit, landing[...].astype(f32) + kept[...].astype(f32))

    def sent(self, unit, stage):
        self.copy(unit, stage).wait_send()


def put_rows(ref, rows):
    def put(unit, value):
        ref[unit * rows : (unit + 1) * rows] = value

    return put


def add_into(target, more):
    def one(i, carry):
        target[i] = target[i] + more[i]
        return carry

    lax.fori_loop(0, target.shape[0], one, 0)


def sum_scratch(units, rows, lanes, with_own):
    piece = (rows, lanes)
    dma = pltpu.SemaphoreType.DMA
    shapes = [pltpu.VMEM((units, 2, 2, 2, 2) + piece, bf16)] if with_own else []
    shapes += [
        pltpu.VMEM((units, 2, 2, 2, 2) + piece, bf16),
        pltpu.VMEM((units, 2, 2, 2) + piece, bf16),
        pltpu.VMEM((units, 2, 2) + piece, bf16),
        pltpu.VMEM((units, 2) + piece, bf16),
        pltpu.VMEM((units,) + piece, bf16),
        dma((units, STAGES)),
        dma((units, STAGES)),
    ]
    return shapes + ([dma((units,))] if with_own else [])


def project_rows(rows_ref, gain_ref, offset_ref, wq_ref, wk_ref, wv_ref, outs):
    unit, unused = normalize_rows(rows_ref[...].astype(f32))
    normed = (unit * gain_ref[...] + offset_ref[...]).astype(bf16)
    outs[0][...] = normed
    outs[1][...] = (nn(normed, wq_ref[...]) * query_scale).astype(bf16)
    outs[2][...] = nn(normed, wk_ref[...]).astype(bf16)
    outs[3][...] = nn(normed, wv_ref[...]).astype(bf16)


def project_local_kernel(rows_ref, gain_ref, offset_ref, wq_ref, wk_ref, wv_ref, *outs):
    project_rows(rows_ref, gain_ref, offset_ref, wq_ref, wk_ref, wv_ref, outs)


def project_local(rows, gain, offset, wq, wk, wv):
    count, width = rows.shape
    tile = pl.BlockSpec((BLOCK, width), lambda i: (i, 0))
    return pl.pallas_call(
        project_local_kernel,
        grid=(count // BLOCK,),
        in_specs=[tile, full((1, width)), full((1, width))] + [once((width, width))] * 3,
        out_specs=[tile] * 4,
        out_shape=[jax.ShapeDtypeStruct((count, width), bf16)] * 4,
        compiler_params=params(),
        cost_estimate=pl.CostEstimate(
            flops=6 * count * width * width, bytes_accessed=12 * count * width, transcendentals=0
        ),
        name="project_local",
    )(rows, gain, offset, wq, wk, wv)


def gather_project_kernel(
    tokens_ref,
    states_ref,
    w1_ref,
    norms_ref,
    wq_in,
    wk_in,
    wv_in,
    h_out,
    q_out,
    k_out,
    v_out,
    x_out,
    all_out,
    gh_out,
    gq_out,
    gk_out,
    gv_out,
    w1t_out,
    wq_ref,
    wk_ref,
    wv_ref,
    x_ref,
    all_ref,
    local_ref,
    global_ref,
    w1s_ref,
    w1t_ref,
    halo_send,
    halo_recv,
    load_sem,
    store_sem,
    gstore_sem,
    more_sem,
    send_sem,
    recv_sem,
):
    bits, partners = my_place()
    batch = lax.axis_index("batch")
    seq = lax.axis_index("seq")
    places = lax.axis_size("seq")
    after = (batch, lax.rem(seq + 1, places))
    before = (batch, lax.rem(seq + places - 1, places))
    rows, width = tokens_ref.shape
    own = states_ref.shape[0]
    core, y, z0, z1 = (bits[name] for name in ("core", "y", "z0", "z1"))
    start = pl.ds(0, HALF)
    most = pl.ds(0, rows - HALF)
    end = pl.ds(rows - HALF, HALF)
    shifted = pl.ds(HALF, rows - HALF)
    loads = [
        pltpu.make_async_copy(source, target, load_sem.at[number])
        for number, (source, target) in enumerate(
            (
                (tokens_ref.at[most], x_ref.at[shifted]),
                (wq_in, wq_ref),
                (wk_in, wk_ref),
                (wv_in, wv_ref),
                (w1_ref, w1s_ref),
            )
        )
    ]
    for load in loads:
        load.start()
    all_ref[z1, z0, y, core] = states_ref[...]
    meet([partners[name] for name, unused in WEIGHTS] + [before, after])
    halo = remote(tokens_ref.at[end], x_ref.at[start], halo_send, halo_recv, after)
    gather = RowGather(all_ref, width // 2, send_sem, recv_sem, bits, partners)
    gather.begin()
    halo.start()

    outs = (h_out, q_out, k_out, v_out)

    def stores(index):
        at = pl.ds(index * HALF, HALF)
        return [
            pltpu.make_async_copy(local_ref.at[which, at], out.at[at], store_sem.at[which, index])
            for which, out in enumerate(outs)
        ]

    def project(index):
        at = pl.ds(index * HALF, HALF)
        project_rows(
            x_ref.at[at],
            norms_ref.at[0:1],
            norms_ref.at[1:2],
            wq_ref,
            wk_ref,
            wv_ref,
            [local_ref.at[which, at] for which in range(4)],
        )
        for store in stores(index):
            store.start()

    for number in range(4):
        loads[number].wait()
    tiles = rows // HALF
    def turn(i, carry):
        at = pl.ds(pl.multiple_of(i * HALF, HALF), HALF)
        w1t_ref[at, :] = w1s_ref[:, at].T
        return carry

    project(1)
    project(2)
    gather.advance(0)
    for index in range(3, tiles):
        project(index)
    loads[4].wait()
    turns = w1t_ref.shape[0] // HALF
    lax.fori_loop(0, turns // 2, turn, 0)
    gather.advance(1)
    lax.fori_loop(turns // 2, turns, turn, 0)
    w1t_store = pltpu.make_async_copy(w1t_ref, w1t_out, more_sem.at[1])
    w1t_store.start()
    gather.advance(2)

    gouts = (gh_out, gq_out, gk_out, gv_out)

    def gstores(first, side):
        return [
            pltpu.make_async_copy(
                global_ref.at[which, first, :, :, side],
                out.at[first, :, :, side],
                gstore_sem.at[which, first, number],
            )
            for which, out in enumerate(gouts)
            for number in ((0 if side is core else 1),)
        ]

    def project_states(side):
        for first in range(2):
            piece = all_ref[first, :, :, side].reshape(4 * own, width)
            unit, unused = normalize_rows(piece.astype(f32))
            normed = (unit * norms_ref[2:3] + norms_ref[3:4]).astype(bf16)
            values = (
                normed,
                (nn(normed, wq_ref[...]) * query_scale).astype(bf16),
                nn(normed, wk_ref[...]).astype(bf16),
                nn(normed, wv_ref[...]).astype(bf16),
            )
            for which, value in enumerate(values):
                global_ref[which, first, :, :, side] = value.reshape(2, 2, own, width)
            for store in gstores(first, side):
                store.start()

    other = 1 - core
    project_states(core)
    gather.advance(3)
    all_store = pltpu.make_async_copy(all_ref, all_out, more_sem.at[2])
    all_store.start()
    project_states(other)
    halo.wait_recv()
    x_store = pltpu.make_async_copy(x_ref, x_out, more_sem.at[0])
    x_store.start()
    project(0)

    for index in range(tiles):
        for store in stores(index):
            store.wait()
    for side in (core, other):
        for first in range(2):
            for store in gstores(first, side):
                store.wait()
    x_store.wait()
    w1t_store.wait()
    all_store.wait()
    halo.wait_send()
    gather.end()


def gather_project(tokens, states, w1, norms, wq, wk, wv):
    rows, width = tokens.shape
    own = states.shape[0]
    vmem = pl.BlockSpec(memory_space=pltpu.VMEM)
    anywhere = pl.BlockSpec(memory_space=pl.ANY)
    dma = pltpu.SemaphoreType.DMA
    local = jax.ShapeDtypeStruct((rows, width), bf16)
    glob = jax.ShapeDtypeStruct((2, 2, 2, 2, own, width), bf16)
    turned = (w1.shape[1], width)
    weight = pltpu.VMEM((width, width), bf16)
    return pl.pallas_call(
        gather_project_kernel,
        in_specs=[anywhere, vmem, anywhere, vmem] + [anywhere] * 3,
        out_specs=[anywhere] * 11,
        out_shape=[local] * 5 + [glob] * 5 + [jax.ShapeDtypeStruct(turned, bf16)],
        scratch_shapes=[
            weight,
            weight,
            weight,
            pltpu.VMEM((rows, width), bf16),
            pltpu.VMEM(glob.shape, bf16),
            pltpu.VMEM((4, rows, width), bf16),
            pltpu.VMEM((4,) + glob.shape, bf16),
            pltpu.VMEM(w1.shape, bf16),
            pltpu.VMEM(turned, bf16),
            dma,
            dma,
            dma((5,)),
            dma((4, rows // HALF)),
            dma((4, 2, 2)),
            dma((3,)),
            dma((4, 2)),
            dma((4, 2)),
        ],
        compiler_params=params(collective_id=1, has_side_effects=True),
        cost_estimate=pl.CostEstimate(
            flops=6 * (rows + 16 * own) * width * width,
            bytes_accessed=24 * rows * width,
            transcendentals=0,
        ),
        name="gather_project",
    )(tokens, states, w1, norms, wq, wk, wv)


def project_global_kernel(
    rows_count,
    group_rows,
    lengths,
    bucket_of,
    place,
    rows_ref,
    gain_ref,
    offset_ref,
    wq_ref,
    wk_ref,
    wv_ref,
    h_ref,
    q_ref,
    k_ref,
    v_ref,
    edges,
):
    slot = pl.program_id(0)

    @pl.when(slot == 0)
    def _():
        read_edges(lengths, bucket_of, place, edges)

    needed = slot == place[2]
    for block in range(rows_count // BLOCK):
        needed = needed | slot_present(slot, place, edges, rows_count, group_rows, block)

    @pl.when(needed)
    def _():
        project_rows(
            rows_ref, gain_ref, offset_ref, wq_ref, wk_ref, wv_ref, (h_ref, q_ref, k_ref, v_ref)
        )


def project_global(scalars, rows_count, group_rows, rows, gain, offset, wq, wk, wv):
    count, width = rows.shape
    tile = pl.BlockSpec((GLOBALS, width), lambda i, *unused: (i, 0))
    return pl.pallas_call(
        functools.partial(project_global_kernel, rows_count, group_rows),
        grid_spec=pltpu.PrefetchScalarGridSpec(
            num_scalar_prefetch=3,
            grid=(SLOTS,),
            in_specs=[tile, full((1, width)), full((1, width))] + [once((width, width))] * 3,
            out_specs=[tile] * 4,
            scratch_shapes=[pltpu.SMEM((16,), jnp.int32)],
        ),
        out_shape=[jax.ShapeDtypeStruct((count, width), bf16)] * 4,
        compiler_params=params(),
        cost_estimate=pl.CostEstimate(
            flops=6 * 256 * width * width, bytes_accessed=12 * count * width, transcendentals=0
        ),
        name="project_global",
    )(*scalars, rows, gain, offset, wq, wk, wv)


def block_columns(place, edges, rows, group_rows, block, step, blocks, query_columns, key_columns):
    @pl.when(step < blocks)
    def _():
        slot_of, segment = row_numbers(place, edges, rows, group_rows, block)
        query_columns[block] = query_extra(slot_of, segment).astype(bf16)
        key_columns[block] = key_extra(slot_of, segment).astype(bf16)


def slot_line(place, edges, rows, group_rows, block):
    token = block_start(place, rows, block) + iota((1, BLOCK), 1)
    token = jnp.where(token < 0, token + group_rows, token)
    slot = jnp.zeros((1, BLOCK), jnp.int32)
    for j in range(SLOTS):
        slot = slot + jnp.where(edges[j + 1] <= token, 1, 0)
    return slot


def side_by_side(stacked):
    return stacked[:HEAD_DIM, : stacked.shape[1] // 2], stacked[HEAD_DIM:, stacked.shape[1] // 2 :]


def slot_forward_kernel(
    rows_count,
    group_rows,
    lengths,
    bucket_of,
    place,
    q_ref,
    k_ref,
    v_ref,
    gq_ref,
    gk_ref,
    gv_ref,
    far_ref,
    far_stat_ref,
    part_ref,
    part_stat_ref,
    edges,
    query_columns,
    key_columns,
    keys_ref,
    queries_ref,
    sum_ref,
    far_sum,
):
    group = pl.program_id(0)
    block = pl.program_id(1)
    blocks = rows_count // BLOCK
    step = group * blocks + block
    together = range(TOGETHER)

    @pl.when(step == 0)
    def _():
        read_edges(lengths, bucket_of, place, edges)

    @pl.when(block == 0)
    def _():
        sum_ref[...] = jnp.zeros_like(sum_ref)
        part_stat_ref[...] = jnp.broadcast_to(
            jnp.where(iota((8, GLOBALS), 0) < 2, masked_score, 0.0), part_stat_ref.shape
        )

    block_columns(
        place, edges, rows_count, group_rows, block, step, blocks, query_columns, key_columns
    )
    extra = query_columns[block]
    for which in together:
        lanes = pl.ds(which * LANES, LANES)
        keys_ref[which, :, :LANES] = k_ref[:, lanes]
        keys_ref[which, :, LANES:] = key_columns[block]
        queries_ref[which, :, :LANES] = stack_pair(q_ref[:, lanes])
        queries_ref[which, :BLOCK, LANES:] = extra
        queries_ref[which, BLOCK:, LANES:] = extra
    line = slot_line(place, edges, rows_count, group_rows, block)
    both_lines = jnp.concatenate([line, line], 1)

    def add(slot, keys_of, values_of):
        at = pl.ds(pl.multiple_of(slot * GLOBALS, GLOBALS), GLOBALS)
        extra = global_query_extra(slot).astype(bf16)
        for which in together:
            lanes = pl.ds(which * LANES, LANES)
            queries = jnp.concatenate(
                [stack_pair(gq_ref[at, lanes]), jnp.concatenate([extra, extra], 0)], axis=1
            )
            score = nt(keys_of(which), queries)
            stat = part_stat_ref[slot, which]
            old = jnp.concatenate([stat[0:1], stat[1:2]], axis=1)
            peak = jnp.maximum(old, jnp.max(score, axis=0, keepdims=True))
            weights = jnp.exp(score - peak)
            keep = jnp.exp(old - peak)
            total = jnp.concatenate([stat[2:3], stat[3:4]], axis=1) * keep + jnp.sum(
                weights, axis=0, keepdims=True
            )
            part_stat_ref[slot, which] = jnp.concatenate(
                [
                    peak[:, :GLOBALS],
                    peak[:, GLOBALS:],
                    total[:, :GLOBALS],
                    total[:, GLOBALS:],
                    jnp.zeros((4, GLOBALS), f32),
                ],
                axis=0,
            )
            low, high = side_by_side(tn(values_of(which), weights.astype(bf16)))
            sums = sum_ref.at[which, slot]
            sums[:HEAD_DIM] = sums[:HEAD_DIM] * keep[:, :GLOBALS] + low
            sums[HEAD_DIM:] = sums[HEAD_DIM:] * keep[:, GLOBALS:] + high

    far_sum[...] = jnp.zeros_like(far_sum)
    far_stat_ref[...] = jnp.zeros_like(far_stat_ref)

    def one_slot(slot, carry):
        @pl.when(slot_present(slot, place, edges, rows_count, group_rows, block))
        def _():
            add(
                slot,
                lambda which: keys_ref[which],
                lambda which: v_ref[:, pl.ds(which * LANES, LANES)],
            )
            at = pl.ds(pl.multiple_of(slot * GLOBALS, GLOBALS), GLOBALS)
            columns = global_key_extra(slot).astype(bf16)
            mine = both_lines == slot
            here = line == slot
            for which in together:
                lanes = pl.ds(which * LANES, LANES)
                slot_keys = jnp.concatenate([gk_ref[at, lanes], columns], 1)
                score = nt(slot_keys, queries_ref[which])
                peak = jnp.max(score, axis=0, keepdims=True)
                weights = jnp.exp(score - peak)
                total = jnp.sum(weights, axis=0, keepdims=True)
                stat = far_stat_ref.at[which, 0]
                stat[0:1] = jnp.where(mine, peak, stat[0:1])
                stat[1:2] = jnp.where(mine, total, stat[1:2])
                low, high = side_by_side(tn(gv_ref[at, lanes], weights.astype(bf16)))
                first = pl.ds(which * LANES, HEAD_DIM)
                second = pl.ds(which * LANES + HEAD_DIM, HEAD_DIM)
                far_sum[first] = jnp.where(here, low, far_sum[first])
                far_sum[second] = jnp.where(here, high, far_sum[second])

        return carry

    lax.fori_loop(0, SLOTS, one_slot, 0)
    far_ref[...] = far_sum[...].astype(bf16)

    @pl.when((block == blocks - 1) & (place[2] >= 0))
    def _():
        slot = place[2]
        at = pl.ds(pl.multiple_of(slot * GLOBALS, GLOBALS), GLOBALS)
        columns = global_key_extra(slot).astype(bf16)
        add(
            slot,
            lambda which: jnp.concatenate(
                [gk_ref[at, pl.ds(which * LANES, LANES)], columns], axis=1
            ),
            lambda which: gv_ref[at, pl.ds(which * LANES, LANES)],
        )

    @pl.when(block == blocks - 1)
    def _():
        for which in together:
            part_ref[:, which] = sum_ref[which].astype(bf16)


def line_spec(pairs=1):
    return pl.BlockSpec((pairs, 1, 8, 2 * BLOCK), lambda p, b, *unused: (p, b, 0, 0))


def column_scratch(blocks):
    return [pltpu.SMEM((16,), jnp.int32)] + [pltpu.VMEM((blocks, BLOCK, LANES), bf16)] * 2


def slot_forward(scalars, rows_count, group_rows, q, k, v, gq, gk, gv):
    blocks = rows_count // BLOCK
    all_globals, width = gq.shape
    block_spec = pl.BlockSpec((BLOCK, TOGETHER * LANES), lambda p, b, *unused: (b, p))
    pair_spec = pl.BlockSpec((all_globals, TOGETHER * LANES), lambda p, b, *unused: (0, p))
    return pl.pallas_call(
        functools.partial(slot_forward_kernel, rows_count, group_rows),
        grid_spec=pltpu.PrefetchScalarGridSpec(
            num_scalar_prefetch=3,
            grid=(PAIRS // TOGETHER, blocks),
            in_specs=[block_spec] * 3 + [pair_spec] * 3,
            out_specs=[
                pl.BlockSpec((TOGETHER * LANES, BLOCK), lambda p, b, *unused: (p, b)),
                line_spec(TOGETHER),
                pl.BlockSpec((SLOTS, TOGETHER, LANES, GLOBALS), lambda p, b, *unused: (0, p, 0, 0)),
                pl.BlockSpec((SLOTS, TOGETHER, 8, GLOBALS), lambda p, b, *unused: (0, p, 0, 0)),
            ],
            scratch_shapes=column_scratch(blocks)
            + [
                pltpu.VMEM((TOGETHER, BLOCK, 2 * LANES), bf16),
                pltpu.VMEM((TOGETHER, 2 * BLOCK, 2 * LANES), bf16),
                pltpu.VMEM((TOGETHER, SLOTS, LANES, GLOBALS), f32),
                pltpu.VMEM((TOGETHER * LANES, BLOCK), f32),
            ],
        ),
        out_shape=[
            jax.ShapeDtypeStruct((width, rows_count), bf16),
            jax.ShapeDtypeStruct((PAIRS, blocks, 8, 2 * BLOCK), f32),
            jax.ShapeDtypeStruct((SLOTS, PAIRS, LANES, GLOBALS), bf16),
            jax.ShapeDtypeStruct((SLOTS, PAIRS, 8, GLOBALS), f32),
        ],
        compiler_params=params(),
        cost_estimate=pl.CostEstimate(
            flops=8 * 4 * rows_count * GLOBALS * width,
            bytes_accessed=20 * all_globals * width,
            transcendentals=2 * HEADS * rows_count * GLOBALS,
        ),
        name="slot_forward",
    )(*scalars, q, k, v, gq, gk, gv)


def merge_parts(stat, sums, more_stat, more_sums):
    peak = jnp.maximum(stat[0:2], more_stat[0:2])
    keep = jnp.exp(stat[0:2] - peak)
    take = jnp.exp(more_stat[0:2] - peak)
    total = stat[2:4] * keep + more_stat[2:4] * take
    low = sums[:HEAD_DIM].astype(f32) * keep[0:1] + more_sums[:HEAD_DIM].astype(f32) * take[0:1]
    high = sums[HEAD_DIM:].astype(f32) * keep[1:2] + more_sums[HEAD_DIM:].astype(f32) * take[1:2]
    return (
        jnp.concatenate([peak, total, jnp.zeros((4, GLOBALS), f32)], 0),
        jnp.concatenate([low, high], 0),
    )


class SlotSum:
    ORDER = ("core", "y", "z0", "z1")

    def __init__(self, source, sums, stats, send_sem, recv_sem, bits, partners):
        self.source = source
        self.sums = sums
        self.stats = stats
        self.send_sem = send_sem
        self.recv_sem = recv_sem
        self.bits = bits
        self.partners = partners

    def held(self, stage, other):
        bit = self.bits[self.ORDER[stage]]
        side = 1 - bit if other else bit
        if stage == 0:
            return self.source(side)
        index = ((), (slice(None), slice(None)), (slice(None),), ())[stage] + (side,)
        return self.sums[stage - 1].at[index], self.stats[stage - 1].at[index]

    def copies(self, stage):
        partner = self.partners[self.ORDER[stage]]
        sums, stat = self.held(stage, True)
        return (
            remote(
                sums,
                self.sums[stage],
                self.send_sem.at[stage, 0],
                self.recv_sem.at[stage, 0],
                partner,
            ),
            remote(
                stat,
                self.stats[stage],
                self.send_sem.at[stage, 1],
                self.recv_sem.at[stage, 1],
                partner,
            ),
        )

    def begin(self, stage):
        for copy in self.copies(stage):
            copy.start()

    def merge(self, stage, kept=None):
        for copy in self.copies(stage):
            copy.wait_recv()
        sums, stat = self.held(stage, False) if kept is None else kept
        lead = self.sums[stage].shape[:-3]
        total = 1
        for size in lead:
            total = total * size

        def one(number, carry):
            index = []
            left = number
            for size in reversed(lead):
                index.append(left % size)
                left = left // size
            index = tuple(reversed(index))
            for which in range(PAIRS // 2):
                spot = index + (which,)
                new_stat, new_sums = merge_parts(
                    self.stats[stage][spot], self.sums[stage][spot], stat[spot], sums[spot]
                )
                self.stats[stage][spot] = new_stat
                self.sums[stage][spot] = new_sums.astype(bf16)
            return carry

        lax.fori_loop(0, total, one, 0)

    def sent(self, stage):
        for copy in self.copies(stage):
            copy.wait_send()


def local_forward_kernel(
    talk,
    rows_count,
    group_rows,
    lengths,
    bucket_of,
    place,
    q_ref,
    k_ref,
    v_ref,
    far_ref,
    far_stat_ref,
    *refs,
):
    if talk:
        part_ref, part_stat_ref, ct_ref = refs[:3]
        o_ref, line_ref, half_ref, half_stat_ref, ct_head_ref = refs[3:8]
        own_ref, own_stat_ref = refs[8:10]
        sums_refs = refs[10:12]
        stat_refs = refs[12:14]
        edges, query_columns, key_columns, send_sem, recv_sem, own_sem = refs[14:20]
        ct_land, halo_send, halo_recv = refs[20:]
    else:
        o_ref, line_ref, edges, query_columns, key_columns = refs
    pair = pl.program_id(0)
    block = pl.program_id(1)
    blocks = rows_count // BLOCK
    step = pair * blocks + block

    @pl.when(step == 0)
    def _():
        read_edges(lengths, bucket_of, place, edges)

    if talk:
        bits, partners = my_place()
        slot_sum = SlotSum(
            lambda side: (part_ref.at[:, :, :, side], part_stat_ref.at[:, :, :, side]),
            sums_refs,
            stat_refs,
            send_sem,
            recv_sem,
            bits,
            partners,
        )
        own_parts = slot_sum.held(0, False)
        own_copies = [
            pltpu.make_async_copy(own_parts[0], own_ref, own_sem.at[0]),
            pltpu.make_async_copy(own_parts[1], own_stat_ref, own_sem.at[1]),
        ]

        batch = lax.axis_index("batch")
        seq = lax.axis_index("seq")
        places = lax.axis_size("seq")
        after = (batch, lax.rem(seq + 1, places))
        before = (batch, lax.rem(seq + places - 1, places))
        halo = remote(
            ct_ref.at[pl.ds(ct_ref.shape[0] - HALF, HALF)], ct_land, halo_send, halo_recv, after
        )

        @pl.when(step == 0)
        def _():
            meet([partners["core"], partners["y"], before, after])
            for copy in own_copies:
                copy.start()
            slot_sum.begin(0)

        @pl.when(step == 4)
        def _():
            halo.start()

        @pl.when(step == 3)
        def _():
            for copy in own_copies:
                copy.wait()
            slot_sum.merge(0, (own_ref, own_stat_ref))
            slot_sum.begin(1)

        @pl.when(step == PAIRS * blocks - 1)
        def _():
            slot_sum.merge(1)
            half_ref[...] = sums_refs[1][...]
            half_stat_ref[...] = stat_refs[1][...]
            halo.wait_recv()
            ct_head_ref[...] = ct_land[...]
            halo.wait_send()
            slot_sum.sent(0)
            slot_sum.sent(1)

    block_columns(
        place, edges, rows_count, group_rows, block, step, blocks, query_columns, key_columns
    )
    extra = query_columns[block]
    queries = jnp.concatenate(
        [stack_pair(q_ref[...]), jnp.concatenate([extra, extra], 0)], axis=1
    )
    keys = jnp.concatenate([k_ref[...], key_columns[block]], axis=1)
    score = nt(keys, queries)
    far_peak = far_stat_ref[0, 0, 0:1]
    peak = jnp.maximum(jnp.max(score, axis=0, keepdims=True), far_peak)
    weights = jnp.exp(score - peak)
    far_keep = jnp.exp(far_peak - peak)
    total = jnp.sum(weights, axis=0, keepdims=True) + far_stat_ref[0, 0, 1:2] * far_keep
    low, high = side_by_side(tn(v_ref[...], weights.astype(bf16)))
    low = (low + far_ref[:HEAD_DIM] * far_keep[:, :BLOCK]) / total[:, :BLOCK]
    high = (high + far_ref[HEAD_DIM:] * far_keep[:, BLOCK:]) / total[:, BLOCK:]
    o_ref[...] = jnp.concatenate([low, high], 0).T.astype(bf16)
    line_ref[0, 0] = jnp.broadcast_to(peak + jnp.log(total), (8, 2 * BLOCK))


def local_forward(
    talk, scalars, rows_count, group_rows, q, k, v, far, far_stat, part, part_stat, ct
):
    blocks = rows_count // BLOCK
    width = q.shape[1]
    block_spec = pl.BlockSpec((BLOCK, LANES), lambda p, b, *unused: (b, p))
    operands = [q, k, v, far, far_stat]
    in_specs = [block_spec] * 3 + [
        pl.BlockSpec((LANES, BLOCK), lambda p, b, *unused: (p, b)),
        line_spec(),
    ]
    out_specs = [block_spec, line_spec()]
    out_shape = [
        jax.ShapeDtypeStruct((rows_count, width), bf16),
        jax.ShapeDtypeStruct((PAIRS, blocks, 8, 2 * BLOCK), f32),
    ]
    scratch = []
    more = {}
    edges = column_scratch(blocks)
    if talk:
        cut = (2, 2, 2, 2, PAIRS // 2)
        operands += [
            part.reshape(cut + part.shape[2:]),
            part_stat.reshape(cut + part_stat.shape[2:]),
            ct,
        ]
        in_specs += [pl.BlockSpec(memory_space=pl.ANY)] * 3
        shapes = [
            (2, 2, PAIRS // 2, LANES, GLOBALS),
            (2, 2, PAIRS // 2, 8, GLOBALS),
        ]
        out_specs += [full(shape) for shape in shapes] + [full((HALF, width))]
        out_shape += [
            jax.ShapeDtypeStruct(shapes[0], bf16),
            jax.ShapeDtypeStruct(shapes[1], f32),
            jax.ShapeDtypeStruct((HALF, width), bf16),
        ]
        leads = [(2, 2, 2), (2, 2, 2), (2, 2)]
        sums = [pltpu.VMEM(lead + shapes[0][2:], bf16) for lead in leads]
        stats = [pltpu.VMEM(lead + shapes[1][2:], f32) for lead in leads]
        dma = pltpu.SemaphoreType.DMA
        scratch = [sums[0], stats[0]] + sums[1:] + stats[1:]
        edges += [dma((2, 2)), dma((2, 2)), dma((2,))]
        edges += [pltpu.VMEM((HALF, width), bf16), dma, dma]
        more = {"collective_id": 2, "has_side_effects": True}
    return pl.pallas_call(
        functools.partial(local_forward_kernel, talk, rows_count, group_rows),
        grid_spec=pltpu.PrefetchScalarGridSpec(
            num_scalar_prefetch=3,
            grid=(PAIRS, blocks),
            in_specs=in_specs,
            out_specs=out_specs,
            scratch_shapes=scratch + edges,
        ),
        out_shape=out_shape,
        compiler_params=params(**more),
        cost_estimate=pl.CostEstimate(
            flops=16 * rows_count * BLOCK * width,
            bytes_accessed=16 * rows_count * width,
            transcendentals=HEADS * rows_count * BLOCK,
        ),
        name="local_forward",
    )(*scalars, *operands)


def put_grouped(ref, value):
    seq, batch, rows, lanes = ref.shape
    for part in range(batch):
        piece = value[:, part * lanes : (part + 1) * lanes].astype(bf16)
        ref[:, part] = piece.reshape(seq, rows, lanes)


def put_unit(ref, value):
    batch, rows, lanes = ref.shape[4:]
    for part in range(batch):
        piece = value[:, part * lanes : (part + 1) * lanes].astype(bf16)
        ref[:, :, :, :, part] = piece.reshape(ref.shape[:4] + (rows, lanes))


TICKS = 3
DELAYS = (0, 2, 3, 4, 6)


def branch_kernel(
    tile,
    talk,
    x_ref,
    o_ref,
    ct_ref,
    ct_head_ref,
    gx_ref,
    go_in_ref,
    gstat_in_ref,
    gct_ref,
    wo_ref,
    w1_ref,
    b1_ref,
    w2_ref,
    b2_ref,
    norms_ref,
    z_ref,
    dy_ref,
    do_ref,
    gz_ref,
    gdy_ref,
    gdo_ref,
    dwo_ref,
    db1_ref,
    db2_ref,
    dgain_ref,
    doffset_ref,
    first_ref,
    second_ref,
    *refs,
):
    if talk:
        message_ref, rest_ref = refs[:2]
        refs = refs[2:]
    os_ref, cts_ref, y_ref, h_ref, z_sum_ref, dh_ref, dft_ref, a_ref, du_ref, load_sem = refs[:10]
    refs = refs[10:]
    step = pl.program_id(0)
    steps = pl.num_programs(0)
    count, width = x_ref.shape
    own = gx_ref.shape[0]
    extra = os_ref.shape[0] - count
    tiles = count // tile
    tail = pl.ds(count, extra)

    def rows_at(i):
        return pl.ds(i * tile, tile)

    def padded(value):
        return jnp.concatenate([value, jnp.zeros((extra - own, width), value.dtype)], axis=0)

    if talk:
        units_ref = refs[0]
        landings = refs[1:6]
        send_sem, recv_sem = refs[6:8]
        half_ref, half_stat_ref = refs[8:10]
        slot_sums = refs[10:12]
        slot_stats = refs[12:14]
        turned_ref, go_land, gstat_land, stat_ref, slot_send, slot_recv = refs[14:]
        last_step = 4
        bits, partners = my_place()
        core = bits["core"]
        chunks = last_step - 1
        slots = units_ref.shape[0]
        plan = [
            (TICKS * chunk + DELAYS[stage], chunk, stage)
            for chunk in range(chunks)
            for stage in range(STAGES if chunk < chunks - 1 else 2)
        ]

        def source(unit):
            return lambda side: units_ref.at[unit % slots, :, :, :, side]

        engine = HalvingSum(
            (X_FIRST, Y_FIRST) * chunks,
            [source(unit) for unit in range(2 * chunks)],
            landings,
            None,
            send_sem,
            recv_sem,
            None,
            put_rows(first_ref, landings[4].shape[1]),
            bits,
            partners,
        )

        def advance(tick):
            for when, chunk, stage in sorted(plan, key=lambda entry: -entry[2]):
                if when == tick:
                    for unit in (2 * chunk, 2 * chunk + 1):
                        engine.advance(unit, stage, stop=chunk == chunks - 1 and stage == 1)

        def tick_at(position):
            for number in range(1, last_step):
                tick = TICKS * (number - 1) + position

                @pl.when(step == number)
                def _():
                    advance(tick)

        slot_sum = SlotSum(
            None,
            (None, half_ref) + tuple(slot_sums),
            (None, half_stat_ref) + tuple(slot_stats),
            slot_send,
            slot_recv,
            bits,
            partners,
        )
        half_pairs = PAIRS // 2
        lanes = half_pairs * LANES
        my_lanes = pl.ds(pl.multiple_of(core * lanes, LANES), lanes)

        def final_copies():
            theirs = pl.ds(pl.multiple_of((1 - core) * own, own), own)
            return (
                remote(
                    turned_ref.at[theirs],
                    go_land.at[:, my_lanes],
                    slot_send.at[4, 0],
                    slot_recv.at[4, 0],
                    partners["core"],
                ),
                remote(
                    gstat_land.at[core],
                    gstat_land.at[core],
                    slot_send.at[4, 1],
                    slot_recv.at[4, 1],
                    partners["core"],
                ),
            )

        def finish_slots():
            slot_sum.merge(3)
            for which in range(half_pairs):
                stat = slot_stats[1][which]
                total = stat[2:4]
                sums = slot_sums[1][which].astype(f32)
                mean = jnp.concatenate(
                    [sums[:HEAD_DIM] / total[0:1], sums[HEAD_DIM:] / total[1:2]], 0
                )
                turned_ref[:, which * LANES : (which + 1) * LANES] = mean.T.astype(bf16)
                whole = stat[0:2] + jnp.log(total)
                gstat_land[core, which] = jnp.concatenate(
                    [whole, jnp.zeros((6, GLOBALS), f32)], 0
                )
            mine = pl.ds(pl.multiple_of(core * own, own), own)
            go_land[:, my_lanes] = turned_ref[mine, :]
            for copy in final_copies():
                copy.start()

        def put_message():
            product = gdo_ref[...].astype(f32) * go_land[...].astype(f32)
            head_of = iota((width, LANES), 0) // HEAD_DIM == iota((width, LANES), 1)
            head_of = jnp.where(head_of, 1.0, 0.0).astype(bf16)
            first = product.astype(bf16)
            second = (product - first.astype(f32)).astype(bf16)
            centre = nn(first, head_of) + nn(second, head_of)
            lines = [gstat_land[half, which, 0:2] for half in (0, 1) for which in range(half_pairs)]
            lines = jnp.concatenate(lines + [jnp.zeros((LANES - HEADS, GLOBALS), f32)], 0)
            stat_ref[...] = lines.T
            total = stat_ref[pl.ds(pl.multiple_of(core * own, own), own), :]
            spread = jnp.zeros((own, LANES), f32)
            for number, value in enumerate((total, centre)):
                for piece in range(3):
                    low = value.astype(bf16)
                    value = value - low.astype(f32)
                    start_lane = (3 * number + piece) * HEADS
                    source_lane = iota((LANES, LANES), 0)
                    moved = iota((LANES, LANES), 1) == source_lane + start_lane
                    moved = jnp.where(moved & (source_lane < HEADS), 1.0, 0.0).astype(bf16)
                    spread = spread + nn(low, moved)
            message_ref[:, :width] = gdo_ref[...]
            message_ref[:, width:] = spread.astype(bf16)

    else:

        def tick_at(position):
            pass

    loads = [
        pltpu.make_async_copy(o_ref, os_ref.at[pl.ds(0, count)], load_sem.at[0]),
        pltpu.make_async_copy(
            ct_ref.at[pl.ds(0, count - HALF)],
            cts_ref.at[pl.ds(HALF, count - HALF)],
            load_sem.at[1],
        ),
        pltpu.make_async_copy(ct_head_ref, cts_ref.at[pl.ds(0, HALF)], load_sem.at[2]),
    ]

    def start(at, size, x, sums):
        y = x.astype(f32) + nn(os_ref[at, :], wo_ref[...])
        unit, unused = normalize_rows(y)
        h_ref[at, :] = (unit * norms_ref[4:5] + norms_ref[5:6]).astype(bf16)
        y_ref[at, :] = y
        sums[...] = y + b2_ref[...]
        dh_ref[at, :] = jnp.zeros((size, width), f32)

    @pl.when(step == 0)
    def _():
        for load in loads:
            load.start()
        if talk:
            half_ref[...] = go_in_ref[...]
            half_stat_ref[...] = gstat_in_ref[...]
            meet([partners[name] for name in AXES])
            slot_sum.begin(2)
        cts_ref[count:] = padded(gct_ref[...])
        loads[0].wait()

        def start_tile(i, carry):
            at = pl.ds(pl.multiple_of(i * tile, tile), tile)
            start(at, tile, x_ref[at, :], dy_ref.at[at])
            return carry

        lax.fori_loop(0, tiles, start_tile, 0)
        loads[1].wait()
        loads[2].wait()
        dft_ref[...] = cts_ref[...].T
        if talk:
            slot_sum.merge(2)
            slot_sum.begin(3)

    db1_ref[...] = jnp.zeros_like(db1_ref)
    w1 = w1_ref[...].reshape(width, width)
    w2 = w2_ref[...].reshape(width, width)

    def chunk_of(at, sums):
        u = nt(h_ref[at, :], w1) + b1_ref[0]
        da = nt(cts_ref[at, :], w2)
        area, density = gelu_parts(u)
        a = (u * area).astype(bf16)
        du = (da * (area + u * density)).astype(bf16)
        a_ref[at, :] = a
        du_ref[at, :] = du
        db1_ref[0] += jnp.sum(du.astype(f32), axis=0, keepdims=True)
        sums[...] = sums[...] + nn(a, w2)
        dh_ref[at, :] = dh_ref[at, :] + nn(du, w1)

    chunk_of(rows_at(0), dy_ref.at[rows_at(0)])
    if talk:

        @pl.when(step == 0)
        def _():
            finish_slots()

    tick_at(0)
    for i in range(1, tiles):
        chunk_of(rows_at(i), dy_ref.at[rows_at(i)])

    @pl.when(step == 0)
    def _():
        if talk:
            for copy in final_copies():
                copy.wait_recv()
            os_ref[count:] = padded(go_land[...])
        else:
            os_ref[count:] = padded(go_in_ref[...])
        start(tail, extra, padded(gx_ref[...]), z_sum_ref)

    chunk_of(tail, z_sum_ref)
    tick_at(1)
    dw1 = tn(du_ref[...], h_ref[...])
    dw2 = nn(dft_ref[...], a_ref[...])
    if talk:
        for number in range(chunks):

            @pl.when(step == number)
            def _():
                for which, value in ((0, dw1), (1, dw2)):
                    unit = 2 * number + which
                    if unit >= slots:
                        engine.sent(unit - slots, 0)
                    put_unit(units_ref.at[unit % slots], value)

        @pl.when(step == chunks)
        def _():
            put_unit(second_ref.at[0], dw1)
            put_unit(second_ref.at[1], dw2)

        tick_at(2)
        for number in range(chunks):

            @pl.when(step == number)
            def _():
                engine.begin(2 * number)
                engine.begin(2 * number + 1)

    else:
        first_ref[...] = dw1.astype(bf16)
        second_ref[...] = dw2.astype(bf16)

    @pl.when(step == steps - 1)
    def _():
        db2_ref[...] = jnp.zeros_like(db2_ref)
        dgain_ref[...] = jnp.zeros_like(dgain_ref)
        doffset_ref[...] = jnp.zeros_like(doffset_ref)

        def finish(at, size, sums, put):
            z = sums[...].astype(bf16)
            unit, scale = normalize_rows(y_ref[at, :])
            dh = dh_ref[at, :]
            ct = cts_ref[at, :].astype(f32)
            dy = ct + norm_back(unit, scale, norms_ref[4:5], dh)
            db2_ref[...] += jnp.sum(ct, axis=0, keepdims=True)
            doffset_ref[...] += jnp.sum(dh, axis=0, keepdims=True)
            dgain_ref[...] += jnp.sum(dh * unit, axis=0, keepdims=True)
            low = dy.astype(bf16)
            h_ref[at, :] = low
            put(z, dy, nt(low, wo_ref[...]).astype(bf16))

        def finish_tile(i, carry):
            at = pl.ds(pl.multiple_of(i * tile, tile), tile)

            def put(z, dy, do):
                z_ref[at, :] = z
                dy_ref[at, :] = dy
                do_ref[at, :] = do

            finish(at, tile, dy_ref.at[at], put)
            return carry

        lax.fori_loop(0, tiles, finish_tile, 0)

        def put_tail(z, dy, do):
            gz_ref[...] = z[:own]
            gdy_ref[...] = dy[:own]
            gdo_ref[...] = do[:own]

        finish(tail, extra, z_sum_ref, put_tail)
        if talk:
            put_message()
        dwo = tn(h_ref[...], os_ref[...])
        if talk:
            put_grouped(dwo_ref, dwo)
            advance(TICKS * chunks)
            rest_ref[...] = landings[1][2 * chunks - 2 :]
            for when, chunk, stage in plan:
                for unit in (2 * chunk, 2 * chunk + 1):
                    if stage > 0 or unit + slots >= 2 * chunks:
                        engine.sent(unit, stage)
            slot_sum.sent(2)
            slot_sum.sent(3)
            for copy in final_copies():
                copy.wait_send()
        else:
            dwo_ref[...] = dwo.astype(bf16)


def branch(grid_of, x, o, ct, ct_head, gx, go, gstat, gct, wo, w1t, b1, w2, b2, norms):
    count, width = x.shape
    own = gx.shape[0]
    hidden = w2.shape[0]
    steps = hidden // FF_CHUNK
    total = count + -(-own // LANES) * LANES
    row = once((count, width))
    few = once((own, width))
    line = full((1, width))
    anywhere = pl.BlockSpec(memory_space=pl.ANY)
    scratch = []
    more = {}
    if grid_of is None:
        weight_spec = pl.BlockSpec((FF_CHUNK, width), lambda j: (j, 0))
        b1 = b1.reshape(steps, 1, FF_CHUNK)
        dw_shapes = [(hidden, width), (width, hidden)]
        dw_types = [bf16, bf16]
        dw_specs = [weight_spec, pl.BlockSpec((width, FF_CHUNK), lambda j: (0, j))]
        dwo_shape = (width, width)
    else:
        seq, batch = grid_of
        rows, lanes = width // seq, width // batch
        weight_spec = pl.BlockSpec((seq, 1, rows, width), lambda j: (0, j, 0, 0))
        w1t = w1t.reshape(seq, steps, rows, width)
        w2 = w2.reshape(seq, steps, rows, width)
        b1 = b1.reshape(seq, steps, rows).transpose(1, 0, 2).reshape(steps, 1, FF_CHUNK)
        units = 2 * (steps - 1)
        sums, stats = go.shape[2:], gstat.shape[2:]
        dw_shapes = [
            ((units - 2) * rows, lanes),
            (2, 2, 2, 2, 2, batch, rows, lanes),
            (own, width + LANES),
            (2, 2, 2, 2, rows, lanes),
        ]
        dw_types = [f32, bf16, bf16, bf16]
        dw_specs = [once(shape) for shape in dw_shapes]
        dwo_shape = (seq, batch, rows, lanes)
        dma = pltpu.SemaphoreType.DMA
        scratch = (
            [pltpu.VMEM((4,) + dw_shapes[1][1:], bf16)]
            + sum_scratch(units, rows, lanes, False)
            + [
                pltpu.VMEM(go.shape, bf16),
                pltpu.VMEM(gstat.shape, f32),
                pltpu.VMEM((2,) + sums, bf16),
                pltpu.VMEM(sums, bf16),
                pltpu.VMEM((2,) + stats, f32),
                pltpu.VMEM(stats, f32),
                pltpu.VMEM((GLOBALS, PAIRS // 2 * LANES), bf16),
                pltpu.VMEM((own, width), bf16),
                pltpu.VMEM((2,) + stats, f32),
                pltpu.VMEM((GLOBALS, LANES), f32),
                dma((5, 2)),
                dma((5, 2)),
            ]
        )
        more = {"collective_id": 3, "has_side_effects": True}
    out = pl.pallas_call(
        functools.partial(branch_kernel, BLOCK, grid_of is not None),
        grid=(steps,),
        in_specs=[
            row,
            anywhere,
            anywhere,
            anywhere,
            few,
            once(go.shape),
            once(gstat.shape),
            few,
            once((width, width)),
            weight_spec,
            pl.BlockSpec((1, 1, FF_CHUNK), lambda j: (j, 0, 0)),
            weight_spec,
            line,
            full(norms.shape),
        ],
        out_specs=[row, row, row, few, few, few]
        + [once(dwo_shape), pl.BlockSpec((1, 1, FF_CHUNK), lambda j: (j, 0, 0)), line, line, line]
        + dw_specs,
        out_shape=[
            jax.ShapeDtypeStruct((count, width), bf16),
            jax.ShapeDtypeStruct((count, width), f32),
            jax.ShapeDtypeStruct((count, width), bf16),
            jax.ShapeDtypeStruct((own, width), bf16),
            jax.ShapeDtypeStruct((own, width), f32),
            jax.ShapeDtypeStruct((own, width), bf16),
            jax.ShapeDtypeStruct(dwo_shape, bf16),
            jax.ShapeDtypeStruct((steps, 1, FF_CHUNK), f32),
            jax.ShapeDtypeStruct((1, width), f32),
            jax.ShapeDtypeStruct((1, width), f32),
            jax.ShapeDtypeStruct((1, width), f32),
        ]
        + [jax.ShapeDtypeStruct(shape, kind) for shape, kind in zip(dw_shapes, dw_types)],
        scratch_shapes=[
            pltpu.VMEM((total, width), bf16),
            pltpu.VMEM((total, width), bf16),
            pltpu.VMEM((total, width), f32),
            pltpu.VMEM((total, width), bf16),
            pltpu.VMEM((total - count, width), f32),
            pltpu.VMEM((total, width), f32),
            pltpu.VMEM((width, total), bf16),
            pltpu.VMEM((total, FF_CHUNK), bf16),
            pltpu.VMEM((total, FF_CHUNK), bf16),
            pltpu.SemaphoreType.DMA((3,)),
        ]
        + scratch,
        compiler_params=params(**more),
        cost_estimate=pl.CostEstimate(
            flops=6 * total * width * (2 * hidden + width),
            bytes_accessed=8 * width * hidden + 16 * total * width,
            transcendentals=2 * total * hidden,
        ),
        name="branch",
    )(x, o, ct, ct_head, gx, go, gstat, gct, wo, w1t, b1, w2, b2, norms)
    db1 = out[7].reshape(steps, FF_CHUNK)
    if grid_of is not None:
        db1 = db1.reshape(steps, seq, rows).transpose(1, 0, 2).reshape(-1, width)
    return [*out[:7], db1, *out[8:]]


def local_backward_kernel(
    talk,
    rows_count,
    group_rows,
    lengths,
    bucket_of,
    place,
    q_ref,
    k_ref,
    v_ref,
    do_ref,
    o_ref,
    line_ref,
    *refs,
):
    if talk:
        message_ref, rest_ref, last_ref, dwo_ref = refs[:4]
        refs = refs[4:]
    dq_ref, dk_ref, dv_ref, centre_ref = refs[:4]
    refs = refs[4:]
    if talk:
        everyone_ref, sums_ref, rest_out_ref = refs[:3]
        refs = refs[3:]
    edges, query_columns, key_columns = refs[:3]
    pair = pl.program_id(0)
    block = pl.program_id(1)
    blocks = rows_count // BLOCK
    step = pair * blocks + block

    @pl.when(step == 0)
    def _():
        read_edges(lengths, bucket_of, place, edges)

    if talk:
        all_ref, gather_send, gather_recv, own_ref = refs[3:7]
        landings = refs[7:12]
        send_sem, recv_sem, own_sem = refs[12:]
        bits, partners = my_place()
        gather = RowGather(all_ref, 3 * LANES, gather_send, gather_recv, bits, partners)
        engine = HalvingSum(
            (X_FIRST, Y_FIRST) * 2 + (X_FIRST,),
            [
                None,
                None,
                lambda side: last_ref.at[0, :, :, :, side],
                lambda side: last_ref.at[1, :, :, :, side],
                lambda side: dwo_ref.at[:, :, :, side],
            ],
            landings,
            own_ref,
            send_sem,
            recv_sem,
            own_sem,
            put_rows(sums_ref, landings[4].shape[1]),
            bits,
            partners,
        )
        plan = {
            3: [(2, 0), (3, 0), (4, 0)],
            4: [(0, 2), (1, 2)],
            7: [(0, 3), (1, 3)],
            11: [(0, 4), (1, 4), (2, 1), (3, 1), (4, 1)],
        }
        gather_plan = {3: 0, 6: 1, 9: 2, 11: 3}

        @pl.when(step == 0)
        def _():
            all_ref[bits["z1"], bits["z0"], bits["y"], bits["core"]] = message_ref[...]
            landings[1][:2] = rest_ref[...]
            meet([partners[name] for name in AXES])
            gather.begin()
            for unit in (0, 1):
                engine.copy(unit, 2).start()
            for unit in (2, 3, 4):
                engine.begin(unit)

        for number in range(PAIRS * blocks):
            if number in plan or number in gather_plan:

                @pl.when(step == number)
                def _():
                    if number in gather_plan:
                        gather.advance(gather_plan[number])
                    for unit, stage in plan.get(number, ()):
                        engine.advance(unit, stage, stop=unit > 1 and stage == 1)

    block_columns(
        place, edges, rows_count, group_rows, block, step, blocks, query_columns, key_columns
    )
    extra = query_columns[block]
    upstream = do_ref[...]
    product = upstream.astype(f32) * o_ref[...].astype(f32)
    first = product.astype(bf16)
    second = (product - first.astype(f32)).astype(bf16)
    head = jnp.where(iota((8, LANES), 1) // HEAD_DIM == iota((8, LANES), 0), 1.0, 0.0).astype(bf16)
    by_head = nt(head, first) + nt(head, second)
    centre = jnp.concatenate([by_head[0:1], by_head[1:2]], axis=1)
    centre_ref[0, 0] = jnp.broadcast_to(centre, (8, 2 * BLOCK))
    queries = stack_pair(q_ref[...])
    grads = stack_pair(upstream)
    keys = k_ref[...]
    score = nt(
        jnp.concatenate([keys, key_columns[block]], 1),
        jnp.concatenate([queries, jnp.concatenate([extra, extra], 0)], 1),
    )
    weights = jnp.exp(score - line_ref[0, 0, 0:1])
    along = nt(v_ref[...], grads) - centre
    score_grad = (weights * along).astype(bf16)
    dv_ref[...] = nn(weights.astype(bf16), grads).astype(bf16)
    dk_ref[...] = nn(score_grad, queries).astype(bf16)
    low, high = side_by_side(tn(keys, score_grad))
    dq_ref[:HEAD_DIM] = low.astype(bf16)
    dq_ref[HEAD_DIM:] = high.astype(bf16)

    if talk:

        @pl.when(step == PAIRS * blocks - 1)
        def _():
            everyone_ref[...] = all_ref[...].reshape(everyone_ref.shape)
            gather.end()
            rest_out_ref[...] = landings[1][2:]
            for entries in plan.values():
                for unit, stage in entries:
                    engine.sent(unit, stage)


def local_backward(
    talk, scalars, rows_count, group_rows, q, k, v, do, o, line, message, rest, last, dwo
):
    blocks = rows_count // BLOCK
    width = q.shape[1]
    block_spec = pl.BlockSpec((BLOCK, LANES), lambda p, b, *unused: (b, p))
    operands = [q, k, v, do, o, line]
    in_specs = [block_spec] * 5 + [line_spec()]
    out_specs = (
        [pl.BlockSpec((LANES, BLOCK), lambda p, b, *unused: (p, b))]
        + [block_spec] * 2
        + [line_spec()]
    )
    out_shape = [
        jax.ShapeDtypeStruct((width, rows_count), bf16),
        jax.ShapeDtypeStruct((rows_count, width), bf16),
        jax.ShapeDtypeStruct((rows_count, width), bf16),
        jax.ShapeDtypeStruct((PAIRS, blocks, 8, 2 * BLOCK), f32),
    ]
    scratch = column_scratch(blocks)
    more = {}
    if talk:
        own, wide = message.shape
        rows, lanes = last.shape[-2:]
        units = 5
        operands += [message, rest, last, dwo.reshape(last.shape[1:])]
        in_specs += [full(message.shape), once(rest.shape)]
        in_specs += [pl.BlockSpec(memory_space=pl.ANY)] * 2
        everyone = (16 * own, wide)
        rest_out = (units - 2,) + rest.shape[1:]
        out_specs += [once(everyone), once((2 * rows, lanes)), once(rest_out)]
        out_shape += [
            jax.ShapeDtypeStruct(everyone, bf16),
            jax.ShapeDtypeStruct((2 * rows, lanes), f32),
            jax.ShapeDtypeStruct(rest_out, bf16),
        ]
        dma = pltpu.SemaphoreType.DMA
        scratch += [pltpu.VMEM((2, 2, 2, 2, own, wide), bf16), dma((4, 2)), dma((4, 2))]
        scratch += sum_scratch(units, rows, lanes, True)
        more = {"collective_id": 4, "has_side_effects": True}
    return pl.pallas_call(
        functools.partial(local_backward_kernel, talk, rows_count, group_rows),
        grid_spec=pltpu.PrefetchScalarGridSpec(
            num_scalar_prefetch=3,
            grid=(PAIRS, blocks),
            in_specs=in_specs,
            out_specs=out_specs,
            scratch_shapes=scratch,
        ),
        out_shape=out_shape,
        compiler_params=params(**more),
        cost_estimate=pl.CostEstimate(
            flops=40 * rows_count * BLOCK * width,
            bytes_accessed=30 * rows_count * width,
            transcendentals=HEADS * rows_count * BLOCK,
        ),
        name="local_backward",
    )(*scalars, *operands)


def slot_backward_kernel(
    rows_count,
    group_rows,
    lengths,
    bucket_of,
    place,
    q_ref,
    k_ref,
    v_ref,
    do_ref,
    line_ref,
    centre_ref,
    dqt_ref,
    dk_in_ref,
    dv_in_ref,
    gq_ref,
    gk_ref,
    gv_ref,
    gdo_ref,
    gstat_ref,
    gx_ref,
    gh_ref,
    wq_ref,
    wk_ref,
    wv_ref,
    dq_ref,
    dk_ref,
    dv_ref,
    dw_ref,
    dgh_ref,
    dnorm_ref,
    edges,
    query_columns,
    key_columns,
    keys_ref,
    queries_ref,
    grads_ref,
    dqt_sum,
    dk_sum,
    dv_sum,
    dgqt_sum,
    dgk_sum,
    dgv_sum,
    lines_ref,
    dw_sum,
    dgh_sum,
):
    group = pl.program_id(0)
    block = pl.program_id(1)
    blocks = rows_count // BLOCK
    step = group * blocks + block
    together = range(TOGETHER)

    def lanes_of(which):
        return pl.ds(which * LANES, LANES)

    @pl.when(step == 0)
    def _():
        read_edges(lengths, bucket_of, place, edges)

        def turn(slot, carry):
            at = pl.ds(pl.multiple_of(slot * GLOBALS, GLOBALS), GLOBALS)
            lines_ref[slot] = gstat_ref[at, :].astype(f32).T
            return carry

        lax.fori_loop(0, SLOTS, turn, 0)
        dgh_sum[...] = jnp.zeros_like(dgh_sum)
        dnorm_ref[...] = jnp.zeros_like(dnorm_ref)

    @pl.when(block == 0)
    def _():
        dgqt_sum[...] = jnp.zeros_like(dgqt_sum)
        dgk_sum[...] = jnp.zeros_like(dgk_sum)
        dgv_sum[...] = jnp.zeros_like(dgv_sum)

    block_columns(
        place, edges, rows_count, group_rows, block, step, blocks, query_columns, key_columns
    )
    extra = query_columns[block]
    for which in together:
        lanes = lanes_of(which)
        keys_ref[which, :, :LANES] = k_ref[:, lanes]
        keys_ref[which, :, LANES:] = key_columns[block]
        queries_ref[which, :, :LANES] = stack_pair(q_ref[:, lanes])
        queries_ref[which, :BLOCK, LANES:] = extra
        queries_ref[which, BLOCK:, LANES:] = extra
        grads_ref[which] = stack_pair(do_ref[:, lanes])
    dqt_sum[...] = dqt_ref[...].astype(f32)
    dk_sum[...] = dk_in_ref[...].astype(f32)
    dv_sum[...] = dv_in_ref[...].astype(f32)

    def line_of(slot, which, first):
        halves = []
        for head in range(2):
            spot = first + 2 * (group * TOGETHER + which) + head
            halves.append(
                lines_ref[slot, pl.ds(spot, 1)]
                + lines_ref[slot, pl.ds(spot + HEADS, 1)]
                + lines_ref[slot, pl.ds(spot + 2 * HEADS, 1)]
            )
        return jnp.concatenate(halves, axis=1)

    def from_global(slot, which, keys, values):
        at = pl.ds(pl.multiple_of(slot * GLOBALS, GLOBALS), GLOBALS)
        extra = global_query_extra(slot).astype(bf16)
        queries = stack_pair(gq_ref[at, lanes_of(which)])
        grads = stack_pair(gdo_ref[at, lanes_of(which)])
        score = nt(keys, jnp.concatenate([queries, jnp.concatenate([extra, extra], 0)], 1))
        weights = jnp.exp(score - line_of(slot, which, 0))
        along = nt(values, grads) - line_of(slot, which, 3 * HEADS)
        score_grad = (weights * along).astype(bf16)
        low, high = side_by_side(tn(keys[:, :LANES], score_grad))
        dgqt_sum[which, slot, :HEAD_DIM] += low
        dgqt_sum[which, slot, HEAD_DIM:] += high
        return nn(score_grad, queries), nn(weights.astype(bf16), grads)

    def one_slot(slot, carry):
        @pl.when(slot_present(slot, place, edges, rows_count, group_rows, block))
        def _():
            at = pl.ds(pl.multiple_of(slot * GLOBALS, GLOBALS), GLOBALS)
            columns = global_key_extra(slot).astype(bf16)
            for which in together:
                lanes = lanes_of(which)
                key_grad, value_grad = from_global(slot, which, keys_ref[which], v_ref[:, lanes])
                dk_sum[:, lanes] += key_grad
                dv_sum[:, lanes] += value_grad
                keys = gk_ref[at, lanes]
                grads = grads_ref[which]
                score = nt(jnp.concatenate([keys, columns], 1), queries_ref[which])
                weights = jnp.exp(score - line_ref[which, 0, 0:1])
                along = nt(gv_ref[at, lanes], grads) - centre_ref[which, 0, 0:1]
                score_grad = (weights * along).astype(bf16)
                dgv_sum[at, lanes] += nn(weights.astype(bf16), grads)
                dgk_sum[at, lanes] += nn(score_grad, queries_ref[which, :, :LANES])
                low, high = side_by_side(tn(keys, score_grad))
                dqt_sum[pl.ds(which * LANES, HEAD_DIM)] += low
                dqt_sum[pl.ds(which * LANES + HEAD_DIM, HEAD_DIM)] += high

        return carry

    lax.fori_loop(0, SLOTS, one_slot, 0)
    dq_ref[...] = dqt_sum[...].T.astype(bf16)
    dk_ref[...] = dk_sum[...].astype(bf16)
    dv_ref[...] = dv_sum[...].astype(bf16)

    @pl.when((block == blocks - 1) & (place[2] >= 0))
    def _():
        slot = place[2]
        at = pl.ds(pl.multiple_of(slot * GLOBALS, GLOBALS), GLOBALS)
        columns = global_key_extra(slot).astype(bf16)
        for which in together:
            lanes = lanes_of(which)
            keys = jnp.concatenate([gk_ref[at, lanes], columns], axis=1)
            key_grad, value_grad = from_global(slot, which, keys, gv_ref[at, lanes])
            dgk_sum[at, lanes] += key_grad
            dgv_sum[at, lanes] += value_grad

    @pl.when(block == blocks - 1)
    def _():
        dw_sum[...] = jnp.zeros_like(dw_sum)

        def through(slot, carry):
            needed = slot == place[2]
            for number in range(blocks):
                needed = needed | slot_present(
                    slot, place, edges, rows_count, group_rows, number
                )

            @pl.when(needed)
            def _():
                at = pl.ds(pl.multiple_of(slot * GLOBALS, GLOBALS), GLOBALS)
                grads = (
                    (
                        jnp.concatenate([dgqt_sum[which, slot].T for which in together], 1)
                        * query_scale
                    ).astype(bf16),
                    dgk_sum[at, :].astype(bf16),
                    dgv_sum[at, :].astype(bf16),
                )
                rows = gh_ref[at, :]
                total = dgh_sum[at, :]
                for index, weight in enumerate((wq_ref, wk_ref, wv_ref)):
                    dw_sum[index] += tn(grads[index], rows)
                    total = total + nt(grads[index], weight[...])
                dgh_sum[at, :] = total

                @pl.when(group == PAIRS // TOGETHER - 1)
                def _():
                    unit, unused = normalize_rows(gx_ref[at, :].astype(f32))
                    dnorm_ref[0:1] += jnp.sum(total * unit, axis=0, keepdims=True)
                    dnorm_ref[1:2] += jnp.sum(total, axis=0, keepdims=True)

            return carry

        lax.fori_loop(0, SLOTS, through, 0)
        dw_ref[...] = dw_sum[...].astype(bf16)

    @pl.when(step == PAIRS // TOGETHER * blocks - 1)
    def _():
        dgh_ref[...] = dgh_sum[...].astype(bf16)


def slot_backward(
    scalars,
    rows_count,
    group_rows,
    q,
    k,
    v,
    do,
    line,
    centre,
    dqt,
    dk,
    dv,
    gq,
    gk,
    gv,
    everyone,
    gx,
    gh,
    wq,
    wk,
    wv,
):
    blocks = rows_count // BLOCK
    all_globals, width = gk.shape
    block_spec = pl.BlockSpec((BLOCK, TOGETHER * LANES), lambda p, b, *unused: (b, p))
    pair_spec = pl.BlockSpec((all_globals, TOGETHER * LANES), lambda p, b, *unused: (0, p))
    local = jax.ShapeDtypeStruct((rows_count, width), bf16)
    glob = jax.ShapeDtypeStruct((all_globals, width), bf16)
    return pl.pallas_call(
        functools.partial(slot_backward_kernel, rows_count, group_rows),
        grid_spec=pltpu.PrefetchScalarGridSpec(
            num_scalar_prefetch=3,
            grid=(PAIRS // TOGETHER, blocks),
            in_specs=[block_spec] * 4
            + [line_spec(TOGETHER)] * 2
            + [pl.BlockSpec((TOGETHER * LANES, BLOCK), lambda p, b, *unused: (p, b))]
            + [block_spec] * 2
            + [pair_spec] * 4
            + [pl.BlockSpec((all_globals, LANES), lambda p, b, *unused: (0, PAIRS))]
            + [once((all_globals, width))] * 2
            + [pl.BlockSpec((width, TOGETHER * LANES), lambda p, b, *unused: (0, p))] * 3,
            out_specs=[block_spec] * 3
            + [
                pl.BlockSpec((3, TOGETHER * LANES, width), lambda p, b, *unused: (0, p, 0)),
                once((all_globals, width)),
                full((8, width)),
            ],
            scratch_shapes=column_scratch(blocks)
            + [
                pltpu.VMEM((TOGETHER, BLOCK, 2 * LANES), bf16),
                pltpu.VMEM((TOGETHER, 2 * BLOCK, 2 * LANES), bf16),
                pltpu.VMEM((TOGETHER, 2 * BLOCK, LANES), bf16),
                pltpu.VMEM((TOGETHER * LANES, BLOCK), f32),
                pltpu.VMEM((BLOCK, TOGETHER * LANES), f32),
                pltpu.VMEM((BLOCK, TOGETHER * LANES), f32),
                pltpu.VMEM((TOGETHER, SLOTS, LANES, GLOBALS), f32),
                pltpu.VMEM((all_globals, TOGETHER * LANES), f32),
                pltpu.VMEM((all_globals, TOGETHER * LANES), f32),
                pltpu.VMEM((SLOTS, LANES, GLOBALS), f32),
                pltpu.VMEM((3, TOGETHER * LANES, width), f32),
                pltpu.VMEM((all_globals, width), f32),
            ],
        ),
        out_shape=[local] * 3
        + [
            jax.ShapeDtypeStruct((3, width, width), bf16),
            glob,
            jax.ShapeDtypeStruct((8, width), f32),
        ],
        compiler_params=params(),
        cost_estimate=pl.CostEstimate(
            flops=80 * rows_count * GLOBALS * width,
            bytes_accessed=40 * rows_count * width,
            transcendentals=2 * HEADS * rows_count * GLOBALS,
        ),
        name="slot_backward",
    )(
        *scalars,
        q,
        k,
        v,
        do,
        line,
        centre,
        dqt,
        dk,
        dv,
        gq,
        gk,
        gv,
        everyone,
        everyone,
        gx,
        gh,
        wq,
        wk,
        wv,
    )


def project_back_kernel(
    tile,
    x_ref,
    dy_ref,
    h_ref,
    dq_ref,
    dk_ref,
    dv_ref,
    dwg_ref,
    wq_ref,
    wk_ref,
    wv_ref,
    gain_ref,
    dx_ref,
    dw_ref,
    dnorm_ref,
):
    count, width = x_ref.shape
    dnorm_ref[...] = jnp.zeros_like(dnorm_ref)

    def one_tile(i, carry):
        at = pl.ds(pl.multiple_of(i * tile, tile), tile)
        dh = (
            nt(dq_ref[at, :], wq_ref[...]) * query_scale
            + nt(dk_ref[at, :], wk_ref[...])
            + nt(dv_ref[at, :], wv_ref[...])
        )
        unit, scale = normalize_rows(x_ref[at, :].astype(f32))
        dnorm_ref[0:1] += jnp.sum(dh * unit, axis=0, keepdims=True)
        dnorm_ref[1:2] += jnp.sum(dh, axis=0, keepdims=True)
        dx_ref[at, :] = dy_ref[at, :] + norm_back(unit, scale, gain_ref[...], dh)
        return carry

    lax.fori_loop(0, count // tile, one_tile, 0)
    for index, source in enumerate((dq_ref, dk_ref, dv_ref)):
        value = tn(source[...], h_ref[...])
        if index == 0:
            value = value * query_scale
        dw_ref[index] = (value + dwg_ref[index].astype(f32)).astype(bf16)


def project_back(x, dy, h, dq, dk, dv, dwg, wq, wk, wv, gain):
    count, width = x.shape
    vmem = pl.BlockSpec(memory_space=pltpu.VMEM)
    return pl.pallas_call(
        functools.partial(project_back_kernel, BLOCK),
        in_specs=[vmem] * 11,
        out_specs=[vmem] * 3,
        out_shape=[
            jax.ShapeDtypeStruct((count, width), f32),
            jax.ShapeDtypeStruct((3, width, width), bf16),
            jax.ShapeDtypeStruct((8, width), f32),
        ],
        compiler_params=params(),
        cost_estimate=pl.CostEstimate(
            flops=12 * count * width * width, bytes_accessed=30 * count * width, transcendentals=0
        ),
        name="project_back",
    )(x, dy, h, dq, dk, dv, dwg, wq, wk, wv, gain)


def finish_kernel(
    rest_ref,
    x_in,
    dy_in,
    h_in,
    dq_in,
    dk_in,
    dv_in,
    dwg_in,
    dgh_ref,
    z_in,
    wq_in,
    wk_in,
    wv_in,
    db1_ref,
    db2_ref,
    dnorm_global_ref,
    dgain2_ref,
    doffset2_ref,
    gx_ref,
    gdy_ref,
    norms_ref,
    out_ref,
    small_out_ref,
    grad_out_ref,
    token_ref,
    halo_dx_out,
    halo_z_out,
    x_ref,
    dy_ref,
    h_ref,
    dq_ref,
    dk_ref,
    dv_ref,
    dwg_ref,
    wq_ref,
    wk_ref,
    wv_ref,
    load_sem,
    units_ref,
    one_ref,
    two_ref,
    three_ref,
    four_ref,
    five_ref,
    send_sem,
    recv_sem,
    gown_ref,
    gone_ref,
    gtwo_ref,
    gthree_ref,
    gfour_ref,
    gsend_sem,
    grecv_sem,
    gown_sem,
    sums_ref,
    here_ref,
    ssend_sem,
    srecv_sem,
    halo_out,
    halo_dx,
    halo_z,
    halo_send,
    halo_recv,
    dnorm_ref,
    dgh_sum_ref,
):
    bits, partners = my_place()
    count, width = x_ref.shape
    came = rest_ref.shape[0]
    units = came + 3
    batch = lax.axis_index("batch")
    seq = lax.axis_index("seq")
    places = lax.axis_size("seq")
    after = (batch, lax.rem(seq + 1, places))
    before = (batch, lax.rem(seq + places - 1, places))

    pairs = [
        (dq_in, dq_ref),
        (h_in, h_ref),
        (dwg_in, dwg_ref),
        (dk_in, dk_ref),
        (dv_in, dv_ref),
        (wq_in, wq_ref),
        (wk_in, wk_ref),
        (wv_in, wv_ref),
        (x_in, x_ref),
        (dy_in, dy_ref),
    ]
    loads = [
        pltpu.make_async_copy(source, target, load_sem.at[number])
        for number, (source, target) in enumerate(pairs)
    ]
    for load in loads:
        load.start()

    def source(unit):
        return lambda side: units_ref.at[unit - came, :, :, :, side]

    engine = HalvingSum(
        (X_FIRST, Y_FIRST, X_FIRST, X_FIRST, Y_FIRST, Z_FIRST),
        [source(unit) for unit in range(units)],
        (one_ref, two_ref, three_ref, four_ref, five_ref),
        None,
        send_sem,
        recv_sem,
        None,
        put_rows(out_ref, five_ref.shape[1]),
        bits,
        partners,
    )
    wide = gone_ref.shape[-1]

    def row_source(unit):
        lanes = pl.ds(unit * wide, wide)
        return lambda side: dgh_ref.at[:, :, :, side, :, lanes]

    def put_dgh(unit, value):
        dgh_sum_ref[:, unit * wide : (unit + 1) * wide] = value

    row_sum = HalvingSum(
        (("core", "y", "z0", "z1"), ("core", "z0", "y", "z1")),
        [row_source(unit) for unit in range(2)],
        (gone_ref, gtwo_ref, gthree_ref, gfour_ref),
        gown_ref,
        gsend_sem,
        grecv_sem,
        gown_sem,
        put_dgh,
        bits,
        partners,
    )

    def rows_advance(stage):
        for unit in range(2):
            row_sum.advance(unit, stage)

    def scopy(stage):
        return remote(
            sums_ref.at[stage],
            here_ref.at[stage],
            ssend_sem.at[stage],
            srecv_sem.at[stage],
            partners[X_FIRST[stage]],
        )

    def small_advance(stage):
        scopy(stage).wait_recv()
        total = sums_ref[stage] + here_ref[stage]
        if stage < STAGES - 1:
            sums_ref[stage + 1] = total
            scopy(stage + 1).start()
        else:
            small_out_ref[...] = total

    halos = [
        remote(halo_out, halo_dx, halo_send.at[0], halo_recv.at[0], before),
        remote(
            z_in.at[pl.ds(0, HALF)], halo_z, halo_send.at[1], halo_recv.at[1], before
        ),
    ]
    two_ref[:came] = rest_ref[...]
    meet([partners[name] for name in AXES] + [before, after])
    for unit in range(came):
        engine.copy(unit, 2).start()
    for unit in range(2):
        row_sum.begin(unit)

    def weight_gradient(index, grads_ref):
        value = tn(grads_ref[...], h_ref[...])
        if index == 0:
            value = value * query_scale
        put_unit(units_ref.at[index], value + dwg_ref[index].astype(f32))
        engine.begin(came + index)

    for number in range(3):
        loads[number].wait()
    weight_gradient(0, dq_ref)
    rows_advance(0)
    loads[3].wait()
    weight_gradient(1, dk_ref)
    engine.advance(came, 0)
    loads[4].wait()
    weight_gradient(2, dv_ref)
    engine.advance(came + 1, 0)
    for unit in range(came):
        engine.advance(unit, 2)
    for number in range(5, 10):
        loads[number].wait()
    dnorm_ref[...] = jnp.zeros_like(dnorm_ref)

    def back(index):
        at = pl.ds(index * HALF, HALF)
        dh = (
            nt(dq_ref[at, :], wq_ref[...]) * query_scale
            + nt(dk_ref[at, :], wk_ref[...])
            + nt(dv_ref[at, :], wv_ref[...])
        )
        unit, scale = normalize_rows(x_ref[at, :].astype(f32))
        dnorm_ref[0:1] += jnp.sum(dh * unit, axis=0, keepdims=True)
        dnorm_ref[1:2] += jnp.sum(dh, axis=0, keepdims=True)
        dx = dy_ref[at, :] + norm_back(unit, scale, norms_ref[0:1], dh)
        if index == 0:
            halo_out[...] = dx.astype(bf16)
        else:
            token_ref[pl.ds((index - 1) * HALF, HALF), :] = dx

    for index in range(count // HALF):
        back(index)
        if index == 0:
            engine.advance(came + 2, 0)
            halos[0].start()
        if index == 1:
            rows_advance(1)
        if index == 2:
            for unit in range(came):
                engine.advance(unit, 3)

    hidden_rows = db1_ref.shape[0]
    parts = [
        db1_ref[...],
        db2_ref[...],
        dnorm_ref[0:2],
        dnorm_global_ref[0:2],
        dgain2_ref[...],
        doffset2_ref[...],
    ]
    filled = hidden_rows + 7
    parts.append(jnp.zeros((sums_ref.shape[1] - filled, width), f32))
    sums_ref[0] = jnp.concatenate(parts, 0)
    scopy(0).start()
    halos[1].start()
    rows_advance(2)
    for unit in range(came, units):
        engine.advance(unit, 1)
    small_advance(0)
    rows_advance(3)
    dgh = dgh_sum_ref[...]
    unit_rows, scale = normalize_rows(gx_ref[...].astype(f32))
    grad_out_ref[...] = gdy_ref[...] + norm_back(unit_rows, scale, norms_ref[2:3], dgh)
    small_advance(1)
    for unit in range(came):
        engine.advance(unit, 4)
    for unit in range(came, units):
        engine.advance(unit, 2)
    small_advance(2)
    for halo in halos:
        halo.wait_recv()
    halo_dx_out[...] = halo_dx[...]
    halo_z_out[...] = halo_z[...]
    for unit in range(came, units):
        engine.advance(unit, 3)
    small_advance(3)
    for unit in range(came, units):
        engine.advance(unit, 4)
    small_advance(4)

    for unit in range(units):
        for stage in range(2 if unit < came else 0, STAGES):
            engine.sent(unit, stage)
    for stage in range(STAGES):
        scopy(stage).wait_send()
    for unit in range(2):
        for stage in range(4):
            row_sum.sent(unit, stage)
    for halo in halos:
        halo.wait_send()


def finish_all(rest, x, dy, h, dq, dk, dv, dwg, dgh, z, wq, wk, wv, small, gx, gdy, norms):
    count, width = x.shape
    rows, lanes = rest.shape[-2:]
    units = rest.shape[0] + 3
    own = gx.shape[0]
    place = (2, 2, 2, 2)
    small_rows = small[0].shape[0] + 7
    small_rows += -small_rows % 8
    anywhere = pl.BlockSpec(memory_space=pl.ANY)
    vmem = pl.BlockSpec(memory_space=pltpu.VMEM)
    dma = pltpu.SemaphoreType.DMA
    row = pltpu.VMEM((count, width), bf16)
    weight = pltpu.VMEM((width, width), bf16)
    half = pltpu.VMEM((HALF, width), bf16)
    return pl.pallas_call(
        finish_kernel,
        in_specs=[vmem] + [anywhere] * 12 + [vmem] * 8,
        out_specs=[vmem] * 6,
        out_shape=[
            jax.ShapeDtypeStruct((units * rows, lanes), f32),
            jax.ShapeDtypeStruct((small_rows, width), f32),
            jax.ShapeDtypeStruct((own, width), f32),
            jax.ShapeDtypeStruct((count - HALF, width), f32),
            jax.ShapeDtypeStruct((HALF, width), bf16),
            jax.ShapeDtypeStruct((HALF, width), bf16),
        ],
        scratch_shapes=[
            row,
            pltpu.VMEM((count, width), f32),
            row,
            row,
            row,
            row,
            pltpu.VMEM((3, width, width), bf16),
            weight,
            weight,
            weight,
            dma((10,)),
            pltpu.VMEM((3, 2, 2, 2, 2, 2, rows, lanes), bf16),
        ]
        + sum_scratch(units, rows, lanes, False)
        + [
            pltpu.VMEM((2, 2, 2, 2, own, width // 2), bf16),
            pltpu.VMEM((2, 2, 2, 2, own, width // 2), bf16),
            pltpu.VMEM((2, 2, 2, own, width // 2), bf16),
            pltpu.VMEM((2, 2, own, width // 2), bf16),
            pltpu.VMEM((2, own, width // 2), bf16),
            dma((2, 4)),
            dma((2, 4)),
            dma((2,)),
            pltpu.VMEM((STAGES, small_rows, width), f32),
            pltpu.VMEM((STAGES, small_rows, width), f32),
            dma((STAGES,)),
            dma((STAGES,)),
            half,
            half,
            half,
            dma((2,)),
            dma((2,)),
            pltpu.VMEM((8, width), f32),
            pltpu.VMEM((own, width), f32),
        ],
        compiler_params=params(collective_id=0, has_side_effects=True),
        cost_estimate=pl.CostEstimate(
            flops=12 * count * width * width, bytes_accessed=30 * count * width, transcendentals=0
        ),
        name="finish_all",
    )(
        rest,
        x,
        dy,
        h,
        dq,
        dk,
        dv,
        dwg,
        dgh.reshape(place + (own, width)),
        z,
        wq,
        wk,
        wv,
        *small,
        gx,
        gdy,
        norms,
    )


def unpack_kernel(
    z_ref,
    halo_z_ref,
    dx_ref,
    halo_dx_ref,
    gz_ref,
    ggrad_ref,
    first_ref,
    second_ref,
    third_ref,
    small_ref,
    layer_ref,
    gz_out,
    token_ref,
    ggrad_out,
    wq_ref,
    wk_ref,
    wv_ref,
    wo_ref,
    w1_ref,
    w2_ref,
    b1_ref,
    b2_ref,
    norms_ref,
    turned_ref,
):
    step = pl.program_id(0)
    last = pl.num_programs(0) - 1

    @pl.when(step < last)
    def _():
        layer_ref[0] = z_ref[...]
        token_ref[0] = dx_ref[...]

    @pl.when(step == last)
    def _():
        layer_ref[0] = halo_z_ref[...]
        token_ref[0] = halo_dx_ref[...].astype(f32)

    rows = wq_ref.shape[0]

    @pl.when(step == 0)
    def _():
        gz_out[0] = gz_ref[...]
        ggrad_out[0] = ggrad_ref[...]
        for ref, unit in ((wo_ref, 2), (wq_ref, 3), (wk_ref, 4), (wv_ref, 5)):
            ref[...] = third_ref[unit * rows : (unit + 1) * rows]
        chunks = w1_ref.shape[0] // rows
        for chunk in range(chunks):
            for ref, unit in ((first_ref, chunk), (second_ref, chunk - 2), (third_ref, chunk - 3)):
                if 0 <= unit < ref.shape[0] // (2 * rows):
                    break
            start = 2 * unit * rows
            w1_ref[chunk * rows : (chunk + 1) * rows] = ref[start : start + rows]
            part = ref[start + rows : start + 2 * rows].T
            for place in range(part.shape[0] // rows):
                spot = (place * chunks + chunk) * rows
                turned_ref[spot : spot + rows, :] = part[place * rows : (place + 1) * rows, :]
        w2_ref[...] = turned_ref[...].T
        pieces_in_row = small_ref.shape[1] // LANES
        hidden_rows = b1_ref.shape[0] // pieces_in_row
        for row in range(hidden_rows + 1):
            for piece in range(pieces_in_row):
                value = small_ref[row : row + 1, piece * LANES : (piece + 1) * LANES]
                if row < hidden_rows:
                    b1_ref[row * pieces_in_row + piece : row * pieces_in_row + piece + 1] = value
                else:
                    b2_ref[piece : piece + 1] = value
        norms_ref[...] = small_ref[hidden_rows + 1 : hidden_rows + 7]


def unpack(z, halo_z, dx, halo_dx, gz, ggrad, first, second, third, small, rows, hidden):
    count, width = z.shape
    own = gz.shape[0]
    lanes = first.shape[1]
    steps = count // HALF
    shapes = [
        ((1, count, width), bf16),
        ((1, own, width), bf16),
        ((1, count, width), f32),
        ((1, own, width), f32),
    ]
    shapes += [((rows, lanes), f32)] * 4
    shapes += [
        ((hidden // width * rows, lanes), f32),
        ((rows, hidden // width * lanes), f32),
        ((hidden // LANES, LANES), f32),
        ((width // LANES, LANES), f32),
        ((6, width), f32),
    ]
    tile = pl.BlockSpec((1, HALF, width), lambda i: (0, i, 0))
    return pl.pallas_call(
        unpack_kernel,
        grid=(steps,),
        in_specs=[
            pl.BlockSpec((HALF, width), lambda i: (jnp.minimum(i + 1, steps - 1), 0)),
            full(halo_z.shape),
            pl.BlockSpec((HALF, width), lambda i: (jnp.minimum(i, steps - 2), 0)),
            full(halo_dx.shape),
            full(gz.shape),
            full(ggrad.shape),
            full(first.shape),
            full(second.shape),
            full(third.shape),
            full(small.shape),
        ],
        out_specs=[
            tile if shape[1] == count else full(shape) for shape, unused in shapes
        ],
        out_shape=[jax.ShapeDtypeStruct(shape, kind) for shape, kind in shapes],
        scratch_shapes=[pltpu.VMEM((hidden // width * lanes, rows), f32)],
        compiler_params=params(),
        cost_estimate=pl.CostEstimate(
            flops=0, bytes_accessed=14 * count * width, transcendentals=0
        ),
        name="unpack",
    )(z, halo_z, dx, halo_dx, gz, ggrad, first, second, third, small)


def from_behind(value, axis, steps):
    count = lax.axis_size(axis)
    pairs = [(source, (source + steps) % count) for source in range(count)]
    return lax.ppermute(value, axis, pairs)


def pieces(value):
    first = lax.reduce_precision(value, 8, 7)
    second = lax.reduce_precision(value - first, 8, 7)
    return [first.astype(bf16), second.astype(bf16), (value - first - second).astype(bf16)]


def scatter_sum(value):
    half = lax.psum_scatter(value, "batch", scatter_dimension=1, tiled=True)
    part = lax.psum_scatter(half, "seq", scatter_dimension=0, tiled=True)
    return part.T.astype(f32)


def on_device(
    tokens,
    global_states,
    lengths,
    bucket_of,
    wq,
    wk,
    wv,
    wo,
    w1,
    b1,
    w2,
    b2,
    norm_params,
    cotangent,
    global_cotangent,
):
    rows = tokens.shape[1]
    width = tokens.shape[2]
    own = global_states.shape[1]
    seq_count = lax.axis_size("seq")
    seq_place = lax.axis_index("seq")
    group_rows = rows * seq_count
    own_start = seq_place * own
    first_of_slot = own_start % GLOBALS == 0
    place = jnp.stack(
        [
            lax.axis_index("batch"),
            seq_place,
            jnp.where(first_of_slot, own_start // GLOBALS, -1),
        ]
    ).astype(jnp.int32)
    scalars = (lengths, bucket_of, place)
    norms = [norm_params[i : i + 1] for i in range(6)]
    b2_line = b2[None]

    batch_count = lax.axis_size("batch")
    grid_of = None
    if seq_count == 16 and batch_count == 2 and 2 * own == GLOBALS and rows == 2 * BLOCK:
        grid_of = (seq_count, batch_count)

    if grid_of is None:
        arrived_tokens, arrived_grads = from_behind(
            (tokens[0, rows - HALF :], cotangent[0, rows - HALF :]), "seq", 1
        )
        x = jnp.concatenate([arrived_tokens, tokens[0, : rows - HALF]], 0)
        ct_head = arrived_grads
        all_states = lax.all_gather(global_states[0], "seq", axis=0, tiled=True)
        w1t = w1.T
        h, q, k, v = project_local(x, norms[0], norms[1], wq, wk, wv)
        gh, gq, gk, gv = project_global(
            scalars, rows, group_rows, all_states, norms[2], norms[3], wq, wk, wv
        )
    else:
        h, q, k, v, x, all_states, gh, gq, gk, gv, w1t = gather_project(
            tokens[0], global_states[0], w1, norm_params, wq, wk, wv
        )
        all_states, gh, gq, gk, gv = (
            value.reshape(-1, width) for value in (all_states, gh, gq, gk, gv)
        )
    far, far_stat, part, part_stat = slot_forward(scalars, rows, group_rows, q, k, v, gq, gk, gv)
    if grid_of is None:
        o, line = local_forward(
            False, scalars, rows, group_rows, q, k, v, far, far_stat, None, None, None
        )
        part_peak = part_stat[:, :, 0:2]
        peak = jnp.max(lax.all_gather(part_peak, "seq"), axis=0)
        factor = jnp.exp(part_peak - peak)
        scaled = part.reshape(SLOTS, PAIRS, 2, HEAD_DIM, GLOBALS).astype(f32) * factor[:, :, :, None]
        scaled = scaled.reshape(SLOTS, width, GLOBALS)
        scaled_total = (part_stat[:, :, 2:4] * factor).reshape(SLOTS, HEADS, GLOBALS)
        payload = jnp.concatenate(
            [scaled, scaled_total, jnp.zeros((SLOTS, 4, GLOBALS), f32)], 1
        ).transpose(0, 2, 1)
        sums = lax.psum_scatter(
            payload.astype(bf16).reshape(SLOTS * GLOBALS, -1), "seq", scatter_dimension=0, tiled=True
        ).astype(f32)
        own_total = sums[:, width : width + HEADS]
        all_peak = peak.reshape(SLOTS, HEADS, GLOBALS).transpose(0, 2, 1).reshape(-1, HEADS)
        own_peak = lax.dynamic_slice_in_dim(all_peak, own_start, own, 0)
        go = (
            (sums[:, :width].reshape(own, HEADS, HEAD_DIM) / own_total[:, :, None])
            .reshape(own, width)
            .astype(bf16)
        )
        gstat = own_peak + jnp.log(own_total)
    else:
        o, line, half_sum, half_stat, ct_head = local_forward(
            True, scalars, rows, group_rows, q, k, v, far, far_stat, part, part_stat, cotangent[0]
        )

    z, dy, do, gz, gdy, gdo, dwo, db1, db2, dgain2, doffset2, *dws = branch(
        grid_of,
        x,
        o,
        cotangent[0],
        ct_head,
        global_states[0],
        go if grid_of is None else half_sum,
        gstat if grid_of is None else half_stat,
        global_cotangent[0],
        wo,
        w1t,
        b1,
        w2,
        b2_line,
        norm_params,
    )
    if grid_of is None:
        gcentre = jnp.sum(
            (gdo.astype(f32) * go.astype(f32)).reshape(own, HEADS, HEAD_DIM), axis=-1
        )
        message = jnp.concatenate(
            [gdo]
            + pieces(gstat)
            + pieces(gcentre)
            + [jnp.zeros((own, LANES - 6 * HEADS), bf16)],
            axis=1,
        )
        everyone = lax.all_gather(message, "seq", axis=0, tiled=True)
        dqt, dk, dv, centre = local_backward(
            False, scalars, rows, group_rows, q, k, v, do, o, line, None, None, None, None
        )
    else:
        sum_first, last, message, rest = dws
        dqt, dk, dv, centre, everyone, sum_second, rest = local_backward(
            True, scalars, rows, group_rows, q, k, v, do, o, line, message, rest, last, dwo
        )
    dq, dk, dv, dwg, dgh, dnorm_global = slot_backward(
        scalars,
        rows,
        group_rows,
        q,
        k,
        v,
        do,
        line,
        centre,
        dqt,
        dk,
        dv,
        gq,
        gk,
        gv,
        everyone,
        all_states,
        gh,
        wq,
        wk,
        wv,
    )
    if grid_of is None:
        dx, dqkv, dnorm = project_back(x, dy, h, dq, dk, dv, dwg, wq, wk, wv, norms[0])
        back_z, back_grad = from_behind((z[:HALF], dx[:HALF].astype(bf16)), "seq", -1)
        layer_out = jnp.concatenate([z[HALF:], back_z], 0)
        token_grad = jnp.concatenate([dx[HALF:], back_grad.astype(f32)], 0)
        small = jnp.concatenate([db1, db2, dnorm[:2], dnorm_global[:2], dgain2, doffset2], 0)
        dgh = lax.psum_scatter(dgh, "seq", scatter_dimension=0, tiled=True).astype(f32)
        gunit, gscale = normalize_rows(global_states[0].astype(f32))
        global_grad = gdy + norm_back(gunit, gscale, norms[2], dgh)
        small = lax.psum(small, ("batch", "seq"))
        dw1, dw2 = dws
        weights = [scatter_sum(value) for value in (dqkv[0], dqkv[1], dqkv[2], dwo, dw1, dw2)]
    else:
        sum_third, small, global_grad, dx, halo_dx, halo_z = finish_all(
            rest,
            x,
            dy,
            h,
            dq,
            dk,
            dv,
            dwg,
            dgh,
            z,
            wq,
            wk,
            wv,
            (db1, db2, dnorm_global, dgain2, doffset2),
            global_states[0],
            gdy,
            norm_params,
        )
        results = unpack(
            z,
            halo_z,
            dx,
            halo_dx,
            gz,
            global_grad,
            sum_first,
            sum_second,
            sum_third,
            small,
            width // seq_count,
            w1.shape[1],
        )
        weights = [value.T for value in results[4:10]]
        biases = [value.reshape(-1) for value in results[10:12]]
        return (*results[:4], *weights, *biases, results[12])
    hidden_rows = w1.shape[1] // width
    return (
        layer_out[None],
        gz[None],
        token_grad[None],
        global_grad[None],
        *weights,
        small[:hidden_rows].reshape(-1),
        small[hidden_rows],
        small[hidden_rows + 1 : hidden_rows + 7],
    )


def solution(mesh):
    split = P("batch", "seq", None)
    return jax.shard_map(
        on_device,
        mesh=mesh,
        in_specs=(split, split) + (P(),) * 11 + (split, split),
        out_specs=(split,) * 4 + (P("batch", "seq"),) * 6 + (P(),) * 3,
        check_vma=False,
    )
```

```python
import functools

import jax
import jax.numpy as jnp
from jax import lax
from jax.experimental import pallas as pl
from jax.experimental.pallas import tpu as pltpu
from jax.sharding import PartitionSpec as P

HEADS = 12
HEAD_DIM = 64
PAIRS = HEADS // 2
LANES = 128
BLOCK = 512
HALF = 256
GLOBALS = 128
SLOTS = 8
FF_CHUNK = 768
TOGETHER = 3

norm_eps = 1e-05
masked_score = -1e30
query_scale = 0.125

SLOT_LANE = 16
GLOBAL_LANE = 32

f32 = jnp.float32
bf16 = jnp.bfloat16
VMEM_LIMIT = 60 * 1024 * 1024


def nn(left, right):
    return jnp.dot(left, right, preferred_element_type=f32)


def nt(left, right):
    return lax.dot_general(left, right, (((1,), (1,)), ((), ())), preferred_element_type=f32)


def tn(left, right):
    return lax.dot_general(left, right, (((0,), (0,)), ((), ())), preferred_element_type=f32)


def iota(shape, dim):
    return lax.broadcasted_iota(jnp.int32, shape, dim)


def stack_pair(pair):
    lane = iota((1, LANES), 1)
    low = jnp.where(lane < HEAD_DIM, 1.0, 0.0).astype(bf16)
    high = jnp.where(lane < HEAD_DIM, 0.0, 1.0).astype(bf16)
    return jnp.concatenate([pair * low, pair * high], axis=0)


def read_edges(lengths, bucket_of, place, edges):
    bucket = bucket_of[place[0]]
    total = jnp.int32(0)
    edges[0] = total
    for slot in range(SLOTS):
        total = total + lengths[bucket, slot]
        edges[slot + 1] = total


def block_start(place, rows, block):
    return place[1] * rows + block * BLOCK - HALF


def slot_present(slot, place, edges, rows, group_rows, block):
    low = edges[slot]
    high = edges[slot + 1]
    found = jnp.bool_(False)
    for part in range(BLOCK // HALF):
        start = block_start(place, rows, block) + part * HALF
        start = jnp.where(start < 0, start + group_rows, start)
        found = found | ((high > low) & (low < start + HALF) & (high > start))
    return found


def row_numbers(place, edges, rows, group_rows, block):
    place_in = block_start(place, rows, block) + iota((BLOCK, LANES), 0)
    wrapped = place_in < 0
    token = jnp.where(wrapped, place_in + group_rows, place_in)
    slot = jnp.zeros((BLOCK, LANES), jnp.int32)
    for j in range(SLOTS):
        slot = slot + jnp.where(edges[j + 1] <= token, 1, 0)
    return slot, slot + jnp.where(wrapped, SLOTS, 0)


def key_extra(slot, segment):
    lane = iota((BLOCK, LANES), 1)
    extra = jnp.where((lane < SLOT_LANE) & (lane != segment), masked_score, 0.0)
    return jnp.where(lane == GLOBAL_LANE + slot, 1.0, extra)


def query_extra(slot, segment):
    lane = iota((BLOCK, LANES), 1)
    return jnp.where((lane == segment) | (lane == SLOT_LANE + slot), 1.0, 0.0)


def global_key_extra(slot):
    lane = iota((GLOBALS, LANES), 1)
    inside = (lane >= SLOT_LANE) & (lane < SLOT_LANE + SLOTS)
    extra = jnp.where(inside & (lane != SLOT_LANE + slot), masked_score, 0.0)
    return jnp.where(lane == GLOBAL_LANE + slot, 1.0, extra)


def global_query_extra(slot):
    lane = iota((GLOBALS, LANES), 1)
    inside = (lane >= GLOBAL_LANE) & (lane < GLOBAL_LANE + SLOTS)
    return jnp.where(inside & (lane != GLOBAL_LANE + slot), masked_score, 0.0)


def normalize_rows(values):
    mean = jnp.mean(values, axis=-1, keepdims=True)
    centered = values - mean
    variance = jnp.mean(centered * centered, axis=-1, keepdims=True)
    scale = lax.rsqrt(variance + norm_eps)
    return centered * scale, scale


def norm_back(unit, scale, gain, upstream):
    inner = upstream * gain
    along = jnp.mean(inner * unit, axis=-1, keepdims=True)
    return scale * (inner - jnp.mean(inner, axis=-1, keepdims=True) - unit * along)


def gelu_parts(value):
    decay = jnp.exp(-0.5 * value * value)
    step = 1.0 / (1.0 + (0.3275911 * 0.7071067811865476) * jnp.abs(value))
    series = 1.061405429 * step - 1.453152027
    series = series * step + 1.421413741
    series = series * step - 0.284496736
    series = series * step + 0.254829592
    tail = (0.5 * series) * step * decay
    area = jnp.where(value >= 0.0, 1.0 - tail, tail)
    return area, decay * 0.3989422804014327


def full(shape):
    return pl.BlockSpec(shape, lambda *unused: (0,) * len(shape))


def once(shape):
    return pl.BlockSpec(
        shape, lambda *unused: (0,) * len(shape), pipeline_mode=pl.Buffered(buffer_count=1)
    )


def params(**more):
    return pltpu.CompilerParams(vmem_limit_bytes=VMEM_LIMIT, **more)


STAGES = 5
MESH = pl.DeviceIdType.MESH
WEIGHTS = (("core", 1), ("y", 2), ("z0", 4), ("z1", 8))


def my_place():
    batch = lax.axis_index("batch")
    seq = lax.axis_index("seq")
    bits = {"x": batch}
    partners = {"x": (1 - batch, seq)}
    for name, weight in WEIGHTS:
        bits[name] = (seq // weight) % 2
        partners[name] = (batch, seq + weight - 2 * weight * bits[name])
    return bits, partners


def meet(devices):
    barrier = pltpu.get_barrier_semaphore()
    for device in devices:
        pl.semaphore_signal(barrier, inc=1, device_id=device, device_id_type=MESH)
    pl.semaphore_wait(barrier, len(devices))


def remote(source, target, send, recv, device):
    return pltpu.make_async_remote_copy(
        src_ref=source,
        dst_ref=target,
        send_sem=send,
        recv_sem=recv,
        device_id=device,
        device_id_type=MESH,
    )


class RowGather:
    def __init__(self, ref, cut, send_sem, recv_sem, bits, partners):
        self.ref = ref
        self.cut = cut
        self.send_sem = send_sem
        self.recv_sem = recv_sem
        self.bits = bits
        self.partners = partners

    def copies(self, number):
        core, y, z0, z1 = (self.bits[name] for name in ("core", "y", "z0", "z1"))
        ref = self.ref
        rows = pl.ds(0, ref.shape[4])
        left = pl.ds(0, self.cut)
        right = pl.ds(self.cut, ref.shape[5] - self.cut)
        if number == 0:
            moves = [
                (ref.at[z1, z0, y, core, rows, left], "z1"),
                (ref.at[z1, z0, y, core, rows, right], "z1"),
            ]
        elif number == 1:
            moves = [
                (ref.at[:, z0, y, core, rows, left], "z0"),
                (ref.at[:, z0, y, core, rows, right], "y"),
            ]
        elif number == 2:
            moves = [
                (ref.at[:, :, y, core, rows, left], "y"),
                (ref.at[:, z0, :, core, rows, right], "z0"),
            ]
        else:
            moves = [
                (ref.at[:, :, :, core, rows, left], "core"),
                (ref.at[:, :, :, core, rows, right], "core"),
            ]
        return [
            remote(
                part,
                part,
                self.send_sem.at[number, side],
                self.recv_sem.at[number, side],
                self.partners[name],
            )
            for side, (part, name) in enumerate(moves)
        ]

    def begin(self, number=0):
        for copy in self.copies(number):
            copy.start()

    def advance(self, number):
        for copy in self.copies(number):
            copy.wait_recv()
        if number < 3:
            self.begin(number + 1)

    def end(self, first=0):
        for number in range(first, 4):
            for copy in self.copies(number):
                copy.wait_send()


X_FIRST = ("core", "x", "y", "z0", "z1")
Y_FIRST = ("core", "y", "x", "z0", "z1")
X_Z_FIRST = ("core", "x", "z0", "y", "z1")
Z_FIRST = ("core", "z0", "x", "z1", "y")
AXES = ("z1", "z0", "y", "core", "x")


class HalvingSum:
    def __init__(
        self, orders, sources, landings, own, send_sem, recv_sem, own_sem, put, bits, partners
    ):
        self.orders = orders
        self.sources = sources
        self.landings = landings
        self.own = own
        self.send_sem = send_sem
        self.recv_sem = recv_sem
        self.own_sem = own_sem
        self.put = put
        self.bits = bits
        self.partners = partners

    def part(self, unit, stage, other):
        order = self.orders[unit]
        name = order[stage]
        side = 1 - self.bits[name] if other else self.bits[name]
        if stage == 0:
            if not other and self.own is not None:
                return self.own.at[unit]
            return self.sources[unit](side)
        left = [axis for axis in AXES if axis in order[stage:]]
        index = (slice(None),) * left.index(name) + (side,)
        return self.landings[stage - 1].at[unit].at[index]

    def copy(self, unit, stage):
        return remote(
            self.part(unit, stage, True),
            self.landings[stage].at[unit],
            self.send_sem.at[unit, stage],
            self.recv_sem.at[unit, stage],
            self.partners[self.orders[unit][stage]],
        )

    def own_copy(self, unit):
        return pltpu.make_async_copy(
            self.sources[unit](self.bits["core"]), self.own.at[unit], self.own_sem.at[unit]
        )

    def begin(self, unit):
        if self.own is not None:
            self.own_copy(unit).start()
        self.copy(unit, 0).start()

    def advance(self, unit, stage, stop=False):
        if stage == 0 and self.own is not None:
            self.own_copy(unit).wait()
        self.copy(unit, stage).wait_recv()
        landing = self.landings[stage].at[unit]
        kept = self.part(unit, stage, False)
        if stage < len(self.orders[unit]) - 1:
            add_into(landing, kept)
            if not stop:
                self.copy(unit, stage + 1).start()
        else:
            self.put(unit, landing[...].astype(f32) + kept[...].astype(f32))

    def sent(self, unit, stage):
        self.copy(unit, stage).wait_send()


def put_rows(ref, rows):
    def put(unit, value):
        ref[unit * rows : (unit + 1) * rows] = value

    return put


def add_into(target, more):
    def one(i, carry):
        target[i] = target[i] + more[i]
        return carry

    lax.fori_loop(0, target.shape[0], one, 0)


def sum_scratch(units, rows, lanes, with_own):
    piece = (rows, lanes)
    dma = pltpu.SemaphoreType.DMA
    shapes = [pltpu.VMEM((units, 2, 2, 2, 2) + piece, bf16)] if with_own else []
    shapes += [
        pltpu.VMEM((units, 2, 2, 2, 2) + piece, bf16),
        pltpu.VMEM((units, 2, 2, 2) + piece, bf16),
        pltpu.VMEM((units, 2, 2) + piece, bf16),
        pltpu.VMEM((units, 2) + piece, bf16),
        pltpu.VMEM((units,) + piece, bf16),
        dma((units, STAGES)),
        dma((units, STAGES)),
    ]
    return shapes + ([dma((units,))] if with_own else [])


def project_rows(rows_ref, gain_ref, offset_ref, wq_ref, wk_ref, wv_ref, outs):
    unit, unused = normalize_rows(rows_ref[...].astype(f32))
    normed = (unit * gain_ref[...] + offset_ref[...]).astype(bf16)
    outs[0][...] = normed
    outs[1][...] = (nn(normed, wq_ref[...]) * query_scale).astype(bf16)
    outs[2][...] = nn(normed, wk_ref[...]).astype(bf16)
    outs[3][...] = nn(normed, wv_ref[...]).astype(bf16)


def project_local_kernel(rows_ref, gain_ref, offset_ref, wq_ref, wk_ref, wv_ref, *outs):
    project_rows(rows_ref, gain_ref, offset_ref, wq_ref, wk_ref, wv_ref, outs)


def project_local(rows, gain, offset, wq, wk, wv):
    count, width = rows.shape
    tile = pl.BlockSpec((BLOCK, width), lambda i: (i, 0))
    return pl.pallas_call(
        project_local_kernel,
        grid=(count // BLOCK,),
        in_specs=[tile, full((1, width)), full((1, width))] + [once((width, width))] * 3,
        out_specs=[tile] * 4,
        out_shape=[jax.ShapeDtypeStruct((count, width), bf16)] * 4,
        compiler_params=params(),
        cost_estimate=pl.CostEstimate(
            flops=6 * count * width * width, bytes_accessed=12 * count * width, transcendentals=0
        ),
        name="project_local",
    )(rows, gain, offset, wq, wk, wv)


def gather_project_kernel(
    tokens_ref,
    states_ref,
    w1_ref,
    norms_ref,
    wq_in,
    wk_in,
    wv_in,
    h_out,
    q_out,
    k_out,
    v_out,
    x_out,
    all_out,
    gh_out,
    gq_out,
    gk_out,
    gv_out,
    w1t_out,
    wq_ref,
    wk_ref,
    wv_ref,
    x_ref,
    all_ref,
    local_ref,
    global_ref,
    w1s_ref,
    w1t_ref,
    halo_send,
    halo_recv,
    load_sem,
    store_sem,
    gstore_sem,
    more_sem,
    send_sem,
    recv_sem,
):
    bits, partners = my_place()
    batch = lax.axis_index("batch")
    seq = lax.axis_index("seq")
    places = lax.axis_size("seq")
    after = (batch, lax.rem(seq + 1, places))
    before = (batch, lax.rem(seq + places - 1, places))
    rows, width = tokens_ref.shape
    own = states_ref.shape[0]
    core, y, z0, z1 = (bits[name] for name in ("core", "y", "z0", "z1"))
    start = pl.ds(0, HALF)
    most = pl.ds(0, rows - HALF)
    end = pl.ds(rows - HALF, HALF)
    shifted = pl.ds(HALF, rows - HALF)
    loads = [
        pltpu.make_async_copy(source, target, load_sem.at[number])
        for number, (source, target) in enumerate(
            (
                (tokens_ref.at[most], x_ref.at[shifted]),
                (wq_in, wq_ref),
                (wk_in, wk_ref),
                (wv_in, wv_ref),
                (w1_ref, w1s_ref),
            )
        )
    ]
    for load in loads:
        load.start()
    all_ref[z1, z0, y, core] = states_ref[...]
    meet([partners[name] for name, unused in WEIGHTS] + [before, after])
    halo = remote(tokens_ref.at[end], x_ref.at[start], halo_send, halo_recv, after)
    gather = RowGather(all_ref, width // 2, send_sem, recv_sem, bits, partners)
    gather.begin()
    halo.start()

    outs = (h_out, q_out, k_out, v_out)

    def stores(index):
        at = pl.ds(index * HALF, HALF)
        return [
            pltpu.make_async_copy(local_ref.at[which, at], out.at[at], store_sem.at[which, index])
            for which, out in enumerate(outs)
        ]

    def project(index):
        at = pl.ds(index * HALF, HALF)
        project_rows(
            x_ref.at[at],
            norms_ref.at[0:1],
            norms_ref.at[1:2],
            wq_ref,
            wk_ref,
            wv_ref,
            [local_ref.at[which, at] for which in range(4)],
        )
        for store in stores(index):
            store.start()

    for number in range(4):
        loads[number].wait()
    tiles = rows // HALF
    def turn(i, carry):
        at = pl.ds(pl.multiple_of(i * HALF, HALF), HALF)
        w1t_ref[at, :] = w1s_ref[:, at].T
        return carry

    project(1)
    project(2)
    gather.advance(0)
    for index in range(3, tiles):
        project(index)
    loads[4].wait()
    turns = w1t_ref.shape[0] // HALF
    lax.fori_loop(0, turns // 2, turn, 0)
    gather.advance(1)
    lax.fori_loop(turns // 2, turns, turn, 0)
    w1t_store = pltpu.make_async_copy(w1t_ref, w1t_out, more_sem.at[1])
    w1t_store.start()
    gather.advance(2)

    gouts = (gh_out, gq_out, gk_out, gv_out)

    def gstores(first, side):
        return [
            pltpu.make_async_copy(
                global_ref.at[which, first, :, :, side],
                out.at[first, :, :, side],
                gstore_sem.at[which, first, number],
            )
            for which, out in enumerate(gouts)
            for number in ((0 if side is core else 1),)
        ]

    def project_states(side):
        for first in range(2):
            piece = all_ref[first, :, :, side].reshape(4 * own, width)
            unit, unused = normalize_rows(piece.astype(f32))
            normed = (unit * norms_ref[2:3] + norms_ref[3:4]).astype(bf16)
            values = (
                normed,
                (nn(normed, wq_ref[...]) * query_scale).astype(bf16),
                nn(normed, wk_ref[...]).astype(bf16),
                nn(normed, wv_ref[...]).astype(bf16),
            )
            for which, value in enumerate(values):
                global_ref[which, first, :, :, side] = value.reshape(2, 2, own, width)
            for store in gstores(first, side):
                store.start()

    other = 1 - core
    project_states(core)
    gather.advance(3)
    all_store = pltpu.make_async_copy(all_ref, all_out, more_sem.at[2])
    all_store.start()
    project_states(other)
    halo.wait_recv()
    x_store = pltpu.make_async_copy(x_ref, x_out, more_sem.at[0])
    x_store.start()
    project(0)

    for index in range(tiles):
        for store in stores(index):
            store.wait()
    for side in (core, other):
        for first in range(2):
            for store in gstores(first, side):
                store.wait()
    x_store.wait()
    w1t_store.wait()
    all_store.wait()
    halo.wait_send()
    gather.end()


def gather_project(tokens, states, w1, norms, wq, wk, wv):
    rows, width = tokens.shape
    own = states.shape[0]
    vmem = pl.BlockSpec(memory_space=pltpu.VMEM)
    anywhere = pl.BlockSpec(memory_space=pl.ANY)
    dma = pltpu.SemaphoreType.DMA
    local = jax.ShapeDtypeStruct((rows, width), bf16)
    glob = jax.ShapeDtypeStruct((2, 2, 2, 2, own, width), bf16)
    turned = (w1.shape[1], width)
    weight = pltpu.VMEM((width, width), bf16)
    return pl.pallas_call(
        gather_project_kernel,
        in_specs=[anywhere, vmem, anywhere, vmem] + [anywhere] * 3,
        out_specs=[anywhere] * 11,
        out_shape=[local] * 5 + [glob] * 5 + [jax.ShapeDtypeStruct(turned, bf16)],
        scratch_shapes=[
            weight,
            weight,
            weight,
            pltpu.VMEM((rows, width), bf16),
            pltpu.VMEM(glob.shape, bf16),
            pltpu.VMEM((4, rows, width), bf16),
            pltpu.VMEM((4,) + glob.shape, bf16),
            pltpu.VMEM(w1.shape, bf16),
            pltpu.VMEM(turned, bf16),
            dma,
            dma,
            dma((5,)),
            dma((4, rows // HALF)),
            dma((4, 2, 2)),
            dma((3,)),
            dma((4, 2)),
            dma((4, 2)),
        ],
        compiler_params=params(collective_id=1, has_side_effects=True),
        cost_estimate=pl.CostEstimate(
            flops=6 * (rows + 16 * own) * width * width,
            bytes_accessed=24 * rows * width,
            transcendentals=0,
        ),
        name="gather_project",
    )(tokens, states, w1, norms, wq, wk, wv)


def project_global_kernel(
    rows_count,
    group_rows,
    lengths,
    bucket_of,
    place,
    rows_ref,
    gain_ref,
    offset_ref,
    wq_ref,
    wk_ref,
    wv_ref,
    h_ref,
    q_ref,
    k_ref,
    v_ref,
    edges,
):
    slot = pl.program_id(0)

    @pl.when(slot == 0)
    def _():
        read_edges(lengths, bucket_of, place, edges)

    needed = slot == place[2]
    for block in range(rows_count // BLOCK):
        needed = needed | slot_present(slot, place, edges, rows_count, group_rows, block)

    @pl.when(needed)
    def _():
        project_rows(
            rows_ref, gain_ref, offset_ref, wq_ref, wk_ref, wv_ref, (h_ref, q_ref, k_ref, v_ref)
        )


def project_global(scalars, rows_count, group_rows, rows, gain, offset, wq, wk, wv):
    count, width = rows.shape
    tile = pl.BlockSpec((GLOBALS, width), lambda i, *unused: (i, 0))
    return pl.pallas_call(
        functools.partial(project_global_kernel, rows_count, group_rows),
        grid_spec=pltpu.PrefetchScalarGridSpec(
            num_scalar_prefetch=3,
            grid=(SLOTS,),
            in_specs=[tile, full((1, width)), full((1, width))] + [once((width, width))] * 3,
            out_specs=[tile] * 4,
            scratch_shapes=[pltpu.SMEM((16,), jnp.int32)],
        ),
        out_shape=[jax.ShapeDtypeStruct((count, width), bf16)] * 4,
        compiler_params=params(),
        cost_estimate=pl.CostEstimate(
            flops=6 * 256 * width * width, bytes_accessed=12 * count * width, transcendentals=0
        ),
        name="project_global",
    )(*scalars, rows, gain, offset, wq, wk, wv)


def block_columns(place, edges, rows, group_rows, block, step, blocks, query_columns, key_columns):
    @pl.when(step < blocks)
    def _():
        slot_of, segment = row_numbers(place, edges, rows, group_rows, block)
        query_columns[block] = query_extra(slot_of, segment).astype(bf16)
        key_columns[block] = key_extra(slot_of, segment).astype(bf16)


def slot_line(place, edges, rows, group_rows, block):
    token = block_start(place, rows, block) + iota((1, BLOCK), 1)
    token = jnp.where(token < 0, token + group_rows, token)
    slot = jnp.zeros((1, BLOCK), jnp.int32)
    for j in range(SLOTS):
        slot = slot + jnp.where(edges[j + 1] <= token, 1, 0)
    return slot


def side_by_side(stacked):
    return stacked[:HEAD_DIM, : stacked.shape[1] // 2], stacked[HEAD_DIM:, stacked.shape[1] // 2 :]


def slot_forward_kernel(
    rows_count,
    group_rows,
    lengths,
    bucket_of,
    place,
    q_ref,
    k_ref,
    v_ref,
    gq_ref,
    gk_ref,
    gv_ref,
    far_ref,
    far_stat_ref,
    part_ref,
    part_stat_ref,
    edges,
    query_columns,
    key_columns,
    keys_ref,
    queries_ref,
    sum_ref,
    far_sum,
):
    group = pl.program_id(0)
    block = pl.program_id(1)
    blocks = rows_count // BLOCK
    step = group * blocks + block
    together = range(TOGETHER)

    @pl.when(step == 0)
    def _():
        read_edges(lengths, bucket_of, place, edges)

    @pl.when(block == 0)
    def _():
        sum_ref[...] = jnp.zeros_like(sum_ref)
        part_stat_ref[...] = jnp.broadcast_to(
            jnp.where(iota((8, GLOBALS), 0) < 2, masked_score, 0.0), part_stat_ref.shape
        )

    block_columns(
        place, edges, rows_count, group_rows, block, step, blocks, query_columns, key_columns
    )
    extra = query_columns[block]
    for which in together:
        lanes = pl.ds(which * LANES, LANES)
        keys_ref[which, :, :LANES] = k_ref[:, lanes]
        keys_ref[which, :, LANES:] = key_columns[block]
        queries_ref[which, :, :LANES] = stack_pair(q_ref[:, lanes])
        queries_ref[which, :BLOCK, LANES:] = extra
        queries_ref[which, BLOCK:, LANES:] = extra
    line = slot_line(place, edges, rows_count, group_rows, block)
    both_lines = jnp.concatenate([line, line], 1)

    def add(slot, keys_of, values_of):
        at = pl.ds(pl.multiple_of(slot * GLOBALS, GLOBALS), GLOBALS)
        extra = global_query_extra(slot).astype(bf16)
        for which in together:
            lanes = pl.ds(which * LANES, LANES)
            queries = jnp.concatenate(
                [stack_pair(gq_ref[at, lanes]), jnp.concatenate([extra, extra], 0)], axis=1
            )
            score = nt(keys_of(which), queries)
            stat = part_stat_ref[slot, which]
            old = jnp.concatenate([stat[0:1], stat[1:2]], axis=1)
            peak = jnp.maximum(old, jnp.max(score, axis=0, keepdims=True))
            weights = jnp.exp(score - peak)
            keep = jnp.exp(old - peak)
            total = jnp.concatenate([stat[2:3], stat[3:4]], axis=1) * keep + jnp.sum(
                weights, axis=0, keepdims=True
            )
            part_stat_ref[slot, which] = jnp.concatenate(
                [
                    peak[:, :GLOBALS],
                    peak[:, GLOBALS:],
                    total[:, :GLOBALS],
                    total[:, GLOBALS:],
                    jnp.zeros((4, GLOBALS), f32),
                ],
                axis=0,
            )
            low, high = side_by_side(tn(values_of(which), weights.astype(bf16)))
            sums = sum_ref.at[which, slot]
            sums[:HEAD_DIM] = sums[:HEAD_DIM] * keep[:, :GLOBALS] + low
            sums[HEAD_DIM:] = sums[HEAD_DIM:] * keep[:, GLOBALS:] + high

    far_sum[...] = jnp.zeros_like(far_sum)
    far_stat_ref[...] = jnp.zeros_like(far_stat_ref)

    def one_slot(slot, carry):
        @pl.when(slot_present(slot, place, edges, rows_count, group_rows, block))
        def _():
            add(
                slot,
                lambda which: keys_ref[which],
                lambda which: v_ref[:, pl.ds(which * LANES, LANES)],
            )
            at = pl.ds(pl.multiple_of(slot * GLOBALS, GLOBALS), GLOBALS)
            columns = global_key_extra(slot).astype(bf16)
            mine = both_lines == slot
            here = line == slot
            for which in together:
                lanes = pl.ds(which * LANES, LANES)
                slot_keys = jnp.concatenate([gk_ref[at, lanes], columns], 1)
                score = nt(slot_keys, queries_ref[which])
                peak = jnp.max(score, axis=0, keepdims=True)
                weights = jnp.exp(score - peak)
                total = jnp.sum(weights, axis=0, keepdims=True)
                stat = far_stat_ref.at[which, 0]
                stat[0:1] = jnp.where(mine, peak, stat[0:1])
                stat[1:2] = jnp.where(mine, total, stat[1:2])
                low, high = side_by_side(tn(gv_ref[at, lanes], weights.astype(bf16)))
                first = pl.ds(which * LANES, HEAD_DIM)
                second = pl.ds(which * LANES + HEAD_DIM, HEAD_DIM)
                far_sum[first] = jnp.where(here, low, far_sum[first])
                far_sum[second] = jnp.where(here, high, far_sum[second])

        return carry

    lax.fori_loop(0, SLOTS, one_slot, 0)
    far_ref[...] = far_sum[...].astype(bf16)

    @pl.when((block == blocks - 1) & (place[2] >= 0))
    def _():
        slot = place[2]
        at = pl.ds(pl.multiple_of(slot * GLOBALS, GLOBALS), GLOBALS)
        columns = global_key_extra(slot).astype(bf16)
        add(
            slot,
            lambda which: jnp.concatenate(
                [gk_ref[at, pl.ds(which * LANES, LANES)], columns], axis=1
            ),
            lambda which: gv_ref[at, pl.ds(which * LANES, LANES)],
        )

    @pl.when(block == blocks - 1)
    def _():
        for which in together:
            part_ref[:, which] = sum_ref[which].astype(bf16)


def line_spec(pairs=1):
    return pl.BlockSpec((pairs, 1, 8, 2 * BLOCK), lambda p, b, *unused: (p, b, 0, 0))


def column_scratch(blocks):
    return [pltpu.SMEM((16,), jnp.int32)] + [pltpu.VMEM((blocks, BLOCK, LANES), bf16)] * 2


def slot_forward(scalars, rows_count, group_rows, q, k, v, gq, gk, gv):
    blocks = rows_count // BLOCK
    all_globals, width = gq.shape
    block_spec = pl.BlockSpec((BLOCK, TOGETHER * LANES), lambda p, b, *unused: (b, p))
    pair_spec = pl.BlockSpec((all_globals, TOGETHER * LANES), lambda p, b, *unused: (0, p))
    return pl.pallas_call(
        functools.partial(slot_forward_kernel, rows_count, group_rows),
        grid_spec=pltpu.PrefetchScalarGridSpec(
            num_scalar_prefetch=3,
            grid=(PAIRS // TOGETHER, blocks),
            in_specs=[block_spec] * 3 + [pair_spec] * 3,
            out_specs=[
                pl.BlockSpec((TOGETHER * LANES, BLOCK), lambda p, b, *unused: (p, b)),
                line_spec(TOGETHER),
                pl.BlockSpec((SLOTS, TOGETHER, LANES, GLOBALS), lambda p, b, *unused: (0, p, 0, 0)),
                pl.BlockSpec((SLOTS, TOGETHER, 8, GLOBALS), lambda p, b, *unused: (0, p, 0, 0)),
            ],
            scratch_shapes=column_scratch(blocks)
            + [
                pltpu.VMEM((TOGETHER, BLOCK, 2 * LANES), bf16),
                pltpu.VMEM((TOGETHER, 2 * BLOCK, 2 * LANES), bf16),
                pltpu.VMEM((TOGETHER, SLOTS, LANES, GLOBALS), f32),
                pltpu.VMEM((TOGETHER * LANES, BLOCK), f32),
            ],
        ),
        out_shape=[
            jax.ShapeDtypeStruct((width, rows_count), bf16),
            jax.ShapeDtypeStruct((PAIRS, blocks, 8, 2 * BLOCK), f32),
            jax.ShapeDtypeStruct((SLOTS, PAIRS, LANES, GLOBALS), bf16),
            jax.ShapeDtypeStruct((SLOTS, PAIRS, 8, GLOBALS), f32),
        ],
        compiler_params=params(),
        cost_estimate=pl.CostEstimate(
            flops=8 * 4 * rows_count * GLOBALS * width,
            bytes_accessed=20 * all_globals * width,
            transcendentals=2 * HEADS * rows_count * GLOBALS,
        ),
        name="slot_forward",
    )(*scalars, q, k, v, gq, gk, gv)


def merge_parts(stat, sums, more_stat, more_sums):
    peak = jnp.maximum(stat[0:2], more_stat[0:2])
    keep = jnp.exp(stat[0:2] - peak)
    take = jnp.exp(more_stat[0:2] - peak)
    total = stat[2:4] * keep + more_stat[2:4] * take
    low = sums[:HEAD_DIM].astype(f32) * keep[0:1] + more_sums[:HEAD_DIM].astype(f32) * take[0:1]
    high = sums[HEAD_DIM:].astype(f32) * keep[1:2] + more_sums[HEAD_DIM:].astype(f32) * take[1:2]
    return (
        jnp.concatenate([peak, total, jnp.zeros((4, GLOBALS), f32)], 0),
        jnp.concatenate([low, high], 0),
    )


class SlotSum:
    ORDER = ("core", "y", "z0", "z1")

    def __init__(self, source, sums, stats, send_sem, recv_sem, bits, partners):
        self.source = source
        self.sums = sums
        self.stats = stats
        self.send_sem = send_sem
        self.recv_sem = recv_sem
        self.bits = bits
        self.partners = partners

    def held(self, stage, other):
        bit = self.bits[self.ORDER[stage]]
        side = 1 - bit if other else bit
        if stage == 0:
            return self.source(side)
        index = ((), (slice(None), slice(None)), (slice(None),), ())[stage] + (side,)
        return self.sums[stage - 1].at[index], self.stats[stage - 1].at[index]

    def copies(self, stage):
        partner = self.partners[self.ORDER[stage]]
        sums, stat = self.held(stage, True)
        return (
            remote(
                sums,
                self.sums[stage],
                self.send_sem.at[stage, 0],
                self.recv_sem.at[stage, 0],
                partner,
            ),
            remote(
                stat,
                self.stats[stage],
                self.send_sem.at[stage, 1],
                self.recv_sem.at[stage, 1],
                partner,
            ),
        )

    def begin(self, stage):
        for copy in self.copies(stage):
            copy.start()

    def merge(self, stage, kept=None):
        for copy in self.copies(stage):
            copy.wait_recv()
        sums, stat = self.held(stage, False) if kept is None else kept
        lead = self.sums[stage].shape[:-3]
        total = 1
        for size in lead:
            total = total * size

        def one(number, carry):
            index = []
            left = number
            for size in reversed(lead):
                index.append(left % size)
                left = left // size
            index = tuple(reversed(index))
            for which in range(PAIRS // 2):
                spot = index + (which,)
                new_stat, new_sums = merge_parts(
                    self.stats[stage][spot], self.sums[stage][spot], stat[spot], sums[spot]
                )
                self.stats[stage][spot] = new_stat
                self.sums[stage][spot] = new_sums.astype(bf16)
            return carry

        lax.fori_loop(0, total, one, 0)

    def sent(self, stage):
        for copy in self.copies(stage):
            copy.wait_send()


def local_forward_kernel(
    talk,
    rows_count,
    group_rows,
    lengths,
    bucket_of,
    place,
    q_ref,
    k_ref,
    v_ref,
    far_ref,
    far_stat_ref,
    *refs,
):
    if talk:
        part_ref, part_stat_ref = refs[:2]
        o_ref, line_ref, half_ref, half_stat_ref = refs[2:6]
        own_ref, own_stat_ref = refs[6:8]
        sums_refs = refs[8:10]
        stat_refs = refs[10:12]
        edges, query_columns, key_columns, send_sem, recv_sem, own_sem = refs[12:]
    else:
        o_ref, line_ref, edges, query_columns, key_columns = refs
    pair = pl.program_id(0)
    block = pl.program_id(1)
    blocks = rows_count // BLOCK
    step = pair * blocks + block

    @pl.when(step == 0)
    def _():
        read_edges(lengths, bucket_of, place, edges)

    if talk:
        bits, partners = my_place()
        slot_sum = SlotSum(
            lambda side: (part_ref.at[:, :, :, side], part_stat_ref.at[:, :, :, side]),
            sums_refs,
            stat_refs,
            send_sem,
            recv_sem,
            bits,
            partners,
        )
        own_parts = slot_sum.held(0, False)
        own_copies = [
            pltpu.make_async_copy(own_parts[0], own_ref, own_sem.at[0]),
            pltpu.make_async_copy(own_parts[1], own_stat_ref, own_sem.at[1]),
        ]

        @pl.when(step == 0)
        def _():
            meet([partners["core"], partners["y"]])
            for copy in own_copies:
                copy.start()
            slot_sum.begin(0)

        @pl.when(step == 3)
        def _():
            for copy in own_copies:
                copy.wait()
            slot_sum.merge(0, (own_ref, own_stat_ref))
            slot_sum.begin(1)

        @pl.when(step == PAIRS * blocks - 1)
        def _():
            slot_sum.merge(1)
            half_ref[...] = sums_refs[1][...]
            half_stat_ref[...] = stat_refs[1][...]
            slot_sum.sent(0)
            slot_sum.sent(1)

    block_columns(
        place, edges, rows_count, group_rows, block, step, blocks, query_columns, key_columns
    )
    extra = query_columns[block]
    queries = jnp.concatenate(
        [stack_pair(q_ref[...]), jnp.concatenate([extra, extra], 0)], axis=1
    )
    keys = jnp.concatenate([k_ref[...], key_columns[block]], axis=1)
    score = nt(keys, queries)
    far_peak = far_stat_ref[0, 0, 0:1]
    peak = jnp.maximum(jnp.max(score, axis=0, keepdims=True), far_peak)
    weights = jnp.exp(score - peak)
    far_keep = jnp.exp(far_peak - peak)
    total = jnp.sum(weights, axis=0, keepdims=True) + far_stat_ref[0, 0, 1:2] * far_keep
    low, high = side_by_side(tn(v_ref[...], weights.astype(bf16)))
    low = (low + far_ref[:HEAD_DIM] * far_keep[:, :BLOCK]) / total[:, :BLOCK]
    high = (high + far_ref[HEAD_DIM:] * far_keep[:, BLOCK:]) / total[:, BLOCK:]
    o_ref[...] = jnp.concatenate([low, high], 0).T.astype(bf16)
    line_ref[0, 0] = jnp.broadcast_to(peak + jnp.log(total), (8, 2 * BLOCK))


def local_forward(
    talk, scalars, rows_count, group_rows, q, k, v, far, far_stat, part, part_stat
):
    blocks = rows_count // BLOCK
    width = q.shape[1]
    block_spec = pl.BlockSpec((BLOCK, LANES), lambda p, b, *unused: (b, p))
    operands = [q, k, v, far, far_stat]
    in_specs = [block_spec] * 3 + [
        pl.BlockSpec((LANES, BLOCK), lambda p, b, *unused: (p, b)),
        line_spec(),
    ]
    out_specs = [block_spec, line_spec()]
    out_shape = [
        jax.ShapeDtypeStruct((rows_count, width), bf16),
        jax.ShapeDtypeStruct((PAIRS, blocks, 8, 2 * BLOCK), f32),
    ]
    scratch = []
    more = {}
    edges = column_scratch(blocks)
    if talk:
        cut = (2, 2, 2, 2, PAIRS // 2)
        operands += [
            part.reshape(cut + part.shape[2:]),
            part_stat.reshape(cut + part_stat.shape[2:]),
        ]
        in_specs += [pl.BlockSpec(memory_space=pl.ANY)] * 2
        shapes = [
            (2, 2, PAIRS // 2, LANES, GLOBALS),
            (2, 2, PAIRS // 2, 8, GLOBALS),
        ]
        out_specs += [full(shape) for shape in shapes]
        out_shape += [
            jax.ShapeDtypeStruct(shapes[0], bf16),
            jax.ShapeDtypeStruct(shapes[1], f32),
        ]
        leads = [(2, 2, 2), (2, 2, 2), (2, 2)]
        sums = [pltpu.VMEM(lead + shapes[0][2:], bf16) for lead in leads]
        stats = [pltpu.VMEM(lead + shapes[1][2:], f32) for lead in leads]
        dma = pltpu.SemaphoreType.DMA
        scratch = [sums[0], stats[0]] + sums[1:] + stats[1:]
        edges += [dma((2, 2)), dma((2, 2)), dma((2,))]
        more = {"collective_id": 2, "has_side_effects": True}
    return pl.pallas_call(
        functools.partial(local_forward_kernel, talk, rows_count, group_rows),
        grid_spec=pltpu.PrefetchScalarGridSpec(
            num_scalar_prefetch=3,
            grid=(PAIRS, blocks),
            in_specs=in_specs,
            out_specs=out_specs,
            scratch_shapes=scratch + edges,
        ),
        out_shape=out_shape,
        compiler_params=params(**more),
        cost_estimate=pl.CostEstimate(
            flops=16 * rows_count * BLOCK * width,
            bytes_accessed=16 * rows_count * width,
            transcendentals=HEADS * rows_count * BLOCK,
        ),
        name="local_forward",
    )(*scalars, *operands)


def put_grouped(ref, value):
    seq, batch, rows, lanes = ref.shape
    for part in range(batch):
        piece = value[:, part * lanes : (part + 1) * lanes].astype(bf16)
        ref[:, part] = piece.reshape(seq, rows, lanes)


def put_unit(ref, value):
    batch, rows, lanes = ref.shape[4:]
    for part in range(batch):
        piece = value[:, part * lanes : (part + 1) * lanes].astype(bf16)
        ref[:, :, :, :, part] = piece.reshape(ref.shape[:4] + (rows, lanes))


TICKS = 3
ENDINGS = ((0, 2, 4, 6, 8), (3, 5, 7, 9, 10), (6, 8))


def branch_kernel(
    tile,
    talk,
    x_ref,
    o_ref,
    ct_ref,
    ct_head_ref,
    gx_ref,
    go_in_ref,
    gstat_in_ref,
    gct_ref,
    wo_ref,
    w1_ref,
    b1_ref,
    w2_ref,
    b2_ref,
    norms_ref,
    z_ref,
    dy_ref,
    do_ref,
    gz_ref,
    gdy_ref,
    gdo_ref,
    dwo_ref,
    db1_ref,
    db2_ref,
    dgain_ref,
    doffset_ref,
    first_ref,
    second_ref,
    *refs,
):
    if talk:
        message_ref, rest_ref = refs[:2]
        refs = refs[2:]
    os_ref, cts_ref, y_ref, h_ref, z_sum_ref, dh_ref, dft_ref, a_ref, du_ref, load_sem = refs[:10]
    refs = refs[10:]
    step = pl.program_id(0)
    steps = pl.num_programs(0)
    count, width = x_ref.shape
    own = gx_ref.shape[0]
    extra = os_ref.shape[0] - count
    tiles = count // tile
    tail = pl.ds(count, extra)

    def rows_at(i):
        return pl.ds(i * tile, tile)

    def padded(value):
        return jnp.concatenate([value, jnp.zeros((extra - own, width), value.dtype)], axis=0)

    if talk:
        units_ref = refs[0]
        landings = refs[1:6]
        send_sem, recv_sem = refs[6:8]
        half_ref, half_stat_ref = refs[8:10]
        slot_sums = refs[10:12]
        slot_stats = refs[12:14]
        turned_ref, go_land, gstat_land, stat_ref, slot_send, slot_recv = refs[14:20]
        message_land, message_send, message_recv, halo_send, halo_recv = refs[20:]
        last_step = 4
        bits, partners = my_place()
        core = bits["core"]
        chunks = last_step - 1
        slots = units_ref.shape[0]
        plan = [
            (tick, chunk, stage)
            for chunk, ticks in enumerate(ENDINGS)
            for stage, tick in enumerate(ticks)
        ]

        def source(unit):
            return lambda side: units_ref.at[unit % slots, :, :, :, side]

        engine = HalvingSum(
            (X_FIRST, Y_FIRST) * chunks,
            [source(unit) for unit in range(2 * chunks)],
            landings,
            None,
            send_sem,
            recv_sem,
            None,
            put_rows(first_ref, landings[4].shape[1]),
            bits,
            partners,
        )

        def advance(tick):
            for when, chunk, stage in sorted(plan, key=lambda entry: -entry[2]):
                if when == tick:
                    for unit in (2 * chunk, 2 * chunk + 1):
                        engine.advance(unit, stage, stop=chunk == chunks - 1 and stage == 1)

        def tick_at(position):
            for number in range(1, last_step):
                tick = TICKS * (number - 1) + position

                @pl.when(step == number)
                def _():
                    advance(tick)

        slot_sum = SlotSum(
            None,
            (None, half_ref) + tuple(slot_sums),
            (None, half_stat_ref) + tuple(slot_stats),
            slot_send,
            slot_recv,
            bits,
            partners,
        )
        half_pairs = PAIRS // 2
        lanes = half_pairs * LANES
        my_lanes = pl.ds(pl.multiple_of(core * lanes, LANES), lanes)

        def final_copies():
            theirs = pl.ds(pl.multiple_of((1 - core) * own, own), own)
            return (
                remote(
                    turned_ref.at[theirs],
                    go_land.at[:, my_lanes],
                    slot_send.at[4, 0],
                    slot_recv.at[4, 0],
                    partners["core"],
                ),
                remote(
                    gstat_land.at[core],
                    gstat_land.at[core],
                    slot_send.at[4, 1],
                    slot_recv.at[4, 1],
                    partners["core"],
                ),
            )

        def finish_slots():
            slot_sum.merge(3)
            for which in range(half_pairs):
                stat = slot_stats[1][which]
                total = stat[2:4]
                sums = slot_sums[1][which].astype(f32)
                mean = jnp.concatenate(
                    [sums[:HEAD_DIM] / total[0:1], sums[HEAD_DIM:] / total[1:2]], 0
                )
                turned_ref[:, which * LANES : (which + 1) * LANES] = mean.T.astype(bf16)
                whole = stat[0:2] + jnp.log(total)
                gstat_land[core, which] = jnp.concatenate(
                    [whole, jnp.zeros((6, GLOBALS), f32)], 0
                )
            mine = pl.ds(pl.multiple_of(core * own, own), own)
            go_land[:, my_lanes] = turned_ref[mine, :]
            for copy in final_copies():
                copy.start()

        def put_message():
            product = gdo_ref[...].astype(f32) * go_land[...].astype(f32)
            head_of = iota((width, LANES), 0) // HEAD_DIM == iota((width, LANES), 1)
            head_of = jnp.where(head_of, 1.0, 0.0).astype(bf16)
            first = product.astype(bf16)
            second = (product - first.astype(f32)).astype(bf16)
            centre = nn(first, head_of) + nn(second, head_of)
            lines = [gstat_land[half, which, 0:2] for half in (0, 1) for which in range(half_pairs)]
            lines = jnp.concatenate(lines + [jnp.zeros((LANES - HEADS, GLOBALS), f32)], 0)
            stat_ref[...] = lines.T
            total = stat_ref[pl.ds(pl.multiple_of(core * own, own), own), :]
            spread = jnp.zeros((own, LANES), f32)
            for number, value in enumerate((total, centre)):
                for piece in range(3):
                    low = value.astype(bf16)
                    value = value - low.astype(f32)
                    start_lane = (3 * number + piece) * HEADS
                    source_lane = iota((LANES, LANES), 0)
                    moved = iota((LANES, LANES), 1) == source_lane + start_lane
                    moved = jnp.where(moved & (source_lane < HEADS), 1.0, 0.0).astype(bf16)
                    spread = spread + nn(low, moved)
            mine = message_land.at[bits["z1"]]
            mine[:, :width] = gdo_ref[...]
            mine[:, width:] = spread.astype(bf16)
            message_copy().start()

        def message_copy():
            mine = message_land.at[bits["z1"]]
            return remote(mine, mine, message_send, message_recv, partners["z1"])

    else:

        def tick_at(position):
            pass

    if talk:
        batch = lax.axis_index("batch")
        seq_place = lax.axis_index("seq")
        places = lax.axis_size("seq")
        after = (batch, lax.rem(seq_place + 1, places))
        before = (batch, lax.rem(seq_place + places - 1, places))
        halo = remote(
            ct_ref.at[pl.ds(count - HALF, HALF)],
            cts_ref.at[pl.ds(0, HALF)],
            halo_send,
            halo_recv,
            after,
        )
    loads = [
        pltpu.make_async_copy(o_ref, os_ref.at[pl.ds(0, count)], load_sem.at[0]),
        pltpu.make_async_copy(
            ct_ref.at[pl.ds(0, count - HALF)],
            cts_ref.at[pl.ds(HALF, count - HALF)],
            load_sem.at[1],
        ),
    ]
    if not talk:
        loads.append(
            pltpu.make_async_copy(ct_head_ref, cts_ref.at[pl.ds(0, HALF)], load_sem.at[2])
        )

    def start(at, size, x, sums):
        y = x.astype(f32) + nn(os_ref[at, :], wo_ref[...])
        unit, unused = normalize_rows(y)
        h_ref[at, :] = (unit * norms_ref[4:5] + norms_ref[5:6]).astype(bf16)
        y_ref[at, :] = y
        b2 = jnp.concatenate([b2_ref[i : i + 1] for i in range(width // LANES)], axis=1)
        sums[...] = y + b2
        dh_ref[at, :] = jnp.zeros((size, width), f32)

    @pl.when(step == 0)
    def _():
        for load in loads:
            load.start()
        if talk:
            half_ref[...] = go_in_ref[...]
            half_stat_ref[...] = gstat_in_ref[...]
            meet([partners[name] for name in AXES] + [before, after])
            slot_sum.begin(2)
            halo.start()
        cts_ref[count:] = padded(gct_ref[...])
        loads[0].wait()

        def start_tile(i, carry):
            at = pl.ds(pl.multiple_of(i * tile, tile), tile)
            start(at, tile, x_ref[at, :], dy_ref.at[at])
            return carry

        lax.fori_loop(0, tiles, start_tile, 0)
        for load in loads[1:]:
            load.wait()

    db1_ref[...] = jnp.zeros_like(db1_ref)
    w1 = w1_ref[...].reshape(width, width)
    w2 = w2_ref[...].reshape(width, width)

    def chunk_of(at, sums):
        u = nt(h_ref[at, :], w1) + b1_ref[0]
        da = nt(cts_ref[at, :], w2)
        area, density = gelu_parts(u)
        a = (u * area).astype(bf16)
        du = (da * (area + u * density)).astype(bf16)
        a_ref[at, :] = a
        du_ref[at, :] = du
        db1_ref[0] += jnp.sum(du.astype(f32), axis=0, keepdims=True)
        sums[...] = sums[...] + nn(a, w2)
        dh_ref[at, :] = dh_ref[at, :] + nn(du, w1)

    for i in range(1, tiles):
        chunk_of(rows_at(i), dy_ref.at[rows_at(i)])

    if talk:

        @pl.when(step == 0)
        def _():
            slot_sum.merge(2)
            slot_sum.begin(3)
            halo.wait_recv()

    tick_at(0)
    chunk_of(rows_at(0), dy_ref.at[rows_at(0)])

    @pl.when(step == 0)
    def _():
        if talk:
            finish_slots()
            halo.wait_send()
        dft_ref[...] = cts_ref[...].T
        if talk:
            for copy in final_copies():
                copy.wait_recv()
            os_ref[count:] = padded(go_land[...])
        else:
            os_ref[count:] = padded(go_in_ref[...])
        start(tail, extra, padded(gx_ref[...]), z_sum_ref)

    chunk_of(tail, z_sum_ref)
    tick_at(1)
    dw1 = tn(du_ref[...], h_ref[...])
    dw2 = nn(dft_ref[...], a_ref[...])
    if talk:
        for number in range(chunks):

            @pl.when(step == number)
            def _():
                for which, value in ((0, dw1), (1, dw2)):
                    unit = 2 * number + which
                    if unit >= slots:
                        engine.sent(unit - slots, 0)
                    put_unit(units_ref.at[unit % slots], value)

        @pl.when(step == chunks)
        def _():
            put_unit(second_ref.at[0], dw1)
            put_unit(second_ref.at[1], dw2)

        tick_at(2)
        for number in range(chunks):

            @pl.when(step == number)
            def _():
                engine.begin(2 * number)
                engine.begin(2 * number + 1)

    else:
        first_ref[...] = dw1.astype(bf16)
        second_ref[...] = dw2.astype(bf16)

    @pl.when(step == steps - 1)
    def _():
        db2_ref[...] = jnp.zeros_like(db2_ref)
        dgain_ref[...] = jnp.zeros_like(dgain_ref)
        doffset_ref[...] = jnp.zeros_like(doffset_ref)

        def finish(at, size, sums, put):
            z = sums[...].astype(bf16)
            unit, scale = normalize_rows(y_ref[at, :])
            dh = dh_ref[at, :]
            ct = cts_ref[at, :].astype(f32)
            dy = ct + norm_back(unit, scale, norms_ref[4:5], dh)
            db2_ref[...] += jnp.sum(ct, axis=0, keepdims=True)
            doffset_ref[...] += jnp.sum(dh, axis=0, keepdims=True)
            dgain_ref[...] += jnp.sum(dh * unit, axis=0, keepdims=True)
            low = dy.astype(bf16)
            h_ref[at, :] = low
            put(z, dy, nt(low, wo_ref[...]).astype(bf16))

        def finish_tile(i, carry):
            at = pl.ds(pl.multiple_of(i * tile, tile), tile)

            def put(z, dy, do):
                z_ref[at, :] = z
                dy_ref[at, :] = dy
                do_ref[at, :] = do

            finish(at, tile, dy_ref.at[at], put)
            return carry

        def put_tail(z, dy, do):
            gz_ref[...] = z[:own]
            gdy_ref[...] = dy[:own]
            gdo_ref[...] = do[:own]

        finish(tail, extra, z_sum_ref, put_tail)
        if talk:
            put_message()
            advance(TICKS * chunks)
        lax.fori_loop(0, tiles, finish_tile, 0)
        dwo = tn(h_ref[...], os_ref[...])
        if talk:
            put_grouped(dwo_ref, dwo)
            advance(TICKS * chunks + 1)
            rest_ref[...] = landings[1][2 * chunks - 2 :]
            for when, chunk, stage in plan:
                for unit in (2 * chunk, 2 * chunk + 1):
                    if stage > 0 or unit + slots >= 2 * chunks:
                        engine.sent(unit, stage)
            slot_sum.sent(2)
            slot_sum.sent(3)
            for copy in final_copies():
                copy.wait_send()
            message_copy().wait_recv()
            message_ref[...] = message_land[...]
            message_copy().wait_send()
        else:
            dwo_ref[...] = dwo.astype(bf16)


def branch(grid_of, x, o, ct, ct_head, gx, go, gstat, gct, wo, w1t, b1, w2, b2, norms):
    count, width = x.shape
    own = gx.shape[0]
    hidden = w2.shape[0]
    steps = hidden // FF_CHUNK
    total = count + -(-own // LANES) * LANES
    row = once((count, width))
    few = once((own, width))
    line = full((1, width))
    anywhere = pl.BlockSpec(memory_space=pl.ANY)
    scratch = []
    more = {}
    if grid_of is None:
        weight_spec = pl.BlockSpec((FF_CHUNK, width), lambda j: (j, 0))
        b1 = b1.reshape(steps, 1, FF_CHUNK)
        dw_shapes = [(hidden, width), (width, hidden)]
        dw_types = [bf16, bf16]
        dw_specs = [weight_spec, pl.BlockSpec((width, FF_CHUNK), lambda j: (0, j))]
        dwo_shape = (width, width)
    else:
        seq, batch = grid_of
        rows, lanes = width // seq, width // batch
        weight_spec = pl.BlockSpec((seq, 1, rows, width), lambda j: (0, j, 0, 0))
        w1t = w1t.reshape(seq, steps, rows, width)
        w2 = w2.reshape(seq, steps, rows, width)
        b1 = b1.reshape(seq, steps, rows).transpose(1, 0, 2).reshape(steps, 1, FF_CHUNK)
        units = 2 * (steps - 1)
        sums, stats = go.shape[2:], gstat.shape[2:]
        dw_shapes = [
            ((units - 2) * rows, lanes),
            (2, 2, 2, 2, 2, batch, rows, lanes),
            (2, own, width + LANES),
            (2, 2, 2, 2, rows, lanes),
        ]
        dw_types = [f32, bf16, bf16, bf16]
        dw_specs = [once(shape) for shape in dw_shapes]
        dwo_shape = (seq, batch, rows, lanes)
        dma = pltpu.SemaphoreType.DMA
        scratch = (
            [pltpu.VMEM((4,) + dw_shapes[1][1:], bf16)]
            + sum_scratch(units, rows, lanes, False)
            + [
                pltpu.VMEM(go.shape, bf16),
                pltpu.VMEM(gstat.shape, f32),
                pltpu.VMEM((2,) + sums, bf16),
                pltpu.VMEM(sums, bf16),
                pltpu.VMEM((2,) + stats, f32),
                pltpu.VMEM(stats, f32),
                pltpu.VMEM((GLOBALS, PAIRS // 2 * LANES), bf16),
                pltpu.VMEM((own, width), bf16),
                pltpu.VMEM((2,) + stats, f32),
                pltpu.VMEM((GLOBALS, LANES), f32),
                dma((5, 2)),
                dma((5, 2)),
                pltpu.VMEM((2, own, width + LANES), bf16),
                dma,
                dma,
                dma,
                dma,
            ]
        )
        more = {"collective_id": 3, "has_side_effects": True}
    out = pl.pallas_call(
        functools.partial(branch_kernel, BLOCK, grid_of is not None),
        grid=(steps,),
        in_specs=[
            row,
            anywhere,
            anywhere,
            anywhere,
            few,
            once(go.shape),
            once(gstat.shape),
            few,
            once((width, width)),
            weight_spec,
            pl.BlockSpec((1, 1, FF_CHUNK), lambda j: (j, 0, 0)),
            weight_spec,
            full(b2.shape),
            full(norms.shape),
        ],
        out_specs=[row, row, row, few, few, few]
        + [once(dwo_shape), pl.BlockSpec((1, 1, FF_CHUNK), lambda j: (j, 0, 0)), line, line, line]
        + dw_specs,
        out_shape=[
            jax.ShapeDtypeStruct((count, width), bf16),
            jax.ShapeDtypeStruct((count, width), f32),
            jax.ShapeDtypeStruct((count, width), bf16),
            jax.ShapeDtypeStruct((own, width), bf16),
            jax.ShapeDtypeStruct((own, width), f32),
            jax.ShapeDtypeStruct((own, width), bf16),
            jax.ShapeDtypeStruct(dwo_shape, bf16),
            jax.ShapeDtypeStruct((steps, 1, FF_CHUNK), f32),
            jax.ShapeDtypeStruct((1, width), f32),
            jax.ShapeDtypeStruct((1, width), f32),
            jax.ShapeDtypeStruct((1, width), f32),
        ]
        + [jax.ShapeDtypeStruct(shape, kind) for shape, kind in zip(dw_shapes, dw_types)],
        scratch_shapes=[
            pltpu.VMEM((total, width), bf16),
            pltpu.VMEM((total, width), bf16),
            pltpu.VMEM((total, width), f32),
            pltpu.VMEM((total, width), bf16),
            pltpu.VMEM((total - count, width), f32),
            pltpu.VMEM((total, width), f32),
            pltpu.VMEM((width, total), bf16),
            pltpu.VMEM((total, FF_CHUNK), bf16),
            pltpu.VMEM((total, FF_CHUNK), bf16),
            pltpu.SemaphoreType.DMA((3,)),
        ]
        + scratch,
        compiler_params=params(**more),
        cost_estimate=pl.CostEstimate(
            flops=6 * total * width * (2 * hidden + width),
            bytes_accessed=8 * width * hidden + 16 * total * width,
            transcendentals=2 * total * hidden,
        ),
        name="branch",
    )(x, o, ct, ct_head, gx, go, gstat, gct, wo, w1t, b1, w2, b2, norms)
    db1 = out[7].reshape(steps, FF_CHUNK)
    if grid_of is not None:
        db1 = db1.reshape(steps, seq, rows).transpose(1, 0, 2).reshape(-1, width)
    return [*out[:7], db1, *out[8:]]


def local_backward_kernel(
    talk,
    rows_count,
    group_rows,
    lengths,
    bucket_of,
    place,
    q_ref,
    k_ref,
    v_ref,
    do_ref,
    o_ref,
    line_ref,
    *refs,
):
    if talk:
        message_ref, rest_ref, last_ref, dwo_ref = refs[:4]
        refs = refs[4:]
    dq_ref, dk_ref, dv_ref, centre_ref = refs[:4]
    refs = refs[4:]
    if talk:
        everyone_ref, sums_ref, rest_out_ref = refs[:3]
        refs = refs[3:]
    edges, query_columns, key_columns = refs[:3]
    pair = pl.program_id(0)
    block = pl.program_id(1)
    blocks = rows_count // BLOCK
    step = pair * blocks + block

    @pl.when(step == 0)
    def _():
        read_edges(lengths, bucket_of, place, edges)

    if talk:
        all_ref, gather_send, gather_recv, own_ref = refs[3:7]
        landings = refs[7:12]
        send_sem, recv_sem, own_sem = refs[12:]
        bits, partners = my_place()
        gather = RowGather(all_ref, 3 * LANES, gather_send, gather_recv, bits, partners)
        engine = HalvingSum(
            (X_FIRST, Y_FIRST) * 2 + (X_FIRST,),
            [
                None,
                None,
                lambda side: last_ref.at[0, :, :, :, side],
                lambda side: last_ref.at[1, :, :, :, side],
                lambda side: dwo_ref.at[:, :, :, side],
            ],
            landings,
            own_ref,
            send_sem,
            recv_sem,
            own_sem,
            put_rows(sums_ref, landings[4].shape[1]),
            bits,
            partners,
        )
        plan = {
            3: [(2, 0), (3, 0), (4, 0)],
            5: [(0, 2), (1, 2)],
            8: [(0, 3), (1, 3)],
            11: [(0, 4), (1, 4), (2, 1), (3, 1), (4, 1)],
        }
        gather_plan = {4: 1, 8: 2, 10: 3}

        @pl.when(step == 0)
        def _():
            all_ref[:, bits["z0"], bits["y"], bits["core"]] = message_ref[...]
            landings[1][:2] = rest_ref[...]
            meet([partners[name] for name in AXES])
            gather.begin(1)
            for unit in (0, 1):
                engine.copy(unit, 2).start()
            for unit in (2, 3, 4):
                engine.begin(unit)

        for number in range(PAIRS * blocks):
            if number in plan or number in gather_plan:

                @pl.when(step == number)
                def _():
                    if number in gather_plan:
                        gather.advance(gather_plan[number])
                    for unit, stage in plan.get(number, ()):
                        engine.advance(unit, stage, stop=unit > 1 and stage == 1)

    block_columns(
        place, edges, rows_count, group_rows, block, step, blocks, query_columns, key_columns
    )
    extra = query_columns[block]
    upstream = do_ref[...]
    product = upstream.astype(f32) * o_ref[...].astype(f32)
    first = product.astype(bf16)
    second = (product - first.astype(f32)).astype(bf16)
    head = jnp.where(iota((8, LANES), 1) // HEAD_DIM == iota((8, LANES), 0), 1.0, 0.0).astype(bf16)
    by_head = nt(head, first) + nt(head, second)
    centre = jnp.concatenate([by_head[0:1], by_head[1:2]], axis=1)
    centre_ref[0, 0] = jnp.broadcast_to(centre, (8, 2 * BLOCK))
    queries = stack_pair(q_ref[...])
    grads = stack_pair(upstream)
    keys = k_ref[...]
    score = nt(
        jnp.concatenate([keys, key_columns[block]], 1),
        jnp.concatenate([queries, jnp.concatenate([extra, extra], 0)], 1),
    )
    weights = jnp.exp(score - line_ref[0, 0, 0:1])
    along = nt(v_ref[...], grads) - centre
    score_grad = (weights * along).astype(bf16)
    dv_ref[...] = nn(weights.astype(bf16), grads).astype(bf16)
    dk_ref[...] = nn(score_grad, queries).astype(bf16)
    low, high = side_by_side(tn(keys, score_grad))
    dq_ref[:HEAD_DIM] = low.astype(bf16)
    dq_ref[HEAD_DIM:] = high.astype(bf16)

    if talk:

        @pl.when(step == PAIRS * blocks - 1)
        def _():
            everyone_ref[...] = all_ref[...].reshape(everyone_ref.shape)
            gather.end(1)
            rest_out_ref[...] = landings[1][2:]
            for entries in plan.values():
                for unit, stage in entries:
                    engine.sent(unit, stage)


def local_backward(
    talk, scalars, rows_count, group_rows, q, k, v, do, o, line, message, rest, last, dwo
):
    blocks = rows_count // BLOCK
    width = q.shape[1]
    block_spec = pl.BlockSpec((BLOCK, LANES), lambda p, b, *unused: (b, p))
    operands = [q, k, v, do, o, line]
    in_specs = [block_spec] * 5 + [line_spec()]
    out_specs = (
        [pl.BlockSpec((LANES, BLOCK), lambda p, b, *unused: (p, b))]
        + [block_spec] * 2
        + [line_spec()]
    )
    out_shape = [
        jax.ShapeDtypeStruct((width, rows_count), bf16),
        jax.ShapeDtypeStruct((rows_count, width), bf16),
        jax.ShapeDtypeStruct((rows_count, width), bf16),
        jax.ShapeDtypeStruct((PAIRS, blocks, 8, 2 * BLOCK), f32),
    ]
    scratch = column_scratch(blocks)
    more = {}
    if talk:
        unused, own, wide = message.shape
        rows, lanes = last.shape[-2:]
        units = 5
        operands += [message, rest, last, dwo.reshape(last.shape[1:])]
        in_specs += [full(message.shape), once(rest.shape)]
        in_specs += [pl.BlockSpec(memory_space=pl.ANY)] * 2
        everyone = (16 * own, wide)
        rest_out = (units - 2,) + rest.shape[1:]
        out_specs += [once(everyone), once((2 * rows, lanes)), once(rest_out)]
        out_shape += [
            jax.ShapeDtypeStruct(everyone, bf16),
            jax.ShapeDtypeStruct((2 * rows, lanes), f32),
            jax.ShapeDtypeStruct(rest_out, bf16),
        ]
        dma = pltpu.SemaphoreType.DMA
        scratch += [pltpu.VMEM((2, 2, 2, 2, own, wide), bf16), dma((4, 2)), dma((4, 2))]
        scratch += sum_scratch(units, rows, lanes, True)
        more = {"collective_id": 4, "has_side_effects": True}
    return pl.pallas_call(
        functools.partial(local_backward_kernel, talk, rows_count, group_rows),
        grid_spec=pltpu.PrefetchScalarGridSpec(
            num_scalar_prefetch=3,
            grid=(PAIRS, blocks),
            in_specs=in_specs,
            out_specs=out_specs,
            scratch_shapes=scratch,
        ),
        out_shape=out_shape,
        compiler_params=params(**more),
        cost_estimate=pl.CostEstimate(
            flops=40 * rows_count * BLOCK * width,
            bytes_accessed=30 * rows_count * width,
            transcendentals=HEADS * rows_count * BLOCK,
        ),
        name="local_backward",
    )(*scalars, *operands)


def slot_backward_kernel(
    rows_count,
    group_rows,
    lengths,
    bucket_of,
    place,
    q_ref,
    k_ref,
    v_ref,
    do_ref,
    line_ref,
    centre_ref,
    dqt_ref,
    dk_in_ref,
    dv_in_ref,
    gq_ref,
    gk_ref,
    gv_ref,
    gdo_ref,
    gstat_ref,
    gx_ref,
    gh_ref,
    wq_ref,
    wk_ref,
    wv_ref,
    dq_ref,
    dk_ref,
    dv_ref,
    dw_ref,
    dgh_ref,
    dnorm_ref,
    edges,
    query_columns,
    key_columns,
    keys_ref,
    queries_ref,
    grads_ref,
    dqt_sum,
    dk_sum,
    dv_sum,
    dgqt_sum,
    dgk_sum,
    dgv_sum,
    lines_ref,
    dw_sum,
    dgh_sum,
):
    group = pl.program_id(0)
    block = pl.program_id(1)
    blocks = rows_count // BLOCK
    step = group * blocks + block
    together = range(TOGETHER)

    def lanes_of(which):
        return pl.ds(which * LANES, LANES)

    @pl.when(step == 0)
    def _():
        read_edges(lengths, bucket_of, place, edges)

        def turn(slot, carry):
            at = pl.ds(pl.multiple_of(slot * GLOBALS, GLOBALS), GLOBALS)
            lines_ref[slot] = gstat_ref[at, :].astype(f32).T
            return carry

        lax.fori_loop(0, SLOTS, turn, 0)
        dgh_sum[...] = jnp.zeros_like(dgh_sum)
        dnorm_ref[...] = jnp.zeros_like(dnorm_ref)

    @pl.when(block == 0)
    def _():
        dgqt_sum[...] = jnp.zeros_like(dgqt_sum)
        dgk_sum[...] = jnp.zeros_like(dgk_sum)
        dgv_sum[...] = jnp.zeros_like(dgv_sum)

    block_columns(
        place, edges, rows_count, group_rows, block, step, blocks, query_columns, key_columns
    )
    extra = query_columns[block]
    for which in together:
        lanes = lanes_of(which)
        keys_ref[which, :, :LANES] = k_ref[:, lanes]
        keys_ref[which, :, LANES:] = key_columns[block]
        queries_ref[which, :, :LANES] = stack_pair(q_ref[:, lanes])
        queries_ref[which, :BLOCK, LANES:] = extra
        queries_ref[which, BLOCK:, LANES:] = extra
        grads_ref[which] = stack_pair(do_ref[:, lanes])
    dqt_sum[...] = dqt_ref[...].astype(f32)
    dk_sum[...] = dk_in_ref[...].astype(f32)
    dv_sum[...] = dv_in_ref[...].astype(f32)

    def line_of(slot, which, first):
        halves = []
        for head in range(2):
            spot = first + 2 * (group * TOGETHER + which) + head
            halves.append(
                lines_ref[slot, pl.ds(spot, 1)]
                + lines_ref[slot, pl.ds(spot + HEADS, 1)]
                + lines_ref[slot, pl.ds(spot + 2 * HEADS, 1)]
            )
        return jnp.concatenate(halves, axis=1)

    def from_global(slot, which, keys, values):
        at = pl.ds(pl.multiple_of(slot * GLOBALS, GLOBALS), GLOBALS)
        extra = global_query_extra(slot).astype(bf16)
        queries = stack_pair(gq_ref[at, lanes_of(which)])
        grads = stack_pair(gdo_ref[at, lanes_of(which)])
        score = nt(keys, jnp.concatenate([queries, jnp.concatenate([extra, extra], 0)], 1))
        weights = jnp.exp(score - line_of(slot, which, 0))
        along = nt(values, grads) - line_of(slot, which, 3 * HEADS)
        score_grad = (weights * along).astype(bf16)
        low, high = side_by_side(tn(keys[:, :LANES], score_grad))
        dgqt_sum[which, slot, :HEAD_DIM] += low
        dgqt_sum[which, slot, HEAD_DIM:] += high
        return nn(score_grad, queries), nn(weights.astype(bf16), grads)

    def one_slot(slot, carry):
        @pl.when(slot_present(slot, place, edges, rows_count, group_rows, block))
        def _():
            at = pl.ds(pl.multiple_of(slot * GLOBALS, GLOBALS), GLOBALS)
            columns = global_key_extra(slot).astype(bf16)
            for which in together:
                lanes = lanes_of(which)
                key_grad, value_grad = from_global(slot, which, keys_ref[which], v_ref[:, lanes])
                dk_sum[:, lanes] += key_grad
                dv_sum[:, lanes] += value_grad
                keys = gk_ref[at, lanes]
                grads = grads_ref[which]
                score = nt(jnp.concatenate([keys, columns], 1), queries_ref[which])
                weights = jnp.exp(score - line_ref[which, 0, 0:1])
                along = nt(gv_ref[at, lanes], grads) - centre_ref[which, 0, 0:1]
                score_grad = (weights * along).astype(bf16)
                dgv_sum[at, lanes] += nn(weights.astype(bf16), grads)
                dgk_sum[at, lanes] += nn(score_grad, queries_ref[which, :, :LANES])
                low, high = side_by_side(tn(keys, score_grad))
                dqt_sum[pl.ds(which * LANES, HEAD_DIM)] += low
                dqt_sum[pl.ds(which * LANES + HEAD_DIM, HEAD_DIM)] += high

        return carry

    lax.fori_loop(0, SLOTS, one_slot, 0)
    dq_ref[...] = dqt_sum[...].T.astype(bf16)
    dk_ref[...] = dk_sum[...].astype(bf16)
    dv_ref[...] = dv_sum[...].astype(bf16)

    @pl.when((block == blocks - 1) & (place[2] >= 0))
    def _():
        slot = place[2]
        at = pl.ds(pl.multiple_of(slot * GLOBALS, GLOBALS), GLOBALS)
        columns = global_key_extra(slot).astype(bf16)
        for which in together:
            lanes = lanes_of(which)
            keys = jnp.concatenate([gk_ref[at, lanes], columns], axis=1)
            key_grad, value_grad = from_global(slot, which, keys, gv_ref[at, lanes])
            dgk_sum[at, lanes] += key_grad
            dgv_sum[at, lanes] += value_grad

    @pl.when(block == blocks - 1)
    def _():
        def through(slot, found):
            needed = slot == place[2]
            for number in range(blocks):
                needed = needed | slot_present(
                    slot, place, edges, rows_count, group_rows, number
                )

            @pl.when(needed)
            def _():
                at = pl.ds(pl.multiple_of(slot * GLOBALS, GLOBALS), GLOBALS)
                grads = (
                    (
                        jnp.concatenate([dgqt_sum[which, slot].T for which in together], 1)
                        * query_scale
                    ).astype(bf16),
                    dgk_sum[at, :].astype(bf16),
                    dgv_sum[at, :].astype(bf16),
                )
                rows = gh_ref[at, :]
                total = dgh_sum[at, :]
                for index, weight in enumerate((wq_ref, wk_ref, wv_ref)):
                    total = total + nt(grads[index], weight[...])
                dgh_sum[at, :] = total

                @pl.when(found == 0)
                def _():
                    for index in range(3):
                        dw_sum[index] = tn(grads[index], rows)

                @pl.when(found > 0)
                def _():
                    for index in range(3):
                        dw_sum[index] += tn(grads[index], rows)

                @pl.when(group == PAIRS // TOGETHER - 1)
                def _():
                    unit, unused = normalize_rows(gx_ref[at, :].astype(f32))
                    dnorm_ref[0:1] += jnp.sum(total * unit, axis=0, keepdims=True)
                    dnorm_ref[1:2] += jnp.sum(total, axis=0, keepdims=True)

            return jnp.where(needed, 1, found)

        lax.fori_loop(0, SLOTS, through, jnp.int32(0))
        dw_ref[...] = dw_sum[...].astype(bf16)

    @pl.when(step == PAIRS // TOGETHER * blocks - 1)
    def _():
        dgh_ref[...] = dgh_sum[...].astype(bf16)


def slot_backward(
    scalars,
    rows_count,
    group_rows,
    q,
    k,
    v,
    do,
    line,
    centre,
    dqt,
    dk,
    dv,
    gq,
    gk,
    gv,
    everyone,
    gx,
    gh,
    wq,
    wk,
    wv,
):
    blocks = rows_count // BLOCK
    all_globals, width = gk.shape
    block_spec = pl.BlockSpec((BLOCK, TOGETHER * LANES), lambda p, b, *unused: (b, p))
    pair_spec = pl.BlockSpec((all_globals, TOGETHER * LANES), lambda p, b, *unused: (0, p))
    local = jax.ShapeDtypeStruct((rows_count, width), bf16)
    glob = jax.ShapeDtypeStruct((all_globals, width), bf16)
    return pl.pallas_call(
        functools.partial(slot_backward_kernel, rows_count, group_rows),
        grid_spec=pltpu.PrefetchScalarGridSpec(
            num_scalar_prefetch=3,
            grid=(PAIRS // TOGETHER, blocks),
            in_specs=[block_spec] * 4
            + [line_spec(TOGETHER)] * 2
            + [pl.BlockSpec((TOGETHER * LANES, BLOCK), lambda p, b, *unused: (p, b))]
            + [block_spec] * 2
            + [pair_spec] * 4
            + [pl.BlockSpec((all_globals, LANES), lambda p, b, *unused: (0, PAIRS))]
            + [once((all_globals, width))] * 2
            + [pl.BlockSpec((width, TOGETHER * LANES), lambda p, b, *unused: (0, p))] * 3,
            out_specs=[block_spec] * 3
            + [
                pl.BlockSpec((3, TOGETHER * LANES, width), lambda p, b, *unused: (0, p, 0)),
                once((all_globals, width)),
                full((8, width)),
            ],
            scratch_shapes=column_scratch(blocks)
            + [
                pltpu.VMEM((TOGETHER, BLOCK, 2 * LANES), bf16),
                pltpu.VMEM((TOGETHER, 2 * BLOCK, 2 * LANES), bf16),
                pltpu.VMEM((TOGETHER, 2 * BLOCK, LANES), bf16),
                pltpu.VMEM((TOGETHER * LANES, BLOCK), f32),
                pltpu.VMEM((BLOCK, TOGETHER * LANES), f32),
                pltpu.VMEM((BLOCK, TOGETHER * LANES), f32),
                pltpu.VMEM((TOGETHER, SLOTS, LANES, GLOBALS), f32),
                pltpu.VMEM((all_globals, TOGETHER * LANES), f32),
                pltpu.VMEM((all_globals, TOGETHER * LANES), f32),
                pltpu.VMEM((SLOTS, LANES, GLOBALS), f32),
                pltpu.VMEM((3, TOGETHER * LANES, width), f32),
                pltpu.VMEM((all_globals, width), f32),
            ],
        ),
        out_shape=[local] * 3
        + [
            jax.ShapeDtypeStruct((3, width, width), bf16),
            glob,
            jax.ShapeDtypeStruct((8, width), f32),
        ],
        compiler_params=params(),
        cost_estimate=pl.CostEstimate(
            flops=80 * rows_count * GLOBALS * width,
            bytes_accessed=40 * rows_count * width,
            transcendentals=2 * HEADS * rows_count * GLOBALS,
        ),
        name="slot_backward",
    )(
        *scalars,
        q,
        k,
        v,
        do,
        line,
        centre,
        dqt,
        dk,
        dv,
        gq,
        gk,
        gv,
        everyone,
        everyone,
        gx,
        gh,
        wq,
        wk,
        wv,
    )


def project_back_kernel(
    tile,
    x_ref,
    dy_ref,
    h_ref,
    dq_ref,
    dk_ref,
    dv_ref,
    dwg_ref,
    wq_ref,
    wk_ref,
    wv_ref,
    gain_ref,
    dx_ref,
    dw_ref,
    dnorm_ref,
):
    count, width = x_ref.shape
    dnorm_ref[...] = jnp.zeros_like(dnorm_ref)

    def one_tile(i, carry):
        at = pl.ds(pl.multiple_of(i * tile, tile), tile)
        dh = (
            nt(dq_ref[at, :], wq_ref[...]) * query_scale
            + nt(dk_ref[at, :], wk_ref[...])
            + nt(dv_ref[at, :], wv_ref[...])
        )
        unit, scale = normalize_rows(x_ref[at, :].astype(f32))
        dnorm_ref[0:1] += jnp.sum(dh * unit, axis=0, keepdims=True)
        dnorm_ref[1:2] += jnp.sum(dh, axis=0, keepdims=True)
        dx_ref[at, :] = dy_ref[at, :] + norm_back(unit, scale, gain_ref[...], dh)
        return carry

    lax.fori_loop(0, count // tile, one_tile, 0)
    for index, source in enumerate((dq_ref, dk_ref, dv_ref)):
        value = tn(source[...], h_ref[...])
        if index == 0:
            value = value * query_scale
        dw_ref[index] = (value + dwg_ref[index].astype(f32)).astype(bf16)


def project_back(x, dy, h, dq, dk, dv, dwg, wq, wk, wv, gain):
    count, width = x.shape
    vmem = pl.BlockSpec(memory_space=pltpu.VMEM)
    return pl.pallas_call(
        functools.partial(project_back_kernel, BLOCK),
        in_specs=[vmem] * 11,
        out_specs=[vmem] * 3,
        out_shape=[
            jax.ShapeDtypeStruct((count, width), f32),
            jax.ShapeDtypeStruct((3, width, width), bf16),
            jax.ShapeDtypeStruct((8, width), f32),
        ],
        compiler_params=params(),
        cost_estimate=pl.CostEstimate(
            flops=12 * count * width * width, bytes_accessed=30 * count * width, transcendentals=0
        ),
        name="project_back",
    )(x, dy, h, dq, dk, dv, dwg, wq, wk, wv, gain)


def finish_kernel(
    rest_ref,
    x_in,
    dy_in,
    h_in,
    dq_in,
    dk_in,
    dv_in,
    dwg_in,
    dgh_ref,
    z_in,
    wq_in,
    wk_in,
    wv_in,
    db1_ref,
    db2_ref,
    dnorm_global_ref,
    dgain2_ref,
    doffset2_ref,
    gx_ref,
    gdy_ref,
    norms_ref,
    out_ref,
    small_out_ref,
    grad_out_ref,
    token_ref,
    halo_dx_out,
    halo_z_out,
    x_ref,
    dy_ref,
    h_ref,
    dq_ref,
    dk_ref,
    dv_ref,
    dwg_ref,
    wq_ref,
    wk_ref,
    wv_ref,
    load_sem,
    units_ref,
    one_ref,
    two_ref,
    three_ref,
    four_ref,
    five_ref,
    send_sem,
    recv_sem,
    gown_ref,
    gone_ref,
    gtwo_ref,
    gthree_ref,
    gfour_ref,
    gsend_sem,
    grecv_sem,
    gown_sem,
    sums_ref,
    here_ref,
    ssend_sem,
    srecv_sem,
    halo_out,
    halo_dx,
    halo_z,
    halo_send,
    halo_recv,
    dnorm_ref,
    dgh_sum_ref,
):
    bits, partners = my_place()
    count, width = x_ref.shape
    came = rest_ref.shape[0]
    units = came + 3
    batch = lax.axis_index("batch")
    seq = lax.axis_index("seq")
    places = lax.axis_size("seq")
    after = (batch, lax.rem(seq + 1, places))
    before = (batch, lax.rem(seq + places - 1, places))

    pairs = [
        (dq_in, dq_ref),
        (h_in, h_ref),
        (dwg_in, dwg_ref),
        (dk_in, dk_ref),
        (dv_in, dv_ref),
        (wq_in, wq_ref),
        (wk_in, wk_ref),
        (wv_in, wv_ref),
        (x_in, x_ref),
        (dy_in, dy_ref),
    ]
    loads = [
        pltpu.make_async_copy(source, target, load_sem.at[number])
        for number, (source, target) in enumerate(pairs)
    ]
    for load in loads:
        load.start()

    def source(unit):
        return lambda side: units_ref.at[unit - came, :, :, :, side]

    engine = HalvingSum(
        (X_Z_FIRST, Y_FIRST, X_FIRST, X_FIRST, Y_FIRST, Z_FIRST),
        [source(unit) for unit in range(units)],
        (one_ref, two_ref, three_ref, four_ref, five_ref),
        None,
        send_sem,
        recv_sem,
        None,
        put_rows(out_ref, five_ref.shape[1]),
        bits,
        partners,
    )
    wide = gone_ref.shape[-1]

    def row_source(unit):
        lanes = pl.ds(unit * wide, wide)
        return lambda side: dgh_ref.at[:, :, :, side, :, lanes]

    def put_dgh(unit, value):
        dgh_sum_ref[:, unit * wide : (unit + 1) * wide] = value

    row_sum = HalvingSum(
        (("core", "y", "z0", "z1"), ("core", "z0", "y", "z1")),
        [row_source(unit) for unit in range(2)],
        (gone_ref, gtwo_ref, gthree_ref, gfour_ref),
        gown_ref,
        gsend_sem,
        grecv_sem,
        gown_sem,
        put_dgh,
        bits,
        partners,
    )

    def rows_advance(stage):
        for unit in range(2):
            row_sum.advance(unit, stage)

    def scopy(stage):
        return remote(
            sums_ref.at[stage],
            here_ref.at[stage],
            ssend_sem.at[stage],
            srecv_sem.at[stage],
            partners[X_FIRST[stage]],
        )

    def small_advance(stage):
        scopy(stage).wait_recv()
        total = sums_ref[stage] + here_ref[stage]
        if stage < STAGES - 1:
            sums_ref[stage + 1] = total
            scopy(stage + 1).start()
        else:
            small_out_ref[...] = total

    halos = [
        remote(halo_out, halo_dx, halo_send.at[0], halo_recv.at[0], before),
        remote(
            z_in.at[pl.ds(0, HALF)], halo_z, halo_send.at[1], halo_recv.at[1], before
        ),
    ]
    two_ref[:came] = rest_ref[...]
    meet([partners[name] for name in AXES] + [before, after])
    for unit in range(came):
        engine.copy(unit, 2).start()
    for unit in range(2):
        row_sum.begin(unit)

    def weight_gradient(index, grads_ref):
        value = tn(grads_ref[...], h_ref[...])
        if index == 0:
            value = value * query_scale
        put_unit(units_ref.at[index], value + dwg_ref[index].astype(f32))
        engine.begin(came + index)

    for number in range(3):
        loads[number].wait()
    weight_gradient(0, dq_ref)
    rows_advance(0)
    loads[3].wait()
    weight_gradient(1, dk_ref)
    engine.advance(came, 0)
    loads[4].wait()
    weight_gradient(2, dv_ref)
    engine.advance(came + 1, 0)
    for unit in range(came):
        engine.advance(unit, 2)
    for number in range(5, 10):
        loads[number].wait()
    dnorm_ref[...] = jnp.zeros_like(dnorm_ref)

    def back(index):
        at = pl.ds(index * HALF, HALF)
        dh = (
            nt(dq_ref[at, :], wq_ref[...]) * query_scale
            + nt(dk_ref[at, :], wk_ref[...])
            + nt(dv_ref[at, :], wv_ref[...])
        )
        unit, scale = normalize_rows(x_ref[at, :].astype(f32))
        dnorm_ref[0:1] += jnp.sum(dh * unit, axis=0, keepdims=True)
        dnorm_ref[1:2] += jnp.sum(dh, axis=0, keepdims=True)
        dx = dy_ref[at, :] + norm_back(unit, scale, norms_ref[0:1], dh)
        if index == 0:
            halo_out[...] = dx.astype(bf16)
        else:
            token_ref[pl.ds((index - 1) * HALF, HALF), :] = dx

    for index in range(count // HALF):
        back(index)
        if index == 0:
            engine.advance(came + 2, 0)
            halos[0].start()
        if index == 1:
            rows_advance(1)
        if index == 2:
            for unit in range(came):
                engine.advance(unit, 3)

    hidden_rows = db1_ref.shape[0]
    parts = [
        db1_ref[...],
        db2_ref[...],
        dnorm_ref[0:2],
        dnorm_global_ref[0:2],
        dgain2_ref[...],
        doffset2_ref[...],
    ]
    filled = hidden_rows + 7
    parts.append(jnp.zeros((sums_ref.shape[1] - filled, width), f32))
    sums_ref[0] = jnp.concatenate(parts, 0)
    scopy(0).start()
    halos[1].start()
    rows_advance(2)
    for unit in range(came, units):
        engine.advance(unit, 1)
    small_advance(0)
    rows_advance(3)
    dgh = dgh_sum_ref[...]
    unit_rows, scale = normalize_rows(gx_ref[...].astype(f32))
    grad_out_ref[...] = gdy_ref[...] + norm_back(unit_rows, scale, norms_ref[2:3], dgh)
    small_advance(1)
    for unit in range(came):
        engine.advance(unit, 4)
    for unit in range(came, units):
        engine.advance(unit, 2)
    small_advance(2)
    for halo in halos:
        halo.wait_recv()
    halo_dx_out[...] = halo_dx[...]
    halo_z_out[...] = halo_z[...]
    for unit in range(came, units):
        engine.advance(unit, 3)
    small_advance(3)
    for unit in range(came, units):
        engine.advance(unit, 4)
    small_advance(4)

    for unit in range(units):
        for stage in range(2 if unit < came else 0, STAGES):
            engine.sent(unit, stage)
    for stage in range(STAGES):
        scopy(stage).wait_send()
    for unit in range(2):
        for stage in range(4):
            row_sum.sent(unit, stage)
    for halo in halos:
        halo.wait_send()


def finish_all(rest, x, dy, h, dq, dk, dv, dwg, dgh, z, wq, wk, wv, small, gx, gdy, norms):
    count, width = x.shape
    rows, lanes = rest.shape[-2:]
    units = rest.shape[0] + 3
    own = gx.shape[0]
    place = (2, 2, 2, 2)
    small_rows = small[0].shape[0] + 7
    small_rows += -small_rows % 8
    anywhere = pl.BlockSpec(memory_space=pl.ANY)
    vmem = pl.BlockSpec(memory_space=pltpu.VMEM)
    dma = pltpu.SemaphoreType.DMA
    row = pltpu.VMEM((count, width), bf16)
    weight = pltpu.VMEM((width, width), bf16)
    half = pltpu.VMEM((HALF, width), bf16)
    return pl.pallas_call(
        finish_kernel,
        in_specs=[vmem] + [anywhere] * 12 + [vmem] * 8,
        out_specs=[vmem] * 6,
        out_shape=[
            jax.ShapeDtypeStruct((units * rows, lanes), f32),
            jax.ShapeDtypeStruct((small_rows, width), f32),
            jax.ShapeDtypeStruct((own, width), f32),
            jax.ShapeDtypeStruct((count - HALF, width), f32),
            jax.ShapeDtypeStruct((HALF, width), bf16),
            jax.ShapeDtypeStruct((HALF, width), bf16),
        ],
        scratch_shapes=[
            row,
            pltpu.VMEM((count, width), f32),
            row,
            row,
            row,
            row,
            pltpu.VMEM((3, width, width), bf16),
            weight,
            weight,
            weight,
            dma((10,)),
            pltpu.VMEM((3, 2, 2, 2, 2, 2, rows, lanes), bf16),
        ]
        + sum_scratch(units, rows, lanes, False)
        + [
            pltpu.VMEM((2, 2, 2, 2, own, width // 2), bf16),
            pltpu.VMEM((2, 2, 2, 2, own, width // 2), bf16),
            pltpu.VMEM((2, 2, 2, own, width // 2), bf16),
            pltpu.VMEM((2, 2, own, width // 2), bf16),
            pltpu.VMEM((2, own, width // 2), bf16),
            dma((2, 4)),
            dma((2, 4)),
            dma((2,)),
            pltpu.VMEM((STAGES, small_rows, width), f32),
            pltpu.VMEM((STAGES, small_rows, width), f32),
            dma((STAGES,)),
            dma((STAGES,)),
            half,
            half,
            half,
            dma((2,)),
            dma((2,)),
            pltpu.VMEM((8, width), f32),
            pltpu.VMEM((own, width), f32),
        ],
        compiler_params=params(collective_id=0, has_side_effects=True),
        cost_estimate=pl.CostEstimate(
            flops=12 * count * width * width, bytes_accessed=30 * count * width, transcendentals=0
        ),
        name="finish_all",
    )(
        rest,
        x,
        dy,
        h,
        dq,
        dk,
        dv,
        dwg,
        dgh.reshape(place + (own, width)),
        z,
        wq,
        wk,
        wv,
        *small,
        gx,
        gdy,
        norms,
    )


def unpack_kernel(
    z_ref,
    halo_z_ref,
    dx_ref,
    halo_dx_ref,
    gz_ref,
    ggrad_ref,
    first_ref,
    second_ref,
    third_ref,
    small_ref,
    layer_ref,
    gz_out,
    token_ref,
    ggrad_out,
    wq_ref,
    wk_ref,
    wv_ref,
    wo_ref,
    w1_ref,
    w2_ref,
    b1_ref,
    b2_ref,
    norms_ref,
    turned_ref,
):
    step = pl.program_id(0)
    last = pl.num_programs(0) - 1

    @pl.when(step < last)
    def _():
        layer_ref[0] = z_ref[...]
        token_ref[0] = dx_ref[...]

    @pl.when(step == last)
    def _():
        layer_ref[0] = halo_z_ref[...]
        token_ref[0] = halo_dx_ref[...].astype(f32)

    rows = wq_ref.shape[0]

    @pl.when(step == 0)
    def _():
        gz_out[0] = gz_ref[...]
        ggrad_out[0] = ggrad_ref[...]
        for ref, unit in ((wo_ref, 2), (wq_ref, 3), (wk_ref, 4), (wv_ref, 5)):
            ref[...] = third_ref[unit * rows : (unit + 1) * rows]
        chunks = w1_ref.shape[0] // rows
        for chunk in range(chunks):
            for ref, unit in ((first_ref, chunk), (second_ref, chunk - 2), (third_ref, chunk - 3)):
                if 0 <= unit < ref.shape[0] // (2 * rows):
                    break
            start = 2 * unit * rows
            w1_ref[chunk * rows : (chunk + 1) * rows] = ref[start : start + rows]
            part = ref[start + rows : start + 2 * rows].T
            for place in range(part.shape[0] // rows):
                spot = (place * chunks + chunk) * rows
                turned_ref[spot : spot + rows, :] = part[place * rows : (place + 1) * rows, :]
        w2_ref[...] = turned_ref[...].T
        pieces_in_row = small_ref.shape[1] // LANES
        hidden_rows = b1_ref.shape[0] // pieces_in_row
        for row in range(hidden_rows + 1):
            for piece in range(pieces_in_row):
                value = small_ref[row : row + 1, piece * LANES : (piece + 1) * LANES]
                if row < hidden_rows:
                    b1_ref[row * pieces_in_row + piece : row * pieces_in_row + piece + 1] = value
                else:
                    b2_ref[piece : piece + 1] = value
        norms_ref[...] = small_ref[hidden_rows + 1 : hidden_rows + 7]


def unpack(z, halo_z, dx, halo_dx, gz, ggrad, first, second, third, small, rows, hidden):
    count, width = z.shape
    own = gz.shape[0]
    lanes = first.shape[1]
    steps = count // HALF
    shapes = [
        ((1, count, width), bf16),
        ((1, own, width), bf16),
        ((1, count, width), f32),
        ((1, own, width), f32),
    ]
    shapes += [((rows, lanes), f32)] * 4
    shapes += [
        ((hidden // width * rows, lanes), f32),
        ((rows, hidden // width * lanes), f32),
        ((hidden // LANES, LANES), f32),
        ((width // LANES, LANES), f32),
        ((6, width), f32),
    ]
    tile = pl.BlockSpec((1, HALF, width), lambda i: (0, i, 0))
    return pl.pallas_call(
        unpack_kernel,
        grid=(steps,),
        in_specs=[
            pl.BlockSpec((HALF, width), lambda i: (jnp.minimum(i + 1, steps - 1), 0)),
            full(halo_z.shape),
            pl.BlockSpec((HALF, width), lambda i: (jnp.minimum(i, steps - 2), 0)),
            full(halo_dx.shape),
            full(gz.shape),
            full(ggrad.shape),
            full(first.shape),
            full(second.shape),
            full(third.shape),
            full(small.shape),
        ],
        out_specs=[
            tile if shape[1] == count else full(shape) for shape, unused in shapes
        ],
        out_shape=[jax.ShapeDtypeStruct(shape, kind) for shape, kind in shapes],
        scratch_shapes=[pltpu.VMEM((hidden // width * lanes, rows), f32)],
        compiler_params=params(),
        cost_estimate=pl.CostEstimate(
            flops=0, bytes_accessed=14 * count * width, transcendentals=0
        ),
        name="unpack",
    )(z, halo_z, dx, halo_dx, gz, ggrad, first, second, third, small)


def from_behind(value, axis, steps):
    count = lax.axis_size(axis)
    pairs = [(source, (source + steps) % count) for source in range(count)]
    return lax.ppermute(value, axis, pairs)


def pieces(value):
    first = lax.reduce_precision(value, 8, 7)
    second = lax.reduce_precision(value - first, 8, 7)
    return [first.astype(bf16), second.astype(bf16), (value - first - second).astype(bf16)]


def scatter_sum(value):
    half = lax.psum_scatter(value, "batch", scatter_dimension=1, tiled=True)
    part = lax.psum_scatter(half, "seq", scatter_dimension=0, tiled=True)
    return part.T.astype(f32)


def on_device(
    tokens,
    global_states,
    lengths,
    bucket_of,
    wq,
    wk,
    wv,
    wo,
    w1,
    b1,
    w2,
    b2,
    norm_params,
    cotangent,
    global_cotangent,
):
    rows = tokens.shape[1]
    width = tokens.shape[2]
    own = global_states.shape[1]
    seq_count = lax.axis_size("seq")
    seq_place = lax.axis_index("seq")
    group_rows = rows * seq_count
    own_start = seq_place * own
    first_of_slot = own_start % GLOBALS == 0
    place = jnp.stack(
        [
            lax.axis_index("batch"),
            seq_place,
            jnp.where(first_of_slot, own_start // GLOBALS, -1),
        ]
    ).astype(jnp.int32)
    scalars = (lengths, bucket_of, place)
    norms = [norm_params[i : i + 1] for i in range(6)]
    b2_rows = b2.reshape(-1, LANES)

    batch_count = lax.axis_size("batch")
    grid_of = None
    if seq_count == 16 and batch_count == 2 and 2 * own == GLOBALS and rows == 2 * BLOCK:
        grid_of = (seq_count, batch_count)

    if grid_of is None:
        arrived_tokens, arrived_grads = from_behind(
            (tokens[0, rows - HALF :], cotangent[0, rows - HALF :]), "seq", 1
        )
        x = jnp.concatenate([arrived_tokens, tokens[0, : rows - HALF]], 0)
        ct_head = arrived_grads
        all_states = lax.all_gather(global_states[0], "seq", axis=0, tiled=True)
        w1t = w1.T
        h, q, k, v = project_local(x, norms[0], norms[1], wq, wk, wv)
        gh, gq, gk, gv = project_global(
            scalars, rows, group_rows, all_states, norms[2], norms[3], wq, wk, wv
        )
    else:
        h, q, k, v, x, all_states, gh, gq, gk, gv, w1t = gather_project(
            tokens[0], global_states[0], w1, norm_params, wq, wk, wv
        )
        all_states, gh, gq, gk, gv = (
            value.reshape(-1, width) for value in (all_states, gh, gq, gk, gv)
        )
    far, far_stat, part, part_stat = slot_forward(scalars, rows, group_rows, q, k, v, gq, gk, gv)
    if grid_of is None:
        o, line = local_forward(
            False, scalars, rows, group_rows, q, k, v, far, far_stat, None, None
        )
        part_peak = part_stat[:, :, 0:2]
        peak = jnp.max(lax.all_gather(part_peak, "seq"), axis=0)
        factor = jnp.exp(part_peak - peak)
        scaled = part.reshape(SLOTS, PAIRS, 2, HEAD_DIM, GLOBALS).astype(f32) * factor[:, :, :, None]
        scaled = scaled.reshape(SLOTS, width, GLOBALS)
        scaled_total = (part_stat[:, :, 2:4] * factor).reshape(SLOTS, HEADS, GLOBALS)
        payload = jnp.concatenate(
            [scaled, scaled_total, jnp.zeros((SLOTS, 4, GLOBALS), f32)], 1
        ).transpose(0, 2, 1)
        sums = lax.psum_scatter(
            payload.astype(bf16).reshape(SLOTS * GLOBALS, -1), "seq", scatter_dimension=0, tiled=True
        ).astype(f32)
        own_total = sums[:, width : width + HEADS]
        all_peak = peak.reshape(SLOTS, HEADS, GLOBALS).transpose(0, 2, 1).reshape(-1, HEADS)
        own_peak = lax.dynamic_slice_in_dim(all_peak, own_start, own, 0)
        go = (
            (sums[:, :width].reshape(own, HEADS, HEAD_DIM) / own_total[:, :, None])
            .reshape(own, width)
            .astype(bf16)
        )
        gstat = own_peak + jnp.log(own_total)
    else:
        o, line, half_sum, half_stat = local_forward(
            True, scalars, rows, group_rows, q, k, v, far, far_stat, part, part_stat
        )

    z, dy, do, gz, gdy, gdo, dwo, db1, db2, dgain2, doffset2, *dws = branch(
        grid_of,
        x,
        o,
        cotangent[0],
        ct_head if grid_of is None else cotangent[0],
        global_states[0],
        go if grid_of is None else half_sum,
        gstat if grid_of is None else half_stat,
        global_cotangent[0],
        wo,
        w1t,
        b1,
        w2,
        b2_rows,
        norm_params,
    )
    if grid_of is None:
        gcentre = jnp.sum(
            (gdo.astype(f32) * go.astype(f32)).reshape(own, HEADS, HEAD_DIM), axis=-1
        )
        message = jnp.concatenate(
            [gdo]
            + pieces(gstat)
            + pieces(gcentre)
            + [jnp.zeros((own, LANES - 6 * HEADS), bf16)],
            axis=1,
        )
        everyone = lax.all_gather(message, "seq", axis=0, tiled=True)
        dqt, dk, dv, centre = local_backward(
            False, scalars, rows, group_rows, q, k, v, do, o, line, None, None, None, None
        )
    else:
        sum_first, last, message, rest = dws
        dqt, dk, dv, centre, everyone, sum_second, rest = local_backward(
            True, scalars, rows, group_rows, q, k, v, do, o, line, message, rest, last, dwo
        )
    dq, dk, dv, dwg, dgh, dnorm_global = slot_backward(
        scalars,
        rows,
        group_rows,
        q,
        k,
        v,
        do,
        line,
        centre,
        dqt,
        dk,
        dv,
        gq,
        gk,
        gv,
        everyone,
        all_states,
        gh,
        wq,
        wk,
        wv,
    )
    if grid_of is None:
        dx, dqkv, dnorm = project_back(x, dy, h, dq, dk, dv, dwg, wq, wk, wv, norms[0])
        back_z, back_grad = from_behind((z[:HALF], dx[:HALF].astype(bf16)), "seq", -1)
        layer_out = jnp.concatenate([z[HALF:], back_z], 0)
        token_grad = jnp.concatenate([dx[HALF:], back_grad.astype(f32)], 0)
        small = jnp.concatenate([db1, db2, dnorm[:2], dnorm_global[:2], dgain2, doffset2], 0)
        dgh = lax.psum_scatter(dgh, "seq", scatter_dimension=0, tiled=True).astype(f32)
        gunit, gscale = normalize_rows(global_states[0].astype(f32))
        global_grad = gdy + norm_back(gunit, gscale, norms[2], dgh)
        small = lax.psum(small, ("batch", "seq"))
        dw1, dw2 = dws
        weights = [scatter_sum(value) for value in (dqkv[0], dqkv[1], dqkv[2], dwo, dw1, dw2)]
    else:
        sum_third, small, global_grad, dx, halo_dx, halo_z = finish_all(
            rest,
            x,
            dy,
            h,
            dq,
            dk,
            dv,
            dwg,
            dgh,
            z,
            wq,
            wk,
            wv,
            (db1, db2, dnorm_global, dgain2, doffset2),
            global_states[0],
            gdy,
            norm_params,
        )
        results = unpack(
            z,
            halo_z,
            dx,
            halo_dx,
            gz,
            global_grad,
            sum_first,
            sum_second,
            sum_third,
            small,
            width // seq_count,
            w1.shape[1],
        )
        weights = [value.T for value in results[4:10]]
        biases = [value.reshape(-1) for value in results[10:12]]
        return (*results[:4], *weights, *biases, results[12])
    hidden_rows = w1.shape[1] // width
    return (
        layer_out[None],
        gz[None],
        token_grad[None],
        global_grad[None],
        *weights,
        small[:hidden_rows].reshape(-1),
        small[hidden_rows],
        small[hidden_rows + 1 : hidden_rows + 7],
    )


def solution(mesh):
    split = P("batch", "seq", None)
    return jax.shard_map(
        on_device,
        mesh=mesh,
        in_specs=(split, split) + (P(),) * 11 + (split, split),
        out_specs=(split,) * 4 + (P("batch", "seq"),) * 6 + (P(),) * 3,
        check_vma=False,
    )
```

```python
import functools

import jax
import jax.numpy as jnp
from jax import lax
from jax.experimental import pallas as pl
from jax.experimental.pallas import tpu as pltpu
from jax.sharding import PartitionSpec as P

HEADS = 12
HEAD_DIM = 64
PAIRS = HEADS // 2
LANES = 128
BLOCK = 512
HALF = 256
GLOBALS = 128
SLOTS = 8
FF_CHUNK = 768
TOGETHER = 3

norm_eps = 1e-05
masked_score = -1e30
query_scale = 0.125

SLOT_LANE = 16
GLOBAL_LANE = 32

f32 = jnp.float32
bf16 = jnp.bfloat16
VMEM_LIMIT = 60 * 1024 * 1024


def nn(left, right):
    return jnp.dot(left, right, preferred_element_type=f32)


def nt(left, right):
    return lax.dot_general(left, right, (((1,), (1,)), ((), ())), preferred_element_type=f32)


def tn(left, right):
    return lax.dot_general(left, right, (((0,), (0,)), ((), ())), preferred_element_type=f32)


def iota(shape, dim):
    return lax.broadcasted_iota(jnp.int32, shape, dim)


def stack_pair(pair):
    lane = iota((1, LANES), 1)
    low = jnp.where(lane < HEAD_DIM, 1.0, 0.0).astype(bf16)
    high = jnp.where(lane < HEAD_DIM, 0.0, 1.0).astype(bf16)
    return jnp.concatenate([pair * low, pair * high], axis=0)


def read_edges(lengths, bucket_of, place, edges):
    bucket = bucket_of[place[0]]
    total = jnp.int32(0)
    edges[0] = total
    for slot in range(SLOTS):
        total = total + lengths[bucket, slot]
        edges[slot + 1] = total


def block_start(place, rows, block):
    return place[1] * rows + block * BLOCK - HALF


def slot_present(slot, place, edges, rows, group_rows, block):
    low = edges[slot]
    high = edges[slot + 1]
    found = jnp.bool_(False)
    for part in range(BLOCK // HALF):
        start = block_start(place, rows, block) + part * HALF
        start = jnp.where(start < 0, start + group_rows, start)
        found = found | ((high > low) & (low < start + HALF) & (high > start))
    return found


def row_numbers(place, edges, rows, group_rows, block):
    place_in = block_start(place, rows, block) + iota((BLOCK, LANES), 0)
    wrapped = place_in < 0
    token = jnp.where(wrapped, place_in + group_rows, place_in)
    slot = jnp.zeros((BLOCK, LANES), jnp.int32)
    for j in range(SLOTS):
        slot = slot + jnp.where(edges[j + 1] <= token, 1, 0)
    return slot, slot + jnp.where(wrapped, SLOTS, 0)


def key_extra(slot, segment):
    lane = iota((BLOCK, LANES), 1)
    extra = jnp.where((lane < SLOT_LANE) & (lane != segment), masked_score, 0.0)
    return jnp.where(lane == GLOBAL_LANE + slot, 1.0, extra)


def query_extra(slot, segment):
    lane = iota((BLOCK, LANES), 1)
    return jnp.where((lane == segment) | (lane == SLOT_LANE + slot), 1.0, 0.0)


def global_key_extra(slot):
    lane = iota((GLOBALS, LANES), 1)
    inside = (lane >= SLOT_LANE) & (lane < SLOT_LANE + SLOTS)
    extra = jnp.where(inside & (lane != SLOT_LANE + slot), masked_score, 0.0)
    return jnp.where(lane == GLOBAL_LANE + slot, 1.0, extra)


def global_query_extra(slot):
    lane = iota((GLOBALS, LANES), 1)
    inside = (lane >= GLOBAL_LANE) & (lane < GLOBAL_LANE + SLOTS)
    return jnp.where(inside & (lane != GLOBAL_LANE + slot), masked_score, 0.0)


def normalize_rows(values):
    mean = jnp.mean(values, axis=-1, keepdims=True)
    centered = values - mean
    variance = jnp.mean(centered * centered, axis=-1, keepdims=True)
    scale = lax.rsqrt(variance + norm_eps)
    return centered * scale, scale


def norm_back(unit, scale, gain, upstream):
    inner = upstream * gain
    along = jnp.mean(inner * unit, axis=-1, keepdims=True)
    return scale * (inner - jnp.mean(inner, axis=-1, keepdims=True) - unit * along)


def gelu_parts(value):
    decay = jnp.exp(-0.5 * value * value)
    step = 1.0 / (1.0 + (0.3275911 * 0.7071067811865476) * jnp.abs(value))
    series = 1.061405429 * step - 1.453152027
    series = series * step + 1.421413741
    series = series * step - 0.284496736
    series = series * step + 0.254829592
    tail = (0.5 * series) * step * decay
    area = jnp.where(value >= 0.0, 1.0 - tail, tail)
    return area, decay * 0.3989422804014327


def full(shape):
    return pl.BlockSpec(shape, lambda *unused: (0,) * len(shape))


def once(shape):
    return pl.BlockSpec(
        shape, lambda *unused: (0,) * len(shape), pipeline_mode=pl.Buffered(buffer_count=1)
    )


def params(**more):
    return pltpu.CompilerParams(vmem_limit_bytes=VMEM_LIMIT, **more)


STAGES = 5
MESH = pl.DeviceIdType.MESH
WEIGHTS = (("core", 1), ("y", 2), ("z0", 4), ("z1", 8))


def my_place():
    batch = lax.axis_index("batch")
    seq = lax.axis_index("seq")
    bits = {"x": batch}
    partners = {"x": (1 - batch, seq)}
    for name, weight in WEIGHTS:
        bits[name] = (seq // weight) % 2
        partners[name] = (batch, seq + weight - 2 * weight * bits[name])
    return bits, partners


def meet(devices):
    barrier = pltpu.get_barrier_semaphore()
    for device in devices:
        pl.semaphore_signal(barrier, inc=1, device_id=device, device_id_type=MESH)
    pl.semaphore_wait(barrier, len(devices))


def remote(source, target, send, recv, device):
    return pltpu.make_async_remote_copy(
        src_ref=source,
        dst_ref=target,
        send_sem=send,
        recv_sem=recv,
        device_id=device,
        device_id_type=MESH,
    )


class RowGather:
    def __init__(self, ref, cut, send_sem, recv_sem, bits, partners):
        self.ref = ref
        self.cut = cut
        self.send_sem = send_sem
        self.recv_sem = recv_sem
        self.bits = bits
        self.partners = partners

    def copies(self, number):
        core, y, z0, z1 = (self.bits[name] for name in ("core", "y", "z0", "z1"))
        ref = self.ref
        rows = pl.ds(0, ref.shape[4])
        left = pl.ds(0, self.cut)
        right = pl.ds(self.cut, ref.shape[5] - self.cut)
        if number == 0:
            moves = [
                (ref.at[z1, z0, y, core, rows, left], "z1"),
                (ref.at[z1, z0, y, core, rows, right], "z1"),
            ]
        elif number == 1:
            moves = [
                (ref.at[:, z0, y, core, rows, left], "z0"),
                (ref.at[:, z0, y, core, rows, right], "y"),
            ]
        elif number == 2:
            moves = [
                (ref.at[:, :, y, core, rows, left], "y"),
                (ref.at[:, z0, :, core, rows, right], "z0"),
            ]
        else:
            moves = [
                (ref.at[:, :, :, core, rows, left], "core"),
                (ref.at[:, :, :, core, rows, right], "core"),
            ]
        return [
            remote(
                part,
                part,
                self.send_sem.at[number, side],
                self.recv_sem.at[number, side],
                self.partners[name],
            )
            for side, (part, name) in enumerate(moves)
        ]

    def begin(self, number=0):
        for copy in self.copies(number):
            copy.start()

    def advance(self, number):
        for copy in self.copies(number):
            copy.wait_recv()
        if number < 3:
            self.begin(number + 1)

    def end(self, first=0):
        for number in range(first, 4):
            for copy in self.copies(number):
                copy.wait_send()


X_FIRST = ("core", "x", "y", "z0", "z1")
Y_FIRST = ("core", "y", "x", "z0", "z1")
X_Z_FIRST = ("core", "x", "z0", "y", "z1")
Z_FIRST = ("core", "z0", "x", "z1", "y")
AXES = ("z1", "z0", "y", "core", "x")


class HalvingSum:
    def __init__(
        self, orders, sources, landings, own, send_sem, recv_sem, own_sem, put, bits, partners
    ):
        self.orders = orders
        self.sources = sources
        self.landings = landings
        self.own = own
        self.send_sem = send_sem
        self.recv_sem = recv_sem
        self.own_sem = own_sem
        self.put = put
        self.bits = bits
        self.partners = partners

    def part(self, unit, stage, other):
        order = self.orders[unit]
        name = order[stage]
        side = 1 - self.bits[name] if other else self.bits[name]
        if stage == 0:
            if not other and self.own is not None:
                return self.own.at[unit]
            return self.sources[unit](side)
        left = [axis for axis in AXES if axis in order[stage:]]
        index = (slice(None),) * left.index(name) + (side,)
        return self.landings[stage - 1].at[unit].at[index]

    def copy(self, unit, stage):
        return remote(
            self.part(unit, stage, True),
            self.landings[stage].at[unit],
            self.send_sem.at[unit, stage],
            self.recv_sem.at[unit, stage],
            self.partners[self.orders[unit][stage]],
        )

    def own_copy(self, unit):
        return pltpu.make_async_copy(
            self.sources[unit](self.bits["core"]), self.own.at[unit], self.own_sem.at[unit]
        )

    def begin(self, unit):
        if self.own is not None:
            self.own_copy(unit).start()
        self.copy(unit, 0).start()

    def advance(self, unit, stage, stop=False):
        if stage == 0 and self.own is not None:
            self.own_copy(unit).wait()
        self.copy(unit, stage).wait_recv()
        landing = self.landings[stage].at[unit]
        kept = self.part(unit, stage, False)
        if stage < len(self.orders[unit]) - 1:
            add_into(landing, kept)
            if not stop:
                self.copy(unit, stage + 1).start()
        else:
            self.put(unit, landing[...].astype(f32) + kept[...].astype(f32))

    def sent(self, unit, stage):
        self.copy(unit, stage).wait_send()


def put_rows(ref, rows):
    def put(unit, value):
        ref[unit * rows : (unit + 1) * rows] = value

    return put


def add_into(target, more):
    def one(i, carry):
        target[i] = target[i] + more[i]
        return carry

    lax.fori_loop(0, target.shape[0], one, 0)


def sum_scratch(units, rows, lanes, with_own):
    piece = (rows, lanes)
    dma = pltpu.SemaphoreType.DMA
    shapes = [pltpu.VMEM((units, 2, 2, 2, 2) + piece, bf16)] if with_own else []
    shapes += [
        pltpu.VMEM((units, 2, 2, 2, 2) + piece, bf16),
        pltpu.VMEM((units, 2, 2, 2) + piece, bf16),
        pltpu.VMEM((units, 2, 2) + piece, bf16),
        pltpu.VMEM((units, 2) + piece, bf16),
        pltpu.VMEM((units,) + piece, bf16),
        dma((units, STAGES)),
        dma((units, STAGES)),
    ]
    return shapes + ([dma((units,))] if with_own else [])


def project_rows(rows_ref, gain_ref, offset_ref, wq_ref, wk_ref, wv_ref, outs):
    unit, unused = normalize_rows(rows_ref[...].astype(f32))
    normed = (unit * gain_ref[...] + offset_ref[...]).astype(bf16)
    outs[0][...] = normed
    outs[1][...] = (nn(normed, wq_ref[...]) * query_scale).astype(bf16)
    outs[2][...] = nn(normed, wk_ref[...]).astype(bf16)
    outs[3][...] = nn(normed, wv_ref[...]).astype(bf16)


def project_local_kernel(rows_ref, gain_ref, offset_ref, wq_ref, wk_ref, wv_ref, *outs):
    project_rows(rows_ref, gain_ref, offset_ref, wq_ref, wk_ref, wv_ref, outs)


def project_local(rows, gain, offset, wq, wk, wv):
    count, width = rows.shape
    tile = pl.BlockSpec((BLOCK, width), lambda i: (i, 0))
    return pl.pallas_call(
        project_local_kernel,
        grid=(count // BLOCK,),
        in_specs=[tile, full((1, width)), full((1, width))] + [once((width, width))] * 3,
        out_specs=[tile] * 4,
        out_shape=[jax.ShapeDtypeStruct((count, width), bf16)] * 4,
        compiler_params=params(),
        cost_estimate=pl.CostEstimate(
            flops=6 * count * width * width, bytes_accessed=12 * count * width, transcendentals=0
        ),
        name="project_local",
    )(rows, gain, offset, wq, wk, wv)


def gather_project_kernel(
    tokens_ref,
    states_ref,
    w1_ref,
    norms_ref,
    wq_in,
    wk_in,
    wv_in,
    h_out,
    q_out,
    k_out,
    v_out,
    x_out,
    all_out,
    gh_out,
    gq_out,
    gk_out,
    gv_out,
    w1t_out,
    wq_ref,
    wk_ref,
    wv_ref,
    x_ref,
    all_ref,
    local_ref,
    global_ref,
    w1s_ref,
    w1t_ref,
    halo_send,
    halo_recv,
    load_sem,
    store_sem,
    gstore_sem,
    more_sem,
    send_sem,
    recv_sem,
):
    bits, partners = my_place()
    batch = lax.axis_index("batch")
    seq = lax.axis_index("seq")
    places = lax.axis_size("seq")
    after = (batch, lax.rem(seq + 1, places))
    before = (batch, lax.rem(seq + places - 1, places))
    rows, width = tokens_ref.shape
    own = states_ref.shape[0]
    core, y, z0, z1 = (bits[name] for name in ("core", "y", "z0", "z1"))
    start = pl.ds(0, HALF)
    most = pl.ds(0, rows - HALF)
    end = pl.ds(rows - HALF, HALF)
    shifted = pl.ds(HALF, rows - HALF)
    loads = [
        pltpu.make_async_copy(source, target, load_sem.at[number])
        for number, (source, target) in enumerate(
            (
                (tokens_ref.at[most], x_ref.at[shifted]),
                (wq_in, wq_ref),
                (wk_in, wk_ref),
                (wv_in, wv_ref),
                (w1_ref, w1s_ref),
            )
        )
    ]
    for load in loads:
        load.start()
    all_ref[z1, z0, y, core] = states_ref[...]
    meet([partners[name] for name, unused in WEIGHTS] + [before, after])
    halo = remote(tokens_ref.at[end], x_ref.at[start], halo_send, halo_recv, after)
    gather = RowGather(all_ref, width // 2, send_sem, recv_sem, bits, partners)
    gather.begin()
    halo.start()

    outs = (h_out, q_out, k_out, v_out)

    def stores(index):
        at = pl.ds(index * HALF, HALF)
        return [
            pltpu.make_async_copy(local_ref.at[which, at], out.at[at], store_sem.at[which, index])
            for which, out in enumerate(outs)
        ]

    def project(index):
        at = pl.ds(index * HALF, HALF)
        project_rows(
            x_ref.at[at],
            norms_ref.at[0:1],
            norms_ref.at[1:2],
            wq_ref,
            wk_ref,
            wv_ref,
            [local_ref.at[which, at] for which in range(4)],
        )
        for store in stores(index):
            store.start()

    for number in range(4):
        loads[number].wait()
    tiles = rows // HALF
    def turn(i, carry):
        at = pl.ds(pl.multiple_of(i * HALF, HALF), HALF)
        w1t_ref[at, :] = w1s_ref[:, at].T
        return carry

    project(1)
    project(2)
    gather.advance(0)
    for index in range(3, tiles):
        project(index)
    loads[4].wait()
    turns = w1t_ref.shape[0] // HALF
    lax.fori_loop(0, turns // 2, turn, 0)
    gather.advance(1)
    lax.fori_loop(turns // 2, turns, turn, 0)
    w1t_store = pltpu.make_async_copy(w1t_ref, w1t_out, more_sem.at[1])
    w1t_store.start()
    gather.advance(2)

    gouts = (gh_out, gq_out, gk_out, gv_out)

    def gstores(first, side):
        return [
            pltpu.make_async_copy(
                global_ref.at[which, first, :, :, side],
                out.at[first, :, :, side],
                gstore_sem.at[which, first, number],
            )
            for which, out in enumerate(gouts)
            for number in ((0 if side is core else 1),)
        ]

    def project_states(side):
        for first in range(2):
            piece = all_ref[first, :, :, side].reshape(4 * own, width)
            unit, unused = normalize_rows(piece.astype(f32))
            normed = (unit * norms_ref[2:3] + norms_ref[3:4]).astype(bf16)
            values = (
                normed,
                (nn(normed, wq_ref[...]) * query_scale).astype(bf16),
                nn(normed, wk_ref[...]).astype(bf16),
                nn(normed, wv_ref[...]).astype(bf16),
            )
            for which, value in enumerate(values):
                global_ref[which, first, :, :, side] = value.reshape(2, 2, own, width)
            for store in gstores(first, side):
                store.start()

    other = 1 - core
    project_states(core)
    gather.advance(3)
    all_store = pltpu.make_async_copy(all_ref, all_out, more_sem.at[2])
    all_store.start()
    project_states(other)
    halo.wait_recv()
    x_store = pltpu.make_async_copy(x_ref, x_out, more_sem.at[0])
    x_store.start()
    project(0)

    for index in range(tiles):
        for store in stores(index):
            store.wait()
    for side in (core, other):
        for first in range(2):
            for store in gstores(first, side):
                store.wait()
    x_store.wait()
    w1t_store.wait()
    all_store.wait()
    halo.wait_send()
    gather.end()


def gather_project(tokens, states, w1, norms, wq, wk, wv):
    rows, width = tokens.shape
    own = states.shape[0]
    vmem = pl.BlockSpec(memory_space=pltpu.VMEM)
    anywhere = pl.BlockSpec(memory_space=pl.ANY)
    dma = pltpu.SemaphoreType.DMA
    local = jax.ShapeDtypeStruct((rows, width), bf16)
    glob = jax.ShapeDtypeStruct((2, 2, 2, 2, own, width), bf16)
    turned = (w1.shape[1], width)
    weight = pltpu.VMEM((width, width), bf16)
    return pl.pallas_call(
        gather_project_kernel,
        in_specs=[anywhere, vmem, anywhere, vmem] + [anywhere] * 3,
        out_specs=[anywhere] * 11,
        out_shape=[local] * 5 + [glob] * 5 + [jax.ShapeDtypeStruct(turned, bf16)],
        scratch_shapes=[
            weight,
            weight,
            weight,
            pltpu.VMEM((rows, width), bf16),
            pltpu.VMEM(glob.shape, bf16),
            pltpu.VMEM((4, rows, width), bf16),
            pltpu.VMEM((4,) + glob.shape, bf16),
            pltpu.VMEM(w1.shape, bf16),
            pltpu.VMEM(turned, bf16),
            dma,
            dma,
            dma((5,)),
            dma((4, rows // HALF)),
            dma((4, 2, 2)),
            dma((3,)),
            dma((4, 2)),
            dma((4, 2)),
        ],
        compiler_params=params(collective_id=1, has_side_effects=True),
        cost_estimate=pl.CostEstimate(
            flops=6 * (rows + 16 * own) * width * width,
            bytes_accessed=24 * rows * width,
            transcendentals=0,
        ),
        name="gather_project",
    )(tokens, states, w1, norms, wq, wk, wv)


def project_global_kernel(
    rows_count,
    group_rows,
    lengths,
    bucket_of,
    place,
    rows_ref,
    gain_ref,
    offset_ref,
    wq_ref,
    wk_ref,
    wv_ref,
    h_ref,
    q_ref,
    k_ref,
    v_ref,
    edges,
):
    slot = pl.program_id(0)

    @pl.when(slot == 0)
    def _():
        read_edges(lengths, bucket_of, place, edges)

    needed = slot == place[2]
    for block in range(rows_count // BLOCK):
        needed = needed | slot_present(slot, place, edges, rows_count, group_rows, block)

    @pl.when(needed)
    def _():
        project_rows(
            rows_ref, gain_ref, offset_ref, wq_ref, wk_ref, wv_ref, (h_ref, q_ref, k_ref, v_ref)
        )


def project_global(scalars, rows_count, group_rows, rows, gain, offset, wq, wk, wv):
    count, width = rows.shape
    tile = pl.BlockSpec((GLOBALS, width), lambda i, *unused: (i, 0))
    return pl.pallas_call(
        functools.partial(project_global_kernel, rows_count, group_rows),
        grid_spec=pltpu.PrefetchScalarGridSpec(
            num_scalar_prefetch=3,
            grid=(SLOTS,),
            in_specs=[tile, full((1, width)), full((1, width))] + [once((width, width))] * 3,
            out_specs=[tile] * 4,
            scratch_shapes=[pltpu.SMEM((16,), jnp.int32)],
        ),
        out_shape=[jax.ShapeDtypeStruct((count, width), bf16)] * 4,
        compiler_params=params(),
        cost_estimate=pl.CostEstimate(
            flops=6 * 256 * width * width, bytes_accessed=12 * count * width, transcendentals=0
        ),
        name="project_global",
    )(*scalars, rows, gain, offset, wq, wk, wv)


def block_columns(place, edges, rows, group_rows, block, step, blocks, query_columns, key_columns):
    @pl.when(step < blocks)
    def _():
        slot_of, segment = row_numbers(place, edges, rows, group_rows, block)
        query_columns[block] = query_extra(slot_of, segment).astype(bf16)
        key_columns[block] = key_extra(slot_of, segment).astype(bf16)


def slot_line(place, edges, rows, group_rows, block):
    token = block_start(place, rows, block) + iota((1, BLOCK), 1)
    token = jnp.where(token < 0, token + group_rows, token)
    slot = jnp.zeros((1, BLOCK), jnp.int32)
    for j in range(SLOTS):
        slot = slot + jnp.where(edges[j + 1] <= token, 1, 0)
    return slot


def side_by_side(stacked):
    return stacked[:HEAD_DIM, : stacked.shape[1] // 2], stacked[HEAD_DIM:, stacked.shape[1] // 2 :]


def slot_forward_kernel(
    rows_count,
    group_rows,
    lengths,
    bucket_of,
    place,
    q_ref,
    k_ref,
    v_ref,
    gq_ref,
    gk_ref,
    gv_ref,
    far_ref,
    far_stat_ref,
    part_ref,
    part_stat_ref,
    edges,
    query_columns,
    key_columns,
    keys_ref,
    queries_ref,
    sum_ref,
    far_sum,
):
    group = pl.program_id(0)
    block = pl.program_id(1)
    blocks = rows_count // BLOCK
    step = group * blocks + block
    together = range(TOGETHER)

    @pl.when(step == 0)
    def _():
        read_edges(lengths, bucket_of, place, edges)

    @pl.when(block == 0)
    def _():
        sum_ref[...] = jnp.zeros_like(sum_ref)
        part_stat_ref[...] = jnp.broadcast_to(
            jnp.where(iota((8, GLOBALS), 0) < 2, masked_score, 0.0), part_stat_ref.shape
        )

    block_columns(
        place, edges, rows_count, group_rows, block, step, blocks, query_columns, key_columns
    )
    extra = query_columns[block]
    for which in together:
        lanes = pl.ds(which * LANES, LANES)
        keys_ref[which, :, :LANES] = k_ref[:, lanes]
        keys_ref[which, :, LANES:] = key_columns[block]
        queries_ref[which, :, :LANES] = stack_pair(q_ref[:, lanes])
        queries_ref[which, :BLOCK, LANES:] = extra
        queries_ref[which, BLOCK:, LANES:] = extra
    line = slot_line(place, edges, rows_count, group_rows, block)
    both_lines = jnp.concatenate([line, line], 1)

    def add(slot, keys_of, values_of):
        at = pl.ds(pl.multiple_of(slot * GLOBALS, GLOBALS), GLOBALS)
        extra = global_query_extra(slot).astype(bf16)
        for which in together:
            lanes = pl.ds(which * LANES, LANES)
            queries = jnp.concatenate(
                [stack_pair(gq_ref[at, lanes]), jnp.concatenate([extra, extra], 0)], axis=1
            )
            score = nt(keys_of(which), queries)
            stat = part_stat_ref[slot, which]
            old = jnp.concatenate([stat[0:1], stat[1:2]], axis=1)
            peak = jnp.maximum(old, jnp.max(score, axis=0, keepdims=True))
            weights = jnp.exp(score - peak)
            keep = jnp.exp(old - peak)
            total = jnp.concatenate([stat[2:3], stat[3:4]], axis=1) * keep + jnp.sum(
                weights, axis=0, keepdims=True
            )
            part_stat_ref[slot, which] = jnp.concatenate(
                [
                    peak[:, :GLOBALS],
                    peak[:, GLOBALS:],
                    total[:, :GLOBALS],
                    total[:, GLOBALS:],
                    jnp.zeros((4, GLOBALS), f32),
                ],
                axis=0,
            )
            low, high = side_by_side(tn(values_of(which), weights.astype(bf16)))
            sums = sum_ref.at[which, slot]
            sums[:HEAD_DIM] = sums[:HEAD_DIM] * keep[:, :GLOBALS] + low
            sums[HEAD_DIM:] = sums[HEAD_DIM:] * keep[:, GLOBALS:] + high

    far_sum[...] = jnp.zeros_like(far_sum)
    far_stat_ref[...] = jnp.zeros_like(far_stat_ref)

    def one_slot(slot, carry):
        @pl.when(slot_present(slot, place, edges, rows_count, group_rows, block))
        def _():
            add(
                slot,
                lambda which: keys_ref[which],
                lambda which: v_ref[:, pl.ds(which * LANES, LANES)],
            )
            at = pl.ds(pl.multiple_of(slot * GLOBALS, GLOBALS), GLOBALS)
            columns = global_key_extra(slot).astype(bf16)
            mine = both_lines == slot
            here = line == slot
            for which in together:
                lanes = pl.ds(which * LANES, LANES)
                slot_keys = jnp.concatenate([gk_ref[at, lanes], columns], 1)
                score = nt(slot_keys, queries_ref[which])
                peak = jnp.max(score, axis=0, keepdims=True)
                weights = jnp.exp(score - peak)
                total = jnp.sum(weights, axis=0, keepdims=True)
                stat = far_stat_ref.at[which, 0]
                stat[0:1] = jnp.where(mine, peak, stat[0:1])
                stat[1:2] = jnp.where(mine, total, stat[1:2])
                low, high = side_by_side(tn(gv_ref[at, lanes], weights.astype(bf16)))
                first = pl.ds(which * LANES, HEAD_DIM)
                second = pl.ds(which * LANES + HEAD_DIM, HEAD_DIM)
                far_sum[first] = jnp.where(here, low, far_sum[first])
                far_sum[second] = jnp.where(here, high, far_sum[second])

        return carry

    lax.fori_loop(0, SLOTS, one_slot, 0)
    far_ref[...] = far_sum[...].astype(bf16)

    @pl.when((block == blocks - 1) & (place[2] >= 0))
    def _():
        slot = place[2]
        at = pl.ds(pl.multiple_of(slot * GLOBALS, GLOBALS), GLOBALS)
        columns = global_key_extra(slot).astype(bf16)
        add(
            slot,
            lambda which: jnp.concatenate(
                [gk_ref[at, pl.ds(which * LANES, LANES)], columns], axis=1
            ),
            lambda which: gv_ref[at, pl.ds(which * LANES, LANES)],
        )

    @pl.when(block == blocks - 1)
    def _():
        for which in together:
            part_ref[:, which] = sum_ref[which].astype(bf16)


def line_spec(pairs=1):
    return pl.BlockSpec((pairs, 1, 8, 2 * BLOCK), lambda p, b, *unused: (p, b, 0, 0))


def column_scratch(blocks):
    return [pltpu.SMEM((16,), jnp.int32)] + [pltpu.VMEM((blocks, BLOCK, LANES), bf16)] * 2


def slot_forward(scalars, rows_count, group_rows, q, k, v, gq, gk, gv):
    blocks = rows_count // BLOCK
    all_globals, width = gq.shape
    block_spec = pl.BlockSpec((BLOCK, TOGETHER * LANES), lambda p, b, *unused: (b, p))
    pair_spec = pl.BlockSpec((all_globals, TOGETHER * LANES), lambda p, b, *unused: (0, p))
    return pl.pallas_call(
        functools.partial(slot_forward_kernel, rows_count, group_rows),
        grid_spec=pltpu.PrefetchScalarGridSpec(
            num_scalar_prefetch=3,
            grid=(PAIRS // TOGETHER, blocks),
            in_specs=[block_spec] * 3 + [pair_spec] * 3,
            out_specs=[
                pl.BlockSpec((TOGETHER * LANES, BLOCK), lambda p, b, *unused: (p, b)),
                line_spec(TOGETHER),
                pl.BlockSpec((SLOTS, TOGETHER, LANES, GLOBALS), lambda p, b, *unused: (0, p, 0, 0)),
                pl.BlockSpec((SLOTS, TOGETHER, 8, GLOBALS), lambda p, b, *unused: (0, p, 0, 0)),
            ],
            scratch_shapes=column_scratch(blocks)
            + [
                pltpu.VMEM((TOGETHER, BLOCK, 2 * LANES), bf16),
                pltpu.VMEM((TOGETHER, 2 * BLOCK, 2 * LANES), bf16),
                pltpu.VMEM((TOGETHER, SLOTS, LANES, GLOBALS), f32),
                pltpu.VMEM((TOGETHER * LANES, BLOCK), f32),
            ],
        ),
        out_shape=[
            jax.ShapeDtypeStruct((width, rows_count), bf16),
            jax.ShapeDtypeStruct((PAIRS, blocks, 8, 2 * BLOCK), f32),
            jax.ShapeDtypeStruct((SLOTS, PAIRS, LANES, GLOBALS), bf16),
            jax.ShapeDtypeStruct((SLOTS, PAIRS, 8, GLOBALS), f32),
        ],
        compiler_params=params(),
        cost_estimate=pl.CostEstimate(
            flops=8 * 4 * rows_count * GLOBALS * width,
            bytes_accessed=20 * all_globals * width,
            transcendentals=2 * HEADS * rows_count * GLOBALS,
        ),
        name="slot_forward",
    )(*scalars, q, k, v, gq, gk, gv)


def merge_parts(stat, sums, more_stat, more_sums):
    peak = jnp.maximum(stat[0:2], more_stat[0:2])
    keep = jnp.exp(stat[0:2] - peak)
    take = jnp.exp(more_stat[0:2] - peak)
    total = stat[2:4] * keep + more_stat[2:4] * take
    low = sums[:HEAD_DIM].astype(f32) * keep[0:1] + more_sums[:HEAD_DIM].astype(f32) * take[0:1]
    high = sums[HEAD_DIM:].astype(f32) * keep[1:2] + more_sums[HEAD_DIM:].astype(f32) * take[1:2]
    return (
        jnp.concatenate([peak, total, jnp.zeros((4, GLOBALS), f32)], 0),
        jnp.concatenate([low, high], 0),
    )


class SlotSum:
    ORDER = ("core", "y", "z0", "z1")

    def __init__(self, source, sums, stats, send_sem, recv_sem, bits, partners):
        self.source = source
        self.sums = sums
        self.stats = stats
        self.send_sem = send_sem
        self.recv_sem = recv_sem
        self.bits = bits
        self.partners = partners

    def held(self, stage, other):
        bit = self.bits[self.ORDER[stage]]
        side = 1 - bit if other else bit
        if stage == 0:
            return self.source(side)
        index = ((), (slice(None), slice(None)), (slice(None),), ())[stage] + (side,)
        return self.sums[stage - 1].at[index], self.stats[stage - 1].at[index]

    def copies(self, stage):
        partner = self.partners[self.ORDER[stage]]
        sums, stat = self.held(stage, True)
        return (
            remote(
                sums,
                self.sums[stage],
                self.send_sem.at[stage, 0],
                self.recv_sem.at[stage, 0],
                partner,
            ),
            remote(
                stat,
                self.stats[stage],
                self.send_sem.at[stage, 1],
                self.recv_sem.at[stage, 1],
                partner,
            ),
        )

    def begin(self, stage):
        for copy in self.copies(stage):
            copy.start()

    def merge(self, stage, kept=None):
        for copy in self.copies(stage):
            copy.wait_recv()
        sums, stat = self.held(stage, False) if kept is None else kept
        lead = self.sums[stage].shape[:-3]
        total = 1
        for size in lead:
            total = total * size

        def one(number, carry):
            index = []
            left = number
            for size in reversed(lead):
                index.append(left % size)
                left = left // size
            index = tuple(reversed(index))
            for which in range(PAIRS // 2):
                spot = index + (which,)
                new_stat, new_sums = merge_parts(
                    self.stats[stage][spot], self.sums[stage][spot], stat[spot], sums[spot]
                )
                self.stats[stage][spot] = new_stat
                self.sums[stage][spot] = new_sums.astype(bf16)
            return carry

        lax.fori_loop(0, total, one, 0)

    def sent(self, stage):
        for copy in self.copies(stage):
            copy.wait_send()


def local_forward_kernel(
    talk,
    rows_count,
    group_rows,
    lengths,
    bucket_of,
    place,
    q_ref,
    k_ref,
    v_ref,
    far_ref,
    far_stat_ref,
    *refs,
):
    if talk:
        part_ref, part_stat_ref = refs[:2]
        o_ref, line_ref, half_ref, half_stat_ref = refs[2:6]
        own_ref, own_stat_ref = refs[6:8]
        sums_refs = refs[8:10]
        stat_refs = refs[10:12]
        edges, query_columns, key_columns, send_sem, recv_sem, own_sem = refs[12:]
    else:
        o_ref, line_ref, edges, query_columns, key_columns = refs
    pair = pl.program_id(0)
    block = pl.program_id(1)
    blocks = rows_count // BLOCK
    step = pair * blocks + block

    @pl.when(step == 0)
    def _():
        read_edges(lengths, bucket_of, place, edges)

    if talk:
        bits, partners = my_place()
        slot_sum = SlotSum(
            lambda side: (part_ref.at[:, :, :, side], part_stat_ref.at[:, :, :, side]),
            sums_refs,
            stat_refs,
            send_sem,
            recv_sem,
            bits,
            partners,
        )
        own_parts = slot_sum.held(0, False)
        own_copies = [
            pltpu.make_async_copy(own_parts[0], own_ref, own_sem.at[0]),
            pltpu.make_async_copy(own_parts[1], own_stat_ref, own_sem.at[1]),
        ]

        @pl.when(step == 0)
        def _():
            meet([partners["core"], partners["y"]])
            for copy in own_copies:
                copy.start()
            slot_sum.begin(0)

        @pl.when(step == 3)
        def _():
            for copy in own_copies:
                copy.wait()
            slot_sum.merge(0, (own_ref, own_stat_ref))
            slot_sum.begin(1)

        @pl.when(step == PAIRS * blocks - 1)
        def _():
            slot_sum.merge(1)
            half_ref[...] = sums_refs[1][...]
            half_stat_ref[...] = stat_refs[1][...]
            slot_sum.sent(0)
            slot_sum.sent(1)

    block_columns(
        place, edges, rows_count, group_rows, block, step, blocks, query_columns, key_columns
    )
    extra = query_columns[block]
    queries = jnp.concatenate(
        [stack_pair(q_ref[...]), jnp.concatenate([extra, extra], 0)], axis=1
    )
    keys = jnp.concatenate([k_ref[...], key_columns[block]], axis=1)
    score = nt(keys, queries)
    far_peak = far_stat_ref[0, 0, 0:1]
    peak = jnp.maximum(jnp.max(score, axis=0, keepdims=True), far_peak)
    weights = jnp.exp(score - peak)
    far_keep = jnp.exp(far_peak - peak)
    total = jnp.sum(weights, axis=0, keepdims=True) + far_stat_ref[0, 0, 1:2] * far_keep
    low, high = side_by_side(tn(v_ref[...], weights.astype(bf16)))
    low = (low + far_ref[:HEAD_DIM] * far_keep[:, :BLOCK]) / total[:, :BLOCK]
    high = (high + far_ref[HEAD_DIM:] * far_keep[:, BLOCK:]) / total[:, BLOCK:]
    o_ref[...] = jnp.concatenate([low, high], 0).T.astype(bf16)
    line_ref[0, 0] = jnp.broadcast_to(peak + jnp.log(total), (8, 2 * BLOCK))


def local_forward(
    talk, scalars, rows_count, group_rows, q, k, v, far, far_stat, part, part_stat
):
    blocks = rows_count // BLOCK
    width = q.shape[1]
    block_spec = pl.BlockSpec((BLOCK, LANES), lambda p, b, *unused: (b, p))
    operands = [q, k, v, far, far_stat]
    in_specs = [block_spec] * 3 + [
        pl.BlockSpec((LANES, BLOCK), lambda p, b, *unused: (p, b)),
        line_spec(),
    ]
    out_specs = [block_spec, line_spec()]
    out_shape = [
        jax.ShapeDtypeStruct((rows_count, width), bf16),
        jax.ShapeDtypeStruct((PAIRS, blocks, 8, 2 * BLOCK), f32),
    ]
    scratch = []
    more = {}
    edges = column_scratch(blocks)
    if talk:
        cut = (2, 2, 2, 2, PAIRS // 2)
        operands += [
            part.reshape(cut + part.shape[2:]),
            part_stat.reshape(cut + part_stat.shape[2:]),
        ]
        in_specs += [pl.BlockSpec(memory_space=pl.ANY)] * 2
        shapes = [
            (2, 2, PAIRS // 2, LANES, GLOBALS),
            (2, 2, PAIRS // 2, 8, GLOBALS),
        ]
        out_specs += [full(shape) for shape in shapes]
        out_shape += [
            jax.ShapeDtypeStruct(shapes[0], bf16),
            jax.ShapeDtypeStruct(shapes[1], f32),
        ]
        leads = [(2, 2, 2), (2, 2, 2), (2, 2)]
        sums = [pltpu.VMEM(lead + shapes[0][2:], bf16) for lead in leads]
        stats = [pltpu.VMEM(lead + shapes[1][2:], f32) for lead in leads]
        dma = pltpu.SemaphoreType.DMA
        scratch = [sums[0], stats[0]] + sums[1:] + stats[1:]
        edges += [dma((2, 2)), dma((2, 2)), dma((2,))]
        more = {"collective_id": 2, "has_side_effects": True}
    return pl.pallas_call(
        functools.partial(local_forward_kernel, talk, rows_count, group_rows),
        grid_spec=pltpu.PrefetchScalarGridSpec(
            num_scalar_prefetch=3,
            grid=(PAIRS, blocks),
            in_specs=in_specs,
            out_specs=out_specs,
            scratch_shapes=scratch + edges,
        ),
        out_shape=out_shape,
        compiler_params=params(**more),
        cost_estimate=pl.CostEstimate(
            flops=16 * rows_count * BLOCK * width,
            bytes_accessed=16 * rows_count * width,
            transcendentals=HEADS * rows_count * BLOCK,
        ),
        name="local_forward",
    )(*scalars, *operands)


def join_rows(ref):
    return jnp.concatenate([ref[i : i + 1] for i in range(ref.shape[0])], axis=1)


def take_lanes(row, starts, length):
    return jnp.concatenate([row[:, start : start + length] for start in starts], axis=1)


def put_grouped(ref, value):
    seq, batch, rows, lanes = ref.shape
    for part in range(batch):
        piece = value[:, part * lanes : (part + 1) * lanes].astype(bf16)
        ref[:, part] = piece.reshape(seq, rows, lanes)


def put_unit(ref, value):
    batch, rows, lanes = ref.shape[4:]
    for part in range(batch):
        piece = value[:, part * lanes : (part + 1) * lanes].astype(bf16)
        ref[:, :, :, :, part] = piece.reshape(ref.shape[:4] + (rows, lanes))


TICKS = 3
ENDINGS = ((0, 2, 4, 6, 8), (3, 5, 7, 9, 10), (6, 8))


def branch_kernel(
    tile,
    seq_size,
    x_ref,
    o_ref,
    ct_ref,
    ct_head_ref,
    gx_ref,
    go_in_ref,
    gstat_in_ref,
    gct_ref,
    wo_ref,
    w1_ref,
    b1_ref,
    w2_ref,
    b2_ref,
    norms_ref,
    z_ref,
    dy_ref,
    do_ref,
    gz_ref,
    gdy_ref,
    gdo_ref,
    dwo_ref,
    db1_ref,
    db2_ref,
    dgain_ref,
    doffset_ref,
    first_ref,
    second_ref,
    *refs,
):
    talk = seq_size > 0
    if talk:
        message_ref, rest_ref, z_head_ref = refs[:3]
        refs = refs[3:]
    os_ref, cts_ref, y_ref, h_ref, z_sum_ref, dh_ref, dft_ref, a_ref, du_ref, load_sem = refs[:10]
    b1s_ref = refs[10]
    refs = refs[11:]
    step = pl.program_id(0)
    steps = pl.num_programs(0)
    count, width = x_ref.shape
    own = gx_ref.shape[0]
    extra = os_ref.shape[0] - count
    tiles = count // tile
    tail = pl.ds(count, extra)

    def rows_at(i):
        return pl.ds(i * tile, tile)

    def padded(value):
        return jnp.concatenate([value, jnp.zeros((extra - own, width), value.dtype)], axis=0)

    if talk:
        units_ref = refs[0]
        landings = refs[1:6]
        send_sem, recv_sem = refs[6:8]
        half_ref, half_stat_ref = refs[8:10]
        slot_sums = refs[10:12]
        slot_stats = refs[12:14]
        turned_ref, go_land, gstat_land, stat_ref, slot_send, slot_recv = refs[14:20]
        message_land, message_send, message_recv, halo_send, halo_recv = refs[20:]
        last_step = 4
        bits, partners = my_place()
        core = bits["core"]
        chunks = last_step - 1
        slots = units_ref.shape[0]
        plan = [
            (tick, chunk, stage)
            for chunk, ticks in enumerate(ENDINGS)
            for stage, tick in enumerate(ticks)
        ]

        def source(unit):
            return lambda side: units_ref.at[unit % slots, :, :, :, side]

        engine = HalvingSum(
            (X_FIRST, Y_FIRST) * chunks,
            [source(unit) for unit in range(2 * chunks)],
            landings,
            None,
            send_sem,
            recv_sem,
            None,
            put_rows(first_ref, landings[4].shape[1]),
            bits,
            partners,
        )

        def advance(tick):
            for when, chunk, stage in sorted(plan, key=lambda entry: -entry[2]):
                if when == tick:
                    for unit in (2 * chunk, 2 * chunk + 1):
                        engine.advance(unit, stage, stop=chunk == chunks - 1 and stage == 1)

        def tick_at(position):
            for number in range(1, last_step):
                tick = TICKS * (number - 1) + position

                @pl.when(step == number)
                def _():
                    advance(tick)

        slot_sum = SlotSum(
            None,
            (None, half_ref) + tuple(slot_sums),
            (None, half_stat_ref) + tuple(slot_stats),
            slot_send,
            slot_recv,
            bits,
            partners,
        )
        half_pairs = PAIRS // 2
        lanes = half_pairs * LANES
        my_lanes = pl.ds(pl.multiple_of(core * lanes, LANES), lanes)

        def final_copies():
            theirs = pl.ds(pl.multiple_of((1 - core) * own, own), own)
            return (
                remote(
                    turned_ref.at[theirs],
                    go_land.at[:, my_lanes],
                    slot_send.at[4, 0],
                    slot_recv.at[4, 0],
                    partners["core"],
                ),
                remote(
                    gstat_land.at[core],
                    gstat_land.at[core],
                    slot_send.at[4, 1],
                    slot_recv.at[4, 1],
                    partners["core"],
                ),
            )

        def finish_slots():
            slot_sum.merge(3)
            for which in range(half_pairs):
                stat = slot_stats[1][which]
                total = stat[2:4]
                sums = slot_sums[1][which].astype(f32)
                mean = jnp.concatenate(
                    [sums[:HEAD_DIM] / total[0:1], sums[HEAD_DIM:] / total[1:2]], 0
                )
                turned_ref[:, which * LANES : (which + 1) * LANES] = mean.T.astype(bf16)
                whole = stat[0:2] + jnp.log(total)
                gstat_land[core, which] = jnp.concatenate(
                    [whole, jnp.zeros((6, GLOBALS), f32)], 0
                )
            mine = pl.ds(pl.multiple_of(core * own, own), own)
            go_land[:, my_lanes] = turned_ref[mine, :]
            for copy in final_copies():
                copy.start()

        def put_message():
            product = gdo_ref[...].astype(f32) * go_land[...].astype(f32)
            head_of = iota((width, LANES), 0) // HEAD_DIM == iota((width, LANES), 1)
            head_of = jnp.where(head_of, 1.0, 0.0).astype(bf16)
            first = product.astype(bf16)
            second = (product - first.astype(f32)).astype(bf16)
            centre = nn(first, head_of) + nn(second, head_of)
            lines = [gstat_land[half, which, 0:2] for half in (0, 1) for which in range(half_pairs)]
            lines = jnp.concatenate(lines + [jnp.zeros((LANES - HEADS, GLOBALS), f32)], 0)
            stat_ref[...] = lines.T
            total = stat_ref[pl.ds(pl.multiple_of(core * own, own), own), :]
            spread = jnp.zeros((own, LANES), f32)
            for number, value in enumerate((total, centre)):
                for piece in range(3):
                    low = value.astype(bf16)
                    value = value - low.astype(f32)
                    start_lane = (3 * number + piece) * HEADS
                    source_lane = iota((LANES, LANES), 0)
                    moved = iota((LANES, LANES), 1) == source_lane + start_lane
                    moved = jnp.where(moved & (source_lane < HEADS), 1.0, 0.0).astype(bf16)
                    spread = spread + nn(low, moved)
            mine = message_land.at[bits["z1"]]
            mine[:, :width] = gdo_ref[...]
            mine[:, width:] = spread.astype(bf16)
            message_copy().start()

        def message_copy():
            mine = message_land.at[bits["z1"]]
            return remote(mine, mine, message_send, message_recv, partners["z1"])

    else:

        def tick_at(position):
            pass

    if talk:
        batch = lax.axis_index("batch")
        seq_place = lax.axis_index("seq")
        places = lax.axis_size("seq")
        after = (batch, lax.rem(seq_place + 1, places))
        before = (batch, lax.rem(seq_place + places - 1, places))
        halo = remote(
            ct_ref.at[pl.ds(count - HALF, HALF)],
            cts_ref.at[pl.ds(0, HALF)],
            halo_send,
            halo_recv,
            after,
        )
    loads = [
        pltpu.make_async_copy(o_ref, os_ref.at[pl.ds(0, count)], load_sem.at[0]),
        pltpu.make_async_copy(
            ct_ref.at[pl.ds(0, count - HALF)],
            cts_ref.at[pl.ds(HALF, count - HALF)],
            load_sem.at[1],
        ),
    ]
    if not talk:
        loads.append(
            pltpu.make_async_copy(ct_head_ref, cts_ref.at[pl.ds(0, HALF)], load_sem.at[2])
        )

    def start(at, size, x, sums):
        y = x.astype(f32) + nn(os_ref[at, :], wo_ref[...])
        unit, unused = normalize_rows(y)
        h_ref[at, :] = (unit * norms_ref[4:5] + norms_ref[5:6]).astype(bf16)
        y_ref[at, :] = y
        sums[...] = y + join_rows(b2_ref)
        dh_ref[at, :] = jnp.zeros((size, width), f32)

    @pl.when(step == 0)
    def _():
        for load in loads:
            load.start()
        if talk:
            half_ref[...] = go_in_ref[...]
            half_stat_ref[...] = gstat_in_ref[...]
            meet([partners[name] for name in AXES] + [before, after])
            slot_sum.begin(2)
            halo.start()
        cts_ref[count:] = padded(gct_ref[...])
        loads[0].wait()

        def start_tile(i, carry):
            at = pl.ds(pl.multiple_of(i * tile, tile), tile)
            start(at, tile, x_ref[at, :], dy_ref.at[at])
            return carry

        lax.fori_loop(0, tiles, start_tile, 0)
        for load in loads[1:]:
            load.wait()

    @pl.when(step == 0)
    def _():
        row = join_rows(b1_ref)
        for number in range(b1s_ref.shape[0]):
            if talk:
                share = FF_CHUNK // seq_size
                starts = [place * b1s_ref.shape[0] * share for place in range(seq_size)]
                starts = [start + number * share for start in starts]
                b1s_ref[number : number + 1] = take_lanes(row, starts, share)
            else:
                b1s_ref[number : number + 1] = row[:, number * FF_CHUNK : (number + 1) * FF_CHUNK]

    my_row = pl.ds(step, 1)
    db1_ref[my_row, :] = jnp.zeros((1, FF_CHUNK), f32)
    w1 = w1_ref[...].reshape(width, width)
    w2 = w2_ref[...].reshape(width, width)

    def chunk_of(at, sums):
        u = nt(h_ref[at, :], w1) + b1s_ref[my_row, :]
        da = nt(cts_ref[at, :], w2)
        area, density = gelu_parts(u)
        a = (u * area).astype(bf16)
        du = (da * (area + u * density)).astype(bf16)
        a_ref[at, :] = a
        du_ref[at, :] = du
        db1_ref[my_row, :] += jnp.sum(du.astype(f32), axis=0, keepdims=True)
        sums[...] = sums[...] + nn(a, w2)
        dh_ref[at, :] = dh_ref[at, :] + nn(du, w1)

    for i in range(1, tiles):
        chunk_of(rows_at(i), dy_ref.at[rows_at(i)])

    if talk:

        @pl.when(step == 0)
        def _():
            slot_sum.merge(2)
            slot_sum.begin(3)
            halo.wait_recv()

    tick_at(0)
    chunk_of(rows_at(0), dy_ref.at[rows_at(0)])

    @pl.when(step == 0)
    def _():
        if talk:
            finish_slots()
            halo.wait_send()
        dft_ref[...] = cts_ref[...].T
        if talk:
            for copy in final_copies():
                copy.wait_recv()
            os_ref[count:] = padded(go_land[...])
        else:
            os_ref[count:] = padded(go_in_ref[...])
        start(tail, extra, padded(gx_ref[...]), z_sum_ref)

    chunk_of(tail, z_sum_ref)
    tick_at(1)
    dw1 = tn(du_ref[...], h_ref[...])
    dw2 = nn(dft_ref[...], a_ref[...])
    if talk:
        for number in range(chunks):

            @pl.when(step == number)
            def _():
                for which, value in ((0, dw1), (1, dw2)):
                    unit = 2 * number + which
                    if unit >= slots:
                        engine.sent(unit - slots, 0)
                    put_unit(units_ref.at[unit % slots], value)

        @pl.when(step == chunks)
        def _():
            put_unit(second_ref.at[0], dw1)
            put_unit(second_ref.at[1], dw2)

        tick_at(2)
        for number in range(chunks):

            @pl.when(step == number)
            def _():
                engine.begin(2 * number)
                engine.begin(2 * number + 1)

    else:
        first_ref[...] = dw1.astype(bf16)
        second_ref[...] = dw2.astype(bf16)

    @pl.when(step == steps - 1)
    def _():
        db2_ref[...] = jnp.zeros_like(db2_ref)
        dgain_ref[...] = jnp.zeros_like(dgain_ref)
        doffset_ref[...] = jnp.zeros_like(doffset_ref)

        def finish(at, size, sums, put):
            z = sums[...].astype(bf16)
            unit, scale = normalize_rows(y_ref[at, :])
            dh = dh_ref[at, :]
            ct = cts_ref[at, :].astype(f32)
            dy = ct + norm_back(unit, scale, norms_ref[4:5], dh)
            db2_ref[...] += jnp.sum(ct, axis=0, keepdims=True)
            doffset_ref[...] += jnp.sum(dh, axis=0, keepdims=True)
            dgain_ref[...] += jnp.sum(dh * unit, axis=0, keepdims=True)
            low = dy.astype(bf16)
            h_ref[at, :] = low
            put(z, dy, nt(low, wo_ref[...]).astype(bf16))

        def finish_tile(i, carry):
            at = pl.ds(pl.multiple_of(i * tile, tile), tile)

            def put(z, dy, do):
                z_ref[at, :] = z
                dy_ref[at, :] = dy
                do_ref[at, :] = do

            finish(at, tile, dy_ref.at[at], put)
            return carry

        def put_tail(z, dy, do):
            gz_ref[...] = z[:own]
            gdy_ref[...] = dy[:own]
            gdo_ref[...] = do[:own]

        finish(tail, extra, z_sum_ref, put_tail)
        if talk:
            put_message()
            advance(TICKS * chunks)
        lax.fori_loop(0, tiles, finish_tile, 0)
        dwo = tn(h_ref[...], os_ref[...])
        if talk:
            put_grouped(dwo_ref, dwo)
            advance(TICKS * chunks + 1)
            rest_ref[...] = landings[1][2 * chunks - 2 :]
            z_head_ref[...] = z_ref[:HALF]
            for when, chunk, stage in plan:
                for unit in (2 * chunk, 2 * chunk + 1):
                    if stage > 0 or unit + slots >= 2 * chunks:
                        engine.sent(unit, stage)
            slot_sum.sent(2)
            slot_sum.sent(3)
            for copy in final_copies():
                copy.wait_send()
            message_copy().wait_recv()
            message_ref[...] = message_land[...]
            message_copy().wait_send()
        else:
            dwo_ref[...] = dwo.astype(bf16)


def branch(grid_of, x, o, ct, ct_head, gx, go, gstat, gct, wo, w1t, b1, w2, b2, norms):
    count, width = x.shape
    own = gx.shape[0]
    hidden = w2.shape[0]
    steps = hidden // FF_CHUNK
    total = count + -(-own // LANES) * LANES
    row = once((count, width))
    few = once((own, width))
    line = full((1, width))
    anywhere = pl.BlockSpec(memory_space=pl.ANY)
    scratch = []
    more = {}
    if grid_of is None:
        weight_spec = pl.BlockSpec((FF_CHUNK, width), lambda j: (j, 0))
        dw_shapes = [(hidden, width), (width, hidden)]
        dw_types = [bf16, bf16]
        dw_specs = [weight_spec, pl.BlockSpec((width, FF_CHUNK), lambda j: (0, j))]
        dwo_shape = (width, width)
    else:
        seq, batch = grid_of
        rows, lanes = width // seq, width // batch
        weight_spec = pl.BlockSpec((seq, 1, rows, width), lambda j: (0, j, 0, 0))
        w1t = w1t.reshape(seq, steps, rows, width)
        w2 = w2.reshape(seq, steps, rows, width)
        units = 2 * (steps - 1)
        sums, stats = go.shape[2:], gstat.shape[2:]
        dw_shapes = [
            ((units - 2) * rows, lanes),
            (2, 2, 2, 2, 2, batch, rows, lanes),
            (2, own, width + LANES),
            (2, 2, 2, 2, rows, lanes),
            (HALF, width),
        ]
        dw_types = [f32, bf16, bf16, bf16, bf16]
        dw_specs = [once(shape) for shape in dw_shapes]
        dwo_shape = (seq, batch, rows, lanes)
        dma = pltpu.SemaphoreType.DMA
        scratch = (
            [pltpu.VMEM((4,) + dw_shapes[1][1:], bf16)]
            + sum_scratch(units, rows, lanes, False)
            + [
                pltpu.VMEM(go.shape, bf16),
                pltpu.VMEM(gstat.shape, f32),
                pltpu.VMEM((2,) + sums, bf16),
                pltpu.VMEM(sums, bf16),
                pltpu.VMEM((2,) + stats, f32),
                pltpu.VMEM(stats, f32),
                pltpu.VMEM((GLOBALS, PAIRS // 2 * LANES), bf16),
                pltpu.VMEM((own, width), bf16),
                pltpu.VMEM((2,) + stats, f32),
                pltpu.VMEM((GLOBALS, LANES), f32),
                dma((5, 2)),
                dma((5, 2)),
                pltpu.VMEM((2, own, width + LANES), bf16),
                dma,
                dma,
                dma,
                dma,
            ]
        )
        more = {"collective_id": 3, "has_side_effects": True}
    out = pl.pallas_call(
        functools.partial(branch_kernel, BLOCK, grid_of[0] if grid_of else 0),
        grid=(steps,),
        in_specs=[
            row,
            anywhere,
            anywhere,
            anywhere,
            few,
            once(go.shape),
            once(gstat.shape),
            few,
            once((width, width)),
            weight_spec,
            full(b1.shape),
            weight_spec,
            full(b2.shape),
            full(norms.shape),
        ],
        out_specs=[row, row, row, few, few, few]
        + [once(dwo_shape), full((steps, FF_CHUNK)), line, line, line]
        + dw_specs,
        out_shape=[
            jax.ShapeDtypeStruct((count, width), bf16),
            jax.ShapeDtypeStruct((count, width), f32),
            jax.ShapeDtypeStruct((count, width), bf16),
            jax.ShapeDtypeStruct((own, width), bf16),
            jax.ShapeDtypeStruct((own, width), f32),
            jax.ShapeDtypeStruct((own, width), bf16),
            jax.ShapeDtypeStruct(dwo_shape, bf16),
            jax.ShapeDtypeStruct((steps, FF_CHUNK), f32),
            jax.ShapeDtypeStruct((1, width), f32),
            jax.ShapeDtypeStruct((1, width), f32),
            jax.ShapeDtypeStruct((1, width), f32),
        ]
        + [jax.ShapeDtypeStruct(shape, kind) for shape, kind in zip(dw_shapes, dw_types)],
        scratch_shapes=[
            pltpu.VMEM((total, width), bf16),
            pltpu.VMEM((total, width), bf16),
            pltpu.VMEM((total, width), f32),
            pltpu.VMEM((total, width), bf16),
            pltpu.VMEM((total - count, width), f32),
            pltpu.VMEM((total, width), f32),
            pltpu.VMEM((width, total), bf16),
            pltpu.VMEM((total, FF_CHUNK), bf16),
            pltpu.VMEM((total, FF_CHUNK), bf16),
            pltpu.SemaphoreType.DMA((3,)),
            pltpu.VMEM((steps, FF_CHUNK), f32),
        ]
        + scratch,
        compiler_params=params(**more),
        cost_estimate=pl.CostEstimate(
            flops=6 * total * width * (2 * hidden + width),
            bytes_accessed=8 * width * hidden + 16 * total * width,
            transcendentals=2 * total * hidden,
        ),
        name="branch",
    )(x, o, ct, ct_head, gx, go, gstat, gct, wo, w1t, b1, w2, b2, norms)
    return out


def local_backward_kernel(
    talk,
    rows_count,
    group_rows,
    lengths,
    bucket_of,
    place,
    q_ref,
    k_ref,
    v_ref,
    do_ref,
    o_ref,
    line_ref,
    *refs,
):
    if talk:
        message_ref, rest_ref, last_ref, dwo_ref = refs[:4]
        refs = refs[4:]
    dq_ref, dk_ref, dv_ref, centre_ref = refs[:4]
    refs = refs[4:]
    if talk:
        everyone_ref, sums_ref, rest_out_ref = refs[:3]
        refs = refs[3:]
    edges, query_columns, key_columns = refs[:3]
    pair = pl.program_id(0)
    block = pl.program_id(1)
    blocks = rows_count // BLOCK
    step = pair * blocks + block

    @pl.when(step == 0)
    def _():
        read_edges(lengths, bucket_of, place, edges)

    if talk:
        all_ref, gather_send, gather_recv, own_ref = refs[3:7]
        landings = refs[7:12]
        send_sem, recv_sem, own_sem = refs[12:]
        bits, partners = my_place()
        gather = RowGather(all_ref, 3 * LANES, gather_send, gather_recv, bits, partners)
        engine = HalvingSum(
            (X_FIRST, Y_FIRST) * 2 + (X_FIRST,),
            [
                None,
                None,
                lambda side: last_ref.at[0, :, :, :, side],
                lambda side: last_ref.at[1, :, :, :, side],
                lambda side: dwo_ref.at[:, :, :, side],
            ],
            landings,
            own_ref,
            send_sem,
            recv_sem,
            own_sem,
            put_rows(sums_ref, landings[4].shape[1]),
            bits,
            partners,
        )
        plan = {
            3: [(2, 0), (3, 0), (4, 0)],
            5: [(0, 2), (1, 2)],
            8: [(0, 3), (1, 3)],
            11: [(0, 4), (1, 4), (2, 1), (3, 1), (4, 1)],
        }
        gather_plan = {4: 1, 8: 2, 10: 3}

        @pl.when(step == 0)
        def _():
            all_ref[:, bits["z0"], bits["y"], bits["core"]] = message_ref[...]
            landings[1][:2] = rest_ref[...]
            meet([partners[name] for name in AXES])
            gather.begin(1)
            for unit in (0, 1):
                engine.copy(unit, 2).start()
            for unit in (2, 3, 4):
                engine.begin(unit)

        for number in range(PAIRS * blocks):
            if number in plan or number in gather_plan:

                @pl.when(step == number)
                def _():
                    if number in gather_plan:
                        gather.advance(gather_plan[number])
                    for unit, stage in plan.get(number, ()):
                        engine.advance(unit, stage, stop=unit > 1 and stage == 1)

    block_columns(
        place, edges, rows_count, group_rows, block, step, blocks, query_columns, key_columns
    )
    extra = query_columns[block]
    upstream = do_ref[...]
    product = upstream.astype(f32) * o_ref[...].astype(f32)
    first = product.astype(bf16)
    second = (product - first.astype(f32)).astype(bf16)
    head = jnp.where(iota((8, LANES), 1) // HEAD_DIM == iota((8, LANES), 0), 1.0, 0.0).astype(bf16)
    by_head = nt(head, first) + nt(head, second)
    centre = jnp.concatenate([by_head[0:1], by_head[1:2]], axis=1)
    centre_ref[0, 0] = jnp.broadcast_to(centre, (8, 2 * BLOCK))
    queries = stack_pair(q_ref[...])
    grads = stack_pair(upstream)
    keys = k_ref[...]
    score = nt(
        jnp.concatenate([keys, key_columns[block]], 1),
        jnp.concatenate([queries, jnp.concatenate([extra, extra], 0)], 1),
    )
    weights = jnp.exp(score - line_ref[0, 0, 0:1])
    along = nt(v_ref[...], grads) - centre
    score_grad = (weights * along).astype(bf16)
    dv_ref[...] = nn(weights.astype(bf16), grads).astype(bf16)
    dk_ref[...] = nn(score_grad, queries).astype(bf16)
    low, high = side_by_side(tn(keys, score_grad))
    dq_ref[:HEAD_DIM] = low.astype(bf16)
    dq_ref[HEAD_DIM:] = high.astype(bf16)

    if talk:

        @pl.when(step == PAIRS * blocks - 1)
        def _():
            everyone_ref[...] = all_ref[...].reshape(everyone_ref.shape)
            gather.end(1)
            rest_out_ref[...] = landings[1][2:]
            for entries in plan.values():
                for unit, stage in entries:
                    engine.sent(unit, stage)


def local_backward(
    talk, scalars, rows_count, group_rows, q, k, v, do, o, line, message, rest, last, dwo
):
    blocks = rows_count // BLOCK
    width = q.shape[1]
    block_spec = pl.BlockSpec((BLOCK, LANES), lambda p, b, *unused: (b, p))
    operands = [q, k, v, do, o, line]
    in_specs = [block_spec] * 5 + [line_spec()]
    out_specs = (
        [pl.BlockSpec((LANES, BLOCK), lambda p, b, *unused: (p, b))]
        + [block_spec] * 2
        + [line_spec()]
    )
    out_shape = [
        jax.ShapeDtypeStruct((width, rows_count), bf16),
        jax.ShapeDtypeStruct((rows_count, width), bf16),
        jax.ShapeDtypeStruct((rows_count, width), bf16),
        jax.ShapeDtypeStruct((PAIRS, blocks, 8, 2 * BLOCK), f32),
    ]
    scratch = column_scratch(blocks)
    more = {}
    if talk:
        unused, own, wide = message.shape
        rows, lanes = last.shape[-2:]
        units = 5
        operands += [message, rest, last, dwo.reshape(last.shape[1:])]
        in_specs += [full(message.shape), once(rest.shape)]
        in_specs += [pl.BlockSpec(memory_space=pl.ANY)] * 2
        everyone = (16 * own, wide)
        rest_out = (units - 2,) + rest.shape[1:]
        out_specs += [once(everyone), once((2 * rows, lanes)), once(rest_out)]
        out_shape += [
            jax.ShapeDtypeStruct(everyone, bf16),
            jax.ShapeDtypeStruct((2 * rows, lanes), f32),
            jax.ShapeDtypeStruct(rest_out, bf16),
        ]
        dma = pltpu.SemaphoreType.DMA
        scratch += [pltpu.VMEM((2, 2, 2, 2, own, wide), bf16), dma((4, 2)), dma((4, 2))]
        scratch += sum_scratch(units, rows, lanes, True)
        more = {"collective_id": 4, "has_side_effects": True}
    return pl.pallas_call(
        functools.partial(local_backward_kernel, talk, rows_count, group_rows),
        grid_spec=pltpu.PrefetchScalarGridSpec(
            num_scalar_prefetch=3,
            grid=(PAIRS, blocks),
            in_specs=in_specs,
            out_specs=out_specs,
            scratch_shapes=scratch,
        ),
        out_shape=out_shape,
        compiler_params=params(**more),
        cost_estimate=pl.CostEstimate(
            flops=40 * rows_count * BLOCK * width,
            bytes_accessed=30 * rows_count * width,
            transcendentals=HEADS * rows_count * BLOCK,
        ),
        name="local_backward",
    )(*scalars, *operands)


def slot_backward_kernel(
    grouped,
    rows_count,
    group_rows,
    lengths,
    bucket_of,
    place,
    q_ref,
    k_ref,
    v_ref,
    do_ref,
    line_ref,
    centre_ref,
    dqt_ref,
    dk_in_ref,
    dv_in_ref,
    gq_ref,
    gk_ref,
    gv_ref,
    gdo_ref,
    gstat_ref,
    gx_in,
    gh_in,
    h_in,
    wq_ref,
    wk_ref,
    wv_ref,
    dq_ref,
    dk_ref,
    dv_ref,
    dw_ref,
    dgh_ref,
    dnorm_ref,
    edges,
    query_columns,
    key_columns,
    keys_ref,
    queries_ref,
    grads_ref,
    dqt_sum,
    dk_sum,
    dv_sum,
    dgqt_sum,
    dgk_sum,
    dgv_sum,
    lines_ref,
    dw_sum,
    dgh_sum,
    rows_ref,
    gx_ref,
    gh_ref,
    h_ref,
    load_sem,
):
    group = pl.program_id(0)
    block = pl.program_id(1)
    blocks = rows_count // BLOCK
    step = group * blocks + block
    together = range(TOGETHER)

    def lanes_of(which):
        return pl.ds(which * LANES, LANES)

    loads = [
        pltpu.make_async_copy(source, target, load_sem.at[number])
        for number, (source, target) in enumerate(
            ((gx_in, gx_ref), (gh_in, gh_ref), (h_in, h_ref))
        )
    ]

    @pl.when(step == 0)
    def _():
        for load in loads:
            load.start()
        read_edges(lengths, bucket_of, place, edges)

        def turn(slot, carry):
            at = pl.ds(pl.multiple_of(slot * GLOBALS, GLOBALS), GLOBALS)
            lines_ref[slot] = gstat_ref[at, :].astype(f32).T
            return carry

        lax.fori_loop(0, SLOTS, turn, 0)
        dgh_sum[...] = jnp.zeros_like(dgh_sum)
        dnorm_ref[...] = jnp.zeros_like(dnorm_ref)

    @pl.when(block == 0)
    def _():
        dgqt_sum[...] = jnp.zeros_like(dgqt_sum)
        dgk_sum[...] = jnp.zeros_like(dgk_sum)
        dgv_sum[...] = jnp.zeros_like(dgv_sum)

    block_columns(
        place, edges, rows_count, group_rows, block, step, blocks, query_columns, key_columns
    )
    extra = query_columns[block]
    for which in together:
        lanes = lanes_of(which)
        keys_ref[which, :, :LANES] = k_ref[:, lanes]
        keys_ref[which, :, LANES:] = key_columns[block]
        queries_ref[which, :, :LANES] = stack_pair(q_ref[:, lanes])
        queries_ref[which, :BLOCK, LANES:] = extra
        queries_ref[which, BLOCK:, LANES:] = extra
        grads_ref[which] = stack_pair(do_ref[:, lanes])
    dqt_sum[...] = dqt_ref[...].astype(f32)
    dk_sum[...] = dk_in_ref[...].astype(f32)
    dv_sum[...] = dv_in_ref[...].astype(f32)

    def line_of(slot, which, first):
        halves = []
        for head in range(2):
            spot = first + 2 * (group * TOGETHER + which) + head
            halves.append(
                lines_ref[slot, pl.ds(spot, 1)]
                + lines_ref[slot, pl.ds(spot + HEADS, 1)]
                + lines_ref[slot, pl.ds(spot + 2 * HEADS, 1)]
            )
        return jnp.concatenate(halves, axis=1)

    def from_global(slot, which, keys, values):
        at = pl.ds(pl.multiple_of(slot * GLOBALS, GLOBALS), GLOBALS)
        extra = global_query_extra(slot).astype(bf16)
        queries = stack_pair(gq_ref[at, lanes_of(which)])
        grads = stack_pair(gdo_ref[at, lanes_of(which)])
        score = nt(keys, jnp.concatenate([queries, jnp.concatenate([extra, extra], 0)], 1))
        weights = jnp.exp(score - line_of(slot, which, 0))
        along = nt(values, grads) - line_of(slot, which, 3 * HEADS)
        score_grad = (weights * along).astype(bf16)
        low, high = side_by_side(tn(keys[:, :LANES], score_grad))
        dgqt_sum[which, slot, :HEAD_DIM] += low
        dgqt_sum[which, slot, HEAD_DIM:] += high
        return nn(score_grad, queries), nn(weights.astype(bf16), grads)

    def one_slot(slot, carry):
        @pl.when(slot_present(slot, place, edges, rows_count, group_rows, block))
        def _():
            at = pl.ds(pl.multiple_of(slot * GLOBALS, GLOBALS), GLOBALS)
            columns = global_key_extra(slot).astype(bf16)
            for which in together:
                lanes = lanes_of(which)
                key_grad, value_grad = from_global(slot, which, keys_ref[which], v_ref[:, lanes])
                dk_sum[:, lanes] += key_grad
                dv_sum[:, lanes] += value_grad
                keys = gk_ref[at, lanes]
                grads = grads_ref[which]
                score = nt(jnp.concatenate([keys, columns], 1), queries_ref[which])
                weights = jnp.exp(score - line_ref[which, 0, 0:1])
                along = nt(gv_ref[at, lanes], grads) - centre_ref[which, 0, 0:1]
                score_grad = (weights * along).astype(bf16)
                dgv_sum[at, lanes] += nn(weights.astype(bf16), grads)
                dgk_sum[at, lanes] += nn(score_grad, queries_ref[which, :, :LANES])
                low, high = side_by_side(tn(keys, score_grad))
                dqt_sum[pl.ds(which * LANES, HEAD_DIM)] += low
                dqt_sum[pl.ds(which * LANES + HEAD_DIM, HEAD_DIM)] += high

        return carry

    lax.fori_loop(0, SLOTS, one_slot, 0)
    here = pl.ds(pl.multiple_of(block * BLOCK, BLOCK), BLOCK)
    for index, (ref, value) in enumerate(
        ((dq_ref, dqt_sum[...].T), (dk_ref, dk_sum[...]), (dv_ref, dv_sum[...]))
    ):
        low = value.astype(bf16)
        ref[...] = low
        rows_ref[index, here, :] = low

    @pl.when(step == blocks - 1)
    def _():
        for load in loads:
            load.wait()

    @pl.when((block == blocks - 1) & (place[2] >= 0))
    def _():
        slot = place[2]
        at = pl.ds(pl.multiple_of(slot * GLOBALS, GLOBALS), GLOBALS)
        columns = global_key_extra(slot).astype(bf16)
        for which in together:
            lanes = lanes_of(which)
            keys = jnp.concatenate([gk_ref[at, lanes], columns], axis=1)
            key_grad, value_grad = from_global(slot, which, keys, gv_ref[at, lanes])
            dgk_sum[at, lanes] += key_grad
            dgv_sum[at, lanes] += value_grad

    @pl.when(block == blocks - 1)
    def _():
        for index in range(3):
            local = tn(rows_ref[index], h_ref[...])
            dw_sum[index] = local * query_scale if index == 0 else local

        def through(slot, carry):
            needed = slot == place[2]
            for number in range(blocks):
                needed = needed | slot_present(
                    slot, place, edges, rows_count, group_rows, number
                )

            @pl.when(needed)
            def _():
                at = pl.ds(pl.multiple_of(slot * GLOBALS, GLOBALS), GLOBALS)
                grads = (
                    (
                        jnp.concatenate([dgqt_sum[which, slot].T for which in together], 1)
                        * query_scale
                    ).astype(bf16),
                    dgk_sum[at, :].astype(bf16),
                    dgv_sum[at, :].astype(bf16),
                )
                rows = gh_ref[at, :]
                total = dgh_sum[at, :]
                for index, weight in enumerate((wq_ref, wk_ref, wv_ref)):
                    total = total + nt(grads[index], weight[...])
                dgh_sum[at, :] = total

                for index in range(3):
                    dw_sum[index] += tn(grads[index], rows)

                @pl.when(group == PAIRS // TOGETHER - 1)
                def _():
                    unit, unused = normalize_rows(gx_ref[at, :].astype(f32))
                    dnorm_ref[0:1] += jnp.sum(total * unit, axis=0, keepdims=True)
                    dnorm_ref[1:2] += jnp.sum(total, axis=0, keepdims=True)

            return carry

        lax.fori_loop(0, SLOTS, through, 0)
        if grouped:
            for index in range(3):
                put_grouped(dw_ref.at[index], dw_sum[index])
        else:
            dw_ref[...] = dw_sum[...].astype(bf16)

    @pl.when(step == PAIRS // TOGETHER * blocks - 1)
    def _():
        dgh_ref[...] = dgh_sum[...].astype(bf16)


def slot_backward(
    grid_of,
    scalars,
    rows_count,
    group_rows,
    q,
    k,
    v,
    do,
    line,
    centre,
    dqt,
    dk,
    dv,
    gq,
    gk,
    gv,
    everyone,
    gx,
    gh,
    h,
    wq,
    wk,
    wv,
):
    blocks = rows_count // BLOCK
    all_globals, width = gk.shape
    block_spec = pl.BlockSpec((BLOCK, TOGETHER * LANES), lambda p, b, *unused: (b, p))
    pair_spec = pl.BlockSpec((all_globals, TOGETHER * LANES), lambda p, b, *unused: (0, p))
    local = jax.ShapeDtypeStruct((rows_count, width), bf16)
    glob = jax.ShapeDtypeStruct((all_globals, width), bf16)
    if grid_of is None:
        dw_shape = (3, width, width)
        dw_spec = pl.BlockSpec((3, TOGETHER * LANES, width), lambda p, b, *unused: (0, p, 0))
    else:
        seq, batch = grid_of
        piece = (batch, width // seq, width // batch)
        dw_shape = (3, seq) + piece
        share = TOGETHER * LANES // piece[1]
        dw_spec = pl.BlockSpec((3, share) + piece, lambda p, b, *unused: (0, p, 0, 0, 0))
    return pl.pallas_call(
        functools.partial(slot_backward_kernel, grid_of is not None, rows_count, group_rows),
        grid_spec=pltpu.PrefetchScalarGridSpec(
            num_scalar_prefetch=3,
            grid=(PAIRS // TOGETHER, blocks),
            in_specs=[block_spec] * 4
            + [line_spec(TOGETHER)] * 2
            + [pl.BlockSpec((TOGETHER * LANES, BLOCK), lambda p, b, *unused: (p, b))]
            + [block_spec] * 2
            + [pair_spec] * 4
            + [pl.BlockSpec((all_globals, LANES), lambda p, b, *unused: (0, PAIRS))]
            + [pl.BlockSpec(memory_space=pl.ANY)] * 3
            + [pl.BlockSpec((width, TOGETHER * LANES), lambda p, b, *unused: (0, p))] * 3,
            out_specs=[block_spec] * 3
            + [
                dw_spec,
                once((all_globals, width)),
                full((8, width)),
            ],
            scratch_shapes=column_scratch(blocks)
            + [
                pltpu.VMEM((TOGETHER, BLOCK, 2 * LANES), bf16),
                pltpu.VMEM((TOGETHER, 2 * BLOCK, 2 * LANES), bf16),
                pltpu.VMEM((TOGETHER, 2 * BLOCK, LANES), bf16),
                pltpu.VMEM((TOGETHER * LANES, BLOCK), f32),
                pltpu.VMEM((BLOCK, TOGETHER * LANES), f32),
                pltpu.VMEM((BLOCK, TOGETHER * LANES), f32),
                pltpu.VMEM((TOGETHER, SLOTS, LANES, GLOBALS), f32),
                pltpu.VMEM((all_globals, TOGETHER * LANES), f32),
                pltpu.VMEM((all_globals, TOGETHER * LANES), f32),
                pltpu.VMEM((SLOTS, LANES, GLOBALS), f32),
                pltpu.VMEM((3, TOGETHER * LANES, width), f32),
                pltpu.VMEM((all_globals, width), f32),
                pltpu.VMEM((3, rows_count, TOGETHER * LANES), bf16),
                pltpu.VMEM((all_globals, width), bf16),
                pltpu.VMEM((all_globals, width), bf16),
                pltpu.VMEM((rows_count, width), bf16),
                pltpu.SemaphoreType.DMA((3,)),
            ],
        ),
        out_shape=[local] * 3
        + [
            jax.ShapeDtypeStruct(dw_shape, bf16),
            glob,
            jax.ShapeDtypeStruct((8, width), f32),
        ],
        compiler_params=params(),
        cost_estimate=pl.CostEstimate(
            flops=80 * rows_count * GLOBALS * width,
            bytes_accessed=40 * rows_count * width,
            transcendentals=2 * HEADS * rows_count * GLOBALS,
        ),
        name="slot_backward",
    )(
        *scalars,
        q,
        k,
        v,
        do,
        line,
        centre,
        dqt,
        dk,
        dv,
        gq,
        gk,
        gv,
        everyone,
        everyone,
        gx,
        gh,
        h,
        wq,
        wk,
        wv,
    )


def project_back_kernel(
    tile,
    x_ref,
    dy_ref,
    dq_ref,
    dk_ref,
    dv_ref,
    wq_ref,
    wk_ref,
    wv_ref,
    gain_ref,
    dx_ref,
    dnorm_ref,
):
    count, width = x_ref.shape
    dnorm_ref[...] = jnp.zeros_like(dnorm_ref)

    def one_tile(i, carry):
        at = pl.ds(pl.multiple_of(i * tile, tile), tile)
        dh = (
            nt(dq_ref[at, :], wq_ref[...]) * query_scale
            + nt(dk_ref[at, :], wk_ref[...])
            + nt(dv_ref[at, :], wv_ref[...])
        )
        unit, scale = normalize_rows(x_ref[at, :].astype(f32))
        dnorm_ref[0:1] += jnp.sum(dh * unit, axis=0, keepdims=True)
        dnorm_ref[1:2] += jnp.sum(dh, axis=0, keepdims=True)
        dx_ref[at, :] = dy_ref[at, :] + norm_back(unit, scale, gain_ref[...], dh)
        return carry

    lax.fori_loop(0, count // tile, one_tile, 0)


def project_back(x, dy, dq, dk, dv, wq, wk, wv, gain):
    count, width = x.shape
    vmem = pl.BlockSpec(memory_space=pltpu.VMEM)
    return pl.pallas_call(
        functools.partial(project_back_kernel, BLOCK),
        in_specs=[vmem] * 9,
        out_specs=[vmem] * 2,
        out_shape=[
            jax.ShapeDtypeStruct((count, width), f32),
            jax.ShapeDtypeStruct((8, width), f32),
        ],
        compiler_params=params(),
        cost_estimate=pl.CostEstimate(
            flops=12 * count * width * width, bytes_accessed=30 * count * width, transcendentals=0
        ),
        name="project_back",
    )(x, dy, dq, dk, dv, wq, wk, wv, gain)


def finish_kernel(
    rest_ref,
    x_in,
    dy_in,
    dq_in,
    dk_in,
    dv_in,
    dqkv_ref,
    dgh_ref,
    wq_in,
    wk_in,
    wv_in,
    db1_ref,
    db2_ref,
    dnorm_global_ref,
    dgain2_ref,
    doffset2_ref,
    gx_ref,
    gdy_ref,
    norms_ref,
    out_ref,
    small_out_ref,
    grad_out_ref,
    token_ref,
    halo_dx_out,
    x_ref,
    dy_ref,
    dq_ref,
    dk_ref,
    dv_ref,
    wq_ref,
    wk_ref,
    wv_ref,
    load_sem,
    own_ref,
    one_ref,
    two_ref,
    three_ref,
    four_ref,
    five_ref,
    send_sem,
    recv_sem,
    own_sem,
    gown_ref,
    gone_ref,
    gtwo_ref,
    gthree_ref,
    gfour_ref,
    gsend_sem,
    grecv_sem,
    gown_sem,
    sums_ref,
    here_ref,
    ssend_sem,
    srecv_sem,
    halo_out,
    halo_dx,
    halo_send,
    halo_recv,
    dnorm_ref,
    dgh_sum_ref,
):
    bits, partners = my_place()
    count, width = x_ref.shape
    came = rest_ref.shape[0]
    units = came + 3
    batch = lax.axis_index("batch")
    seq = lax.axis_index("seq")
    places = lax.axis_size("seq")
    after = (batch, lax.rem(seq + 1, places))
    before = (batch, lax.rem(seq + places - 1, places))

    pairs = [
        (dq_in, dq_ref),
        (dk_in, dk_ref),
        (dv_in, dv_ref),
        (wq_in, wq_ref),
        (wk_in, wk_ref),
        (wv_in, wv_ref),
        (x_in, x_ref),
        (dy_in, dy_ref),
    ]
    loads = [
        pltpu.make_async_copy(source, target, load_sem.at[number])
        for number, (source, target) in enumerate(pairs)
    ]
    def source(unit):
        return lambda side: dqkv_ref.at[unit - came, :, :, :, side]

    engine = HalvingSum(
        (X_Z_FIRST, Y_FIRST, X_FIRST, X_FIRST, Y_FIRST, Z_FIRST),
        [source(unit) for unit in range(units)],
        (one_ref, two_ref, three_ref, four_ref, five_ref),
        own_ref,
        send_sem,
        recv_sem,
        own_sem,
        put_rows(out_ref, five_ref.shape[1]),
        bits,
        partners,
    )
    wide = gone_ref.shape[-1]

    def row_source(unit):
        lanes = pl.ds(unit * wide, wide)
        return lambda side: dgh_ref.at[:, :, :, side, :, lanes]

    def put_dgh(unit, value):
        dgh_sum_ref[:, unit * wide : (unit + 1) * wide] = value

    row_sum = HalvingSum(
        (("core", "y", "z0", "z1"), ("core", "z0", "y", "z1")),
        [row_source(unit) for unit in range(2)],
        (gone_ref, gtwo_ref, gthree_ref, gfour_ref),
        gown_ref,
        gsend_sem,
        grecv_sem,
        gown_sem,
        put_dgh,
        bits,
        partners,
    )

    def rows_advance(stage):
        for unit in range(2):
            row_sum.advance(unit, stage)

    def scopy(stage):
        return remote(
            sums_ref.at[stage],
            here_ref.at[stage],
            ssend_sem.at[stage],
            srecv_sem.at[stage],
            partners[X_FIRST[stage]],
        )

    def small_advance(stage):
        scopy(stage).wait_recv()
        total = sums_ref[stage] + here_ref[stage]
        if stage < STAGES - 1:
            sums_ref[stage + 1] = total
            scopy(stage + 1).start()
        else:
            small_out_ref[...] = total

    halo = remote(halo_out, halo_dx, halo_send, halo_recv, before)
    two_ref[:came] = rest_ref[...]
    meet([partners[name] for name in AXES] + [before, after])
    for unit in range(came, units):
        engine.begin(unit)
    for load in loads:
        load.start()
    for unit in range(came):
        engine.copy(unit, 2).start()
    for unit in range(2):
        row_sum.begin(unit)
    for unit in range(came, units):
        engine.advance(unit, 0)
    for load in loads:
        load.wait()
    dnorm_ref[...] = jnp.zeros_like(dnorm_ref)

    def back(index):
        at = pl.ds(index * HALF, HALF)
        dh = (
            nt(dq_ref[at, :], wq_ref[...]) * query_scale
            + nt(dk_ref[at, :], wk_ref[...])
            + nt(dv_ref[at, :], wv_ref[...])
        )
        unit, scale = normalize_rows(x_ref[at, :].astype(f32))
        dnorm_ref[0:1] += jnp.sum(dh * unit, axis=0, keepdims=True)
        dnorm_ref[1:2] += jnp.sum(dh, axis=0, keepdims=True)
        dx = dy_ref[at, :] + norm_back(unit, scale, norms_ref[0:1], dh)
        if index == 0:
            halo_out[...] = dx.astype(bf16)
        else:
            token_ref[pl.ds((index - 1) * HALF, HALF), :] = dx

    for index in range(count // HALF):
        back(index)
        if index == 0:
            halo.start()
            rows_advance(0)
            for unit in range(came):
                engine.advance(unit, 2)
        if index == 2:
            rows_advance(1)
            for unit in range(came):
                engine.advance(unit, 3)

    hidden_rows = db1_ref.shape[0]
    parts = [
        db1_ref[...],
        db2_ref[...],
        dnorm_ref[0:2],
        dnorm_global_ref[0:2],
        dgain2_ref[...],
        doffset2_ref[...],
    ]
    filled = hidden_rows + 7
    parts.append(jnp.zeros((sums_ref.shape[1] - filled, width), f32))
    sums_ref[0] = jnp.concatenate(parts, 0)
    scopy(0).start()

    def weights_advance(stage):
        for unit in range(came, units):
            engine.advance(unit, stage)

    small_advance(0)
    weights_advance(1)
    small_advance(1)
    rows_advance(2)
    small_advance(2)
    weights_advance(2)
    small_advance(3)
    for unit in range(came):
        engine.advance(unit, 4)
    rows_advance(3)
    dgh = dgh_sum_ref[...]
    unit_rows, scale = normalize_rows(gx_ref[...].astype(f32))
    grad_out_ref[...] = gdy_ref[...] + norm_back(unit_rows, scale, norms_ref[2:3], dgh)
    small_advance(4)
    halo.wait_recv()
    halo_dx_out[...] = halo_dx[...]
    weights_advance(3)
    weights_advance(4)

    for unit in range(units):
        for stage in range(2 if unit < came else 0, STAGES):
            engine.sent(unit, stage)
    for stage in range(STAGES):
        scopy(stage).wait_send()
    for unit in range(2):
        for stage in range(4):
            row_sum.sent(unit, stage)
    halo.wait_send()


def finish_all(rest, x, dy, dq, dk, dv, dqkv, dgh, wq, wk, wv, small, gx, gdy, norms):
    count, width = x.shape
    rows, lanes = rest.shape[-2:]
    units = rest.shape[0] + 3
    own = gx.shape[0]
    place = (2, 2, 2, 2)
    small_rows = small[0].shape[0] + 7
    small_rows += -small_rows % 8
    anywhere = pl.BlockSpec(memory_space=pl.ANY)
    vmem = pl.BlockSpec(memory_space=pltpu.VMEM)
    dma = pltpu.SemaphoreType.DMA
    row = pltpu.VMEM((count, width), bf16)
    weight = pltpu.VMEM((width, width), bf16)
    half = pltpu.VMEM((HALF, width), bf16)
    return pl.pallas_call(
        finish_kernel,
        in_specs=[vmem] + [anywhere] * 10 + [vmem] * 8,
        out_specs=[vmem] * 5,
        out_shape=[
            jax.ShapeDtypeStruct((units * rows, lanes), f32),
            jax.ShapeDtypeStruct((small_rows, width), f32),
            jax.ShapeDtypeStruct((own, width), f32),
            jax.ShapeDtypeStruct((count - HALF, width), f32),
            jax.ShapeDtypeStruct((HALF, width), bf16),
        ],
        scratch_shapes=[
            row,
            pltpu.VMEM((count, width), f32),
            row,
            row,
            row,
            weight,
            weight,
            weight,
            dma((8,)),
        ]
        + sum_scratch(units, rows, lanes, True)
        + [
            pltpu.VMEM((2, 2, 2, 2, own, width // 2), bf16),
            pltpu.VMEM((2, 2, 2, 2, own, width // 2), bf16),
            pltpu.VMEM((2, 2, 2, own, width // 2), bf16),
            pltpu.VMEM((2, 2, own, width // 2), bf16),
            pltpu.VMEM((2, own, width // 2), bf16),
            dma((2, 4)),
            dma((2, 4)),
            dma((2,)),
            pltpu.VMEM((STAGES, small_rows, width), f32),
            pltpu.VMEM((STAGES, small_rows, width), f32),
            dma((STAGES,)),
            dma((STAGES,)),
            half,
            half,
            dma,
            dma,
            pltpu.VMEM((8, width), f32),
            pltpu.VMEM((own, width), f32),
        ],
        compiler_params=params(collective_id=0, has_side_effects=True),
        cost_estimate=pl.CostEstimate(
            flops=12 * count * width * width, bytes_accessed=30 * count * width, transcendentals=0
        ),
        name="finish_all",
    )(
        rest,
        x,
        dy,
        dq,
        dk,
        dv,
        dqkv.reshape((3,) + place + (2, rows, lanes)),
        dgh.reshape(place + (own, width)),
        wq,
        wk,
        wv,
        *small,
        gx,
        gdy,
        norms,
    )


def unpack_kernel(
    z_ref,
    halo_z_ref,
    dx_ref,
    halo_dx_ref,
    gz_ref,
    ggrad_ref,
    first_ref,
    second_ref,
    third_ref,
    small_ref,
    layer_ref,
    gz_out,
    token_ref,
    ggrad_out,
    wq_ref,
    wk_ref,
    wv_ref,
    wo_ref,
    w1_ref,
    w2_ref,
    b1_ref,
    b2_ref,
    norms_ref,
    turned_ref,
):
    step = pl.program_id(0)
    last = pl.num_programs(0) - 1

    @pl.when(step < last)
    def _():
        layer_ref[0] = z_ref[...]
        token_ref[0] = dx_ref[...]

    @pl.when(step == last)
    def _():
        layer_ref[0] = halo_z_ref[...]
        token_ref[0] = halo_dx_ref[...].astype(f32)

    rows = wq_ref.shape[0]

    @pl.when(step == 0)
    def _():
        gz_out[0] = gz_ref[...]
        ggrad_out[0] = ggrad_ref[...]
        for ref, unit in ((wo_ref, 2), (wq_ref, 3), (wk_ref, 4), (wv_ref, 5)):
            ref[...] = third_ref[unit * rows : (unit + 1) * rows]
        chunks = w1_ref.shape[0] // rows
        for chunk in range(chunks):
            for ref, unit in ((first_ref, chunk), (second_ref, chunk - 2), (third_ref, chunk - 3)):
                if 0 <= unit < ref.shape[0] // (2 * rows):
                    break
            start = 2 * unit * rows
            w1_ref[chunk * rows : (chunk + 1) * rows] = ref[start : start + rows]
            part = ref[start + rows : start + 2 * rows].T
            for place in range(part.shape[0] // rows):
                spot = (place * chunks + chunk) * rows
                turned_ref[spot : spot + rows, :] = part[place * rows : (place + 1) * rows, :]
        w2_ref[...] = turned_ref[...].T
        pieces_in_row = small_ref.shape[1] // LANES
        hidden_rows = b1_ref.shape[0] // pieces_in_row
        per_chunk = small_ref.shape[1] // rows
        natural = jnp.concatenate(
            [
                small_ref[chunk : chunk + 1, place * rows : (place + 1) * rows]
                for place in range(per_chunk)
                for chunk in range(hidden_rows)
            ],
            axis=1,
        )
        for piece in range(hidden_rows * pieces_in_row):
            b1_ref[piece : piece + 1] = natural[:, piece * LANES : (piece + 1) * LANES]
        for piece in range(pieces_in_row):
            b2_ref[piece : piece + 1] = small_ref[
                hidden_rows : hidden_rows + 1, piece * LANES : (piece + 1) * LANES
            ]
        norms_ref[...] = small_ref[hidden_rows + 1 : hidden_rows + 7]


def unpack(z, halo_z, dx, halo_dx, gz, ggrad, first, second, third, small, rows, hidden):
    count, width = z.shape
    own = gz.shape[0]
    lanes = first.shape[1]
    steps = count // HALF
    shapes = [
        ((1, count, width), bf16),
        ((1, own, width), bf16),
        ((1, count, width), f32),
        ((1, own, width), f32),
    ]
    shapes += [((rows, lanes), f32)] * 4
    shapes += [
        ((hidden // width * rows, lanes), f32),
        ((rows, hidden // width * lanes), f32),
        ((hidden // LANES, LANES), f32),
        ((width // LANES, LANES), f32),
        ((6, width), f32),
    ]
    tile = pl.BlockSpec((1, HALF, width), lambda i: (0, i, 0))
    return pl.pallas_call(
        unpack_kernel,
        grid=(steps,),
        in_specs=[
            pl.BlockSpec((HALF, width), lambda i: (jnp.minimum(i + 1, steps - 1), 0)),
            full(halo_z.shape),
            pl.BlockSpec((HALF, width), lambda i: (jnp.minimum(i, steps - 2), 0)),
            full(halo_dx.shape),
            full(gz.shape),
            full(ggrad.shape),
            full(first.shape),
            full(second.shape),
            full(third.shape),
            full(small.shape),
        ],
        out_specs=[
            tile if shape[1] == count else full(shape) for shape, unused in shapes
        ],
        out_shape=[jax.ShapeDtypeStruct(shape, kind) for shape, kind in shapes],
        scratch_shapes=[pltpu.VMEM((hidden // width * lanes, rows), f32)],
        compiler_params=params(),
        cost_estimate=pl.CostEstimate(
            flops=0, bytes_accessed=14 * count * width, transcendentals=0
        ),
        name="unpack",
    )(z, halo_z, dx, halo_dx, gz, ggrad, first, second, third, small)


def from_behind(value, axis, steps):
    count = lax.axis_size(axis)
    pairs = [(source, (source + steps) % count) for source in range(count)]
    return lax.ppermute(value, axis, pairs)


def pieces(value):
    first = lax.reduce_precision(value, 8, 7)
    second = lax.reduce_precision(value - first, 8, 7)
    return [first.astype(bf16), second.astype(bf16), (value - first - second).astype(bf16)]


def scatter_sum(value):
    half = lax.psum_scatter(value, "batch", scatter_dimension=1, tiled=True)
    part = lax.psum_scatter(half, "seq", scatter_dimension=0, tiled=True)
    return part.T.astype(f32)


def on_device(
    tokens,
    global_states,
    lengths,
    bucket_of,
    wq,
    wk,
    wv,
    wo,
    w1,
    b1,
    w2,
    b2,
    norm_params,
    cotangent,
    global_cotangent,
):
    rows = tokens.shape[1]
    width = tokens.shape[2]
    own = global_states.shape[1]
    seq_count = lax.axis_size("seq")
    seq_place = lax.axis_index("seq")
    group_rows = rows * seq_count
    own_start = seq_place * own
    first_of_slot = own_start % GLOBALS == 0
    place = jnp.stack(
        [
            lax.axis_index("batch"),
            seq_place,
            jnp.where(first_of_slot, own_start // GLOBALS, -1),
        ]
    ).astype(jnp.int32)
    scalars = (lengths, bucket_of, place)
    norms = [norm_params[i : i + 1] for i in range(6)]
    b2_rows = b2.reshape(-1, LANES)

    batch_count = lax.axis_size("batch")
    grid_of = None
    if seq_count == 16 and batch_count == 2 and 2 * own == GLOBALS and rows == 2 * BLOCK:
        grid_of = (seq_count, batch_count)

    if grid_of is None:
        arrived_tokens, arrived_grads = from_behind(
            (tokens[0, rows - HALF :], cotangent[0, rows - HALF :]), "seq", 1
        )
        x = jnp.concatenate([arrived_tokens, tokens[0, : rows - HALF]], 0)
        ct_head = arrived_grads
        all_states = lax.all_gather(global_states[0], "seq", axis=0, tiled=True)
        w1t = w1.T
        h, q, k, v = project_local(x, norms[0], norms[1], wq, wk, wv)
        gh, gq, gk, gv = project_global(
            scalars, rows, group_rows, all_states, norms[2], norms[3], wq, wk, wv
        )
    else:
        h, q, k, v, x, all_states, gh, gq, gk, gv, w1t = gather_project(
            tokens[0], global_states[0], w1, norm_params, wq, wk, wv
        )
        all_states, gh, gq, gk, gv = (
            value.reshape(-1, width) for value in (all_states, gh, gq, gk, gv)
        )
    far, far_stat, part, part_stat = slot_forward(scalars, rows, group_rows, q, k, v, gq, gk, gv)
    if grid_of is None:
        o, line = local_forward(
            False, scalars, rows, group_rows, q, k, v, far, far_stat, None, None
        )
        part_peak = part_stat[:, :, 0:2]
        peak = jnp.max(lax.all_gather(part_peak, "seq"), axis=0)
        factor = jnp.exp(part_peak - peak)
        scaled = part.reshape(SLOTS, PAIRS, 2, HEAD_DIM, GLOBALS).astype(f32) * factor[:, :, :, None]
        scaled = scaled.reshape(SLOTS, width, GLOBALS)
        scaled_total = (part_stat[:, :, 2:4] * factor).reshape(SLOTS, HEADS, GLOBALS)
        payload = jnp.concatenate(
            [scaled, scaled_total, jnp.zeros((SLOTS, 4, GLOBALS), f32)], 1
        ).transpose(0, 2, 1)
        sums = lax.psum_scatter(
            payload.astype(bf16).reshape(SLOTS * GLOBALS, -1), "seq", scatter_dimension=0, tiled=True
        ).astype(f32)
        own_total = sums[:, width : width + HEADS]
        all_peak = peak.reshape(SLOTS, HEADS, GLOBALS).transpose(0, 2, 1).reshape(-1, HEADS)
        own_peak = lax.dynamic_slice_in_dim(all_peak, own_start, own, 0)
        go = (
            (sums[:, :width].reshape(own, HEADS, HEAD_DIM) / own_total[:, :, None])
            .reshape(own, width)
            .astype(bf16)
        )
        gstat = own_peak + jnp.log(own_total)
    else:
        o, line, half_sum, half_stat = local_forward(
            True, scalars, rows, group_rows, q, k, v, far, far_stat, part, part_stat
        )

    z, dy, do, gz, gdy, gdo, dwo, db1, db2, dgain2, doffset2, *dws = branch(
        grid_of,
        x,
        o,
        cotangent[0],
        ct_head if grid_of is None else cotangent[0],
        global_states[0],
        go if grid_of is None else half_sum,
        gstat if grid_of is None else half_stat,
        global_cotangent[0],
        wo,
        w1t,
        b1.reshape(-1, LANES),
        w2,
        b2_rows,
        norm_params,
    )
    if grid_of is None:
        gcentre = jnp.sum(
            (gdo.astype(f32) * go.astype(f32)).reshape(own, HEADS, HEAD_DIM), axis=-1
        )
        message = jnp.concatenate(
            [gdo]
            + pieces(gstat)
            + pieces(gcentre)
            + [jnp.zeros((own, LANES - 6 * HEADS), bf16)],
            axis=1,
        )
        everyone = lax.all_gather(message, "seq", axis=0, tiled=True)
        dqt, dk, dv, centre = local_backward(
            False, scalars, rows, group_rows, q, k, v, do, o, line, None, None, None, None
        )
    else:
        sum_first, last, message, rest, z_head = dws
        dqt, dk, dv, centre, everyone, sum_second, rest = local_backward(
            True, scalars, rows, group_rows, q, k, v, do, o, line, message, rest, last, dwo
        )
        z_head, rest = lax.optimization_barrier((z_head, rest))
        halo_z = from_behind(z_head, "seq", -1)
    dq, dk, dv, dqkv, dgh, dnorm_global = slot_backward(
        grid_of,
        scalars,
        rows,
        group_rows,
        q,
        k,
        v,
        do,
        line,
        centre,
        dqt,
        dk,
        dv,
        gq,
        gk,
        gv,
        everyone,
        all_states,
        gh,
        h,
        wq,
        wk,
        wv,
    )
    if grid_of is None:
        dx, dnorm = project_back(x, dy, dq, dk, dv, wq, wk, wv, norms[0])
        back_z, back_grad = from_behind((z[:HALF], dx[:HALF].astype(bf16)), "seq", -1)
        layer_out = jnp.concatenate([z[HALF:], back_z], 0)
        token_grad = jnp.concatenate([dx[HALF:], back_grad.astype(f32)], 0)
        small = jnp.concatenate([db1, db2, dnorm[:2], dnorm_global[:2], dgain2, doffset2], 0)
        dgh = lax.psum_scatter(dgh, "seq", scatter_dimension=0, tiled=True).astype(f32)
        gunit, gscale = normalize_rows(global_states[0].astype(f32))
        global_grad = gdy + norm_back(gunit, gscale, norms[2], dgh)
        small = lax.psum(small, ("batch", "seq"))
        dw1, dw2 = dws
        weights = [scatter_sum(value) for value in (dqkv[0], dqkv[1], dqkv[2], dwo, dw1, dw2)]
    else:
        sum_third, small, global_grad, dx, halo_dx = finish_all(
            rest,
            x,
            dy,
            dq,
            dk,
            dv,
            dqkv,
            dgh,
            wq,
            wk,
            wv,
            (db1, db2, dnorm_global, dgain2, doffset2),
            global_states[0],
            gdy,
            norm_params,
        )
        results = unpack(
            z,
            halo_z,
            dx,
            halo_dx,
            gz,
            global_grad,
            sum_first,
            sum_second,
            sum_third,
            small,
            width // seq_count,
            w1.shape[1],
        )
        weights = [value.T for value in results[4:10]]
        biases = [value.reshape(-1) for value in results[10:12]]
        return (*results[:4], *weights, *biases, results[12])
    hidden_rows = w1.shape[1] // width
    return (
        layer_out[None],
        gz[None],
        token_grad[None],
        global_grad[None],
        *weights,
        small[:hidden_rows].reshape(-1),
        small[hidden_rows],
        small[hidden_rows + 1 : hidden_rows + 7],
    )


def solution(mesh):
    split = P("batch", "seq", None)
    return jax.shard_map(
        on_device,
        mesh=mesh,
        in_specs=(split, split) + (P(),) * 11 + (split, split),
        out_specs=(split,) * 4 + (P("batch", "seq"),) * 6 + (P(),) * 3,
        check_vma=False,
    )
```

```python
import functools

import jax
import jax.numpy as jnp
from jax import lax
from jax.experimental import pallas as pl
from jax.experimental.pallas import tpu as pltpu
from jax.sharding import PartitionSpec as P

HEADS = 12
HEAD_DIM = 64
PAIRS = HEADS // 2
LANES = 128
BLOCK = 512
HALF = 256
GLOBALS = 128
SLOTS = 8
FF_CHUNK = 768
TOGETHER = 3

norm_eps = 1e-05
masked_score = -1e30
query_scale = 0.125

SLOT_LANE = 16
GLOBAL_LANE = 32

f32 = jnp.float32
bf16 = jnp.bfloat16
VMEM_LIMIT = 60 * 1024 * 1024


def nn(left, right):
    return jnp.dot(left, right, preferred_element_type=f32)


def nt(left, right):
    return lax.dot_general(left, right, (((1,), (1,)), ((), ())), preferred_element_type=f32)


def tn(left, right):
    return lax.dot_general(left, right, (((0,), (0,)), ((), ())), preferred_element_type=f32)


def iota(shape, dim):
    return lax.broadcasted_iota(jnp.int32, shape, dim)


def stack_pair(pair):
    lane = iota((1, LANES), 1)
    low = jnp.where(lane < HEAD_DIM, 1.0, 0.0).astype(bf16)
    high = jnp.where(lane < HEAD_DIM, 0.0, 1.0).astype(bf16)
    return jnp.concatenate([pair * low, pair * high], axis=0)


def read_edges(lengths, bucket_of, place, edges):
    bucket = bucket_of[place[0]]
    total = jnp.int32(0)
    edges[0] = total
    for slot in range(SLOTS):
        total = total + lengths[bucket, slot]
        edges[slot + 1] = total


def block_start(place, rows, block):
    return place[1] * rows + block * BLOCK - HALF


def slot_present(slot, place, edges, rows, group_rows, block):
    low = edges[slot]
    high = edges[slot + 1]
    found = jnp.bool_(False)
    for part in range(BLOCK // HALF):
        start = block_start(place, rows, block) + part * HALF
        start = jnp.where(start < 0, start + group_rows, start)
        found = found | ((high > low) & (low < start + HALF) & (high > start))
    return found


def row_numbers(place, edges, rows, group_rows, block):
    place_in = block_start(place, rows, block) + iota((BLOCK, LANES), 0)
    wrapped = place_in < 0
    token = jnp.where(wrapped, place_in + group_rows, place_in)
    slot = jnp.zeros((BLOCK, LANES), jnp.int32)
    for j in range(SLOTS):
        slot = slot + jnp.where(edges[j + 1] <= token, 1, 0)
    return slot, slot + jnp.where(wrapped, SLOTS, 0)


def key_extra(slot, segment):
    lane = iota((BLOCK, LANES), 1)
    extra = jnp.where((lane < SLOT_LANE) & (lane != segment), masked_score, 0.0)
    return jnp.where(lane == GLOBAL_LANE + slot, 1.0, extra)


def query_extra(slot, segment):
    lane = iota((BLOCK, LANES), 1)
    return jnp.where((lane == segment) | (lane == SLOT_LANE + slot), 1.0, 0.0)


def global_key_extra(slot):
    lane = iota((GLOBALS, LANES), 1)
    inside = (lane >= SLOT_LANE) & (lane < SLOT_LANE + SLOTS)
    extra = jnp.where(inside & (lane != SLOT_LANE + slot), masked_score, 0.0)
    return jnp.where(lane == GLOBAL_LANE + slot, 1.0, extra)


def global_query_extra(slot):
    lane = iota((GLOBALS, LANES), 1)
    inside = (lane >= GLOBAL_LANE) & (lane < GLOBAL_LANE + SLOTS)
    return jnp.where(inside & (lane != GLOBAL_LANE + slot), masked_score, 0.0)


def normalize_rows(values):
    mean = jnp.mean(values, axis=-1, keepdims=True)
    centered = values - mean
    variance = jnp.mean(centered * centered, axis=-1, keepdims=True)
    scale = lax.rsqrt(variance + norm_eps)
    return centered * scale, scale


def norm_back(unit, scale, gain, upstream):
    inner = upstream * gain
    along = jnp.mean(inner * unit, axis=-1, keepdims=True)
    return scale * (inner - jnp.mean(inner, axis=-1, keepdims=True) - unit * along)


def gelu_parts(value):
    decay = jnp.exp(-0.5 * value * value)
    step = 1.0 / (1.0 + (0.3275911 * 0.7071067811865476) * jnp.abs(value))
    series = 1.061405429 * step - 1.453152027
    series = series * step + 1.421413741
    series = series * step - 0.284496736
    series = series * step + 0.254829592
    tail = (0.5 * series) * step * decay
    area = jnp.where(value >= 0.0, 1.0 - tail, tail)
    return area, decay * 0.3989422804014327


def full(shape):
    return pl.BlockSpec(shape, lambda *unused: (0,) * len(shape))


def once(shape):
    return pl.BlockSpec(
        shape, lambda *unused: (0,) * len(shape), pipeline_mode=pl.Buffered(buffer_count=1)
    )


def params(**more):
    return pltpu.CompilerParams(vmem_limit_bytes=VMEM_LIMIT, **more)


STAGES = 5
MESH = pl.DeviceIdType.MESH
WEIGHTS = (("core", 1), ("y", 2), ("z0", 4), ("z1", 8))


def my_place():
    batch = lax.axis_index("batch")
    seq = lax.axis_index("seq")
    bits = {"x": batch}
    partners = {"x": (1 - batch, seq)}
    for name, weight in WEIGHTS:
        bits[name] = (seq // weight) % 2
        partners[name] = (batch, seq + weight - 2 * weight * bits[name])
    return bits, partners


def meet(devices):
    barrier = pltpu.get_barrier_semaphore()
    for device in devices:
        pl.semaphore_signal(barrier, inc=1, device_id=device, device_id_type=MESH)
    pl.semaphore_wait(barrier, len(devices))


def remote(source, target, send, recv, device):
    return pltpu.make_async_remote_copy(
        src_ref=source,
        dst_ref=target,
        send_sem=send,
        recv_sem=recv,
        device_id=device,
        device_id_type=MESH,
    )


class RowGather:
    def __init__(self, ref, cut, send_sem, recv_sem, bits, partners):
        self.ref = ref
        self.cut = cut
        self.send_sem = send_sem
        self.recv_sem = recv_sem
        self.bits = bits
        self.partners = partners

    def copies(self, number):
        core, y, z0, z1 = (self.bits[name] for name in ("core", "y", "z0", "z1"))
        ref = self.ref
        rows = pl.ds(0, ref.shape[4])
        left = pl.ds(0, self.cut)
        right = pl.ds(self.cut, ref.shape[5] - self.cut)
        if number == 0:
            moves = [
                (ref.at[z1, z0, y, core, rows, left], "z1"),
                (ref.at[z1, z0, y, core, rows, right], "z1"),
            ]
        elif number == 1:
            moves = [
                (ref.at[:, z0, y, core, rows, left], "z0"),
                (ref.at[:, z0, y, core, rows, right], "y"),
            ]
        elif number == 2:
            moves = [
                (ref.at[:, :, y, core, rows, left], "y"),
                (ref.at[:, z0, :, core, rows, right], "z0"),
            ]
        else:
            moves = [
                (ref.at[:, :, :, core, rows, left], "core"),
                (ref.at[:, :, :, core, rows, right], "core"),
            ]
        return [
            remote(
                part,
                part,
                self.send_sem.at[number, side],
                self.recv_sem.at[number, side],
                self.partners[name],
            )
            for side, (part, name) in enumerate(moves)
        ]

    def begin(self, number=0):
        for copy in self.copies(number):
            copy.start()

    def advance(self, number):
        for copy in self.copies(number):
            copy.wait_recv()
        if number < 3:
            self.begin(number + 1)

    def end(self, first=0):
        for number in range(first, 4):
            for copy in self.copies(number):
                copy.wait_send()


X_FIRST = ("core", "x", "y", "z0", "z1")
Y_FIRST = ("core", "y", "x", "z0", "z1")
X_Z_FIRST = ("core", "x", "z0", "y", "z1")
Z_FIRST = ("core", "z0", "x", "z1", "y")
AXES = ("z1", "z0", "y", "core", "x")


class HalvingSum:
    def __init__(
        self, orders, sources, landings, own, send_sem, recv_sem, own_sem, put, bits, partners
    ):
        self.orders = orders
        self.sources = sources
        self.landings = landings
        self.own = own
        self.send_sem = send_sem
        self.recv_sem = recv_sem
        self.own_sem = own_sem
        self.put = put
        self.bits = bits
        self.partners = partners

    def part(self, unit, stage, other):
        order = self.orders[unit]
        name = order[stage]
        side = 1 - self.bits[name] if other else self.bits[name]
        if stage == 0:
            if not other and self.own is not None:
                return self.own.at[unit]
            return self.sources[unit](side)
        left = [axis for axis in AXES if axis in order[stage:]]
        index = (slice(None),) * left.index(name) + (side,)
        return self.landings[stage - 1].at[unit].at[index]

    def copy(self, unit, stage):
        return remote(
            self.part(unit, stage, True),
            self.landings[stage].at[unit],
            self.send_sem.at[unit, stage],
            self.recv_sem.at[unit, stage],
            self.partners[self.orders[unit][stage]],
        )

    def own_copy(self, unit):
        return pltpu.make_async_copy(
            self.sources[unit](self.bits["core"]), self.own.at[unit], self.own_sem.at[unit]
        )

    def begin(self, unit):
        if self.own is not None:
            self.own_copy(unit).start()
        self.copy(unit, 0).start()

    def advance(self, unit, stage, stop=False):
        if stage == 0 and self.own is not None:
            self.own_copy(unit).wait()
        self.copy(unit, stage).wait_recv()
        landing = self.landings[stage].at[unit]
        kept = self.part(unit, stage, False)
        if stage < len(self.orders[unit]) - 1:
            add_into(landing, kept)
            if not stop:
                self.copy(unit, stage + 1).start()
        else:
            self.put(unit, landing[...].astype(f32) + kept[...].astype(f32))

    def sent(self, unit, stage):
        self.copy(unit, stage).wait_send()


def put_rows(ref, rows):
    def put(unit, value):
        ref[unit * rows : (unit + 1) * rows] = value

    return put


def add_into(target, more):
    def one(i, carry):
        target[i] = target[i] + more[i]
        return carry

    lax.fori_loop(0, target.shape[0], one, 0)


def sum_scratch(units, rows, lanes, with_own):
    piece = (rows, lanes)
    dma = pltpu.SemaphoreType.DMA
    shapes = [pltpu.VMEM((units, 2, 2, 2, 2) + piece, bf16)] if with_own else []
    shapes += [
        pltpu.VMEM((units, 2, 2, 2, 2) + piece, bf16),
        pltpu.VMEM((units, 2, 2, 2) + piece, bf16),
        pltpu.VMEM((units, 2, 2) + piece, bf16),
        pltpu.VMEM((units, 2) + piece, bf16),
        pltpu.VMEM((units,) + piece, bf16),
        dma((units, STAGES)),
        dma((units, STAGES)),
    ]
    return shapes + ([dma((units,))] if with_own else [])


def project_rows(rows_ref, gain_ref, offset_ref, wq_ref, wk_ref, wv_ref, outs):
    unit, unused = normalize_rows(rows_ref[...].astype(f32))
    normed = (unit * gain_ref[...] + offset_ref[...]).astype(bf16)
    outs[0][...] = normed
    outs[1][...] = (nn(normed, wq_ref[...]) * query_scale).astype(bf16)
    outs[2][...] = nn(normed, wk_ref[...]).astype(bf16)
    outs[3][...] = nn(normed, wv_ref[...]).astype(bf16)


def project_local_kernel(rows_ref, gain_ref, offset_ref, wq_ref, wk_ref, wv_ref, *outs):
    project_rows(rows_ref, gain_ref, offset_ref, wq_ref, wk_ref, wv_ref, outs)


def project_local(rows, gain, offset, wq, wk, wv):
    count, width = rows.shape
    tile = pl.BlockSpec((BLOCK, width), lambda i: (i, 0))
    return pl.pallas_call(
        project_local_kernel,
        grid=(count // BLOCK,),
        in_specs=[tile, full((1, width)), full((1, width))] + [once((width, width))] * 3,
        out_specs=[tile] * 4,
        out_shape=[jax.ShapeDtypeStruct((count, width), bf16)] * 4,
        compiler_params=params(),
        cost_estimate=pl.CostEstimate(
            flops=6 * count * width * width, bytes_accessed=12 * count * width, transcendentals=0
        ),
        name="project_local",
    )(rows, gain, offset, wq, wk, wv)


def gather_project_kernel(
    tokens_ref,
    states_ref,
    w1_ref,
    norms_ref,
    wq_in,
    wk_in,
    wv_in,
    h_out,
    q_out,
    k_out,
    v_out,
    x_out,
    all_out,
    gh_out,
    gq_out,
    gk_out,
    gv_out,
    w1t_out,
    wq_ref,
    wk_ref,
    wv_ref,
    x_ref,
    all_ref,
    local_ref,
    global_ref,
    w1s_ref,
    w1t_ref,
    halo_send,
    halo_recv,
    load_sem,
    store_sem,
    gstore_sem,
    more_sem,
    send_sem,
    recv_sem,
):
    bits, partners = my_place()
    batch = lax.axis_index("batch")
    seq = lax.axis_index("seq")
    places = lax.axis_size("seq")
    after = (batch, lax.rem(seq + 1, places))
    before = (batch, lax.rem(seq + places - 1, places))
    rows, width = tokens_ref.shape
    own = states_ref.shape[0]
    core, y, z0, z1 = (bits[name] for name in ("core", "y", "z0", "z1"))
    start = pl.ds(0, HALF)
    most = pl.ds(0, rows - HALF)
    end = pl.ds(rows - HALF, HALF)
    shifted = pl.ds(HALF, rows - HALF)
    loads = [
        pltpu.make_async_copy(source, target, load_sem.at[number])
        for number, (source, target) in enumerate(
            (
                (tokens_ref.at[most], x_ref.at[shifted]),
                (wq_in, wq_ref),
                (wk_in, wk_ref),
                (wv_in, wv_ref),
                (w1_ref, w1s_ref),
            )
        )
    ]
    for load in loads:
        load.start()
    all_ref[z1, z0, y, core] = states_ref[...]
    meet([partners[name] for name, unused in WEIGHTS] + [before, after])
    halo = remote(tokens_ref.at[end], x_ref.at[start], halo_send, halo_recv, after)
    gather = RowGather(all_ref, width // 2, send_sem, recv_sem, bits, partners)
    gather.begin()
    halo.start()

    outs = (h_out, q_out, k_out, v_out)

    def stores(index):
        at = pl.ds(index * HALF, HALF)
        return [
            pltpu.make_async_copy(local_ref.at[which, at], out.at[at], store_sem.at[which, index])
            for which, out in enumerate(outs)
        ]

    def project(index):
        at = pl.ds(index * HALF, HALF)
        project_rows(
            x_ref.at[at],
            norms_ref.at[0:1],
            norms_ref.at[1:2],
            wq_ref,
            wk_ref,
            wv_ref,
            [local_ref.at[which, at] for which in range(4)],
        )
        for store in stores(index):
            store.start()

    for number in range(4):
        loads[number].wait()
    tiles = rows // HALF
    def turn(i, carry):
        at = pl.ds(pl.multiple_of(i * HALF, HALF), HALF)
        w1t_ref[at, :] = w1s_ref[:, at].T
        return carry

    project(1)
    project(2)
    gather.advance(0)
    for index in range(3, tiles):
        project(index)
    loads[4].wait()
    turns = w1t_ref.shape[0] // HALF
    lax.fori_loop(0, turns // 2, turn, 0)
    gather.advance(1)
    lax.fori_loop(turns // 2, turns, turn, 0)
    w1t_store = pltpu.make_async_copy(w1t_ref, w1t_out, more_sem.at[1])
    w1t_store.start()
    gather.advance(2)

    gouts = (gh_out, gq_out, gk_out, gv_out)

    def gstores(first, side):
        return [
            pltpu.make_async_copy(
                global_ref.at[which, first, :, :, side],
                out.at[first, :, :, side],
                gstore_sem.at[which, first, number],
            )
            for which, out in enumerate(gouts)
            for number in ((0 if side is core else 1),)
        ]

    def project_states(side):
        for first in range(2):
            piece = all_ref[first, :, :, side].reshape(4 * own, width)
            unit, unused = normalize_rows(piece.astype(f32))
            normed = (unit * norms_ref[2:3] + norms_ref[3:4]).astype(bf16)
            values = (
                normed,
                (nn(normed, wq_ref[...]) * query_scale).astype(bf16),
                nn(normed, wk_ref[...]).astype(bf16),
                nn(normed, wv_ref[...]).astype(bf16),
            )
            for which, value in enumerate(values):
                global_ref[which, first, :, :, side] = value.reshape(2, 2, own, width)
            for store in gstores(first, side):
                store.start()

    other = 1 - core
    project_states(core)
    gather.advance(3)
    all_store = pltpu.make_async_copy(all_ref, all_out, more_sem.at[2])
    all_store.start()
    project_states(other)
    halo.wait_recv()
    x_store = pltpu.make_async_copy(x_ref, x_out, more_sem.at[0])
    x_store.start()
    project(0)

    for index in range(tiles):
        for store in stores(index):
            store.wait()
    for side in (core, other):
        for first in range(2):
            for store in gstores(first, side):
                store.wait()
    x_store.wait()
    w1t_store.wait()
    all_store.wait()
    halo.wait_send()
    gather.end()


def gather_project(tokens, states, w1, norms, wq, wk, wv):
    rows, width = tokens.shape
    own = states.shape[0]
    vmem = pl.BlockSpec(memory_space=pltpu.VMEM)
    anywhere = pl.BlockSpec(memory_space=pl.ANY)
    dma = pltpu.SemaphoreType.DMA
    local = jax.ShapeDtypeStruct((rows, width), bf16)
    glob = jax.ShapeDtypeStruct((2, 2, 2, 2, own, width), bf16)
    turned = (w1.shape[1], width)
    weight = pltpu.VMEM((width, width), bf16)
    return pl.pallas_call(
        gather_project_kernel,
        in_specs=[anywhere, vmem, anywhere, vmem] + [anywhere] * 3,
        out_specs=[anywhere] * 11,
        out_shape=[local] * 5 + [glob] * 5 + [jax.ShapeDtypeStruct(turned, bf16)],
        scratch_shapes=[
            weight,
            weight,
            weight,
            pltpu.VMEM((rows, width), bf16),
            pltpu.VMEM(glob.shape, bf16),
            pltpu.VMEM((4, rows, width), bf16),
            pltpu.VMEM((4,) + glob.shape, bf16),
            pltpu.VMEM(w1.shape, bf16),
            pltpu.VMEM(turned, bf16),
            dma,
            dma,
            dma((5,)),
            dma((4, rows // HALF)),
            dma((4, 2, 2)),
            dma((3,)),
            dma((4, 2)),
            dma((4, 2)),
        ],
        compiler_params=params(collective_id=1, has_side_effects=True),
        cost_estimate=pl.CostEstimate(
            flops=6 * (rows + 16 * own) * width * width,
            bytes_accessed=24 * rows * width,
            transcendentals=0,
        ),
        name="gather_project",
    )(tokens, states, w1, norms, wq, wk, wv)


def project_global_kernel(
    rows_count,
    group_rows,
    lengths,
    bucket_of,
    place,
    rows_ref,
    gain_ref,
    offset_ref,
    wq_ref,
    wk_ref,
    wv_ref,
    h_ref,
    q_ref,
    k_ref,
    v_ref,
    edges,
):
    slot = pl.program_id(0)

    @pl.when(slot == 0)
    def _():
        read_edges(lengths, bucket_of, place, edges)

    needed = slot == place[2]
    for block in range(rows_count // BLOCK):
        needed = needed | slot_present(slot, place, edges, rows_count, group_rows, block)

    @pl.when(needed)
    def _():
        project_rows(
            rows_ref, gain_ref, offset_ref, wq_ref, wk_ref, wv_ref, (h_ref, q_ref, k_ref, v_ref)
        )


def project_global(scalars, rows_count, group_rows, rows, gain, offset, wq, wk, wv):
    count, width = rows.shape
    tile = pl.BlockSpec((GLOBALS, width), lambda i, *unused: (i, 0))
    return pl.pallas_call(
        functools.partial(project_global_kernel, rows_count, group_rows),
        grid_spec=pltpu.PrefetchScalarGridSpec(
            num_scalar_prefetch=3,
            grid=(SLOTS,),
            in_specs=[tile, full((1, width)), full((1, width))] + [once((width, width))] * 3,
            out_specs=[tile] * 4,
            scratch_shapes=[pltpu.SMEM((16,), jnp.int32)],
        ),
        out_shape=[jax.ShapeDtypeStruct((count, width), bf16)] * 4,
        compiler_params=params(),
        cost_estimate=pl.CostEstimate(
            flops=6 * 256 * width * width, bytes_accessed=12 * count * width, transcendentals=0
        ),
        name="project_global",
    )(*scalars, rows, gain, offset, wq, wk, wv)


def block_columns(place, edges, rows, group_rows, block, step, blocks, query_columns, key_columns):
    @pl.when(step < blocks)
    def _():
        slot_of, segment = row_numbers(place, edges, rows, group_rows, block)
        query_columns[block] = query_extra(slot_of, segment).astype(bf16)
        key_columns[block] = key_extra(slot_of, segment).astype(bf16)


def slot_line(place, edges, rows, group_rows, block):
    token = block_start(place, rows, block) + iota((1, BLOCK), 1)
    token = jnp.where(token < 0, token + group_rows, token)
    slot = jnp.zeros((1, BLOCK), jnp.int32)
    for j in range(SLOTS):
        slot = slot + jnp.where(edges[j + 1] <= token, 1, 0)
    return slot


def side_by_side(stacked):
    return stacked[:HEAD_DIM, : stacked.shape[1] // 2], stacked[HEAD_DIM:, stacked.shape[1] // 2 :]


def slot_forward_kernel(
    rows_count,
    group_rows,
    lengths,
    bucket_of,
    place,
    q_ref,
    k_ref,
    v_ref,
    gq_ref,
    gk_ref,
    gv_ref,
    far_ref,
    far_stat_ref,
    part_ref,
    part_stat_ref,
    edges,
    query_columns,
    key_columns,
    keys_ref,
    queries_ref,
    sum_ref,
    far_sum,
):
    group = pl.program_id(0)
    block = pl.program_id(1)
    blocks = rows_count // BLOCK
    step = group * blocks + block
    together = range(TOGETHER)

    @pl.when(step == 0)
    def _():
        read_edges(lengths, bucket_of, place, edges)

    @pl.when(block == 0)
    def _():
        sum_ref[...] = jnp.zeros_like(sum_ref)
        part_stat_ref[...] = jnp.broadcast_to(
            jnp.where(iota((8, GLOBALS), 0) < 2, masked_score, 0.0), part_stat_ref.shape
        )

    block_columns(
        place, edges, rows_count, group_rows, block, step, blocks, query_columns, key_columns
    )
    extra = query_columns[block]
    for which in together:
        lanes = pl.ds(which * LANES, LANES)
        keys_ref[which, :, :LANES] = k_ref[:, lanes]
        keys_ref[which, :, LANES:] = key_columns[block]
        queries_ref[which, :, :LANES] = stack_pair(q_ref[:, lanes])
        queries_ref[which, :BLOCK, LANES:] = extra
        queries_ref[which, BLOCK:, LANES:] = extra
    line = slot_line(place, edges, rows_count, group_rows, block)
    both_lines = jnp.concatenate([line, line], 1)

    def add(slot, keys_of, values_of):
        at = pl.ds(pl.multiple_of(slot * GLOBALS, GLOBALS), GLOBALS)
        extra = global_query_extra(slot).astype(bf16)
        for which in together:
            lanes = pl.ds(which * LANES, LANES)
            queries = jnp.concatenate(
                [stack_pair(gq_ref[at, lanes]), jnp.concatenate([extra, extra], 0)], axis=1
            )
            score = nt(keys_of(which), queries)
            stat = part_stat_ref[slot, which]
            old = jnp.concatenate([stat[0:1], stat[1:2]], axis=1)
            peak = jnp.maximum(old, jnp.max(score, axis=0, keepdims=True))
            weights = jnp.exp(score - peak)
            keep = jnp.exp(old - peak)
            total = jnp.concatenate([stat[2:3], stat[3:4]], axis=1) * keep + jnp.sum(
                weights, axis=0, keepdims=True
            )
            part_stat_ref[slot, which] = jnp.concatenate(
                [
                    peak[:, :GLOBALS],
                    peak[:, GLOBALS:],
                    total[:, :GLOBALS],
                    total[:, GLOBALS:],
                    jnp.zeros((4, GLOBALS), f32),
                ],
                axis=0,
            )
            low, high = side_by_side(tn(values_of(which), weights.astype(bf16)))
            sums = sum_ref.at[which, slot]
            sums[:HEAD_DIM] = sums[:HEAD_DIM] * keep[:, :GLOBALS] + low
            sums[HEAD_DIM:] = sums[HEAD_DIM:] * keep[:, GLOBALS:] + high

    far_sum[...] = jnp.zeros_like(far_sum)
    far_stat_ref[...] = jnp.zeros_like(far_stat_ref)

    def one_slot(slot, carry):
        @pl.when(slot_present(slot, place, edges, rows_count, group_rows, block))
        def _():
            add(
                slot,
                lambda which: keys_ref[which],
                lambda which: v_ref[:, pl.ds(which * LANES, LANES)],
            )
            at = pl.ds(pl.multiple_of(slot * GLOBALS, GLOBALS), GLOBALS)
            columns = global_key_extra(slot).astype(bf16)
            mine = both_lines == slot
            here = line == slot
            for which in together:
                lanes = pl.ds(which * LANES, LANES)
                slot_keys = jnp.concatenate([gk_ref[at, lanes], columns], 1)
                score = nt(slot_keys, queries_ref[which])
                peak = jnp.max(score, axis=0, keepdims=True)
                weights = jnp.exp(score - peak)
                total = jnp.sum(weights, axis=0, keepdims=True)
                stat = far_stat_ref.at[which, 0]
                stat[0:1] = jnp.where(mine, peak, stat[0:1])
                stat[1:2] = jnp.where(mine, total, stat[1:2])
                low, high = side_by_side(tn(gv_ref[at, lanes], weights.astype(bf16)))
                first = pl.ds(which * LANES, HEAD_DIM)
                second = pl.ds(which * LANES + HEAD_DIM, HEAD_DIM)
                far_sum[first] = jnp.where(here, low, far_sum[first])
                far_sum[second] = jnp.where(here, high, far_sum[second])

        return carry

    lax.fori_loop(0, SLOTS, one_slot, 0)
    far_ref[...] = far_sum[...].astype(bf16)

    @pl.when((block == blocks - 1) & (place[2] >= 0))
    def _():
        slot = place[2]
        at = pl.ds(pl.multiple_of(slot * GLOBALS, GLOBALS), GLOBALS)
        columns = global_key_extra(slot).astype(bf16)
        add(
            slot,
            lambda which: jnp.concatenate(
                [gk_ref[at, pl.ds(which * LANES, LANES)], columns], axis=1
            ),
            lambda which: gv_ref[at, pl.ds(which * LANES, LANES)],
        )

    @pl.when(block == blocks - 1)
    def _():
        for which in together:
            part_ref[:, which] = sum_ref[which].astype(bf16)


def line_spec(pairs=1):
    return pl.BlockSpec((pairs, 1, 8, 2 * BLOCK), lambda p, b, *unused: (p, b, 0, 0))


def column_scratch(blocks):
    return [pltpu.SMEM((16,), jnp.int32)] + [pltpu.VMEM((blocks, BLOCK, LANES), bf16)] * 2


def slot_forward(scalars, rows_count, group_rows, q, k, v, gq, gk, gv):
    blocks = rows_count // BLOCK
    all_globals, width = gq.shape
    block_spec = pl.BlockSpec((BLOCK, TOGETHER * LANES), lambda p, b, *unused: (b, p))
    pair_spec = pl.BlockSpec((all_globals, TOGETHER * LANES), lambda p, b, *unused: (0, p))
    return pl.pallas_call(
        functools.partial(slot_forward_kernel, rows_count, group_rows),
        grid_spec=pltpu.PrefetchScalarGridSpec(
            num_scalar_prefetch=3,
            grid=(PAIRS // TOGETHER, blocks),
            in_specs=[block_spec] * 3 + [pair_spec] * 3,
            out_specs=[
                pl.BlockSpec((TOGETHER * LANES, BLOCK), lambda p, b, *unused: (p, b)),
                line_spec(TOGETHER),
                pl.BlockSpec((SLOTS, TOGETHER, LANES, GLOBALS), lambda p, b, *unused: (0, p, 0, 0)),
                pl.BlockSpec((SLOTS, TOGETHER, 8, GLOBALS), lambda p, b, *unused: (0, p, 0, 0)),
            ],
            scratch_shapes=column_scratch(blocks)
            + [
                pltpu.VMEM((TOGETHER, BLOCK, 2 * LANES), bf16),
                pltpu.VMEM((TOGETHER, 2 * BLOCK, 2 * LANES), bf16),
                pltpu.VMEM((TOGETHER, SLOTS, LANES, GLOBALS), f32),
                pltpu.VMEM((TOGETHER * LANES, BLOCK), f32),
            ],
        ),
        out_shape=[
            jax.ShapeDtypeStruct((width, rows_count), bf16),
            jax.ShapeDtypeStruct((PAIRS, blocks, 8, 2 * BLOCK), f32),
            jax.ShapeDtypeStruct((SLOTS, PAIRS, LANES, GLOBALS), bf16),
            jax.ShapeDtypeStruct((SLOTS, PAIRS, 8, GLOBALS), f32),
        ],
        compiler_params=params(),
        cost_estimate=pl.CostEstimate(
            flops=8 * 4 * rows_count * GLOBALS * width,
            bytes_accessed=20 * all_globals * width,
            transcendentals=2 * HEADS * rows_count * GLOBALS,
        ),
        name="slot_forward",
    )(*scalars, q, k, v, gq, gk, gv)


def merge_parts(stat, sums, more_stat, more_sums):
    peak = jnp.maximum(stat[0:2], more_stat[0:2])
    keep = jnp.exp(stat[0:2] - peak)
    take = jnp.exp(more_stat[0:2] - peak)
    total = stat[2:4] * keep + more_stat[2:4] * take
    low = sums[:HEAD_DIM].astype(f32) * keep[0:1] + more_sums[:HEAD_DIM].astype(f32) * take[0:1]
    high = sums[HEAD_DIM:].astype(f32) * keep[1:2] + more_sums[HEAD_DIM:].astype(f32) * take[1:2]
    return (
        jnp.concatenate([peak, total, jnp.zeros((4, GLOBALS), f32)], 0),
        jnp.concatenate([low, high], 0),
    )


class SlotSum:
    ORDER = ("core", "y", "z0", "z1")

    def __init__(self, source, sums, stats, send_sem, recv_sem, bits, partners):
        self.source = source
        self.sums = sums
        self.stats = stats
        self.send_sem = send_sem
        self.recv_sem = recv_sem
        self.bits = bits
        self.partners = partners

    def held(self, stage, other):
        bit = self.bits[self.ORDER[stage]]
        side = 1 - bit if other else bit
        if stage == 0:
            return self.source(side)
        index = ((), (slice(None), slice(None)), (slice(None),), ())[stage] + (side,)
        return self.sums[stage - 1].at[index], self.stats[stage - 1].at[index]

    def copies(self, stage):
        partner = self.partners[self.ORDER[stage]]
        sums, stat = self.held(stage, True)
        return (
            remote(
                sums,
                self.sums[stage],
                self.send_sem.at[stage, 0],
                self.recv_sem.at[stage, 0],
                partner,
            ),
            remote(
                stat,
                self.stats[stage],
                self.send_sem.at[stage, 1],
                self.recv_sem.at[stage, 1],
                partner,
            ),
        )

    def begin(self, stage):
        for copy in self.copies(stage):
            copy.start()

    def merge(self, stage, kept=None):
        for copy in self.copies(stage):
            copy.wait_recv()
        sums, stat = self.held(stage, False) if kept is None else kept
        lead = self.sums[stage].shape[:-3]
        total = 1
        for size in lead:
            total = total * size

        def one(number, carry):
            index = []
            left = number
            for size in reversed(lead):
                index.append(left % size)
                left = left // size
            index = tuple(reversed(index))
            for which in range(PAIRS // 2):
                spot = index + (which,)
                new_stat, new_sums = merge_parts(
                    self.stats[stage][spot], self.sums[stage][spot], stat[spot], sums[spot]
                )
                self.stats[stage][spot] = new_stat
                self.sums[stage][spot] = new_sums.astype(bf16)
            return carry

        lax.fori_loop(0, total, one, 0)

    def sent(self, stage):
        for copy in self.copies(stage):
            copy.wait_send()


def local_forward_kernel(
    talk,
    rows_count,
    group_rows,
    lengths,
    bucket_of,
    place,
    q_ref,
    k_ref,
    v_ref,
    far_ref,
    far_stat_ref,
    *refs,
):
    if talk:
        part_ref, part_stat_ref = refs[:2]
        o_ref, line_ref, half_ref, half_stat_ref = refs[2:6]
        own_ref, own_stat_ref = refs[6:8]
        sums_refs = refs[8:10]
        stat_refs = refs[10:12]
        edges, query_columns, key_columns, send_sem, recv_sem, own_sem = refs[12:]
    else:
        o_ref, line_ref, edges, query_columns, key_columns = refs
    pair = pl.program_id(0)
    block = pl.program_id(1)
    blocks = rows_count // BLOCK
    step = pair * blocks + block

    @pl.when(step == 0)
    def _():
        read_edges(lengths, bucket_of, place, edges)

    if talk:
        bits, partners = my_place()
        slot_sum = SlotSum(
            lambda side: (part_ref.at[:, :, :, side], part_stat_ref.at[:, :, :, side]),
            sums_refs,
            stat_refs,
            send_sem,
            recv_sem,
            bits,
            partners,
        )
        own_parts = slot_sum.held(0, False)
        own_copies = [
            pltpu.make_async_copy(own_parts[0], own_ref, own_sem.at[0]),
            pltpu.make_async_copy(own_parts[1], own_stat_ref, own_sem.at[1]),
        ]

        @pl.when(step == 0)
        def _():
            meet([partners["core"], partners["y"]])
            for copy in own_copies:
                copy.start()
            slot_sum.begin(0)

        @pl.when(step == 3)
        def _():
            for copy in own_copies:
                copy.wait()
            slot_sum.merge(0, (own_ref, own_stat_ref))
            slot_sum.begin(1)

        @pl.when(step == PAIRS * blocks - 1)
        def _():
            slot_sum.merge(1)
            half_ref[...] = sums_refs[1][...]
            half_stat_ref[...] = stat_refs[1][...]
            slot_sum.sent(0)
            slot_sum.sent(1)

    block_columns(
        place, edges, rows_count, group_rows, block, step, blocks, query_columns, key_columns
    )
    extra = query_columns[block]
    queries = jnp.concatenate(
        [stack_pair(q_ref[...]), jnp.concatenate([extra, extra], 0)], axis=1
    )
    keys = jnp.concatenate([k_ref[...], key_columns[block]], axis=1)
    score = nt(keys, queries)
    far_peak = far_stat_ref[0, 0, 0:1]
    peak = jnp.maximum(jnp.max(score, axis=0, keepdims=True), far_peak)
    weights = jnp.exp(score - peak)
    far_keep = jnp.exp(far_peak - peak)
    total = jnp.sum(weights, axis=0, keepdims=True) + far_stat_ref[0, 0, 1:2] * far_keep
    low, high = side_by_side(tn(v_ref[...], weights.astype(bf16)))
    low = (low + far_ref[:HEAD_DIM] * far_keep[:, :BLOCK]) / total[:, :BLOCK]
    high = (high + far_ref[HEAD_DIM:] * far_keep[:, BLOCK:]) / total[:, BLOCK:]
    o_ref[...] = jnp.concatenate([low, high], 0).T.astype(bf16)
    line_ref[0, 0] = jnp.broadcast_to(peak + jnp.log(total), (8, 2 * BLOCK))


def local_forward(
    talk, scalars, rows_count, group_rows, q, k, v, far, far_stat, part, part_stat
):
    blocks = rows_count // BLOCK
    width = q.shape[1]
    block_spec = pl.BlockSpec((BLOCK, LANES), lambda p, b, *unused: (b, p))
    operands = [q, k, v, far, far_stat]
    in_specs = [block_spec] * 3 + [
        pl.BlockSpec((LANES, BLOCK), lambda p, b, *unused: (p, b)),
        line_spec(),
    ]
    out_specs = [block_spec, line_spec()]
    out_shape = [
        jax.ShapeDtypeStruct((rows_count, width), bf16),
        jax.ShapeDtypeStruct((PAIRS, blocks, 8, 2 * BLOCK), f32),
    ]
    scratch = []
    more = {}
    edges = column_scratch(blocks)
    if talk:
        cut = (2, 2, 2, 2, PAIRS // 2)
        operands += [
            part.reshape(cut + part.shape[2:]),
            part_stat.reshape(cut + part_stat.shape[2:]),
        ]
        in_specs += [pl.BlockSpec(memory_space=pl.ANY)] * 2
        shapes = [
            (2, 2, PAIRS // 2, LANES, GLOBALS),
            (2, 2, PAIRS // 2, 8, GLOBALS),
        ]
        out_specs += [full(shape) for shape in shapes]
        out_shape += [
            jax.ShapeDtypeStruct(shapes[0], bf16),
            jax.ShapeDtypeStruct(shapes[1], f32),
        ]
        leads = [(2, 2, 2), (2, 2, 2), (2, 2)]
        sums = [pltpu.VMEM(lead + shapes[0][2:], bf16) for lead in leads]
        stats = [pltpu.VMEM(lead + shapes[1][2:], f32) for lead in leads]
        dma = pltpu.SemaphoreType.DMA
        scratch = [sums[0], stats[0]] + sums[1:] + stats[1:]
        edges += [dma((2, 2)), dma((2, 2)), dma((2,))]
        more = {"collective_id": 2, "has_side_effects": True}
    return pl.pallas_call(
        functools.partial(local_forward_kernel, talk, rows_count, group_rows),
        grid_spec=pltpu.PrefetchScalarGridSpec(
            num_scalar_prefetch=3,
            grid=(PAIRS, blocks),
            in_specs=in_specs,
            out_specs=out_specs,
            scratch_shapes=scratch + edges,
        ),
        out_shape=out_shape,
        compiler_params=params(**more),
        cost_estimate=pl.CostEstimate(
            flops=16 * rows_count * BLOCK * width,
            bytes_accessed=16 * rows_count * width,
            transcendentals=HEADS * rows_count * BLOCK,
        ),
        name="local_forward",
    )(*scalars, *operands)


def join_rows(ref):
    return jnp.concatenate([ref[i : i + 1] for i in range(ref.shape[0])], axis=1)


def take_lanes(row, starts, length):
    return jnp.concatenate([row[:, start : start + length] for start in starts], axis=1)


def put_grouped(ref, value):
    seq, batch, rows, lanes = ref.shape
    for part in range(batch):
        piece = value[:, part * lanes : (part + 1) * lanes].astype(bf16)
        ref[:, part] = piece.reshape(seq, rows, lanes)


def put_unit(ref, value):
    batch, rows, lanes = ref.shape[4:]
    for part in range(batch):
        piece = value[:, part * lanes : (part + 1) * lanes].astype(bf16)
        ref[:, :, :, :, part] = piece.reshape(ref.shape[:4] + (rows, lanes))


TICKS = 3
ENDINGS = ((0, 2, 4, 6, 8), (3, 5, 7, 9, 10), (6, 8))


def branch_kernel(
    tile,
    seq_size,
    x_ref,
    o_ref,
    ct_ref,
    ct_head_ref,
    gx_ref,
    go_in_ref,
    gstat_in_ref,
    gct_ref,
    wo_ref,
    w1_ref,
    b1_ref,
    w2_ref,
    b2_ref,
    norms_ref,
    z_ref,
    dy_ref,
    do_ref,
    gz_ref,
    gdy_ref,
    gdo_ref,
    dwo_ref,
    db1_ref,
    db2_ref,
    dgain_ref,
    doffset_ref,
    first_ref,
    second_ref,
    *refs,
):
    talk = seq_size > 0
    if talk:
        message_ref, rest_ref, z_head_ref = refs[:3]
        refs = refs[3:]
    os_ref, cts_ref, y_ref, h_ref, z_sum_ref, dh_ref, dft_ref, a_ref, du_ref, load_sem = refs[:10]
    b1s_ref = refs[10]
    refs = refs[11:]
    step = pl.program_id(0)
    steps = pl.num_programs(0)
    count, width = x_ref.shape
    own = gx_ref.shape[0]
    extra = os_ref.shape[0] - count
    tiles = count // tile
    tail = pl.ds(count, extra)

    def rows_at(i):
        return pl.ds(i * tile, tile)

    def padded(value):
        return jnp.concatenate([value, jnp.zeros((extra - own, width), value.dtype)], axis=0)

    if talk:
        units_ref = refs[0]
        landings = refs[1:6]
        send_sem, recv_sem = refs[6:8]
        half_ref, half_stat_ref = refs[8:10]
        slot_sums = refs[10:12]
        slot_stats = refs[12:14]
        turned_ref, go_land, gstat_land, stat_ref, slot_send, slot_recv = refs[14:20]
        message_land, message_send, message_recv, halo_send, halo_recv = refs[20:]
        last_step = 4
        bits, partners = my_place()
        core = bits["core"]
        chunks = last_step - 1
        slots = units_ref.shape[0]
        plan = [
            (tick, chunk, stage)
            for chunk, ticks in enumerate(ENDINGS)
            for stage, tick in enumerate(ticks)
        ]

        def source(unit):
            return lambda side: units_ref.at[unit % slots, :, :, :, side]

        engine = HalvingSum(
            (X_FIRST, Y_FIRST) * chunks,
            [source(unit) for unit in range(2 * chunks)],
            landings,
            None,
            send_sem,
            recv_sem,
            None,
            put_rows(first_ref, landings[4].shape[1]),
            bits,
            partners,
        )

        def advance(tick):
            for when, chunk, stage in sorted(plan, key=lambda entry: -entry[2]):
                if when == tick:
                    for unit in (2 * chunk, 2 * chunk + 1):
                        engine.advance(unit, stage, stop=chunk == chunks - 1 and stage == 1)

        def tick_at(position):
            for number in range(1, last_step):
                tick = TICKS * (number - 1) + position

                @pl.when(step == number)
                def _():
                    advance(tick)

        slot_sum = SlotSum(
            None,
            (None, half_ref) + tuple(slot_sums),
            (None, half_stat_ref) + tuple(slot_stats),
            slot_send,
            slot_recv,
            bits,
            partners,
        )
        half_pairs = PAIRS // 2
        lanes = half_pairs * LANES
        my_lanes = pl.ds(pl.multiple_of(core * lanes, LANES), lanes)

        def final_copies():
            theirs = pl.ds(pl.multiple_of((1 - core) * own, own), own)
            return (
                remote(
                    turned_ref.at[theirs],
                    go_land.at[:, my_lanes],
                    slot_send.at[4, 0],
                    slot_recv.at[4, 0],
                    partners["core"],
                ),
                remote(
                    gstat_land.at[core],
                    gstat_land.at[core],
                    slot_send.at[4, 1],
                    slot_recv.at[4, 1],
                    partners["core"],
                ),
            )

        def finish_slots():
            slot_sum.merge(3)
            for which in range(half_pairs):
                stat = slot_stats[1][which]
                total = stat[2:4]
                sums = slot_sums[1][which].astype(f32)
                mean = jnp.concatenate(
                    [sums[:HEAD_DIM] / total[0:1], sums[HEAD_DIM:] / total[1:2]], 0
                )
                turned_ref[:, which * LANES : (which + 1) * LANES] = mean.T.astype(bf16)
                whole = stat[0:2] + jnp.log(total)
                gstat_land[core, which] = jnp.concatenate(
                    [whole, jnp.zeros((6, GLOBALS), f32)], 0
                )
            mine = pl.ds(pl.multiple_of(core * own, own), own)
            go_land[:, my_lanes] = turned_ref[mine, :]
            for copy in final_copies():
                copy.start()

        def put_message():
            product = gdo_ref[...].astype(f32) * go_land[...].astype(f32)
            head_of = iota((width, LANES), 0) // HEAD_DIM == iota((width, LANES), 1)
            head_of = jnp.where(head_of, 1.0, 0.0).astype(bf16)
            first = product.astype(bf16)
            second = (product - first.astype(f32)).astype(bf16)
            centre = nn(first, head_of) + nn(second, head_of)
            lines = [gstat_land[half, which, 0:2] for half in (0, 1) for which in range(half_pairs)]
            lines = jnp.concatenate(lines + [jnp.zeros((LANES - HEADS, GLOBALS), f32)], 0)
            stat_ref[...] = lines.T
            total = stat_ref[pl.ds(pl.multiple_of(core * own, own), own), :]
            spread = jnp.zeros((own, LANES), f32)
            for number, value in enumerate((total, centre)):
                for piece in range(3):
                    low = value.astype(bf16)
                    value = value - low.astype(f32)
                    start_lane = (3 * number + piece) * HEADS
                    source_lane = iota((LANES, LANES), 0)
                    moved = iota((LANES, LANES), 1) == source_lane + start_lane
                    moved = jnp.where(moved & (source_lane < HEADS), 1.0, 0.0).astype(bf16)
                    spread = spread + nn(low, moved)
            mine = message_land.at[bits["z1"]]
            mine[:, :width] = gdo_ref[...]
            mine[:, width:] = spread.astype(bf16)
            message_copy().start()

        def message_copy():
            mine = message_land.at[bits["z1"]]
            return remote(mine, mine, message_send, message_recv, partners["z1"])

    else:

        def tick_at(position):
            pass

    if talk:
        batch = lax.axis_index("batch")
        seq_place = lax.axis_index("seq")
        places = lax.axis_size("seq")
        after = (batch, lax.rem(seq_place + 1, places))
        before = (batch, lax.rem(seq_place + places - 1, places))
        halo = remote(
            ct_ref.at[pl.ds(count - HALF, HALF)],
            cts_ref.at[pl.ds(0, HALF)],
            halo_send,
            halo_recv,
            after,
        )
    loads = [
        pltpu.make_async_copy(o_ref, os_ref.at[pl.ds(0, count)], load_sem.at[0]),
        pltpu.make_async_copy(
            ct_ref.at[pl.ds(0, count - HALF)],
            cts_ref.at[pl.ds(HALF, count - HALF)],
            load_sem.at[1],
        ),
    ]
    if not talk:
        loads.append(
            pltpu.make_async_copy(ct_head_ref, cts_ref.at[pl.ds(0, HALF)], load_sem.at[2])
        )

    def start(at, size, x, sums):
        y = x.astype(f32) + nn(os_ref[at, :], wo_ref[...])
        unit, unused = normalize_rows(y)
        h_ref[at, :] = (unit * norms_ref[4:5] + norms_ref[5:6]).astype(bf16)
        y_ref[at, :] = y
        sums[...] = y + join_rows(b2_ref)
        dh_ref[at, :] = jnp.zeros((size, width), f32)

    @pl.when(step == 0)
    def _():
        for load in loads:
            load.start()
        if talk:
            half_ref[...] = go_in_ref[...]
            half_stat_ref[...] = gstat_in_ref[...]
            meet([partners[name] for name in AXES] + [before, after])
            slot_sum.begin(2)
            halo.start()
        cts_ref[count:] = padded(gct_ref[...])
        loads[0].wait()

        def start_tile(i, carry):
            at = pl.ds(pl.multiple_of(i * tile, tile), tile)
            start(at, tile, x_ref[at, :], dy_ref.at[at])
            return carry

        lax.fori_loop(0, tiles, start_tile, 0)
        for load in loads[1:]:
            load.wait()

    @pl.when(step == 0)
    def _():
        row = join_rows(b1_ref)
        for number in range(b1s_ref.shape[0]):
            if talk:
                share = FF_CHUNK // seq_size
                starts = [place * b1s_ref.shape[0] * share for place in range(seq_size)]
                starts = [start + number * share for start in starts]
                b1s_ref[number : number + 1] = take_lanes(row, starts, share)
            else:
                b1s_ref[number : number + 1] = row[:, number * FF_CHUNK : (number + 1) * FF_CHUNK]

    my_row = pl.ds(step, 1)
    db1_ref[my_row, :] = jnp.zeros((1, FF_CHUNK), f32)
    w1 = w1_ref[...].reshape(width, width)
    w2 = w2_ref[...].reshape(width, width)

    def chunk_of(at, sums):
        u = nt(h_ref[at, :], w1) + b1s_ref[my_row, :]
        da = nt(cts_ref[at, :], w2)
        area, density = gelu_parts(u)
        a = (u * area).astype(bf16)
        du = (da * (area + u * density)).astype(bf16)
        a_ref[at, :] = a
        du_ref[at, :] = du
        db1_ref[my_row, :] += jnp.sum(du.astype(f32), axis=0, keepdims=True)
        sums[...] = sums[...] + nn(a, w2)
        dh_ref[at, :] = dh_ref[at, :] + nn(du, w1)

    for i in range(1, tiles):
        chunk_of(rows_at(i), dy_ref.at[rows_at(i)])

    if talk:

        @pl.when(step == 0)
        def _():
            slot_sum.merge(2)
            slot_sum.begin(3)
            halo.wait_recv()

    tick_at(0)
    chunk_of(rows_at(0), dy_ref.at[rows_at(0)])

    @pl.when(step == 0)
    def _():
        if talk:
            finish_slots()
            halo.wait_send()
        dft_ref[...] = cts_ref[...].T
        if talk:
            for copy in final_copies():
                copy.wait_recv()
            os_ref[count:] = padded(go_land[...])
        else:
            os_ref[count:] = padded(go_in_ref[...])
        start(tail, extra, padded(gx_ref[...]), z_sum_ref)

    chunk_of(tail, z_sum_ref)
    tick_at(1)
    dw1 = tn(du_ref[...], h_ref[...])
    dw2 = nn(dft_ref[...], a_ref[...])
    if talk:
        for number in range(chunks):

            @pl.when(step == number)
            def _():
                for which, value in ((0, dw1), (1, dw2)):
                    unit = 2 * number + which
                    if unit >= slots:
                        engine.sent(unit - slots, 0)
                    put_unit(units_ref.at[unit % slots], value)

        @pl.when(step == chunks)
        def _():
            put_unit(second_ref.at[0], dw1)
            put_unit(second_ref.at[1], dw2)

        tick_at(2)
        for number in range(chunks):

            @pl.when(step == number)
            def _():
                engine.begin(2 * number)
                engine.begin(2 * number + 1)

    else:
        first_ref[...] = dw1.astype(bf16)
        second_ref[...] = dw2.astype(bf16)

    @pl.when(step == steps - 1)
    def _():
        db2_ref[...] = jnp.zeros_like(db2_ref)
        dgain_ref[...] = jnp.zeros_like(dgain_ref)
        doffset_ref[...] = jnp.zeros_like(doffset_ref)

        def finish(at, size, sums, put):
            z = sums[...].astype(bf16)
            unit, scale = normalize_rows(y_ref[at, :])
            dh = dh_ref[at, :]
            ct = cts_ref[at, :].astype(f32)
            dy = ct + norm_back(unit, scale, norms_ref[4:5], dh)
            db2_ref[...] += jnp.sum(ct, axis=0, keepdims=True)
            doffset_ref[...] += jnp.sum(dh, axis=0, keepdims=True)
            dgain_ref[...] += jnp.sum(dh * unit, axis=0, keepdims=True)
            low = dy.astype(bf16)
            h_ref[at, :] = low
            put(z, dy, nt(low, wo_ref[...]).astype(bf16))

        def finish_tile(i, carry):
            at = pl.ds(pl.multiple_of(i * tile, tile), tile)

            def put(z, dy, do):
                z_ref[at, :] = z
                dy_ref[at, :] = dy
                do_ref[at, :] = do

            finish(at, tile, dy_ref.at[at], put)
            return carry

        def put_tail(z, dy, do):
            gz_ref[...] = z[:own]
            gdy_ref[...] = dy[:own]
            gdo_ref[...] = do[:own]

        finish(tail, extra, z_sum_ref, put_tail)
        if talk:
            put_message()
            advance(TICKS * chunks)
        lax.fori_loop(0, tiles, finish_tile, 0)
        dwo = tn(h_ref[...], os_ref[...])
        if talk:
            put_grouped(dwo_ref, dwo)
            advance(TICKS * chunks + 1)
            rest_ref[...] = landings[1][2 * chunks - 2 :]
            z_head_ref[...] = z_ref[:HALF]
            for when, chunk, stage in plan:
                for unit in (2 * chunk, 2 * chunk + 1):
                    if stage > 0 or unit + slots >= 2 * chunks:
                        engine.sent(unit, stage)
            slot_sum.sent(2)
            slot_sum.sent(3)
            for copy in final_copies():
                copy.wait_send()
            message_copy().wait_recv()
            message_ref[...] = message_land[...]
            message_copy().wait_send()
        else:
            dwo_ref[...] = dwo.astype(bf16)


def branch(grid_of, x, o, ct, ct_head, gx, go, gstat, gct, wo, w1t, b1, w2, b2, norms):
    count, width = x.shape
    own = gx.shape[0]
    hidden = w2.shape[0]
    steps = hidden // FF_CHUNK
    total = count + -(-own // LANES) * LANES
    row = once((count, width))
    few = once((own, width))
    line = full((1, width))
    anywhere = pl.BlockSpec(memory_space=pl.ANY)
    scratch = []
    more = {}
    if grid_of is None:
        weight_spec = pl.BlockSpec((FF_CHUNK, width), lambda j: (j, 0))
        dw_shapes = [(hidden, width), (width, hidden)]
        dw_types = [bf16, bf16]
        dw_specs = [weight_spec, pl.BlockSpec((width, FF_CHUNK), lambda j: (0, j))]
        dwo_shape = (width, width)
    else:
        seq, batch = grid_of
        rows, lanes = width // seq, width // batch
        weight_spec = pl.BlockSpec((seq, 1, rows, width), lambda j: (0, j, 0, 0))
        w1t = w1t.reshape(seq, steps, rows, width)
        w2 = w2.reshape(seq, steps, rows, width)
        units = 2 * (steps - 1)
        sums, stats = go.shape[2:], gstat.shape[2:]
        dw_shapes = [
            ((units - 2) * rows, lanes),
            (2, 2, 2, 2, 2, batch, rows, lanes),
            (2, own, width + LANES),
            (2, 2, 2, 2, rows, lanes),
            (HALF, width),
        ]
        dw_types = [f32, bf16, bf16, bf16, bf16]
        dw_specs = [once(shape) for shape in dw_shapes]
        dwo_shape = (seq, batch, rows, lanes)
        dma = pltpu.SemaphoreType.DMA
        scratch = (
            [pltpu.VMEM((4,) + dw_shapes[1][1:], bf16)]
            + sum_scratch(units, rows, lanes, False)
            + [
                pltpu.VMEM(go.shape, bf16),
                pltpu.VMEM(gstat.shape, f32),
                pltpu.VMEM((2,) + sums, bf16),
                pltpu.VMEM(sums, bf16),
                pltpu.VMEM((2,) + stats, f32),
                pltpu.VMEM(stats, f32),
                pltpu.VMEM((GLOBALS, PAIRS // 2 * LANES), bf16),
                pltpu.VMEM((own, width), bf16),
                pltpu.VMEM((2,) + stats, f32),
                pltpu.VMEM((GLOBALS, LANES), f32),
                dma((5, 2)),
                dma((5, 2)),
                pltpu.VMEM((2, own, width + LANES), bf16),
                dma,
                dma,
                dma,
                dma,
            ]
        )
        more = {"collective_id": 3, "has_side_effects": True}
    out = pl.pallas_call(
        functools.partial(branch_kernel, BLOCK, grid_of[0] if grid_of else 0),
        grid=(steps,),
        in_specs=[
            row,
            anywhere,
            anywhere,
            anywhere,
            few,
            once(go.shape),
            once(gstat.shape),
            few,
            once((width, width)),
            weight_spec,
            full(b1.shape),
            weight_spec,
            full(b2.shape),
            full(norms.shape),
        ],
        out_specs=[row, row, row, few, few, few]
        + [once(dwo_shape), full((steps, FF_CHUNK)), line, line, line]
        + dw_specs,
        out_shape=[
            jax.ShapeDtypeStruct((count, width), bf16),
            jax.ShapeDtypeStruct((count, width), f32),
            jax.ShapeDtypeStruct((count, width), bf16),
            jax.ShapeDtypeStruct((own, width), bf16),
            jax.ShapeDtypeStruct((own, width), f32),
            jax.ShapeDtypeStruct((own, width), bf16),
            jax.ShapeDtypeStruct(dwo_shape, bf16),
            jax.ShapeDtypeStruct((steps, FF_CHUNK), f32),
            jax.ShapeDtypeStruct((1, width), f32),
            jax.ShapeDtypeStruct((1, width), f32),
            jax.ShapeDtypeStruct((1, width), f32),
        ]
        + [jax.ShapeDtypeStruct(shape, kind) for shape, kind in zip(dw_shapes, dw_types)],
        scratch_shapes=[
            pltpu.VMEM((total, width), bf16),
            pltpu.VMEM((total, width), bf16),
            pltpu.VMEM((total, width), f32),
            pltpu.VMEM((total, width), bf16),
            pltpu.VMEM((total - count, width), f32),
            pltpu.VMEM((total, width), f32),
            pltpu.VMEM((width, total), bf16),
            pltpu.VMEM((total, FF_CHUNK), bf16),
            pltpu.VMEM((total, FF_CHUNK), bf16),
            pltpu.SemaphoreType.DMA((3,)),
            pltpu.VMEM((steps, FF_CHUNK), f32),
        ]
        + scratch,
        compiler_params=params(**more),
        cost_estimate=pl.CostEstimate(
            flops=6 * total * width * (2 * hidden + width),
            bytes_accessed=8 * width * hidden + 16 * total * width,
            transcendentals=2 * total * hidden,
        ),
        name="branch",
    )(x, o, ct, ct_head, gx, go, gstat, gct, wo, w1t, b1, w2, b2, norms)
    return out


def local_backward_kernel(
    talk,
    rows_count,
    group_rows,
    lengths,
    bucket_of,
    place,
    q_ref,
    k_ref,
    v_ref,
    do_ref,
    o_ref,
    line_ref,
    *refs,
):
    if talk:
        message_ref, rest_ref, last_ref, dwo_ref = refs[:4]
        refs = refs[4:]
    dq_ref, dk_ref, dv_ref, centre_ref = refs[:4]
    refs = refs[4:]
    if talk:
        everyone_ref, sums_ref, rest_out_ref = refs[:3]
        refs = refs[3:]
    edges, query_columns, key_columns = refs[:3]
    pair = pl.program_id(0)
    block = pl.program_id(1)
    blocks = rows_count // BLOCK
    step = pair * blocks + block

    @pl.when(step == 0)
    def _():
        read_edges(lengths, bucket_of, place, edges)

    if talk:
        all_ref, gather_send, gather_recv, own_ref = refs[3:7]
        landings = refs[7:12]
        send_sem, recv_sem, own_sem = refs[12:]
        bits, partners = my_place()
        gather = RowGather(all_ref, 3 * LANES, gather_send, gather_recv, bits, partners)
        engine = HalvingSum(
            (X_FIRST, Y_FIRST) * 2 + (X_FIRST,),
            [
                None,
                None,
                lambda side: last_ref.at[0, :, :, :, side],
                lambda side: last_ref.at[1, :, :, :, side],
                lambda side: dwo_ref.at[:, :, :, side],
            ],
            landings,
            own_ref,
            send_sem,
            recv_sem,
            own_sem,
            put_rows(sums_ref, landings[4].shape[1]),
            bits,
            partners,
        )
        plan = {
            3: [(2, 0), (3, 0), (4, 0)],
            5: [(0, 2), (1, 2)],
            8: [(0, 3), (1, 3)],
            11: [(0, 4), (1, 4), (2, 1), (3, 1), (4, 1)],
        }
        gather_plan = {4: 1, 8: 2, 10: 3}

        @pl.when(step == 0)
        def _():
            all_ref[:, bits["z0"], bits["y"], bits["core"]] = message_ref[...]
            landings[1][:2] = rest_ref[...]
            meet([partners[name] for name in AXES])
            gather.begin(1)
            for unit in (0, 1):
                engine.copy(unit, 2).start()
            for unit in (2, 3, 4):
                engine.begin(unit)

        for number in range(PAIRS * blocks):
            if number in plan or number in gather_plan:

                @pl.when(step == number)
                def _():
                    if number in gather_plan:
                        gather.advance(gather_plan[number])
                    for unit, stage in plan.get(number, ()):
                        engine.advance(unit, stage, stop=unit > 1 and stage == 1)

    block_columns(
        place, edges, rows_count, group_rows, block, step, blocks, query_columns, key_columns
    )
    extra = query_columns[block]
    upstream = do_ref[...]
    product = upstream.astype(f32) * o_ref[...].astype(f32)
    first = product.astype(bf16)
    second = (product - first.astype(f32)).astype(bf16)
    head = jnp.where(iota((8, LANES), 1) // HEAD_DIM == iota((8, LANES), 0), 1.0, 0.0).astype(bf16)
    by_head = nt(head, first) + nt(head, second)
    centre = jnp.concatenate([by_head[0:1], by_head[1:2]], axis=1)
    centre_ref[0, 0] = jnp.broadcast_to(centre, (8, 2 * BLOCK))
    queries = stack_pair(q_ref[...])
    grads = stack_pair(upstream)
    keys = k_ref[...]
    score = nt(
        jnp.concatenate([keys, key_columns[block]], 1),
        jnp.concatenate([queries, jnp.concatenate([extra, extra], 0)], 1),
    )
    weights = jnp.exp(score - line_ref[0, 0, 0:1])
    along = nt(v_ref[...], grads) - centre
    score_grad = (weights * along).astype(bf16)
    dv_ref[...] = nn(weights.astype(bf16), grads).astype(bf16)
    dk_ref[...] = nn(score_grad, queries).astype(bf16)
    low, high = side_by_side(tn(keys, score_grad))
    dq_ref[:HEAD_DIM] = low.astype(bf16)
    dq_ref[HEAD_DIM:] = high.astype(bf16)

    if talk:

        @pl.when(step == PAIRS * blocks - 1)
        def _():
            everyone_ref[...] = all_ref[...].reshape(everyone_ref.shape)
            gather.end(1)
            rest_out_ref[...] = landings[1][2:]
            for entries in plan.values():
                for unit, stage in entries:
                    engine.sent(unit, stage)


def local_backward(
    talk, scalars, rows_count, group_rows, q, k, v, do, o, line, message, rest, last, dwo
):
    blocks = rows_count // BLOCK
    width = q.shape[1]
    block_spec = pl.BlockSpec((BLOCK, LANES), lambda p, b, *unused: (b, p))
    operands = [q, k, v, do, o, line]
    in_specs = [block_spec] * 5 + [line_spec()]
    out_specs = (
        [pl.BlockSpec((LANES, BLOCK), lambda p, b, *unused: (p, b))]
        + [block_spec] * 2
        + [line_spec()]
    )
    out_shape = [
        jax.ShapeDtypeStruct((width, rows_count), bf16),
        jax.ShapeDtypeStruct((rows_count, width), bf16),
        jax.ShapeDtypeStruct((rows_count, width), bf16),
        jax.ShapeDtypeStruct((PAIRS, blocks, 8, 2 * BLOCK), f32),
    ]
    scratch = column_scratch(blocks)
    more = {}
    if talk:
        unused, own, wide = message.shape
        rows, lanes = last.shape[-2:]
        units = 5
        operands += [message, rest, last, dwo.reshape(last.shape[1:])]
        in_specs += [full(message.shape), once(rest.shape)]
        in_specs += [pl.BlockSpec(memory_space=pl.ANY)] * 2
        everyone = (16 * own, wide)
        rest_out = (units - 2,) + rest.shape[1:]
        out_specs += [once(everyone), once((2 * rows, lanes)), once(rest_out)]
        out_shape += [
            jax.ShapeDtypeStruct(everyone, bf16),
            jax.ShapeDtypeStruct((2 * rows, lanes), f32),
            jax.ShapeDtypeStruct(rest_out, bf16),
        ]
        dma = pltpu.SemaphoreType.DMA
        scratch += [pltpu.VMEM((2, 2, 2, 2, own, wide), bf16), dma((4, 2)), dma((4, 2))]
        scratch += sum_scratch(units, rows, lanes, True)
        more = {"collective_id": 4, "has_side_effects": True}
    return pl.pallas_call(
        functools.partial(local_backward_kernel, talk, rows_count, group_rows),
        grid_spec=pltpu.PrefetchScalarGridSpec(
            num_scalar_prefetch=3,
            grid=(PAIRS, blocks),
            in_specs=in_specs,
            out_specs=out_specs,
            scratch_shapes=scratch,
        ),
        out_shape=out_shape,
        compiler_params=params(**more),
        cost_estimate=pl.CostEstimate(
            flops=40 * rows_count * BLOCK * width,
            bytes_accessed=30 * rows_count * width,
            transcendentals=HEADS * rows_count * BLOCK,
        ),
        name="local_backward",
    )(*scalars, *operands)


def slot_backward_kernel(
    grouped,
    rows_count,
    group_rows,
    lengths,
    bucket_of,
    place,
    q_ref,
    k_ref,
    v_ref,
    do_ref,
    line_ref,
    centre_ref,
    dqt_ref,
    dk_in_ref,
    dv_in_ref,
    gq_ref,
    gk_ref,
    gv_ref,
    gdo_ref,
    gstat_ref,
    gx_in,
    gh_in,
    h_in,
    wq_ref,
    wk_ref,
    wv_ref,
    dq_ref,
    dk_ref,
    dv_ref,
    dw_ref,
    dgh_ref,
    dnorm_ref,
    edges,
    query_columns,
    key_columns,
    keys_ref,
    queries_ref,
    grads_ref,
    dqt_sum,
    dk_sum,
    dv_sum,
    dgqt_sum,
    dgk_sum,
    dgv_sum,
    lines_ref,
    dw_sum,
    dgh_sum,
    rows_ref,
    gx_ref,
    gh_ref,
    h_ref,
    load_sem,
):
    group = pl.program_id(0)
    block = pl.program_id(1)
    blocks = rows_count // BLOCK
    step = group * blocks + block
    together = range(TOGETHER)

    def lanes_of(which):
        return pl.ds(which * LANES, LANES)

    loads = [
        pltpu.make_async_copy(source, target, load_sem.at[number])
        for number, (source, target) in enumerate(
            ((gx_in, gx_ref), (gh_in, gh_ref), (h_in, h_ref))
        )
    ]

    @pl.when(step == 0)
    def _():
        for load in loads:
            load.start()
        read_edges(lengths, bucket_of, place, edges)

        def turn(slot, carry):
            at = pl.ds(pl.multiple_of(slot * GLOBALS, GLOBALS), GLOBALS)
            lines_ref[slot] = gstat_ref[at, :].astype(f32).T
            return carry

        lax.fori_loop(0, SLOTS, turn, 0)
        dgh_sum[...] = jnp.zeros_like(dgh_sum)
        dnorm_ref[...] = jnp.zeros_like(dnorm_ref)

    @pl.when(block == 0)
    def _():
        dgqt_sum[...] = jnp.zeros_like(dgqt_sum)
        dgk_sum[...] = jnp.zeros_like(dgk_sum)
        dgv_sum[...] = jnp.zeros_like(dgv_sum)

    block_columns(
        place, edges, rows_count, group_rows, block, step, blocks, query_columns, key_columns
    )
    extra = query_columns[block]
    for which in together:
        lanes = lanes_of(which)
        keys_ref[which, :, :LANES] = k_ref[:, lanes]
        keys_ref[which, :, LANES:] = key_columns[block]
        queries_ref[which, :, :LANES] = stack_pair(q_ref[:, lanes])
        queries_ref[which, :BLOCK, LANES:] = extra
        queries_ref[which, BLOCK:, LANES:] = extra
        grads_ref[which] = stack_pair(do_ref[:, lanes])
    dqt_sum[...] = dqt_ref[...].astype(f32)
    dk_sum[...] = dk_in_ref[...].astype(f32)
    dv_sum[...] = dv_in_ref[...].astype(f32)

    def line_of(slot, which, first):
        halves = []
        for head in range(2):
            spot = first + 2 * (group * TOGETHER + which) + head
            halves.append(
                lines_ref[slot, pl.ds(spot, 1)]
                + lines_ref[slot, pl.ds(spot + HEADS, 1)]
                + lines_ref[slot, pl.ds(spot + 2 * HEADS, 1)]
            )
        return jnp.concatenate(halves, axis=1)

    def from_global(slot, which, keys, values):
        at = pl.ds(pl.multiple_of(slot * GLOBALS, GLOBALS), GLOBALS)
        extra = global_query_extra(slot).astype(bf16)
        queries = stack_pair(gq_ref[at, lanes_of(which)])
        grads = stack_pair(gdo_ref[at, lanes_of(which)])
        score = nt(keys, jnp.concatenate([queries, jnp.concatenate([extra, extra], 0)], 1))
        weights = jnp.exp(score - line_of(slot, which, 0))
        along = nt(values, grads) - line_of(slot, which, 3 * HEADS)
        score_grad = (weights * along).astype(bf16)
        low, high = side_by_side(tn(keys[:, :LANES], score_grad))
        dgqt_sum[which, slot, :HEAD_DIM] += low
        dgqt_sum[which, slot, HEAD_DIM:] += high
        return nn(score_grad, queries), nn(weights.astype(bf16), grads)

    def one_slot(slot, carry):
        @pl.when(slot_present(slot, place, edges, rows_count, group_rows, block))
        def _():
            at = pl.ds(pl.multiple_of(slot * GLOBALS, GLOBALS), GLOBALS)
            columns = global_key_extra(slot).astype(bf16)
            for which in together:
                lanes = lanes_of(which)
                key_grad, value_grad = from_global(slot, which, keys_ref[which], v_ref[:, lanes])
                dk_sum[:, lanes] += key_grad
                dv_sum[:, lanes] += value_grad
                keys = gk_ref[at, lanes]
                grads = grads_ref[which]
                score = nt(jnp.concatenate([keys, columns], 1), queries_ref[which])
                weights = jnp.exp(score - line_ref[which, 0, 0:1])
                along = nt(gv_ref[at, lanes], grads) - centre_ref[which, 0, 0:1]
                score_grad = (weights * along).astype(bf16)
                dgv_sum[at, lanes] += nn(weights.astype(bf16), grads)
                dgk_sum[at, lanes] += nn(score_grad, queries_ref[which, :, :LANES])
                low, high = side_by_side(tn(keys, score_grad))
                dqt_sum[pl.ds(which * LANES, HEAD_DIM)] += low
                dqt_sum[pl.ds(which * LANES + HEAD_DIM, HEAD_DIM)] += high

        return carry

    lax.fori_loop(0, SLOTS, one_slot, 0)
    here = pl.ds(pl.multiple_of(block * BLOCK, BLOCK), BLOCK)
    for index, (ref, value) in enumerate(
        ((dq_ref, dqt_sum[...].T), (dk_ref, dk_sum[...]), (dv_ref, dv_sum[...]))
    ):
        low = value.astype(bf16)
        ref[...] = low
        rows_ref[index, here, :] = low

    @pl.when(step == blocks - 1)
    def _():
        for load in loads:
            load.wait()

    @pl.when((block == blocks - 1) & (place[2] >= 0))
    def _():
        slot = place[2]
        at = pl.ds(pl.multiple_of(slot * GLOBALS, GLOBALS), GLOBALS)
        columns = global_key_extra(slot).astype(bf16)
        for which in together:
            lanes = lanes_of(which)
            keys = jnp.concatenate([gk_ref[at, lanes], columns], axis=1)
            key_grad, value_grad = from_global(slot, which, keys, gv_ref[at, lanes])
            dgk_sum[at, lanes] += key_grad
            dgv_sum[at, lanes] += value_grad

    @pl.when(block == blocks - 1)
    def _():
        for index in range(3):
            local = tn(rows_ref[index], h_ref[...])
            dw_sum[index] = local * query_scale if index == 0 else local

        def through(slot, carry):
            needed = slot == place[2]
            for number in range(blocks):
                needed = needed | slot_present(
                    slot, place, edges, rows_count, group_rows, number
                )

            @pl.when(needed)
            def _():
                at = pl.ds(pl.multiple_of(slot * GLOBALS, GLOBALS), GLOBALS)
                grads = (
                    (
                        jnp.concatenate([dgqt_sum[which, slot].T for which in together], 1)
                        * query_scale
                    ).astype(bf16),
                    dgk_sum[at, :].astype(bf16),
                    dgv_sum[at, :].astype(bf16),
                )
                rows = gh_ref[at, :]
                total = dgh_sum[at, :]
                for index, weight in enumerate((wq_ref, wk_ref, wv_ref)):
                    total = total + nt(grads[index], weight[...])
                dgh_sum[at, :] = total

                for index in range(3):
                    dw_sum[index] += tn(grads[index], rows)

                @pl.when(group == PAIRS // TOGETHER - 1)
                def _():
                    unit, unused = normalize_rows(gx_ref[at, :].astype(f32))
                    dnorm_ref[0:1] += jnp.sum(total * unit, axis=0, keepdims=True)
                    dnorm_ref[1:2] += jnp.sum(total, axis=0, keepdims=True)

            return carry

        lax.fori_loop(0, SLOTS, through, 0)
        if grouped:
            for index in range(3):
                put_grouped(dw_ref.at[index], dw_sum[index])
        else:
            dw_ref[...] = dw_sum[...].astype(bf16)

    @pl.when(step == PAIRS // TOGETHER * blocks - 1)
    def _():
        dgh_ref[...] = dgh_sum[...].astype(bf16)


def slot_backward(
    grid_of,
    scalars,
    rows_count,
    group_rows,
    q,
    k,
    v,
    do,
    line,
    centre,
    dqt,
    dk,
    dv,
    gq,
    gk,
    gv,
    everyone,
    gx,
    gh,
    h,
    wq,
    wk,
    wv,
):
    blocks = rows_count // BLOCK
    all_globals, width = gk.shape
    block_spec = pl.BlockSpec((BLOCK, TOGETHER * LANES), lambda p, b, *unused: (b, p))
    pair_spec = pl.BlockSpec((all_globals, TOGETHER * LANES), lambda p, b, *unused: (0, p))
    local = jax.ShapeDtypeStruct((rows_count, width), bf16)
    glob = jax.ShapeDtypeStruct((all_globals, width), bf16)
    if grid_of is None:
        dw_shape = (3, width, width)
        dw_spec = pl.BlockSpec((3, TOGETHER * LANES, width), lambda p, b, *unused: (0, p, 0))
    else:
        seq, batch = grid_of
        piece = (batch, width // seq, width // batch)
        dw_shape = (3, seq) + piece
        share = TOGETHER * LANES // piece[1]
        dw_spec = pl.BlockSpec((3, share) + piece, lambda p, b, *unused: (0, p, 0, 0, 0))
    return pl.pallas_call(
        functools.partial(slot_backward_kernel, grid_of is not None, rows_count, group_rows),
        grid_spec=pltpu.PrefetchScalarGridSpec(
            num_scalar_prefetch=3,
            grid=(PAIRS // TOGETHER, blocks),
            in_specs=[block_spec] * 4
            + [line_spec(TOGETHER)] * 2
            + [pl.BlockSpec((TOGETHER * LANES, BLOCK), lambda p, b, *unused: (p, b))]
            + [block_spec] * 2
            + [pair_spec] * 4
            + [pl.BlockSpec((all_globals, LANES), lambda p, b, *unused: (0, PAIRS))]
            + [pl.BlockSpec(memory_space=pl.ANY)] * 3
            + [pl.BlockSpec((width, TOGETHER * LANES), lambda p, b, *unused: (0, p))] * 3,
            out_specs=[block_spec] * 3
            + [
                dw_spec,
                once((all_globals, width)),
                full((8, width)),
            ],
            scratch_shapes=column_scratch(blocks)
            + [
                pltpu.VMEM((TOGETHER, BLOCK, 2 * LANES), bf16),
                pltpu.VMEM((TOGETHER, 2 * BLOCK, 2 * LANES), bf16),
                pltpu.VMEM((TOGETHER, 2 * BLOCK, LANES), bf16),
                pltpu.VMEM((TOGETHER * LANES, BLOCK), f32),
                pltpu.VMEM((BLOCK, TOGETHER * LANES), f32),
                pltpu.VMEM((BLOCK, TOGETHER * LANES), f32),
                pltpu.VMEM((TOGETHER, SLOTS, LANES, GLOBALS), f32),
                pltpu.VMEM((all_globals, TOGETHER * LANES), f32),
                pltpu.VMEM((all_globals, TOGETHER * LANES), f32),
                pltpu.VMEM((SLOTS, LANES, GLOBALS), f32),
                pltpu.VMEM((3, TOGETHER * LANES, width), f32),
                pltpu.VMEM((all_globals, width), f32),
                pltpu.VMEM((3, rows_count, TOGETHER * LANES), bf16),
                pltpu.VMEM((all_globals, width), bf16),
                pltpu.VMEM((all_globals, width), bf16),
                pltpu.VMEM((rows_count, width), bf16),
                pltpu.SemaphoreType.DMA((3,)),
            ],
        ),
        out_shape=[local] * 3
        + [
            jax.ShapeDtypeStruct(dw_shape, bf16),
            glob,
            jax.ShapeDtypeStruct((8, width), f32),
        ],
        compiler_params=params(),
        cost_estimate=pl.CostEstimate(
            flops=80 * rows_count * GLOBALS * width,
            bytes_accessed=40 * rows_count * width,
            transcendentals=2 * HEADS * rows_count * GLOBALS,
        ),
        name="slot_backward",
    )(
        *scalars,
        q,
        k,
        v,
        do,
        line,
        centre,
        dqt,
        dk,
        dv,
        gq,
        gk,
        gv,
        everyone,
        everyone,
        gx,
        gh,
        h,
        wq,
        wk,
        wv,
    )


def project_back_kernel(
    tile,
    x_ref,
    dy_ref,
    dq_ref,
    dk_ref,
    dv_ref,
    wq_ref,
    wk_ref,
    wv_ref,
    gain_ref,
    dx_ref,
    dnorm_ref,
):
    count, width = x_ref.shape
    dnorm_ref[...] = jnp.zeros_like(dnorm_ref)

    def one_tile(i, carry):
        at = pl.ds(pl.multiple_of(i * tile, tile), tile)
        dh = (
            nt(dq_ref[at, :], wq_ref[...]) * query_scale
            + nt(dk_ref[at, :], wk_ref[...])
            + nt(dv_ref[at, :], wv_ref[...])
        )
        unit, scale = normalize_rows(x_ref[at, :].astype(f32))
        dnorm_ref[0:1] += jnp.sum(dh * unit, axis=0, keepdims=True)
        dnorm_ref[1:2] += jnp.sum(dh, axis=0, keepdims=True)
        dx_ref[at, :] = dy_ref[at, :] + norm_back(unit, scale, gain_ref[...], dh)
        return carry

    lax.fori_loop(0, count // tile, one_tile, 0)


def project_back(x, dy, dq, dk, dv, wq, wk, wv, gain):
    count, width = x.shape
    vmem = pl.BlockSpec(memory_space=pltpu.VMEM)
    return pl.pallas_call(
        functools.partial(project_back_kernel, BLOCK),
        in_specs=[vmem] * 9,
        out_specs=[vmem] * 2,
        out_shape=[
            jax.ShapeDtypeStruct((count, width), f32),
            jax.ShapeDtypeStruct((8, width), f32),
        ],
        compiler_params=params(),
        cost_estimate=pl.CostEstimate(
            flops=12 * count * width * width, bytes_accessed=30 * count * width, transcendentals=0
        ),
        name="project_back",
    )(x, dy, dq, dk, dv, wq, wk, wv, gain)


def finish_kernel(
    rest_ref,
    x_in,
    dy_in,
    dq_in,
    dk_in,
    dv_in,
    dqkv_ref,
    dgh_ref,
    wq_in,
    wk_in,
    wv_in,
    db1_ref,
    db2_ref,
    dnorm_global_ref,
    dgain2_ref,
    doffset2_ref,
    gx_ref,
    gdy_ref,
    norms_ref,
    out_ref,
    small_out_ref,
    grad_out_ref,
    token_ref,
    halo_dx_out,
    x_ref,
    dy_ref,
    dq_ref,
    dk_ref,
    dv_ref,
    wq_ref,
    wk_ref,
    wv_ref,
    load_sem,
    own_ref,
    one_ref,
    two_ref,
    three_ref,
    four_ref,
    five_ref,
    send_sem,
    recv_sem,
    own_sem,
    gown_ref,
    gone_ref,
    gtwo_ref,
    gthree_ref,
    gfour_ref,
    gsend_sem,
    grecv_sem,
    gown_sem,
    sums_ref,
    here_ref,
    ssend_sem,
    srecv_sem,
    halo_out,
    halo_dx,
    halo_send,
    halo_recv,
    dnorm_ref,
    dgh_sum_ref,
):
    bits, partners = my_place()
    count, width = x_ref.shape
    came = rest_ref.shape[0]
    units = came + 3
    batch = lax.axis_index("batch")
    seq = lax.axis_index("seq")
    places = lax.axis_size("seq")
    after = (batch, lax.rem(seq + 1, places))
    before = (batch, lax.rem(seq + places - 1, places))

    pairs = [
        (dq_in, dq_ref),
        (dk_in, dk_ref),
        (dv_in, dv_ref),
        (wq_in, wq_ref),
        (wk_in, wk_ref),
        (wv_in, wv_ref),
        (x_in, x_ref),
        (dy_in, dy_ref),
    ]
    loads = [
        pltpu.make_async_copy(source, target, load_sem.at[number])
        for number, (source, target) in enumerate(pairs)
    ]
    def source(unit):
        return lambda side: dqkv_ref.at[unit - came, :, :, :, side]

    engine = HalvingSum(
        (X_Z_FIRST, Y_FIRST, X_FIRST, X_FIRST, Y_FIRST, Z_FIRST),
        [source(unit) for unit in range(units)],
        (one_ref, two_ref, three_ref, four_ref, five_ref),
        own_ref,
        send_sem,
        recv_sem,
        own_sem,
        put_rows(out_ref, five_ref.shape[1]),
        bits,
        partners,
    )
    wide = gone_ref.shape[-1]

    def row_source(unit):
        lanes = pl.ds(unit * wide, wide)
        return lambda side: dgh_ref.at[:, :, :, side, :, lanes]

    def put_dgh(unit, value):
        dgh_sum_ref[:, unit * wide : (unit + 1) * wide] = value

    row_sum = HalvingSum(
        (("core", "y", "z0", "z1"), ("core", "z0", "y", "z1")),
        [row_source(unit) for unit in range(2)],
        (gone_ref, gtwo_ref, gthree_ref, gfour_ref),
        gown_ref,
        gsend_sem,
        grecv_sem,
        gown_sem,
        put_dgh,
        bits,
        partners,
    )

    def rows_advance(stage):
        for unit in range(2):
            row_sum.advance(unit, stage)

    def scopy(stage):
        return remote(
            sums_ref.at[stage],
            here_ref.at[stage],
            ssend_sem.at[stage],
            srecv_sem.at[stage],
            partners[X_FIRST[stage]],
        )

    def small_advance(stage):
        scopy(stage).wait_recv()
        total = sums_ref[stage] + here_ref[stage]
        if stage < STAGES - 1:
            sums_ref[stage + 1] = total
            scopy(stage + 1).start()
        else:
            small_out_ref[...] = total

    halo = remote(halo_out, halo_dx, halo_send, halo_recv, before)
    two_ref[:came] = rest_ref[...]
    meet([partners[name] for name in AXES] + [before, after])
    for unit in range(came, units):
        engine.begin(unit)
    for load in loads:
        load.start()
    for unit in range(came):
        engine.copy(unit, 2).start()
    for unit in range(2):
        row_sum.begin(unit)
    for unit in range(came, units):
        engine.advance(unit, 0)
    for load in loads:
        load.wait()
    dnorm_ref[...] = jnp.zeros_like(dnorm_ref)

    def back(index):
        at = pl.ds(index * HALF, HALF)
        dh = (
            nt(dq_ref[at, :], wq_ref[...]) * query_scale
            + nt(dk_ref[at, :], wk_ref[...])
            + nt(dv_ref[at, :], wv_ref[...])
        )
        unit, scale = normalize_rows(x_ref[at, :].astype(f32))
        dnorm_ref[0:1] += jnp.sum(dh * unit, axis=0, keepdims=True)
        dnorm_ref[1:2] += jnp.sum(dh, axis=0, keepdims=True)
        dx = dy_ref[at, :] + norm_back(unit, scale, norms_ref[0:1], dh)
        if index == 0:
            halo_out[...] = dx.astype(bf16)
        else:
            token_ref[pl.ds((index - 1) * HALF, HALF), :] = dx

    for index in range(count // HALF):
        back(index)
        if index == 0:
            halo.start()
            rows_advance(0)
        if index == 2:
            for unit in range(came):
                engine.advance(unit, 2)

    hidden_rows = db1_ref.shape[0]
    parts = [
        db1_ref[...],
        db2_ref[...],
        dnorm_ref[0:2],
        dnorm_global_ref[0:2],
        dgain2_ref[...],
        doffset2_ref[...],
    ]
    filled = hidden_rows + 7
    parts.append(jnp.zeros((sums_ref.shape[1] - filled, width), f32))
    sums_ref[0] = jnp.concatenate(parts, 0)
    scopy(0).start()

    def weights_advance(stage):
        for unit in range(came, units):
            engine.advance(unit, stage)

    small_advance(0)
    rows_advance(1)
    weights_advance(1)
    for unit in range(came):
        engine.advance(unit, 3)
    small_advance(1)
    rows_advance(2)
    small_advance(2)
    weights_advance(2)
    small_advance(3)
    for unit in range(came):
        engine.advance(unit, 4)
    rows_advance(3)
    dgh = dgh_sum_ref[...]
    unit_rows, scale = normalize_rows(gx_ref[...].astype(f32))
    grad_out_ref[...] = gdy_ref[...] + norm_back(unit_rows, scale, norms_ref[2:3], dgh)
    small_advance(4)
    halo.wait_recv()
    halo_dx_out[...] = halo_dx[...]
    weights_advance(3)
    weights_advance(4)

    for unit in range(units):
        for stage in range(2 if unit < came else 0, STAGES):
            engine.sent(unit, stage)
    for stage in range(STAGES):
        scopy(stage).wait_send()
    for unit in range(2):
        for stage in range(4):
            row_sum.sent(unit, stage)
    halo.wait_send()


def finish_all(rest, x, dy, dq, dk, dv, dqkv, dgh, wq, wk, wv, small, gx, gdy, norms):
    count, width = x.shape
    rows, lanes = rest.shape[-2:]
    units = rest.shape[0] + 3
    own = gx.shape[0]
    place = (2, 2, 2, 2)
    small_rows = small[0].shape[0] + 7
    small_rows += -small_rows % 8
    anywhere = pl.BlockSpec(memory_space=pl.ANY)
    vmem = pl.BlockSpec(memory_space=pltpu.VMEM)
    dma = pltpu.SemaphoreType.DMA
    row = pltpu.VMEM((count, width), bf16)
    weight = pltpu.VMEM((width, width), bf16)
    half = pltpu.VMEM((HALF, width), bf16)
    return pl.pallas_call(
        finish_kernel,
        in_specs=[vmem] + [anywhere] * 10 + [vmem] * 8,
        out_specs=[vmem] * 5,
        out_shape=[
            jax.ShapeDtypeStruct((units * rows, lanes), f32),
            jax.ShapeDtypeStruct((small_rows, width), f32),
            jax.ShapeDtypeStruct((own, width), f32),
            jax.ShapeDtypeStruct((count - HALF, width), f32),
            jax.ShapeDtypeStruct((HALF, width), bf16),
        ],
        scratch_shapes=[
            row,
            pltpu.VMEM((count, width), f32),
            row,
            row,
            row,
            weight,
            weight,
            weight,
            dma((8,)),
        ]
        + sum_scratch(units, rows, lanes, True)
        + [
            pltpu.VMEM((2, 2, 2, 2, own, width // 2), bf16),
            pltpu.VMEM((2, 2, 2, 2, own, width // 2), bf16),
            pltpu.VMEM((2, 2, 2, own, width // 2), bf16),
            pltpu.VMEM((2, 2, own, width // 2), bf16),
            pltpu.VMEM((2, own, width // 2), bf16),
            dma((2, 4)),
            dma((2, 4)),
            dma((2,)),
            pltpu.VMEM((STAGES, small_rows, width), f32),
            pltpu.VMEM((STAGES, small_rows, width), f32),
            dma((STAGES,)),
            dma((STAGES,)),
            half,
            half,
            dma,
            dma,
            pltpu.VMEM((8, width), f32),
            pltpu.VMEM((own, width), f32),
        ],
        compiler_params=params(collective_id=0, has_side_effects=True),
        cost_estimate=pl.CostEstimate(
            flops=12 * count * width * width, bytes_accessed=30 * count * width, transcendentals=0
        ),
        name="finish_all",
    )(
        rest,
        x,
        dy,
        dq,
        dk,
        dv,
        dqkv.reshape((3,) + place + (2, rows, lanes)),
        dgh.reshape(place + (own, width)),
        wq,
        wk,
        wv,
        *small,
        gx,
        gdy,
        norms,
    )


def unpack_kernel(
    z_ref,
    halo_z_ref,
    dx_ref,
    halo_dx_ref,
    gz_ref,
    ggrad_ref,
    first_ref,
    second_ref,
    third_ref,
    small_ref,
    layer_ref,
    gz_out,
    token_ref,
    ggrad_out,
    wq_ref,
    wk_ref,
    wv_ref,
    wo_ref,
    w1_ref,
    w2_ref,
    b1_ref,
    b2_ref,
    norms_ref,
    turned_ref,
):
    step = pl.program_id(0)
    last = pl.num_programs(0) - 1

    @pl.when(step < last)
    def _():
        layer_ref[0] = z_ref[...]
        token_ref[0] = dx_ref[...]

    @pl.when(step == last)
    def _():
        layer_ref[0] = halo_z_ref[...]
        token_ref[0] = halo_dx_ref[...].astype(f32)

    rows = wq_ref.shape[0]

    @pl.when(step == 0)
    def _():
        gz_out[0] = gz_ref[...]
        ggrad_out[0] = ggrad_ref[...]
        for ref, unit in ((wo_ref, 2), (wq_ref, 3), (wk_ref, 4), (wv_ref, 5)):
            ref[...] = third_ref[unit * rows : (unit + 1) * rows]
        chunks = w1_ref.shape[0] // rows
        for chunk in range(chunks):
            for ref, unit in ((first_ref, chunk), (second_ref, chunk - 2), (third_ref, chunk - 3)):
                if 0 <= unit < ref.shape[0] // (2 * rows):
                    break
            start = 2 * unit * rows
            w1_ref[chunk * rows : (chunk + 1) * rows] = ref[start : start + rows]
            part = ref[start + rows : start + 2 * rows].T
            for place in range(part.shape[0] // rows):
                spot = (place * chunks + chunk) * rows
                turned_ref[spot : spot + rows, :] = part[place * rows : (place + 1) * rows, :]
        w2_ref[...] = turned_ref[...].T
        pieces_in_row = small_ref.shape[1] // LANES
        hidden_rows = b1_ref.shape[0] // pieces_in_row
        per_chunk = small_ref.shape[1] // rows
        natural = jnp.concatenate(
            [
                small_ref[chunk : chunk + 1, place * rows : (place + 1) * rows]
                for place in range(per_chunk)
                for chunk in range(hidden_rows)
            ],
            axis=1,
        )
        for piece in range(hidden_rows * pieces_in_row):
            b1_ref[piece : piece + 1] = natural[:, piece * LANES : (piece + 1) * LANES]
        for piece in range(pieces_in_row):
            b2_ref[piece : piece + 1] = small_ref[
                hidden_rows : hidden_rows + 1, piece * LANES : (piece + 1) * LANES
            ]
        norms_ref[...] = small_ref[hidden_rows + 1 : hidden_rows + 7]


def unpack(z, halo_z, dx, halo_dx, gz, ggrad, first, second, third, small, rows, hidden):
    count, width = z.shape
    own = gz.shape[0]
    lanes = first.shape[1]
    steps = count // HALF
    shapes = [
        ((1, count, width), bf16),
        ((1, own, width), bf16),
        ((1, count, width), f32),
        ((1, own, width), f32),
    ]
    shapes += [((rows, lanes), f32)] * 4
    shapes += [
        ((hidden // width * rows, lanes), f32),
        ((rows, hidden // width * lanes), f32),
        ((hidden // LANES, LANES), f32),
        ((width // LANES, LANES), f32),
        ((6, width), f32),
    ]
    tile = pl.BlockSpec((1, HALF, width), lambda i: (0, i, 0))
    return pl.pallas_call(
        unpack_kernel,
        grid=(steps,),
        in_specs=[
            pl.BlockSpec((HALF, width), lambda i: (jnp.minimum(i + 1, steps - 1), 0)),
            full(halo_z.shape),
            pl.BlockSpec((HALF, width), lambda i: (jnp.minimum(i, steps - 2), 0)),
            full(halo_dx.shape),
            full(gz.shape),
            full(ggrad.shape),
            full(first.shape),
            full(second.shape),
            full(third.shape),
            full(small.shape),
        ],
        out_specs=[
            tile if shape[1] == count else full(shape) for shape, unused in shapes
        ],
        out_shape=[jax.ShapeDtypeStruct(shape, kind) for shape, kind in shapes],
        scratch_shapes=[pltpu.VMEM((hidden // width * lanes, rows), f32)],
        compiler_params=params(),
        cost_estimate=pl.CostEstimate(
            flops=0, bytes_accessed=14 * count * width, transcendentals=0
        ),
        name="unpack",
    )(z, halo_z, dx, halo_dx, gz, ggrad, first, second, third, small)


def from_behind(value, axis, steps):
    count = lax.axis_size(axis)
    pairs = [(source, (source + steps) % count) for source in range(count)]
    return lax.ppermute(value, axis, pairs)


def pieces(value):
    first = lax.reduce_precision(value, 8, 7)
    second = lax.reduce_precision(value - first, 8, 7)
    return [first.astype(bf16), second.astype(bf16), (value - first - second).astype(bf16)]


def scatter_sum(value):
    half = lax.psum_scatter(value, "batch", scatter_dimension=1, tiled=True)
    part = lax.psum_scatter(half, "seq", scatter_dimension=0, tiled=True)
    return part.T.astype(f32)


def on_device(
    tokens,
    global_states,
    lengths,
    bucket_of,
    wq,
    wk,
    wv,
    wo,
    w1,
    b1,
    w2,
    b2,
    norm_params,
    cotangent,
    global_cotangent,
):
    rows = tokens.shape[1]
    width = tokens.shape[2]
    own = global_states.shape[1]
    seq_count = lax.axis_size("seq")
    seq_place = lax.axis_index("seq")
    group_rows = rows * seq_count
    own_start = seq_place * own
    first_of_slot = own_start % GLOBALS == 0
    place = jnp.stack(
        [
            lax.axis_index("batch"),
            seq_place,
            jnp.where(first_of_slot, own_start // GLOBALS, -1),
        ]
    ).astype(jnp.int32)
    scalars = (lengths, bucket_of, place)
    norms = [norm_params[i : i + 1] for i in range(6)]
    b2_rows = b2.reshape(-1, LANES)

    batch_count = lax.axis_size("batch")
    grid_of = None
    if seq_count == 16 and batch_count == 2 and 2 * own == GLOBALS and rows == 2 * BLOCK:
        grid_of = (seq_count, batch_count)

    if grid_of is None:
        arrived_tokens, arrived_grads = from_behind(
            (tokens[0, rows - HALF :], cotangent[0, rows - HALF :]), "seq", 1
        )
        x = jnp.concatenate([arrived_tokens, tokens[0, : rows - HALF]], 0)
        ct_head = arrived_grads
        all_states = lax.all_gather(global_states[0], "seq", axis=0, tiled=True)
        w1t = w1.T
        h, q, k, v = project_local(x, norms[0], norms[1], wq, wk, wv)
        gh, gq, gk, gv = project_global(
            scalars, rows, group_rows, all_states, norms[2], norms[3], wq, wk, wv
        )
    else:
        h, q, k, v, x, all_states, gh, gq, gk, gv, w1t = gather_project(
            tokens[0], global_states[0], w1, norm_params, wq, wk, wv
        )
        all_states, gh, gq, gk, gv = (
            value.reshape(-1, width) for value in (all_states, gh, gq, gk, gv)
        )
    far, far_stat, part, part_stat = slot_forward(scalars, rows, group_rows, q, k, v, gq, gk, gv)
    if grid_of is None:
        o, line = local_forward(
            False, scalars, rows, group_rows, q, k, v, far, far_stat, None, None
        )
        part_peak = part_stat[:, :, 0:2]
        peak = jnp.max(lax.all_gather(part_peak, "seq"), axis=0)
        factor = jnp.exp(part_peak - peak)
        scaled = part.reshape(SLOTS, PAIRS, 2, HEAD_DIM, GLOBALS).astype(f32) * factor[:, :, :, None]
        scaled = scaled.reshape(SLOTS, width, GLOBALS)
        scaled_total = (part_stat[:, :, 2:4] * factor).reshape(SLOTS, HEADS, GLOBALS)
        payload = jnp.concatenate(
            [scaled, scaled_total, jnp.zeros((SLOTS, 4, GLOBALS), f32)], 1
        ).transpose(0, 2, 1)
        sums = lax.psum_scatter(
            payload.astype(bf16).reshape(SLOTS * GLOBALS, -1), "seq", scatter_dimension=0, tiled=True
        ).astype(f32)
        own_total = sums[:, width : width + HEADS]
        all_peak = peak.reshape(SLOTS, HEADS, GLOBALS).transpose(0, 2, 1).reshape(-1, HEADS)
        own_peak = lax.dynamic_slice_in_dim(all_peak, own_start, own, 0)
        go = (
            (sums[:, :width].reshape(own, HEADS, HEAD_DIM) / own_total[:, :, None])
            .reshape(own, width)
            .astype(bf16)
        )
        gstat = own_peak + jnp.log(own_total)
    else:
        o, line, half_sum, half_stat = local_forward(
            True, scalars, rows, group_rows, q, k, v, far, far_stat, part, part_stat
        )

    z, dy, do, gz, gdy, gdo, dwo, db1, db2, dgain2, doffset2, *dws = branch(
        grid_of,
        x,
        o,
        cotangent[0],
        ct_head if grid_of is None else cotangent[0],
        global_states[0],
        go if grid_of is None else half_sum,
        gstat if grid_of is None else half_stat,
        global_cotangent[0],
        wo,
        w1t,
        b1.reshape(-1, LANES),
        w2,
        b2_rows,
        norm_params,
    )
    if grid_of is None:
        gcentre = jnp.sum(
            (gdo.astype(f32) * go.astype(f32)).reshape(own, HEADS, HEAD_DIM), axis=-1
        )
        message = jnp.concatenate(
            [gdo]
            + pieces(gstat)
            + pieces(gcentre)
            + [jnp.zeros((own, LANES - 6 * HEADS), bf16)],
            axis=1,
        )
        everyone = lax.all_gather(message, "seq", axis=0, tiled=True)
        dqt, dk, dv, centre = local_backward(
            False, scalars, rows, group_rows, q, k, v, do, o, line, None, None, None, None
        )
    else:
        sum_first, last, message, rest, z_head = dws
        dqt, dk, dv, centre, everyone, sum_second, rest = local_backward(
            True, scalars, rows, group_rows, q, k, v, do, o, line, message, rest, last, dwo
        )
        z_head, rest = lax.optimization_barrier((z_head, rest))
        halo_z = from_behind(z_head, "seq", -1)
    dq, dk, dv, dqkv, dgh, dnorm_global = slot_backward(
        grid_of,
        scalars,
        rows,
        group_rows,
        q,
        k,
        v,
        do,
        line,
        centre,
        dqt,
        dk,
        dv,
        gq,
        gk,
        gv,
        everyone,
        all_states,
        gh,
        h,
        wq,
        wk,
        wv,
    )
    if grid_of is None:
        dx, dnorm = project_back(x, dy, dq, dk, dv, wq, wk, wv, norms[0])
        back_z, back_grad = from_behind((z[:HALF], dx[:HALF].astype(bf16)), "seq", -1)
        layer_out = jnp.concatenate([z[HALF:], back_z], 0)
        token_grad = jnp.concatenate([dx[HALF:], back_grad.astype(f32)], 0)
        small = jnp.concatenate([db1, db2, dnorm[:2], dnorm_global[:2], dgain2, doffset2], 0)
        dgh = lax.psum_scatter(dgh, "seq", scatter_dimension=0, tiled=True).astype(f32)
        gunit, gscale = normalize_rows(global_states[0].astype(f32))
        global_grad = gdy + norm_back(gunit, gscale, norms[2], dgh)
        small = lax.psum(small, ("batch", "seq"))
        dw1, dw2 = dws
        weights = [scatter_sum(value) for value in (dqkv[0], dqkv[1], dqkv[2], dwo, dw1, dw2)]
    else:
        sum_third, small, global_grad, dx, halo_dx = finish_all(
            rest,
            x,
            dy,
            dq,
            dk,
            dv,
            dqkv,
            dgh,
            wq,
            wk,
            wv,
            (db1, db2, dnorm_global, dgain2, doffset2),
            global_states[0],
            gdy,
            norm_params,
        )
        results = unpack(
            z,
            halo_z,
            dx,
            halo_dx,
            gz,
            global_grad,
            sum_first,
            sum_second,
            sum_third,
            small,
            width // seq_count,
            w1.shape[1],
        )
        weights = [value.T for value in results[4:10]]
        biases = [value.reshape(-1) for value in results[10:12]]
        return (*results[:4], *weights, *biases, results[12])
    hidden_rows = w1.shape[1] // width
    return (
        layer_out[None],
        gz[None],
        token_grad[None],
        global_grad[None],
        *weights,
        small[:hidden_rows].reshape(-1),
        small[hidden_rows],
        small[hidden_rows + 1 : hidden_rows + 7],
    )


def solution(mesh):
    split = P("batch", "seq", None)
    return jax.shard_map(
        on_device,
        mesh=mesh,
        in_specs=(split, split) + (P(),) * 11 + (split, split),
        out_specs=(split,) * 4 + (P("batch", "seq"),) * 6 + (P(),) * 3,
        check_vma=False,
    )
```

```python
import functools

import jax
import jax.numpy as jnp
from jax import lax
from jax.experimental import pallas as pl
from jax.experimental.pallas import tpu as pltpu
from jax.sharding import PartitionSpec as P

HEADS = 12
HEAD_DIM = 64
PAIRS = HEADS // 2
LANES = 128
BLOCK = 512
HALF = 256
GLOBALS = 128
SLOTS = 8
FF_CHUNK = 768
TOGETHER = 3

norm_eps = 1e-05
masked_score = -1e30
query_scale = 0.125

SLOT_LANE = 16
GLOBAL_LANE = 32

f32 = jnp.float32
bf16 = jnp.bfloat16
VMEM_LIMIT = 60 * 1024 * 1024


def nn(left, right):
    return jnp.dot(left, right, preferred_element_type=f32)


def nt(left, right):
    return lax.dot_general(left, right, (((1,), (1,)), ((), ())), preferred_element_type=f32)


def tn(left, right):
    return lax.dot_general(left, right, (((0,), (0,)), ((), ())), preferred_element_type=f32)


def iota(shape, dim):
    return lax.broadcasted_iota(jnp.int32, shape, dim)


def stack_pair(pair):
    lane = iota((1, LANES), 1)
    low = jnp.where(lane < HEAD_DIM, 1.0, 0.0).astype(bf16)
    high = jnp.where(lane < HEAD_DIM, 0.0, 1.0).astype(bf16)
    return jnp.concatenate([pair * low, pair * high], axis=0)


def read_edges(lengths, bucket_of, place, edges):
    bucket = bucket_of[place[0]]
    total = jnp.int32(0)
    edges[0] = total
    for slot in range(SLOTS):
        total = total + lengths[bucket, slot]
        edges[slot + 1] = total


def block_start(place, rows, block):
    return place[1] * rows + block * BLOCK - HALF


def slot_present(slot, place, edges, rows, group_rows, block):
    low = edges[slot]
    high = edges[slot + 1]
    found = jnp.bool_(False)
    for part in range(BLOCK // HALF):
        start = block_start(place, rows, block) + part * HALF
        start = jnp.where(start < 0, start + group_rows, start)
        found = found | ((high > low) & (low < start + HALF) & (high > start))
    return found


def row_numbers(place, edges, rows, group_rows, block):
    place_in = block_start(place, rows, block) + iota((BLOCK, LANES), 0)
    wrapped = place_in < 0
    token = jnp.where(wrapped, place_in + group_rows, place_in)
    slot = jnp.zeros((BLOCK, LANES), jnp.int32)
    for j in range(SLOTS):
        slot = slot + jnp.where(edges[j + 1] <= token, 1, 0)
    return slot, slot + jnp.where(wrapped, SLOTS, 0)


def key_extra(slot, segment):
    lane = iota((BLOCK, LANES), 1)
    extra = jnp.where((lane < SLOT_LANE) & (lane != segment), masked_score, 0.0)
    return jnp.where(lane == GLOBAL_LANE + slot, 1.0, extra)


def query_extra(slot, segment):
    lane = iota((BLOCK, LANES), 1)
    return jnp.where((lane == segment) | (lane == SLOT_LANE + slot), 1.0, 0.0)


def global_key_extra(slot):
    lane = iota((GLOBALS, LANES), 1)
    inside = (lane >= SLOT_LANE) & (lane < SLOT_LANE + SLOTS)
    extra = jnp.where(inside & (lane != SLOT_LANE + slot), masked_score, 0.0)
    return jnp.where(lane == GLOBAL_LANE + slot, 1.0, extra)


def global_query_extra(slot):
    lane = iota((GLOBALS, LANES), 1)
    inside = (lane >= GLOBAL_LANE) & (lane < GLOBAL_LANE + SLOTS)
    return jnp.where(inside & (lane != GLOBAL_LANE + slot), masked_score, 0.0)


def normalize_rows(values):
    mean = jnp.mean(values, axis=-1, keepdims=True)
    centered = values - mean
    variance = jnp.mean(centered * centered, axis=-1, keepdims=True)
    scale = lax.rsqrt(variance + norm_eps)
    return centered * scale, scale


def norm_back(unit, scale, gain, upstream):
    inner = upstream * gain
    along = jnp.mean(inner * unit, axis=-1, keepdims=True)
    return scale * (inner - jnp.mean(inner, axis=-1, keepdims=True) - unit * along)


def gelu_parts(value):
    decay = jnp.exp(-0.5 * value * value)
    step = 1.0 / (1.0 + (0.3275911 * 0.7071067811865476) * jnp.abs(value))
    series = 1.061405429 * step - 1.453152027
    series = series * step + 1.421413741
    series = series * step - 0.284496736
    series = series * step + 0.254829592
    tail = (0.5 * series) * step * decay
    area = jnp.where(value >= 0.0, 1.0 - tail, tail)
    return area, decay * 0.3989422804014327


def full(shape):
    return pl.BlockSpec(shape, lambda *unused: (0,) * len(shape))


def once(shape):
    return pl.BlockSpec(
        shape, lambda *unused: (0,) * len(shape), pipeline_mode=pl.Buffered(buffer_count=1)
    )


def params(**more):
    return pltpu.CompilerParams(vmem_limit_bytes=VMEM_LIMIT, **more)


STAGES = 5
MESH = pl.DeviceIdType.MESH
WEIGHTS = (("core", 1), ("y", 2), ("z0", 4), ("z1", 8))


def my_place():
    batch = lax.axis_index("batch")
    seq = lax.axis_index("seq")
    bits = {"x": batch}
    partners = {"x": (1 - batch, seq)}
    for name, weight in WEIGHTS:
        bits[name] = (seq // weight) % 2
        partners[name] = (batch, seq + weight - 2 * weight * bits[name])
    return bits, partners


def meet(devices):
    barrier = pltpu.get_barrier_semaphore()
    for device in devices:
        pl.semaphore_signal(barrier, inc=1, device_id=device, device_id_type=MESH)
    pl.semaphore_wait(barrier, len(devices))


def remote(source, target, send, recv, device):
    return pltpu.make_async_remote_copy(
        src_ref=source,
        dst_ref=target,
        send_sem=send,
        recv_sem=recv,
        device_id=device,
        device_id_type=MESH,
    )


class RowGather:
    def __init__(self, ref, cut, send_sem, recv_sem, bits, partners):
        self.ref = ref
        self.cut = cut
        self.send_sem = send_sem
        self.recv_sem = recv_sem
        self.bits = bits
        self.partners = partners

    def copies(self, number):
        core, y, z0, z1 = (self.bits[name] for name in ("core", "y", "z0", "z1"))
        ref = self.ref
        rows = pl.ds(0, ref.shape[4])
        left = pl.ds(0, self.cut)
        right = pl.ds(self.cut, ref.shape[5] - self.cut)
        if number == 0:
            moves = [
                (ref.at[z1, z0, y, core, rows, left], "z1"),
                (ref.at[z1, z0, y, core, rows, right], "z1"),
            ]
        elif number == 1:
            moves = [
                (ref.at[:, z0, y, core, rows, left], "z0"),
                (ref.at[:, z0, y, core, rows, right], "y"),
            ]
        elif number == 2:
            moves = [
                (ref.at[:, :, y, core, rows, left], "y"),
                (ref.at[:, z0, :, core, rows, right], "z0"),
            ]
        else:
            moves = [
                (ref.at[:, :, :, core, rows, left], "core"),
                (ref.at[:, :, :, core, rows, right], "core"),
            ]
        return [
            remote(
                part,
                part,
                self.send_sem.at[number, side],
                self.recv_sem.at[number, side],
                self.partners[name],
            )
            for side, (part, name) in enumerate(moves)
        ]

    def begin(self, number=0):
        for copy in self.copies(number):
            copy.start()

    def advance(self, number):
        for copy in self.copies(number):
            copy.wait_recv()
        if number < 3:
            self.begin(number + 1)

    def end(self, first=0):
        for number in range(first, 4):
            for copy in self.copies(number):
                copy.wait_send()


X_FIRST = ("core", "x", "y", "z0", "z1")
Y_FIRST = ("core", "y", "x", "z0", "z1")
X_Z_FIRST = ("core", "x", "z0", "y", "z1")
Z_FIRST = ("core", "z0", "x", "z1", "y")
AXES = ("z1", "z0", "y", "core", "x")


class HalvingSum:
    def __init__(
        self, orders, sources, landings, own, send_sem, recv_sem, own_sem, put, bits, partners
    ):
        self.orders = orders
        self.sources = sources
        self.landings = landings
        self.own = own
        self.send_sem = send_sem
        self.recv_sem = recv_sem
        self.own_sem = own_sem
        self.put = put
        self.bits = bits
        self.partners = partners

    def part(self, unit, stage, other):
        order = self.orders[unit]
        name = order[stage]
        side = 1 - self.bits[name] if other else self.bits[name]
        if stage == 0:
            if not other and self.own is not None:
                return self.own.at[unit]
            return self.sources[unit](side)
        left = [axis for axis in AXES if axis in order[stage:]]
        index = (slice(None),) * left.index(name) + (side,)
        return self.landings[stage - 1].at[unit].at[index]

    def copy(self, unit, stage):
        return remote(
            self.part(unit, stage, True),
            self.landings[stage].at[unit],
            self.send_sem.at[unit, stage],
            self.recv_sem.at[unit, stage],
            self.partners[self.orders[unit][stage]],
        )

    def own_copy(self, unit):
        return pltpu.make_async_copy(
            self.sources[unit](self.bits["core"]), self.own.at[unit], self.own_sem.at[unit]
        )

    def begin(self, unit):
        if self.own is not None:
            self.own_copy(unit).start()
        self.copy(unit, 0).start()

    def advance(self, unit, stage, stop=False):
        if stage == 0 and self.own is not None:
            self.own_copy(unit).wait()
        self.copy(unit, stage).wait_recv()
        landing = self.landings[stage].at[unit]
        kept = self.part(unit, stage, False)
        if stage < len(self.orders[unit]) - 1:
            add_into(landing, kept)
            if not stop:
                self.copy(unit, stage + 1).start()
        else:
            self.put(unit, landing[...].astype(f32) + kept[...].astype(f32))

    def sent(self, unit, stage):
        self.copy(unit, stage).wait_send()


def put_rows(ref, rows):
    def put(unit, value):
        ref[unit * rows : (unit + 1) * rows] = value

    return put


def add_into(target, more):
    def one(i, carry):
        target[i] = target[i] + more[i]
        return carry

    lax.fori_loop(0, target.shape[0], one, 0)


def sum_scratch(units, rows, lanes, with_own):
    piece = (rows, lanes)
    dma = pltpu.SemaphoreType.DMA
    shapes = [pltpu.VMEM((units, 2, 2, 2, 2) + piece, bf16)] if with_own else []
    shapes += [
        pltpu.VMEM((units, 2, 2, 2, 2) + piece, bf16),
        pltpu.VMEM((units, 2, 2, 2) + piece, bf16),
        pltpu.VMEM((units, 2, 2) + piece, bf16),
        pltpu.VMEM((units, 2) + piece, bf16),
        pltpu.VMEM((units,) + piece, bf16),
        dma((units, STAGES)),
        dma((units, STAGES)),
    ]
    return shapes + ([dma((units,))] if with_own else [])


def project_rows(rows_ref, gain_ref, offset_ref, wq_ref, wk_ref, wv_ref, outs):
    unit, unused = normalize_rows(rows_ref[...].astype(f32))
    normed = (unit * gain_ref[...] + offset_ref[...]).astype(bf16)
    outs[0][...] = normed
    outs[1][...] = (nn(normed, wq_ref[...]) * query_scale).astype(bf16)
    outs[2][...] = nn(normed, wk_ref[...]).astype(bf16)
    outs[3][...] = nn(normed, wv_ref[...]).astype(bf16)


def project_local_kernel(rows_ref, gain_ref, offset_ref, wq_ref, wk_ref, wv_ref, *outs):
    project_rows(rows_ref, gain_ref, offset_ref, wq_ref, wk_ref, wv_ref, outs)


def project_local(rows, gain, offset, wq, wk, wv):
    count, width = rows.shape
    tile = pl.BlockSpec((BLOCK, width), lambda i: (i, 0))
    return pl.pallas_call(
        project_local_kernel,
        grid=(count // BLOCK,),
        in_specs=[tile, full((1, width)), full((1, width))] + [once((width, width))] * 3,
        out_specs=[tile] * 4,
        out_shape=[jax.ShapeDtypeStruct((count, width), bf16)] * 4,
        compiler_params=params(),
        cost_estimate=pl.CostEstimate(
            flops=6 * count * width * width, bytes_accessed=12 * count * width, transcendentals=0
        ),
        name="project_local",
    )(rows, gain, offset, wq, wk, wv)


def gather_project_kernel(
    tokens_ref,
    states_ref,
    w1_ref,
    norms_ref,
    wq_in,
    wk_in,
    wv_in,
    h_out,
    q_out,
    k_out,
    v_out,
    x_out,
    all_out,
    gh_out,
    gq_out,
    gk_out,
    gv_out,
    w1t_out,
    wq_ref,
    wk_ref,
    wv_ref,
    x_ref,
    all_ref,
    local_ref,
    global_ref,
    w1s_ref,
    w1t_ref,
    halo_send,
    halo_recv,
    load_sem,
    store_sem,
    gstore_sem,
    more_sem,
    send_sem,
    recv_sem,
):
    bits, partners = my_place()
    batch = lax.axis_index("batch")
    seq = lax.axis_index("seq")
    places = lax.axis_size("seq")
    after = (batch, lax.rem(seq + 1, places))
    before = (batch, lax.rem(seq + places - 1, places))
    rows, width = tokens_ref.shape
    own = states_ref.shape[0]
    core, y, z0, z1 = (bits[name] for name in ("core", "y", "z0", "z1"))
    start = pl.ds(0, HALF)
    most = pl.ds(0, rows - HALF)
    end = pl.ds(rows - HALF, HALF)
    shifted = pl.ds(HALF, rows - HALF)
    loads = [
        pltpu.make_async_copy(source, target, load_sem.at[number])
        for number, (source, target) in enumerate(
            (
                (tokens_ref.at[most], x_ref.at[shifted]),
                (wq_in, wq_ref),
                (wk_in, wk_ref),
                (wv_in, wv_ref),
                (w1_ref, w1s_ref),
            )
        )
    ]
    for load in loads:
        load.start()
    all_ref[z1, z0, y, core] = states_ref[...]
    meet([partners[name] for name, unused in WEIGHTS] + [before, after])
    halo = remote(tokens_ref.at[end], x_ref.at[start], halo_send, halo_recv, after)
    gather = RowGather(all_ref, width // 2, send_sem, recv_sem, bits, partners)
    gather.begin()
    halo.start()

    outs = (h_out, q_out, k_out, v_out)

    def stores(index):
        at = pl.ds(index * HALF, HALF)
        return [
            pltpu.make_async_copy(local_ref.at[which, at], out.at[at], store_sem.at[which, index])
            for which, out in enumerate(outs)
        ]

    def project(index):
        at = pl.ds(index * HALF, HALF)
        project_rows(
            x_ref.at[at],
            norms_ref.at[0:1],
            norms_ref.at[1:2],
            wq_ref,
            wk_ref,
            wv_ref,
            [local_ref.at[which, at] for which in range(4)],
        )
        for store in stores(index):
            store.start()

    for number in range(4):
        loads[number].wait()
    tiles = rows // HALF
    def turn(i, carry):
        at = pl.ds(pl.multiple_of(i * HALF, HALF), HALF)
        w1t_ref[at, :] = w1s_ref[:, at].T
        return carry

    project(1)
    project(2)
    gather.advance(0)
    for index in range(3, tiles):
        project(index)
    loads[4].wait()
    turns = w1t_ref.shape[0] // HALF
    lax.fori_loop(0, turns // 2, turn, 0)
    gather.advance(1)
    lax.fori_loop(turns // 2, turns, turn, 0)
    w1t_store = pltpu.make_async_copy(w1t_ref, w1t_out, more_sem.at[1])
    w1t_store.start()
    gather.advance(2)

    gouts = (gh_out, gq_out, gk_out, gv_out)

    def gstores(first, side):
        return [
            pltpu.make_async_copy(
                global_ref.at[which, first, :, :, side],
                out.at[first, :, :, side],
                gstore_sem.at[which, first, number],
            )
            for which, out in enumerate(gouts)
            for number in ((0 if side is core else 1),)
        ]

    def project_states(side):
        for first in range(2):
            piece = all_ref[first, :, :, side].reshape(4 * own, width)
            unit, unused = normalize_rows(piece.astype(f32))
            normed = (unit * norms_ref[2:3] + norms_ref[3:4]).astype(bf16)
            values = (
                normed,
                (nn(normed, wq_ref[...]) * query_scale).astype(bf16),
                nn(normed, wk_ref[...]).astype(bf16),
                nn(normed, wv_ref[...]).astype(bf16),
            )
            for which, value in enumerate(values):
                global_ref[which, first, :, :, side] = value.reshape(2, 2, own, width)
            for store in gstores(first, side):
                store.start()

    other = 1 - core
    project_states(core)
    gather.advance(3)
    all_store = pltpu.make_async_copy(all_ref, all_out, more_sem.at[2])
    all_store.start()
    project_states(other)
    halo.wait_recv()
    x_store = pltpu.make_async_copy(x_ref, x_out, more_sem.at[0])
    x_store.start()
    project(0)

    for index in range(tiles):
        for store in stores(index):
            store.wait()
    for side in (core, other):
        for first in range(2):
            for store in gstores(first, side):
                store.wait()
    x_store.wait()
    w1t_store.wait()
    all_store.wait()
    halo.wait_send()
    gather.end()


def gather_project(tokens, states, w1, norms, wq, wk, wv):
    rows, width = tokens.shape
    own = states.shape[0]
    vmem = pl.BlockSpec(memory_space=pltpu.VMEM)
    anywhere = pl.BlockSpec(memory_space=pl.ANY)
    dma = pltpu.SemaphoreType.DMA
    local = jax.ShapeDtypeStruct((rows, width), bf16)
    glob = jax.ShapeDtypeStruct((2, 2, 2, 2, own, width), bf16)
    turned = (w1.shape[1], width)
    weight = pltpu.VMEM((width, width), bf16)
    return pl.pallas_call(
        gather_project_kernel,
        in_specs=[anywhere, vmem, anywhere, vmem] + [anywhere] * 3,
        out_specs=[anywhere] * 11,
        out_shape=[local] * 5 + [glob] * 5 + [jax.ShapeDtypeStruct(turned, bf16)],
        scratch_shapes=[
            weight,
            weight,
            weight,
            pltpu.VMEM((rows, width), bf16),
            pltpu.VMEM(glob.shape, bf16),
            pltpu.VMEM((4, rows, width), bf16),
            pltpu.VMEM((4,) + glob.shape, bf16),
            pltpu.VMEM(w1.shape, bf16),
            pltpu.VMEM(turned, bf16),
            dma,
            dma,
            dma((5,)),
            dma((4, rows // HALF)),
            dma((4, 2, 2)),
            dma((3,)),
            dma((4, 2)),
            dma((4, 2)),
        ],
        compiler_params=params(collective_id=1, has_side_effects=True),
        cost_estimate=pl.CostEstimate(
            flops=6 * (rows + 16 * own) * width * width,
            bytes_accessed=24 * rows * width,
            transcendentals=0,
        ),
        name="gather_project",
    )(tokens, states, w1, norms, wq, wk, wv)


def project_global_kernel(
    rows_count,
    group_rows,
    lengths,
    bucket_of,
    place,
    rows_ref,
    gain_ref,
    offset_ref,
    wq_ref,
    wk_ref,
    wv_ref,
    h_ref,
    q_ref,
    k_ref,
    v_ref,
    edges,
):
    slot = pl.program_id(0)

    @pl.when(slot == 0)
    def _():
        read_edges(lengths, bucket_of, place, edges)

    needed = slot == place[2]
    for block in range(rows_count // BLOCK):
        needed = needed | slot_present(slot, place, edges, rows_count, group_rows, block)

    @pl.when(needed)
    def _():
        project_rows(
            rows_ref, gain_ref, offset_ref, wq_ref, wk_ref, wv_ref, (h_ref, q_ref, k_ref, v_ref)
        )


def project_global(scalars, rows_count, group_rows, rows, gain, offset, wq, wk, wv):
    count, width = rows.shape
    tile = pl.BlockSpec((GLOBALS, width), lambda i, *unused: (i, 0))
    return pl.pallas_call(
        functools.partial(project_global_kernel, rows_count, group_rows),
        grid_spec=pltpu.PrefetchScalarGridSpec(
            num_scalar_prefetch=3,
            grid=(SLOTS,),
            in_specs=[tile, full((1, width)), full((1, width))] + [once((width, width))] * 3,
            out_specs=[tile] * 4,
            scratch_shapes=[pltpu.SMEM((16,), jnp.int32)],
        ),
        out_shape=[jax.ShapeDtypeStruct((count, width), bf16)] * 4,
        compiler_params=params(),
        cost_estimate=pl.CostEstimate(
            flops=6 * 256 * width * width, bytes_accessed=12 * count * width, transcendentals=0
        ),
        name="project_global",
    )(*scalars, rows, gain, offset, wq, wk, wv)


def block_columns(place, edges, rows, group_rows, block, step, blocks, query_columns, key_columns):
    @pl.when(step < blocks)
    def _():
        slot_of, segment = row_numbers(place, edges, rows, group_rows, block)
        query_columns[block] = query_extra(slot_of, segment).astype(bf16)
        key_columns[block] = key_extra(slot_of, segment).astype(bf16)


def slot_line(place, edges, rows, group_rows, block):
    token = block_start(place, rows, block) + iota((1, BLOCK), 1)
    token = jnp.where(token < 0, token + group_rows, token)
    slot = jnp.zeros((1, BLOCK), jnp.int32)
    for j in range(SLOTS):
        slot = slot + jnp.where(edges[j + 1] <= token, 1, 0)
    return slot


def side_by_side(stacked):
    return stacked[:HEAD_DIM, : stacked.shape[1] // 2], stacked[HEAD_DIM:, stacked.shape[1] // 2 :]


def slot_forward_kernel(
    rows_count,
    group_rows,
    lengths,
    bucket_of,
    place,
    q_ref,
    k_ref,
    v_ref,
    gq_ref,
    gk_ref,
    gv_ref,
    far_ref,
    far_stat_ref,
    part_ref,
    part_stat_ref,
    edges,
    query_columns,
    key_columns,
    keys_ref,
    queries_ref,
    sum_ref,
    far_sum,
):
    group = pl.program_id(0)
    block = pl.program_id(1)
    blocks = rows_count // BLOCK
    step = group * blocks + block
    together = range(TOGETHER)

    @pl.when(step == 0)
    def _():
        read_edges(lengths, bucket_of, place, edges)

    @pl.when(block == 0)
    def _():
        sum_ref[...] = jnp.zeros_like(sum_ref)
        part_stat_ref[...] = jnp.broadcast_to(
            jnp.where(iota((8, GLOBALS), 0) < 2, masked_score, 0.0), part_stat_ref.shape
        )

    block_columns(
        place, edges, rows_count, group_rows, block, step, blocks, query_columns, key_columns
    )
    extra = query_columns[block]
    for which in together:
        lanes = pl.ds(which * LANES, LANES)
        keys_ref[which, :, :LANES] = k_ref[:, lanes]
        keys_ref[which, :, LANES:] = key_columns[block]
        queries_ref[which, :, :LANES] = stack_pair(q_ref[:, lanes])
        queries_ref[which, :BLOCK, LANES:] = extra
        queries_ref[which, BLOCK:, LANES:] = extra
    line = slot_line(place, edges, rows_count, group_rows, block)
    both_lines = jnp.concatenate([line, line], 1)

    def add(slot, keys_of, values_of):
        at = pl.ds(pl.multiple_of(slot * GLOBALS, GLOBALS), GLOBALS)
        extra = global_query_extra(slot).astype(bf16)
        for which in together:
            lanes = pl.ds(which * LANES, LANES)
            queries = jnp.concatenate(
                [stack_pair(gq_ref[at, lanes]), jnp.concatenate([extra, extra], 0)], axis=1
            )
            score = nt(keys_of(which), queries)
            stat = part_stat_ref[slot, which]
            old = jnp.concatenate([stat[0:1], stat[1:2]], axis=1)
            peak = jnp.maximum(old, jnp.max(score, axis=0, keepdims=True))
            weights = jnp.exp(score - peak)
            keep = jnp.exp(old - peak)
            total = jnp.concatenate([stat[2:3], stat[3:4]], axis=1) * keep + jnp.sum(
                weights, axis=0, keepdims=True
            )
            part_stat_ref[slot, which] = jnp.concatenate(
                [
                    peak[:, :GLOBALS],
                    peak[:, GLOBALS:],
                    total[:, :GLOBALS],
                    total[:, GLOBALS:],
                    jnp.zeros((4, GLOBALS), f32),
                ],
                axis=0,
            )
            low, high = side_by_side(tn(values_of(which), weights.astype(bf16)))
            sums = sum_ref.at[which, slot]
            sums[:HEAD_DIM] = sums[:HEAD_DIM] * keep[:, :GLOBALS] + low
            sums[HEAD_DIM:] = sums[HEAD_DIM:] * keep[:, GLOBALS:] + high

    far_sum[...] = jnp.zeros_like(far_sum)
    far_stat_ref[...] = jnp.zeros_like(far_stat_ref)

    def one_slot(slot, carry):
        @pl.when(slot_present(slot, place, edges, rows_count, group_rows, block))
        def _():
            add(
                slot,
                lambda which: keys_ref[which],
                lambda which: v_ref[:, pl.ds(which * LANES, LANES)],
            )
            at = pl.ds(pl.multiple_of(slot * GLOBALS, GLOBALS), GLOBALS)
            columns = global_key_extra(slot).astype(bf16)
            mine = both_lines == slot
            here = line == slot
            for which in together:
                lanes = pl.ds(which * LANES, LANES)
                slot_keys = jnp.concatenate([gk_ref[at, lanes], columns], 1)
                score = nt(slot_keys, queries_ref[which])
                peak = jnp.max(score, axis=0, keepdims=True)
                weights = jnp.exp(score - peak)
                total = jnp.sum(weights, axis=0, keepdims=True)
                stat = far_stat_ref.at[which, 0]
                stat[0:1] = jnp.where(mine, peak, stat[0:1])
                stat[1:2] = jnp.where(mine, total, stat[1:2])
                low, high = side_by_side(tn(gv_ref[at, lanes], weights.astype(bf16)))
                first = pl.ds(which * LANES, HEAD_DIM)
                second = pl.ds(which * LANES + HEAD_DIM, HEAD_DIM)
                far_sum[first] = jnp.where(here, low, far_sum[first])
                far_sum[second] = jnp.where(here, high, far_sum[second])

        return carry

    lax.fori_loop(0, SLOTS, one_slot, 0)
    far_ref[...] = far_sum[...].astype(bf16)

    @pl.when((block == blocks - 1) & (place[2] >= 0))
    def _():
        slot = place[2]
        at = pl.ds(pl.multiple_of(slot * GLOBALS, GLOBALS), GLOBALS)
        columns = global_key_extra(slot).astype(bf16)
        add(
            slot,
            lambda which: jnp.concatenate(
                [gk_ref[at, pl.ds(which * LANES, LANES)], columns], axis=1
            ),
            lambda which: gv_ref[at, pl.ds(which * LANES, LANES)],
        )

    @pl.when(block == blocks - 1)
    def _():
        for which in together:
            part_ref[:, which] = sum_ref[which].astype(bf16)


def line_spec(pairs=1):
    return pl.BlockSpec((pairs, 1, 8, 2 * BLOCK), lambda p, b, *unused: (p, b, 0, 0))


def column_scratch(blocks):
    return [pltpu.SMEM((16,), jnp.int32)] + [pltpu.VMEM((blocks, BLOCK, LANES), bf16)] * 2


def slot_forward(scalars, rows_count, group_rows, q, k, v, gq, gk, gv):
    blocks = rows_count // BLOCK
    all_globals, width = gq.shape
    block_spec = pl.BlockSpec((BLOCK, TOGETHER * LANES), lambda p, b, *unused: (b, p))
    pair_spec = pl.BlockSpec((all_globals, TOGETHER * LANES), lambda p, b, *unused: (0, p))
    return pl.pallas_call(
        functools.partial(slot_forward_kernel, rows_count, group_rows),
        grid_spec=pltpu.PrefetchScalarGridSpec(
            num_scalar_prefetch=3,
            grid=(PAIRS // TOGETHER, blocks),
            in_specs=[block_spec] * 3 + [pair_spec] * 3,
            out_specs=[
                pl.BlockSpec((TOGETHER * LANES, BLOCK), lambda p, b, *unused: (p, b)),
                line_spec(TOGETHER),
                pl.BlockSpec((SLOTS, TOGETHER, LANES, GLOBALS), lambda p, b, *unused: (0, p, 0, 0)),
                pl.BlockSpec((SLOTS, TOGETHER, 8, GLOBALS), lambda p, b, *unused: (0, p, 0, 0)),
            ],
            scratch_shapes=column_scratch(blocks)
            + [
                pltpu.VMEM((TOGETHER, BLOCK, 2 * LANES), bf16),
                pltpu.VMEM((TOGETHER, 2 * BLOCK, 2 * LANES), bf16),
                pltpu.VMEM((TOGETHER, SLOTS, LANES, GLOBALS), f32),
                pltpu.VMEM((TOGETHER * LANES, BLOCK), f32),
            ],
        ),
        out_shape=[
            jax.ShapeDtypeStruct((width, rows_count), bf16),
            jax.ShapeDtypeStruct((PAIRS, blocks, 8, 2 * BLOCK), f32),
            jax.ShapeDtypeStruct((SLOTS, PAIRS, LANES, GLOBALS), bf16),
            jax.ShapeDtypeStruct((SLOTS, PAIRS, 8, GLOBALS), f32),
        ],
        compiler_params=params(),
        cost_estimate=pl.CostEstimate(
            flops=8 * 4 * rows_count * GLOBALS * width,
            bytes_accessed=20 * all_globals * width,
            transcendentals=2 * HEADS * rows_count * GLOBALS,
        ),
        name="slot_forward",
    )(*scalars, q, k, v, gq, gk, gv)


def merge_parts(stat, sums, more_stat, more_sums):
    peak = jnp.maximum(stat[0:2], more_stat[0:2])
    keep = jnp.exp(stat[0:2] - peak)
    take = jnp.exp(more_stat[0:2] - peak)
    total = stat[2:4] * keep + more_stat[2:4] * take
    low = sums[:HEAD_DIM].astype(f32) * keep[0:1] + more_sums[:HEAD_DIM].astype(f32) * take[0:1]
    high = sums[HEAD_DIM:].astype(f32) * keep[1:2] + more_sums[HEAD_DIM:].astype(f32) * take[1:2]
    return (
        jnp.concatenate([peak, total, jnp.zeros((4, GLOBALS), f32)], 0),
        jnp.concatenate([low, high], 0),
    )


class SlotSum:
    ORDER = ("core", "y", "z0", "z1")

    def __init__(self, source, sums, stats, send_sem, recv_sem, bits, partners):
        self.source = source
        self.sums = sums
        self.stats = stats
        self.send_sem = send_sem
        self.recv_sem = recv_sem
        self.bits = bits
        self.partners = partners

    def held(self, stage, other):
        bit = self.bits[self.ORDER[stage]]
        side = 1 - bit if other else bit
        if stage == 0:
            return self.source(side)
        index = ((), (slice(None), slice(None)), (slice(None),), ())[stage] + (side,)
        return self.sums[stage - 1].at[index], self.stats[stage - 1].at[index]

    def copies(self, stage):
        partner = self.partners[self.ORDER[stage]]
        sums, stat = self.held(stage, True)
        return (
            remote(
                sums,
                self.sums[stage],
                self.send_sem.at[stage, 0],
                self.recv_sem.at[stage, 0],
                partner,
            ),
            remote(
                stat,
                self.stats[stage],
                self.send_sem.at[stage, 1],
                self.recv_sem.at[stage, 1],
                partner,
            ),
        )

    def begin(self, stage):
        for copy in self.copies(stage):
            copy.start()

    def merge(self, stage, kept=None):
        for copy in self.copies(stage):
            copy.wait_recv()
        sums, stat = self.held(stage, False) if kept is None else kept
        lead = self.sums[stage].shape[:-3]
        total = 1
        for size in lead:
            total = total * size

        def one(number, carry):
            index = []
            left = number
            for size in reversed(lead):
                index.append(left % size)
                left = left // size
            index = tuple(reversed(index))
            for which in range(PAIRS // 2):
                spot = index + (which,)
                new_stat, new_sums = merge_parts(
                    self.stats[stage][spot], self.sums[stage][spot], stat[spot], sums[spot]
                )
                self.stats[stage][spot] = new_stat
                self.sums[stage][spot] = new_sums.astype(bf16)
            return carry

        lax.fori_loop(0, total, one, 0)

    def sent(self, stage):
        for copy in self.copies(stage):
            copy.wait_send()


def local_forward_kernel(
    talk,
    rows_count,
    group_rows,
    lengths,
    bucket_of,
    place,
    q_ref,
    k_ref,
    v_ref,
    far_ref,
    far_stat_ref,
    *refs,
):
    if talk:
        part_ref, part_stat_ref = refs[:2]
        o_ref, line_ref, half_ref, half_stat_ref = refs[2:6]
        own_ref, own_stat_ref = refs[6:8]
        sums_refs = refs[8:10]
        stat_refs = refs[10:12]
        edges, query_columns, key_columns, send_sem, recv_sem, own_sem = refs[12:]
    else:
        o_ref, line_ref, edges, query_columns, key_columns = refs
    pair = pl.program_id(0)
    block = pl.program_id(1)
    blocks = rows_count // BLOCK
    step = pair * blocks + block

    @pl.when(step == 0)
    def _():
        read_edges(lengths, bucket_of, place, edges)

    if talk:
        bits, partners = my_place()
        slot_sum = SlotSum(
            lambda side: (part_ref.at[:, :, :, side], part_stat_ref.at[:, :, :, side]),
            sums_refs,
            stat_refs,
            send_sem,
            recv_sem,
            bits,
            partners,
        )
        own_parts = slot_sum.held(0, False)
        own_copies = [
            pltpu.make_async_copy(own_parts[0], own_ref, own_sem.at[0]),
            pltpu.make_async_copy(own_parts[1], own_stat_ref, own_sem.at[1]),
        ]

        @pl.when(step == 0)
        def _():
            meet([partners["core"], partners["y"]])
            for copy in own_copies:
                copy.start()
            slot_sum.begin(0)

        @pl.when(step == 2)
        def _():
            for copy in own_copies:
                copy.wait()
            slot_sum.merge(0, (own_ref, own_stat_ref))
            slot_sum.begin(1)

        @pl.when(step == PAIRS * blocks - 1)
        def _():
            slot_sum.merge(1)
            half_ref[...] = sums_refs[1][...]
            half_stat_ref[...] = stat_refs[1][...]
            slot_sum.sent(0)
            slot_sum.sent(1)

    block_columns(
        place, edges, rows_count, group_rows, block, step, blocks, query_columns, key_columns
    )
    extra = query_columns[block]
    queries = jnp.concatenate(
        [stack_pair(q_ref[...]), jnp.concatenate([extra, extra], 0)], axis=1
    )
    keys = jnp.concatenate([k_ref[...], key_columns[block]], axis=1)
    score = nt(keys, queries)
    far_peak = far_stat_ref[0, 0, 0:1]
    peak = jnp.maximum(jnp.max(score, axis=0, keepdims=True), far_peak)
    weights = jnp.exp(score - peak)
    far_keep = jnp.exp(far_peak - peak)
    total = jnp.sum(weights, axis=0, keepdims=True) + far_stat_ref[0, 0, 1:2] * far_keep
    low, high = side_by_side(tn(v_ref[...], weights.astype(bf16)))
    low = (low + far_ref[:HEAD_DIM] * far_keep[:, :BLOCK]) / total[:, :BLOCK]
    high = (high + far_ref[HEAD_DIM:] * far_keep[:, BLOCK:]) / total[:, BLOCK:]
    o_ref[...] = jnp.concatenate([low, high], 0).T.astype(bf16)
    line_ref[0, 0] = jnp.broadcast_to(peak + jnp.log(total), (8, 2 * BLOCK))


def local_forward(
    talk, scalars, rows_count, group_rows, q, k, v, far, far_stat, part, part_stat
):
    blocks = rows_count // BLOCK
    width = q.shape[1]
    block_spec = pl.BlockSpec((BLOCK, LANES), lambda p, b, *unused: (b, p))
    operands = [q, k, v, far, far_stat]
    in_specs = [block_spec] * 3 + [
        pl.BlockSpec((LANES, BLOCK), lambda p, b, *unused: (p, b)),
        line_spec(),
    ]
    out_specs = [block_spec, line_spec()]
    out_shape = [
        jax.ShapeDtypeStruct((rows_count, width), bf16),
        jax.ShapeDtypeStruct((PAIRS, blocks, 8, 2 * BLOCK), f32),
    ]
    scratch = []
    more = {}
    edges = column_scratch(blocks)
    if talk:
        cut = (2, 2, 2, 2, PAIRS // 2)
        operands += [
            part.reshape(cut + part.shape[2:]),
            part_stat.reshape(cut + part_stat.shape[2:]),
        ]
        in_specs += [pl.BlockSpec(memory_space=pl.ANY)] * 2
        shapes = [
            (2, 2, PAIRS // 2, LANES, GLOBALS),
            (2, 2, PAIRS // 2, 8, GLOBALS),
        ]
        out_specs += [full(shape) for shape in shapes]
        out_shape += [
            jax.ShapeDtypeStruct(shapes[0], bf16),
            jax.ShapeDtypeStruct(shapes[1], f32),
        ]
        leads = [(2, 2, 2), (2, 2, 2), (2, 2)]
        sums = [pltpu.VMEM(lead + shapes[0][2:], bf16) for lead in leads]
        stats = [pltpu.VMEM(lead + shapes[1][2:], f32) for lead in leads]
        dma = pltpu.SemaphoreType.DMA
        scratch = [sums[0], stats[0]] + sums[1:] + stats[1:]
        edges += [dma((2, 2)), dma((2, 2)), dma((2,))]
        more = {"collective_id": 2, "has_side_effects": True}
    return pl.pallas_call(
        functools.partial(local_forward_kernel, talk, rows_count, group_rows),
        grid_spec=pltpu.PrefetchScalarGridSpec(
            num_scalar_prefetch=3,
            grid=(PAIRS, blocks),
            in_specs=in_specs,
            out_specs=out_specs,
            scratch_shapes=scratch + edges,
        ),
        out_shape=out_shape,
        compiler_params=params(**more),
        cost_estimate=pl.CostEstimate(
            flops=16 * rows_count * BLOCK * width,
            bytes_accessed=16 * rows_count * width,
            transcendentals=HEADS * rows_count * BLOCK,
        ),
        name="local_forward",
    )(*scalars, *operands)


def join_rows(ref):
    return jnp.concatenate([ref[i : i + 1] for i in range(ref.shape[0])], axis=1)


def take_lanes(row, starts, length):
    return jnp.concatenate([row[:, start : start + length] for start in starts], axis=1)


def put_grouped(ref, value):
    seq, batch, rows, lanes = ref.shape
    for part in range(batch):
        piece = value[:, part * lanes : (part + 1) * lanes].astype(bf16)
        ref[:, part] = piece.reshape(seq, rows, lanes)


def put_unit(ref, value):
    batch, rows, lanes = ref.shape[4:]
    for part in range(batch):
        piece = value[:, part * lanes : (part + 1) * lanes].astype(bf16)
        ref[:, :, :, :, part] = piece.reshape(ref.shape[:4] + (rows, lanes))


TICKS = 3
ENDINGS = ((0, 2, 4, 6, 8), (3, 5, 7, 9, 10), (6, 8))


def branch_kernel(
    tile,
    seq_size,
    x_ref,
    o_ref,
    ct_ref,
    ct_head_ref,
    gx_ref,
    go_in_ref,
    gstat_in_ref,
    gct_ref,
    wo_ref,
    w1_ref,
    b1_ref,
    w2_ref,
    b2_ref,
    norms_ref,
    z_ref,
    dy_ref,
    do_ref,
    gz_ref,
    gdy_ref,
    gdo_ref,
    dwo_ref,
    db1_ref,
    db2_ref,
    dgain_ref,
    doffset_ref,
    first_ref,
    second_ref,
    *refs,
):
    talk = seq_size > 0
    if talk:
        message_ref, rest_ref, z_head_ref = refs[:3]
        refs = refs[3:]
    os_ref, cts_ref, y_ref, h_ref, z_sum_ref, dh_ref, dft_ref, a_ref, du_ref, load_sem = refs[:10]
    b1s_ref = refs[10]
    refs = refs[11:]
    step = pl.program_id(0)
    steps = pl.num_programs(0)
    count, width = x_ref.shape
    own = gx_ref.shape[0]
    extra = os_ref.shape[0] - count
    tiles = count // tile
    tail = pl.ds(count, extra)

    def rows_at(i):
        return pl.ds(i * tile, tile)

    def padded(value):
        return jnp.concatenate([value, jnp.zeros((extra - own, width), value.dtype)], axis=0)

    if talk:
        units_ref = refs[0]
        landings = refs[1:6]
        send_sem, recv_sem = refs[6:8]
        half_ref, half_stat_ref = refs[8:10]
        slot_sums = refs[10:12]
        slot_stats = refs[12:14]
        turned_ref, go_land, gstat_land, stat_ref, slot_send, slot_recv = refs[14:20]
        message_land, message_send, message_recv, halo_send, halo_recv = refs[20:]
        last_step = 4
        bits, partners = my_place()
        core = bits["core"]
        chunks = last_step - 1
        slots = units_ref.shape[0]
        plan = [
            (tick, chunk, stage)
            for chunk, ticks in enumerate(ENDINGS)
            for stage, tick in enumerate(ticks)
        ]

        def source(unit):
            return lambda side: units_ref.at[unit % slots, :, :, :, side]

        engine = HalvingSum(
            (X_FIRST, Y_FIRST) * chunks,
            [source(unit) for unit in range(2 * chunks)],
            landings,
            None,
            send_sem,
            recv_sem,
            None,
            put_rows(first_ref, landings[4].shape[1]),
            bits,
            partners,
        )

        def advance(tick):
            for when, chunk, stage in sorted(plan, key=lambda entry: -entry[2]):
                if when == tick:
                    for unit in (2 * chunk, 2 * chunk + 1):
                        engine.advance(unit, stage, stop=chunk == chunks - 1 and stage == 1)

        def tick_at(position):
            for number in range(1, last_step):
                tick = TICKS * (number - 1) + position

                @pl.when(step == number)
                def _():
                    advance(tick)

        slot_sum = SlotSum(
            None,
            (None, half_ref) + tuple(slot_sums),
            (None, half_stat_ref) + tuple(slot_stats),
            slot_send,
            slot_recv,
            bits,
            partners,
        )
        half_pairs = PAIRS // 2
        lanes = half_pairs * LANES
        my_lanes = pl.ds(pl.multiple_of(core * lanes, LANES), lanes)

        def final_copies():
            theirs = pl.ds(pl.multiple_of((1 - core) * own, own), own)
            return (
                remote(
                    turned_ref.at[theirs],
                    go_land.at[:, my_lanes],
                    slot_send.at[4, 0],
                    slot_recv.at[4, 0],
                    partners["core"],
                ),
                remote(
                    gstat_land.at[core],
                    gstat_land.at[core],
                    slot_send.at[4, 1],
                    slot_recv.at[4, 1],
                    partners["core"],
                ),
            )

        def finish_slots():
            slot_sum.merge(3)
            for which in range(half_pairs):
                stat = slot_stats[1][which]
                total = stat[2:4]
                sums = slot_sums[1][which].astype(f32)
                mean = jnp.concatenate(
                    [sums[:HEAD_DIM] / total[0:1], sums[HEAD_DIM:] / total[1:2]], 0
                )
                turned_ref[:, which * LANES : (which + 1) * LANES] = mean.T.astype(bf16)
                whole = stat[0:2] + jnp.log(total)
                gstat_land[core, which] = jnp.concatenate(
                    [whole, jnp.zeros((6, GLOBALS), f32)], 0
                )
            mine = pl.ds(pl.multiple_of(core * own, own), own)
            go_land[:, my_lanes] = turned_ref[mine, :]
            for copy in final_copies():
                copy.start()

        def put_message():
            product = gdo_ref[...].astype(f32) * go_land[...].astype(f32)
            head_of = iota((width, LANES), 0) // HEAD_DIM == iota((width, LANES), 1)
            head_of = jnp.where(head_of, 1.0, 0.0).astype(bf16)
            first = product.astype(bf16)
            second = (product - first.astype(f32)).astype(bf16)
            centre = nn(first, head_of) + nn(second, head_of)
            lines = [gstat_land[half, which, 0:2] for half in (0, 1) for which in range(half_pairs)]
            lines = jnp.concatenate(lines + [jnp.zeros((LANES - HEADS, GLOBALS), f32)], 0)
            stat_ref[...] = lines.T
            total = stat_ref[pl.ds(pl.multiple_of(core * own, own), own), :]
            spread = jnp.zeros((own, LANES), f32)
            for number, value in enumerate((total, centre)):
                for piece in range(3):
                    low = value.astype(bf16)
                    value = value - low.astype(f32)
                    start_lane = (3 * number + piece) * HEADS
                    source_lane = iota((LANES, LANES), 0)
                    moved = iota((LANES, LANES), 1) == source_lane + start_lane
                    moved = jnp.where(moved & (source_lane < HEADS), 1.0, 0.0).astype(bf16)
                    spread = spread + nn(low, moved)
            mine = message_land.at[bits["z1"]]
            mine[:, :width] = gdo_ref[...]
            mine[:, width:] = spread.astype(bf16)
            message_copy().start()

        def message_copy():
            mine = message_land.at[bits["z1"]]
            return remote(mine, mine, message_send, message_recv, partners["z1"])

    else:

        def tick_at(position):
            pass

    if talk:
        batch = lax.axis_index("batch")
        seq_place = lax.axis_index("seq")
        places = lax.axis_size("seq")
        after = (batch, lax.rem(seq_place + 1, places))
        before = (batch, lax.rem(seq_place + places - 1, places))
        halo = remote(
            ct_ref.at[pl.ds(count - HALF, HALF)],
            cts_ref.at[pl.ds(0, HALF)],
            halo_send,
            halo_recv,
            after,
        )
    loads = [
        pltpu.make_async_copy(o_ref, os_ref.at[pl.ds(0, count)], load_sem.at[0]),
        pltpu.make_async_copy(
            ct_ref.at[pl.ds(0, count - HALF)],
            cts_ref.at[pl.ds(HALF, count - HALF)],
            load_sem.at[1],
        ),
    ]
    if not talk:
        loads.append(
            pltpu.make_async_copy(ct_head_ref, cts_ref.at[pl.ds(0, HALF)], load_sem.at[2])
        )

    def start(at, size, x, sums):
        y = x.astype(f32) + nn(os_ref[at, :], wo_ref[...])
        unit, unused = normalize_rows(y)
        h_ref[at, :] = (unit * norms_ref[4:5] + norms_ref[5:6]).astype(bf16)
        y_ref[at, :] = y
        sums[...] = y + join_rows(b2_ref)
        dh_ref[at, :] = jnp.zeros((size, width), f32)

    @pl.when(step == 0)
    def _():
        for load in loads:
            load.start()
        if talk:
            half_ref[...] = go_in_ref[...]
            half_stat_ref[...] = gstat_in_ref[...]
            meet([partners[name] for name in AXES] + [before, after])
            slot_sum.begin(2)
            halo.start()
        cts_ref[count:] = padded(gct_ref[...])
        loads[0].wait()

        def start_tile(i, carry):
            at = pl.ds(pl.multiple_of(i * tile, tile), tile)
            start(at, tile, x_ref[at, :], dy_ref.at[at])
            return carry

        lax.fori_loop(0, tiles, start_tile, 0)
        for load in loads[1:]:
            load.wait()

    @pl.when(step == 0)
    def _():
        row = join_rows(b1_ref)
        for number in range(b1s_ref.shape[0]):
            if talk:
                share = FF_CHUNK // seq_size
                starts = [place * b1s_ref.shape[0] * share for place in range(seq_size)]
                starts = [start + number * share for start in starts]
                b1s_ref[number : number + 1] = take_lanes(row, starts, share)
            else:
                b1s_ref[number : number + 1] = row[:, number * FF_CHUNK : (number + 1) * FF_CHUNK]

    my_row = pl.ds(step, 1)
    db1_ref[my_row, :] = jnp.zeros((1, FF_CHUNK), f32)
    w1 = w1_ref[...].reshape(width, width)
    w2 = w2_ref[...].reshape(width, width)

    def chunk_of(at, sums):
        u = nt(h_ref[at, :], w1) + b1s_ref[my_row, :]
        da = nt(cts_ref[at, :], w2)
        area, density = gelu_parts(u)
        a = (u * area).astype(bf16)
        du = (da * (area + u * density)).astype(bf16)
        a_ref[at, :] = a
        du_ref[at, :] = du
        db1_ref[my_row, :] += jnp.sum(du.astype(f32), axis=0, keepdims=True)
        sums[...] = sums[...] + nn(a, w2)
        dh_ref[at, :] = dh_ref[at, :] + nn(du, w1)

    for i in range(1, tiles):
        chunk_of(rows_at(i), dy_ref.at[rows_at(i)])

    if talk:

        @pl.when(step == 0)
        def _():
            slot_sum.merge(2)
            slot_sum.begin(3)
            halo.wait_recv()

    tick_at(0)
    chunk_of(rows_at(0), dy_ref.at[rows_at(0)])

    @pl.when(step == 0)
    def _():
        if talk:
            finish_slots()
            halo.wait_send()
        dft_ref[...] = cts_ref[...].T
        if talk:
            for copy in final_copies():
                copy.wait_recv()
            os_ref[count:] = padded(go_land[...])
        else:
            os_ref[count:] = padded(go_in_ref[...])
        start(tail, extra, padded(gx_ref[...]), z_sum_ref)

    chunk_of(tail, z_sum_ref)
    tick_at(1)
    dw1 = tn(du_ref[...], h_ref[...])
    dw2 = nn(dft_ref[...], a_ref[...])
    if talk:
        for number in range(chunks):

            @pl.when(step == number)
            def _():
                for which, value in ((0, dw1), (1, dw2)):
                    unit = 2 * number + which
                    if unit >= slots:
                        engine.sent(unit - slots, 0)
                    put_unit(units_ref.at[unit % slots], value)

        @pl.when(step == chunks)
        def _():
            put_unit(second_ref.at[0], dw1)
            put_unit(second_ref.at[1], dw2)

        tick_at(2)
        for number in range(chunks):

            @pl.when(step == number)
            def _():
                engine.begin(2 * number)
                engine.begin(2 * number + 1)

    else:
        first_ref[...] = dw1.astype(bf16)
        second_ref[...] = dw2.astype(bf16)

    @pl.when(step == steps - 1)
    def _():
        db2_ref[...] = jnp.zeros_like(db2_ref)
        dgain_ref[...] = jnp.zeros_like(dgain_ref)
        doffset_ref[...] = jnp.zeros_like(doffset_ref)

        def finish(at, size, sums, put):
            z = sums[...].astype(bf16)
            unit, scale = normalize_rows(y_ref[at, :])
            dh = dh_ref[at, :]
            ct = cts_ref[at, :].astype(f32)
            dy = ct + norm_back(unit, scale, norms_ref[4:5], dh)
            db2_ref[...] += jnp.sum(ct, axis=0, keepdims=True)
            doffset_ref[...] += jnp.sum(dh, axis=0, keepdims=True)
            dgain_ref[...] += jnp.sum(dh * unit, axis=0, keepdims=True)
            low = dy.astype(bf16)
            h_ref[at, :] = low
            put(z, dy, nt(low, wo_ref[...]).astype(bf16))

        def finish_tile(i, carry):
            at = pl.ds(pl.multiple_of(i * tile, tile), tile)

            def put(z, dy, do):
                z_ref[at, :] = z
                dy_ref[at, :] = dy
                do_ref[at, :] = do

            finish(at, tile, dy_ref.at[at], put)
            return carry

        def put_tail(z, dy, do):
            gz_ref[...] = z[:own]
            gdy_ref[...] = dy[:own]
            gdo_ref[...] = do[:own]

        finish(tail, extra, z_sum_ref, put_tail)
        if talk:
            put_message()
            advance(TICKS * chunks)
        lax.fori_loop(0, tiles, finish_tile, 0)
        dwo = tn(h_ref[...], os_ref[...])
        if talk:
            put_grouped(dwo_ref, dwo)
            advance(TICKS * chunks + 1)
            rest_ref[...] = landings[1][2 * chunks - 2 :]
            z_head_ref[...] = z_ref[:HALF]
            for when, chunk, stage in plan:
                for unit in (2 * chunk, 2 * chunk + 1):
                    if stage > 0 or unit + slots >= 2 * chunks:
                        engine.sent(unit, stage)
            slot_sum.sent(2)
            slot_sum.sent(3)
            for copy in final_copies():
                copy.wait_send()
            message_copy().wait_recv()
            message_ref[...] = message_land[...]
            message_copy().wait_send()
        else:
            dwo_ref[...] = dwo.astype(bf16)


def branch(grid_of, x, o, ct, ct_head, gx, go, gstat, gct, wo, w1t, b1, w2, b2, norms):
    count, width = x.shape
    own = gx.shape[0]
    hidden = w2.shape[0]
    steps = hidden // FF_CHUNK
    total = count + -(-own // LANES) * LANES
    row = once((count, width))
    few = once((own, width))
    line = full((1, width))
    anywhere = pl.BlockSpec(memory_space=pl.ANY)
    scratch = []
    more = {}
    if grid_of is None:
        weight_spec = pl.BlockSpec((FF_CHUNK, width), lambda j: (j, 0))
        dw_shapes = [(hidden, width), (width, hidden)]
        dw_types = [bf16, bf16]
        dw_specs = [weight_spec, pl.BlockSpec((width, FF_CHUNK), lambda j: (0, j))]
        dwo_shape = (width, width)
    else:
        seq, batch = grid_of
        rows, lanes = width // seq, width // batch
        weight_spec = pl.BlockSpec((seq, 1, rows, width), lambda j: (0, j, 0, 0))
        w1t = w1t.reshape(seq, steps, rows, width)
        w2 = w2.reshape(seq, steps, rows, width)
        units = 2 * (steps - 1)
        sums, stats = go.shape[2:], gstat.shape[2:]
        dw_shapes = [
            ((units - 2) * rows, lanes),
            (2, 2, 2, 2, 2, batch, rows, lanes),
            (2, own, width + LANES),
            (2, 2, 2, 2, rows, lanes),
            (HALF, width),
        ]
        dw_types = [f32, bf16, bf16, bf16, bf16]
        dw_specs = [once(shape) for shape in dw_shapes]
        dwo_shape = (seq, batch, rows, lanes)
        dma = pltpu.SemaphoreType.DMA
        scratch = (
            [pltpu.VMEM((4,) + dw_shapes[1][1:], bf16)]
            + sum_scratch(units, rows, lanes, False)
            + [
                pltpu.VMEM(go.shape, bf16),
                pltpu.VMEM(gstat.shape, f32),
                pltpu.VMEM((2,) + sums, bf16),
                pltpu.VMEM(sums, bf16),
                pltpu.VMEM((2,) + stats, f32),
                pltpu.VMEM(stats, f32),
                pltpu.VMEM((GLOBALS, PAIRS // 2 * LANES), bf16),
                pltpu.VMEM((own, width), bf16),
                pltpu.VMEM((2,) + stats, f32),
                pltpu.VMEM((GLOBALS, LANES), f32),
                dma((5, 2)),
                dma((5, 2)),
                pltpu.VMEM((2, own, width + LANES), bf16),
                dma,
                dma,
                dma,
                dma,
            ]
        )
        more = {"collective_id": 3, "has_side_effects": True}
    out = pl.pallas_call(
        functools.partial(branch_kernel, BLOCK, grid_of[0] if grid_of else 0),
        grid=(steps,),
        in_specs=[
            row,
            anywhere,
            anywhere,
            anywhere,
            few,
            once(go.shape),
            once(gstat.shape),
            few,
            once((width, width)),
            weight_spec,
            full(b1.shape),
            weight_spec,
            full(b2.shape),
            full(norms.shape),
        ],
        out_specs=[row, row, row, few, few, few]
        + [once(dwo_shape), full((steps, FF_CHUNK)), line, line, line]
        + dw_specs,
        out_shape=[
            jax.ShapeDtypeStruct((count, width), bf16),
            jax.ShapeDtypeStruct((count, width), f32),
            jax.ShapeDtypeStruct((count, width), bf16),
            jax.ShapeDtypeStruct((own, width), bf16),
            jax.ShapeDtypeStruct((own, width), f32),
            jax.ShapeDtypeStruct((own, width), bf16),
            jax.ShapeDtypeStruct(dwo_shape, bf16),
            jax.ShapeDtypeStruct((steps, FF_CHUNK), f32),
            jax.ShapeDtypeStruct((1, width), f32),
            jax.ShapeDtypeStruct((1, width), f32),
            jax.ShapeDtypeStruct((1, width), f32),
        ]
        + [jax.ShapeDtypeStruct(shape, kind) for shape, kind in zip(dw_shapes, dw_types)],
        scratch_shapes=[
            pltpu.VMEM((total, width), bf16),
            pltpu.VMEM((total, width), bf16),
            pltpu.VMEM((total, width), f32),
            pltpu.VMEM((total, width), bf16),
            pltpu.VMEM((total - count, width), f32),
            pltpu.VMEM((total, width), f32),
            pltpu.VMEM((width, total), bf16),
            pltpu.VMEM((total, FF_CHUNK), bf16),
            pltpu.VMEM((total, FF_CHUNK), bf16),
            pltpu.SemaphoreType.DMA((3,)),
            pltpu.VMEM((steps, FF_CHUNK), f32),
        ]
        + scratch,
        compiler_params=params(**more),
        cost_estimate=pl.CostEstimate(
            flops=6 * total * width * (2 * hidden + width),
            bytes_accessed=8 * width * hidden + 16 * total * width,
            transcendentals=2 * total * hidden,
        ),
        name="branch",
    )(x, o, ct, ct_head, gx, go, gstat, gct, wo, w1t, b1, w2, b2, norms)
    return out


def local_backward_kernel(
    talk,
    rows_count,
    group_rows,
    lengths,
    bucket_of,
    place,
    q_ref,
    k_ref,
    v_ref,
    do_ref,
    o_ref,
    line_ref,
    *refs,
):
    if talk:
        message_ref, rest_ref, last_ref, dwo_ref = refs[:4]
        refs = refs[4:]
    dq_ref, dk_ref, dv_ref, centre_ref = refs[:4]
    refs = refs[4:]
    if talk:
        everyone_ref, sums_ref, rest_out_ref = refs[:3]
        refs = refs[3:]
    edges, query_columns, key_columns = refs[:3]
    pair = pl.program_id(0)
    block = pl.program_id(1)
    blocks = rows_count // BLOCK
    step = pair * blocks + block

    @pl.when(step == 0)
    def _():
        read_edges(lengths, bucket_of, place, edges)

    if talk:
        all_ref, gather_send, gather_recv, own_ref = refs[3:7]
        landings = refs[7:12]
        send_sem, recv_sem, own_sem = refs[12:]
        bits, partners = my_place()
        gather = RowGather(all_ref, 3 * LANES, gather_send, gather_recv, bits, partners)
        engine = HalvingSum(
            (X_FIRST, Y_FIRST) * 2 + (X_FIRST,),
            [
                None,
                None,
                lambda side: last_ref.at[0, :, :, :, side],
                lambda side: last_ref.at[1, :, :, :, side],
                lambda side: dwo_ref.at[:, :, :, side],
            ],
            landings,
            own_ref,
            send_sem,
            recv_sem,
            own_sem,
            put_rows(sums_ref, landings[4].shape[1]),
            bits,
            partners,
        )
        plan = {
            3: [(2, 0), (3, 0), (4, 0)],
            5: [(0, 2), (1, 2)],
            8: [(0, 3), (1, 3)],
            11: [(0, 4), (1, 4), (2, 1), (3, 1), (4, 1)],
        }
        gather_plan = {4: 1, 8: 2, 10: 3}

        @pl.when(step == 0)
        def _():
            all_ref[:, bits["z0"], bits["y"], bits["core"]] = message_ref[...]
            landings[1][:2] = rest_ref[...]
            meet([partners[name] for name in AXES])
            gather.begin(1)
            for unit in (0, 1):
                engine.copy(unit, 2).start()
            for unit in (2, 3, 4):
                engine.begin(unit)

        for number in range(PAIRS * blocks):
            if number in plan or number in gather_plan:

                @pl.when(step == number)
                def _():
                    if number in gather_plan:
                        gather.advance(gather_plan[number])
                    for unit, stage in plan.get(number, ()):
                        engine.advance(unit, stage, stop=unit > 1 and stage == 1)

    block_columns(
        place, edges, rows_count, group_rows, block, step, blocks, query_columns, key_columns
    )
    extra = query_columns[block]
    upstream = do_ref[...]
    product = upstream.astype(f32) * o_ref[...].astype(f32)
    first = product.astype(bf16)
    second = (product - first.astype(f32)).astype(bf16)
    head = jnp.where(iota((8, LANES), 1) // HEAD_DIM == iota((8, LANES), 0), 1.0, 0.0).astype(bf16)
    by_head = nt(head, first) + nt(head, second)
    centre = jnp.concatenate([by_head[0:1], by_head[1:2]], axis=1)
    centre_ref[0, 0] = jnp.broadcast_to(centre, (8, 2 * BLOCK))
    queries = stack_pair(q_ref[...])
    grads = stack_pair(upstream)
    keys = k_ref[...]
    score = nt(
        jnp.concatenate([keys, key_columns[block]], 1),
        jnp.concatenate([queries, jnp.concatenate([extra, extra], 0)], 1),
    )
    weights = jnp.exp(score - line_ref[0, 0, 0:1])
    along = nt(v_ref[...], grads) - centre
    score_grad = (weights * along).astype(bf16)
    dv_ref[...] = nn(weights.astype(bf16), grads).astype(bf16)
    dk_ref[...] = nn(score_grad, queries).astype(bf16)
    low, high = side_by_side(tn(keys, score_grad))
    dq_ref[:HEAD_DIM] = low.astype(bf16)
    dq_ref[HEAD_DIM:] = high.astype(bf16)

    if talk:

        @pl.when(step == PAIRS * blocks - 1)
        def _():
            everyone_ref[...] = all_ref[...].reshape(everyone_ref.shape)
            gather.end(1)
            rest_out_ref[...] = landings[1][2:]
            for entries in plan.values():
                for unit, stage in entries:
                    engine.sent(unit, stage)


def local_backward(
    talk, scalars, rows_count, group_rows, q, k, v, do, o, line, message, rest, last, dwo
):
    blocks = rows_count // BLOCK
    width = q.shape[1]
    block_spec = pl.BlockSpec((BLOCK, LANES), lambda p, b, *unused: (b, p))
    operands = [q, k, v, do, o, line]
    in_specs = [block_spec] * 5 + [line_spec()]
    out_specs = (
        [pl.BlockSpec((LANES, BLOCK), lambda p, b, *unused: (p, b))]
        + [block_spec] * 2
        + [line_spec()]
    )
    out_shape = [
        jax.ShapeDtypeStruct((width, rows_count), bf16),
        jax.ShapeDtypeStruct((rows_count, width), bf16),
        jax.ShapeDtypeStruct((rows_count, width), bf16),
        jax.ShapeDtypeStruct((PAIRS, blocks, 8, 2 * BLOCK), f32),
    ]
    scratch = column_scratch(blocks)
    more = {}
    if talk:
        unused, own, wide = message.shape
        rows, lanes = last.shape[-2:]
        units = 5
        operands += [message, rest, last, dwo.reshape(last.shape[1:])]
        in_specs += [full(message.shape), once(rest.shape)]
        in_specs += [pl.BlockSpec(memory_space=pl.ANY)] * 2
        everyone = (16 * own, wide)
        rest_out = (units - 2,) + rest.shape[1:]
        out_specs += [once(everyone), once((2 * rows, lanes)), once(rest_out)]
        out_shape += [
            jax.ShapeDtypeStruct(everyone, bf16),
            jax.ShapeDtypeStruct((2 * rows, lanes), f32),
            jax.ShapeDtypeStruct(rest_out, bf16),
        ]
        dma = pltpu.SemaphoreType.DMA
        scratch += [pltpu.VMEM((2, 2, 2, 2, own, wide), bf16), dma((4, 2)), dma((4, 2))]
        scratch += sum_scratch(units, rows, lanes, True)
        more = {"collective_id": 4, "has_side_effects": True}
    return pl.pallas_call(
        functools.partial(local_backward_kernel, talk, rows_count, group_rows),
        grid_spec=pltpu.PrefetchScalarGridSpec(
            num_scalar_prefetch=3,
            grid=(PAIRS, blocks),
            in_specs=in_specs,
            out_specs=out_specs,
            scratch_shapes=scratch,
        ),
        out_shape=out_shape,
        compiler_params=params(**more),
        cost_estimate=pl.CostEstimate(
            flops=40 * rows_count * BLOCK * width,
            bytes_accessed=30 * rows_count * width,
            transcendentals=HEADS * rows_count * BLOCK,
        ),
        name="local_backward",
    )(*scalars, *operands)


def slot_backward_kernel(
    grouped,
    rows_count,
    group_rows,
    lengths,
    bucket_of,
    place,
    q_ref,
    k_ref,
    v_ref,
    do_ref,
    line_ref,
    centre_ref,
    dqt_ref,
    dk_in_ref,
    dv_in_ref,
    gq_ref,
    gk_ref,
    gv_ref,
    gdo_ref,
    gstat_ref,
    gx_in,
    gh_in,
    h_in,
    wq_ref,
    wk_ref,
    wv_ref,
    dq_ref,
    dk_ref,
    dv_ref,
    dw_ref,
    dgh_ref,
    dnorm_ref,
    edges,
    query_columns,
    key_columns,
    keys_ref,
    queries_ref,
    grads_ref,
    dqt_sum,
    dk_sum,
    dv_sum,
    dgqt_sum,
    dgk_sum,
    dgv_sum,
    lines_ref,
    dw_sum,
    dgh_sum,
    rows_ref,
    gx_ref,
    gh_ref,
    h_ref,
    load_sem,
):
    group = pl.program_id(0)
    block = pl.program_id(1)
    blocks = rows_count // BLOCK
    step = group * blocks + block
    together = range(TOGETHER)

    def lanes_of(which):
        return pl.ds(which * LANES, LANES)

    loads = [
        pltpu.make_async_copy(source, target, load_sem.at[number])
        for number, (source, target) in enumerate(
            ((gx_in, gx_ref), (gh_in, gh_ref), (h_in, h_ref))
        )
    ]

    @pl.when(step == 0)
    def _():
        for load in loads:
            load.start()
        read_edges(lengths, bucket_of, place, edges)

        def turn(slot, carry):
            at = pl.ds(pl.multiple_of(slot * GLOBALS, GLOBALS), GLOBALS)
            lines_ref[slot] = gstat_ref[at, :].astype(f32).T
            return carry

        lax.fori_loop(0, SLOTS, turn, 0)
        dgh_sum[...] = jnp.zeros_like(dgh_sum)
        dnorm_ref[...] = jnp.zeros_like(dnorm_ref)

    @pl.when(block == 0)
    def _():
        dgqt_sum[...] = jnp.zeros_like(dgqt_sum)
        dgk_sum[...] = jnp.zeros_like(dgk_sum)
        dgv_sum[...] = jnp.zeros_like(dgv_sum)

    block_columns(
        place, edges, rows_count, group_rows, block, step, blocks, query_columns, key_columns
    )
    extra = query_columns[block]
    for which in together:
        lanes = lanes_of(which)
        keys_ref[which, :, :LANES] = k_ref[:, lanes]
        keys_ref[which, :, LANES:] = key_columns[block]
        queries_ref[which, :, :LANES] = stack_pair(q_ref[:, lanes])
        queries_ref[which, :BLOCK, LANES:] = extra
        queries_ref[which, BLOCK:, LANES:] = extra
        grads_ref[which] = stack_pair(do_ref[:, lanes])
    dqt_sum[...] = dqt_ref[...].astype(f32)
    dk_sum[...] = dk_in_ref[...].astype(f32)
    dv_sum[...] = dv_in_ref[...].astype(f32)

    def line_of(slot, which, first):
        halves = []
        for head in range(2):
            spot = first + 2 * (group * TOGETHER + which) + head
            halves.append(
                lines_ref[slot, pl.ds(spot, 1)]
                + lines_ref[slot, pl.ds(spot + HEADS, 1)]
                + lines_ref[slot, pl.ds(spot + 2 * HEADS, 1)]
            )
        return jnp.concatenate(halves, axis=1)

    def from_global(slot, which, keys, values):
        at = pl.ds(pl.multiple_of(slot * GLOBALS, GLOBALS), GLOBALS)
        extra = global_query_extra(slot).astype(bf16)
        queries = stack_pair(gq_ref[at, lanes_of(which)])
        grads = stack_pair(gdo_ref[at, lanes_of(which)])
        score = nt(keys, jnp.concatenate([queries, jnp.concatenate([extra, extra], 0)], 1))
        weights = jnp.exp(score - line_of(slot, which, 0))
        along = nt(values, grads) - line_of(slot, which, 3 * HEADS)
        score_grad = (weights * along).astype(bf16)
        low, high = side_by_side(tn(keys[:, :LANES], score_grad))
        dgqt_sum[which, slot, :HEAD_DIM] += low
        dgqt_sum[which, slot, HEAD_DIM:] += high
        return nn(score_grad, queries), nn(weights.astype(bf16), grads)

    def one_slot(slot, carry):
        @pl.when(slot_present(slot, place, edges, rows_count, group_rows, block))
        def _():
            at = pl.ds(pl.multiple_of(slot * GLOBALS, GLOBALS), GLOBALS)
            columns = global_key_extra(slot).astype(bf16)
            for which in together:
                lanes = lanes_of(which)
                key_grad, value_grad = from_global(slot, which, keys_ref[which], v_ref[:, lanes])
                dk_sum[:, lanes] += key_grad
                dv_sum[:, lanes] += value_grad
                keys = gk_ref[at, lanes]
                grads = grads_ref[which]
                score = nt(jnp.concatenate([keys, columns], 1), queries_ref[which])
                weights = jnp.exp(score - line_ref[which, 0, 0:1])
                along = nt(gv_ref[at, lanes], grads) - centre_ref[which, 0, 0:1]
                score_grad = (weights * along).astype(bf16)
                dgv_sum[at, lanes] += nn(weights.astype(bf16), grads)
                dgk_sum[at, lanes] += nn(score_grad, queries_ref[which, :, :LANES])
                low, high = side_by_side(tn(keys, score_grad))
                dqt_sum[pl.ds(which * LANES, HEAD_DIM)] += low
                dqt_sum[pl.ds(which * LANES + HEAD_DIM, HEAD_DIM)] += high

        return carry

    lax.fori_loop(0, SLOTS, one_slot, 0)
    here = pl.ds(pl.multiple_of(block * BLOCK, BLOCK), BLOCK)
    for index, (ref, value) in enumerate(
        ((dq_ref, dqt_sum[...].T), (dk_ref, dk_sum[...]), (dv_ref, dv_sum[...]))
    ):
        low = value.astype(bf16)
        ref[...] = low
        rows_ref[index, here, :] = low

    @pl.when(step == blocks - 1)
    def _():
        for load in loads:
            load.wait()

    @pl.when((block == blocks - 1) & (place[2] >= 0))
    def _():
        slot = place[2]
        at = pl.ds(pl.multiple_of(slot * GLOBALS, GLOBALS), GLOBALS)
        columns = global_key_extra(slot).astype(bf16)
        for which in together:
            lanes = lanes_of(which)
            keys = jnp.concatenate([gk_ref[at, lanes], columns], axis=1)
            key_grad, value_grad = from_global(slot, which, keys, gv_ref[at, lanes])
            dgk_sum[at, lanes] += key_grad
            dgv_sum[at, lanes] += value_grad

    @pl.when(block == blocks - 1)
    def _():
        for index in range(3):
            local = tn(rows_ref[index], h_ref[...])
            dw_sum[index] = local * query_scale if index == 0 else local

        def through(slot, carry):
            needed = slot == place[2]
            for number in range(blocks):
                needed = needed | slot_present(
                    slot, place, edges, rows_count, group_rows, number
                )

            @pl.when(needed)
            def _():
                at = pl.ds(pl.multiple_of(slot * GLOBALS, GLOBALS), GLOBALS)
                grads = (
                    (
                        jnp.concatenate([dgqt_sum[which, slot].T for which in together], 1)
                        * query_scale
                    ).astype(bf16),
                    dgk_sum[at, :].astype(bf16),
                    dgv_sum[at, :].astype(bf16),
                )
                rows = gh_ref[at, :]
                total = dgh_sum[at, :]
                for index, weight in enumerate((wq_ref, wk_ref, wv_ref)):
                    total = total + nt(grads[index], weight[...])
                dgh_sum[at, :] = total

                for index in range(3):
                    dw_sum[index] += tn(grads[index], rows)

                @pl.when(group == PAIRS // TOGETHER - 1)
                def _():
                    unit, unused = normalize_rows(gx_ref[at, :].astype(f32))
                    dnorm_ref[0:1] += jnp.sum(total * unit, axis=0, keepdims=True)
                    dnorm_ref[1:2] += jnp.sum(total, axis=0, keepdims=True)

            return carry

        lax.fori_loop(0, SLOTS, through, 0)
        if grouped:
            for index in range(3):
                put_grouped(dw_ref.at[index], dw_sum[index])
        else:
            dw_ref[...] = dw_sum[...].astype(bf16)

    @pl.when(step == PAIRS // TOGETHER * blocks - 1)
    def _():
        dgh_ref[...] = dgh_sum[...].astype(bf16)


def slot_backward(
    grid_of,
    scalars,
    rows_count,
    group_rows,
    q,
    k,
    v,
    do,
    line,
    centre,
    dqt,
    dk,
    dv,
    gq,
    gk,
    gv,
    everyone,
    gx,
    gh,
    h,
    wq,
    wk,
    wv,
):
    blocks = rows_count // BLOCK
    all_globals, width = gk.shape
    block_spec = pl.BlockSpec((BLOCK, TOGETHER * LANES), lambda p, b, *unused: (b, p))
    pair_spec = pl.BlockSpec((all_globals, TOGETHER * LANES), lambda p, b, *unused: (0, p))
    local = jax.ShapeDtypeStruct((rows_count, width), bf16)
    glob = jax.ShapeDtypeStruct((all_globals, width), bf16)
    if grid_of is None:
        dw_shape = (3, width, width)
        dw_spec = pl.BlockSpec((3, TOGETHER * LANES, width), lambda p, b, *unused: (0, p, 0))
    else:
        seq, batch = grid_of
        piece = (batch, width // seq, width // batch)
        dw_shape = (3, seq) + piece
        share = TOGETHER * LANES // piece[1]
        dw_spec = pl.BlockSpec((3, share) + piece, lambda p, b, *unused: (0, p, 0, 0, 0))
    return pl.pallas_call(
        functools.partial(slot_backward_kernel, grid_of is not None, rows_count, group_rows),
        grid_spec=pltpu.PrefetchScalarGridSpec(
            num_scalar_prefetch=3,
            grid=(PAIRS // TOGETHER, blocks),
            in_specs=[block_spec] * 4
            + [line_spec(TOGETHER)] * 2
            + [pl.BlockSpec((TOGETHER * LANES, BLOCK), lambda p, b, *unused: (p, b))]
            + [block_spec] * 2
            + [pair_spec] * 4
            + [pl.BlockSpec((all_globals, LANES), lambda p, b, *unused: (0, PAIRS))]
            + [pl.BlockSpec(memory_space=pl.ANY)] * 3
            + [pl.BlockSpec((width, TOGETHER * LANES), lambda p, b, *unused: (0, p))] * 3,
            out_specs=[block_spec] * 3
            + [
                dw_spec,
                once((all_globals, width)),
                full((8, width)),
            ],
            scratch_shapes=column_scratch(blocks)
            + [
                pltpu.VMEM((TOGETHER, BLOCK, 2 * LANES), bf16),
                pltpu.VMEM((TOGETHER, 2 * BLOCK, 2 * LANES), bf16),
                pltpu.VMEM((TOGETHER, 2 * BLOCK, LANES), bf16),
                pltpu.VMEM((TOGETHER * LANES, BLOCK), f32),
                pltpu.VMEM((BLOCK, TOGETHER * LANES), f32),
                pltpu.VMEM((BLOCK, TOGETHER * LANES), f32),
                pltpu.VMEM((TOGETHER, SLOTS, LANES, GLOBALS), f32),
                pltpu.VMEM((all_globals, TOGETHER * LANES), f32),
                pltpu.VMEM((all_globals, TOGETHER * LANES), f32),
                pltpu.VMEM((SLOTS, LANES, GLOBALS), f32),
                pltpu.VMEM((3, TOGETHER * LANES, width), f32),
                pltpu.VMEM((all_globals, width), f32),
                pltpu.VMEM((3, rows_count, TOGETHER * LANES), bf16),
                pltpu.VMEM((all_globals, width), bf16),
                pltpu.VMEM((all_globals, width), bf16),
                pltpu.VMEM((rows_count, width), bf16),
                pltpu.SemaphoreType.DMA((3,)),
            ],
        ),
        out_shape=[local] * 3
        + [
            jax.ShapeDtypeStruct(dw_shape, bf16),
            glob,
            jax.ShapeDtypeStruct((8, width), f32),
        ],
        compiler_params=params(),
        cost_estimate=pl.CostEstimate(
            flops=80 * rows_count * GLOBALS * width,
            bytes_accessed=40 * rows_count * width,
            transcendentals=2 * HEADS * rows_count * GLOBALS,
        ),
        name="slot_backward",
    )(
        *scalars,
        q,
        k,
        v,
        do,
        line,
        centre,
        dqt,
        dk,
        dv,
        gq,
        gk,
        gv,
        everyone,
        everyone,
        gx,
        gh,
        h,
        wq,
        wk,
        wv,
    )


def project_back_kernel(
    tile,
    x_ref,
    dy_ref,
    dq_ref,
    dk_ref,
    dv_ref,
    wq_ref,
    wk_ref,
    wv_ref,
    gain_ref,
    dx_ref,
    dnorm_ref,
):
    count, width = x_ref.shape
    dnorm_ref[...] = jnp.zeros_like(dnorm_ref)

    def one_tile(i, carry):
        at = pl.ds(pl.multiple_of(i * tile, tile), tile)
        dh = (
            nt(dq_ref[at, :], wq_ref[...]) * query_scale
            + nt(dk_ref[at, :], wk_ref[...])
            + nt(dv_ref[at, :], wv_ref[...])
        )
        unit, scale = normalize_rows(x_ref[at, :].astype(f32))
        dnorm_ref[0:1] += jnp.sum(dh * unit, axis=0, keepdims=True)
        dnorm_ref[1:2] += jnp.sum(dh, axis=0, keepdims=True)
        dx_ref[at, :] = dy_ref[at, :] + norm_back(unit, scale, gain_ref[...], dh)
        return carry

    lax.fori_loop(0, count // tile, one_tile, 0)


def project_back(x, dy, dq, dk, dv, wq, wk, wv, gain):
    count, width = x.shape
    vmem = pl.BlockSpec(memory_space=pltpu.VMEM)
    return pl.pallas_call(
        functools.partial(project_back_kernel, BLOCK),
        in_specs=[vmem] * 9,
        out_specs=[vmem] * 2,
        out_shape=[
            jax.ShapeDtypeStruct((count, width), f32),
            jax.ShapeDtypeStruct((8, width), f32),
        ],
        compiler_params=params(),
        cost_estimate=pl.CostEstimate(
            flops=12 * count * width * width, bytes_accessed=30 * count * width, transcendentals=0
        ),
        name="project_back",
    )(x, dy, dq, dk, dv, wq, wk, wv, gain)


def finish_kernel(
    rest_ref,
    x_in,
    dy_in,
    dq_in,
    dk_in,
    dv_in,
    dqkv_ref,
    dgh_ref,
    wq_in,
    wk_in,
    wv_in,
    db1_ref,
    db2_ref,
    dnorm_global_ref,
    dgain2_ref,
    doffset2_ref,
    gx_ref,
    gdy_ref,
    norms_ref,
    out_ref,
    small_out_ref,
    grad_out_ref,
    token_ref,
    halo_dx_out,
    x_ref,
    dy_ref,
    dq_ref,
    dk_ref,
    dv_ref,
    wq_ref,
    wk_ref,
    wv_ref,
    load_sem,
    own_ref,
    one_ref,
    two_ref,
    three_ref,
    four_ref,
    five_ref,
    send_sem,
    recv_sem,
    own_sem,
    gown_ref,
    gone_ref,
    gtwo_ref,
    gthree_ref,
    gfour_ref,
    gsend_sem,
    grecv_sem,
    gown_sem,
    sums_ref,
    here_ref,
    ssend_sem,
    srecv_sem,
    halo_out,
    halo_dx,
    halo_send,
    halo_recv,
    dnorm_ref,
    dgh_sum_ref,
):
    bits, partners = my_place()
    count, width = x_ref.shape
    came = rest_ref.shape[0]
    units = came + 3
    batch = lax.axis_index("batch")
    seq = lax.axis_index("seq")
    places = lax.axis_size("seq")
    after = (batch, lax.rem(seq + 1, places))
    before = (batch, lax.rem(seq + places - 1, places))

    pairs = [
        (dq_in, dq_ref),
        (dk_in, dk_ref),
        (dv_in, dv_ref),
        (wq_in, wq_ref),
        (wk_in, wk_ref),
        (wv_in, wv_ref),
        (x_in, x_ref),
        (dy_in, dy_ref),
    ]
    loads = [
        pltpu.make_async_copy(source, target, load_sem.at[number])
        for number, (source, target) in enumerate(pairs)
    ]
    def source(unit):
        return lambda side: dqkv_ref.at[unit - came, :, :, :, side]

    engine = HalvingSum(
        (X_Z_FIRST, Y_FIRST, X_FIRST, X_FIRST, Y_FIRST, Z_FIRST),
        [source(unit) for unit in range(units)],
        (one_ref, two_ref, three_ref, four_ref, five_ref),
        own_ref,
        send_sem,
        recv_sem,
        own_sem,
        put_rows(out_ref, five_ref.shape[1]),
        bits,
        partners,
    )
    wide = gone_ref.shape[-1]

    def row_source(unit):
        lanes = pl.ds(unit * wide, wide)
        return lambda side: dgh_ref.at[:, :, :, side, :, lanes]

    def put_dgh(unit, value):
        dgh_sum_ref[:, unit * wide : (unit + 1) * wide] = value

    row_sum = HalvingSum(
        (("core", "y", "z0", "z1"), ("core", "z0", "y", "z1")),
        [row_source(unit) for unit in range(2)],
        (gone_ref, gtwo_ref, gthree_ref, gfour_ref),
        gown_ref,
        gsend_sem,
        grecv_sem,
        gown_sem,
        put_dgh,
        bits,
        partners,
    )

    def rows_advance(stage):
        for unit in range(2):
            row_sum.advance(unit, stage)

    def scopy(stage):
        return remote(
            sums_ref.at[stage],
            here_ref.at[stage],
            ssend_sem.at[stage],
            srecv_sem.at[stage],
            partners[X_FIRST[stage]],
        )

    def small_advance(stage):
        scopy(stage).wait_recv()
        total = sums_ref[stage] + here_ref[stage]
        if stage < STAGES - 1:
            sums_ref[stage + 1] = total
            scopy(stage + 1).start()
        else:
            small_out_ref[...] = total

    halo = remote(halo_out, halo_dx, halo_send, halo_recv, before)
    two_ref[:came] = rest_ref[...]
    meet([partners[name] for name in AXES] + [before, after])
    for unit in range(came, units):
        engine.begin(unit)
    for load in loads:
        load.start()
    for unit in range(came):
        engine.copy(unit, 2).start()
    for unit in range(2):
        row_sum.begin(unit)
    for unit in range(came, units):
        engine.advance(unit, 0)
    for load in loads:
        load.wait()
    dnorm_ref[...] = jnp.zeros_like(dnorm_ref)

    def back(index):
        at = pl.ds(index * HALF, HALF)
        dh = (
            nt(dq_ref[at, :], wq_ref[...]) * query_scale
            + nt(dk_ref[at, :], wk_ref[...])
            + nt(dv_ref[at, :], wv_ref[...])
        )
        unit, scale = normalize_rows(x_ref[at, :].astype(f32))
        dnorm_ref[0:1] += jnp.sum(dh * unit, axis=0, keepdims=True)
        dnorm_ref[1:2] += jnp.sum(dh, axis=0, keepdims=True)
        dx = dy_ref[at, :] + norm_back(unit, scale, norms_ref[0:1], dh)
        if index == 0:
            halo_out[...] = dx.astype(bf16)
        else:
            token_ref[pl.ds((index - 1) * HALF, HALF), :] = dx

    for index in range(count // HALF):
        back(index)
        if index == 0:
            halo.start()
            rows_advance(0)
        if index == 2:
            for unit in range(came):
                engine.advance(unit, 2)

    hidden_rows = db1_ref.shape[0]
    parts = [
        db1_ref[...],
        db2_ref[...],
        dnorm_ref[0:2],
        dnorm_global_ref[0:2],
        dgain2_ref[...],
        doffset2_ref[...],
    ]
    filled = hidden_rows + 7
    parts.append(jnp.zeros((sums_ref.shape[1] - filled, width), f32))
    sums_ref[0] = jnp.concatenate(parts, 0)
    scopy(0).start()

    def weights_advance(stage):
        for unit in range(came, units):
            engine.advance(unit, stage)

    small_advance(0)
    rows_advance(1)
    weights_advance(1)
    for unit in range(came):
        engine.advance(unit, 3)
    small_advance(1)
    rows_advance(2)
    small_advance(2)
    weights_advance(2)
    small_advance(3)
    for unit in range(came):
        engine.advance(unit, 4)
    rows_advance(3)
    dgh = dgh_sum_ref[...]
    unit_rows, scale = normalize_rows(gx_ref[...].astype(f32))
    grad_out_ref[...] = gdy_ref[...] + norm_back(unit_rows, scale, norms_ref[2:3], dgh)
    small_advance(4)
    halo.wait_recv()
    halo_dx_out[...] = halo_dx[...]
    weights_advance(3)
    weights_advance(4)

    for unit in range(units):
        for stage in range(2 if unit < came else 0, STAGES):
            engine.sent(unit, stage)
    for stage in range(STAGES):
        scopy(stage).wait_send()
    for unit in range(2):
        for stage in range(4):
            row_sum.sent(unit, stage)
    halo.wait_send()


def finish_all(rest, x, dy, dq, dk, dv, dqkv, dgh, wq, wk, wv, small, gx, gdy, norms):
    count, width = x.shape
    rows, lanes = rest.shape[-2:]
    units = rest.shape[0] + 3
    own = gx.shape[0]
    place = (2, 2, 2, 2)
    small_rows = small[0].shape[0] + 7
    small_rows += -small_rows % 8
    anywhere = pl.BlockSpec(memory_space=pl.ANY)
    vmem = pl.BlockSpec(memory_space=pltpu.VMEM)
    dma = pltpu.SemaphoreType.DMA
    row = pltpu.VMEM((count, width), bf16)
    weight = pltpu.VMEM((width, width), bf16)
    half = pltpu.VMEM((HALF, width), bf16)
    return pl.pallas_call(
        finish_kernel,
        in_specs=[vmem] + [anywhere] * 10 + [vmem] * 8,
        out_specs=[vmem] * 5,
        out_shape=[
            jax.ShapeDtypeStruct((units * rows, lanes), f32),
            jax.ShapeDtypeStruct((small_rows, width), f32),
            jax.ShapeDtypeStruct((own, width), f32),
            jax.ShapeDtypeStruct((count - HALF, width), f32),
            jax.ShapeDtypeStruct((HALF, width), bf16),
        ],
        scratch_shapes=[
            row,
            pltpu.VMEM((count, width), f32),
            row,
            row,
            row,
            weight,
            weight,
            weight,
            dma((8,)),
        ]
        + sum_scratch(units, rows, lanes, True)
        + [
            pltpu.VMEM((2, 2, 2, 2, own, width // 2), bf16),
            pltpu.VMEM((2, 2, 2, 2, own, width // 2), bf16),
            pltpu.VMEM((2, 2, 2, own, width // 2), bf16),
            pltpu.VMEM((2, 2, own, width // 2), bf16),
            pltpu.VMEM((2, own, width // 2), bf16),
            dma((2, 4)),
            dma((2, 4)),
            dma((2,)),
            pltpu.VMEM((STAGES, small_rows, width), f32),
            pltpu.VMEM((STAGES, small_rows, width), f32),
            dma((STAGES,)),
            dma((STAGES,)),
            half,
            half,
            dma,
            dma,
            pltpu.VMEM((8, width), f32),
            pltpu.VMEM((own, width), f32),
        ],
        compiler_params=params(collective_id=0, has_side_effects=True),
        cost_estimate=pl.CostEstimate(
            flops=12 * count * width * width, bytes_accessed=30 * count * width, transcendentals=0
        ),
        name="finish_all",
    )(
        rest,
        x,
        dy,
        dq,
        dk,
        dv,
        dqkv.reshape((3,) + place + (2, rows, lanes)),
        dgh.reshape(place + (own, width)),
        wq,
        wk,
        wv,
        *small,
        gx,
        gdy,
        norms,
    )


def unpack_kernel(
    z_ref,
    halo_z_ref,
    dx_ref,
    halo_dx_ref,
    gz_ref,
    ggrad_ref,
    first_ref,
    second_ref,
    third_ref,
    small_ref,
    layer_ref,
    gz_out,
    token_ref,
    ggrad_out,
    wq_ref,
    wk_ref,
    wv_ref,
    wo_ref,
    w1_ref,
    w2_ref,
    b1_ref,
    b2_ref,
    norms_ref,
    turned_ref,
):
    step = pl.program_id(0)
    last = pl.num_programs(0) - 1

    @pl.when(step < last)
    def _():
        layer_ref[0] = z_ref[...]
        token_ref[0] = dx_ref[...]

    @pl.when(step == last)
    def _():
        layer_ref[0] = halo_z_ref[...]
        token_ref[0] = halo_dx_ref[...].astype(f32)

    rows = wq_ref.shape[0]

    @pl.when(step == 0)
    def _():
        gz_out[0] = gz_ref[...]
        ggrad_out[0] = ggrad_ref[...]
        for ref, unit in ((wo_ref, 2), (wq_ref, 3), (wk_ref, 4), (wv_ref, 5)):
            ref[...] = third_ref[unit * rows : (unit + 1) * rows]
        chunks = w1_ref.shape[0] // rows
        for chunk in range(chunks):
            for ref, unit in ((first_ref, chunk), (second_ref, chunk - 2), (third_ref, chunk - 3)):
                if 0 <= unit < ref.shape[0] // (2 * rows):
                    break
            start = 2 * unit * rows
            w1_ref[chunk * rows : (chunk + 1) * rows] = ref[start : start + rows]
            part = ref[start + rows : start + 2 * rows].T
            for place in range(part.shape[0] // rows):
                spot = (place * chunks + chunk) * rows
                turned_ref[spot : spot + rows, :] = part[place * rows : (place + 1) * rows, :]
        w2_ref[...] = turned_ref[...].T
        pieces_in_row = small_ref.shape[1] // LANES
        hidden_rows = b1_ref.shape[0] // pieces_in_row
        per_chunk = small_ref.shape[1] // rows
        natural = jnp.concatenate(
            [
                small_ref[chunk : chunk + 1, place * rows : (place + 1) * rows]
                for place in range(per_chunk)
                for chunk in range(hidden_rows)
            ],
            axis=1,
        )
        for piece in range(hidden_rows * pieces_in_row):
            b1_ref[piece : piece + 1] = natural[:, piece * LANES : (piece + 1) * LANES]
        for piece in range(pieces_in_row):
            b2_ref[piece : piece + 1] = small_ref[
                hidden_rows : hidden_rows + 1, piece * LANES : (piece + 1) * LANES
            ]
        norms_ref[...] = small_ref[hidden_rows + 1 : hidden_rows + 7]


def unpack(z, halo_z, dx, halo_dx, gz, ggrad, first, second, third, small, rows, hidden):
    count, width = z.shape
    own = gz.shape[0]
    lanes = first.shape[1]
    steps = count // HALF
    shapes = [
        ((1, count, width), bf16),
        ((1, own, width), bf16),
        ((1, count, width), f32),
        ((1, own, width), f32),
    ]
    shapes += [((rows, lanes), f32)] * 4
    shapes += [
        ((hidden // width * rows, lanes), f32),
        ((rows, hidden // width * lanes), f32),
        ((hidden // LANES, LANES), f32),
        ((width // LANES, LANES), f32),
        ((6, width), f32),
    ]
    tile = pl.BlockSpec((1, HALF, width), lambda i: (0, i, 0))
    return pl.pallas_call(
        unpack_kernel,
        grid=(steps,),
        in_specs=[
            pl.BlockSpec((HALF, width), lambda i: (jnp.minimum(i + 1, steps - 1), 0)),
            full(halo_z.shape),
            pl.BlockSpec((HALF, width), lambda i: (jnp.minimum(i, steps - 2), 0)),
            full(halo_dx.shape),
            full(gz.shape),
            full(ggrad.shape),
            full(first.shape),
            full(second.shape),
            full(third.shape),
            full(small.shape),
        ],
        out_specs=[
            tile if shape[1] == count else full(shape) for shape, unused in shapes
        ],
        out_shape=[jax.ShapeDtypeStruct(shape, kind) for shape, kind in shapes],
        scratch_shapes=[pltpu.VMEM((hidden // width * lanes, rows), f32)],
        compiler_params=params(),
        cost_estimate=pl.CostEstimate(
            flops=0, bytes_accessed=14 * count * width, transcendentals=0
        ),
        name="unpack",
    )(z, halo_z, dx, halo_dx, gz, ggrad, first, second, third, small)


def from_behind(value, axis, steps):
    count = lax.axis_size(axis)
    pairs = [(source, (source + steps) % count) for source in range(count)]
    return lax.ppermute(value, axis, pairs)


def pieces(value):
    first = lax.reduce_precision(value, 8, 7)
    second = lax.reduce_precision(value - first, 8, 7)
    return [first.astype(bf16), second.astype(bf16), (value - first - second).astype(bf16)]


def scatter_sum(value):
    half = lax.psum_scatter(value, "batch", scatter_dimension=1, tiled=True)
    part = lax.psum_scatter(half, "seq", scatter_dimension=0, tiled=True)
    return part.T.astype(f32)


def on_device(
    tokens,
    global_states,
    lengths,
    bucket_of,
    wq,
    wk,
    wv,
    wo,
    w1,
    b1,
    w2,
    b2,
    norm_params,
    cotangent,
    global_cotangent,
):
    rows = tokens.shape[1]
    width = tokens.shape[2]
    own = global_states.shape[1]
    seq_count = lax.axis_size("seq")
    seq_place = lax.axis_index("seq")
    group_rows = rows * seq_count
    own_start = seq_place * own
    first_of_slot = own_start % GLOBALS == 0
    place = jnp.stack(
        [
            lax.axis_index("batch"),
            seq_place,
            jnp.where(first_of_slot, own_start // GLOBALS, -1),
        ]
    ).astype(jnp.int32)
    scalars = (lengths, bucket_of, place)
    norms = [norm_params[i : i + 1] for i in range(6)]
    b2_rows = b2.reshape(-1, LANES)

    batch_count = lax.axis_size("batch")
    grid_of = None
    if seq_count == 16 and batch_count == 2 and 2 * own == GLOBALS and rows == 2 * BLOCK:
        grid_of = (seq_count, batch_count)

    if grid_of is None:
        arrived_tokens, arrived_grads = from_behind(
            (tokens[0, rows - HALF :], cotangent[0, rows - HALF :]), "seq", 1
        )
        x = jnp.concatenate([arrived_tokens, tokens[0, : rows - HALF]], 0)
        ct_head = arrived_grads
        all_states = lax.all_gather(global_states[0], "seq", axis=0, tiled=True)
        w1t = w1.T
        h, q, k, v = project_local(x, norms[0], norms[1], wq, wk, wv)
        gh, gq, gk, gv = project_global(
            scalars, rows, group_rows, all_states, norms[2], norms[3], wq, wk, wv
        )
    else:
        h, q, k, v, x, all_states, gh, gq, gk, gv, w1t = gather_project(
            tokens[0], global_states[0], w1, norm_params, wq, wk, wv
        )
        all_states, gh, gq, gk, gv = (
            value.reshape(-1, width) for value in (all_states, gh, gq, gk, gv)
        )
    far, far_stat, part, part_stat = slot_forward(scalars, rows, group_rows, q, k, v, gq, gk, gv)
    if grid_of is None:
        o, line = local_forward(
            False, scalars, rows, group_rows, q, k, v, far, far_stat, None, None
        )
        part_peak = part_stat[:, :, 0:2]
        peak = jnp.max(lax.all_gather(part_peak, "seq"), axis=0)
        factor = jnp.exp(part_peak - peak)
        scaled = part.reshape(SLOTS, PAIRS, 2, HEAD_DIM, GLOBALS).astype(f32) * factor[:, :, :, None]
        scaled = scaled.reshape(SLOTS, width, GLOBALS)
        scaled_total = (part_stat[:, :, 2:4] * factor).reshape(SLOTS, HEADS, GLOBALS)
        payload = jnp.concatenate(
            [scaled, scaled_total, jnp.zeros((SLOTS, 4, GLOBALS), f32)], 1
        ).transpose(0, 2, 1)
        sums = lax.psum_scatter(
            payload.astype(bf16).reshape(SLOTS * GLOBALS, -1), "seq", scatter_dimension=0, tiled=True
        ).astype(f32)
        own_total = sums[:, width : width + HEADS]
        all_peak = peak.reshape(SLOTS, HEADS, GLOBALS).transpose(0, 2, 1).reshape(-1, HEADS)
        own_peak = lax.dynamic_slice_in_dim(all_peak, own_start, own, 0)
        go = (
            (sums[:, :width].reshape(own, HEADS, HEAD_DIM) / own_total[:, :, None])
            .reshape(own, width)
            .astype(bf16)
        )
        gstat = own_peak + jnp.log(own_total)
    else:
        o, line, half_sum, half_stat = local_forward(
            True, scalars, rows, group_rows, q, k, v, far, far_stat, part, part_stat
        )

    z, dy, do, gz, gdy, gdo, dwo, db1, db2, dgain2, doffset2, *dws = branch(
        grid_of,
        x,
        o,
        cotangent[0],
        ct_head if grid_of is None else cotangent[0],
        global_states[0],
        go if grid_of is None else half_sum,
        gstat if grid_of is None else half_stat,
        global_cotangent[0],
        wo,
        w1t,
        b1.reshape(-1, LANES),
        w2,
        b2_rows,
        norm_params,
    )
    if grid_of is None:
        gcentre = jnp.sum(
            (gdo.astype(f32) * go.astype(f32)).reshape(own, HEADS, HEAD_DIM), axis=-1
        )
        message = jnp.concatenate(
            [gdo]
            + pieces(gstat)
            + pieces(gcentre)
            + [jnp.zeros((own, LANES - 6 * HEADS), bf16)],
            axis=1,
        )
        everyone = lax.all_gather(message, "seq", axis=0, tiled=True)
        dqt, dk, dv, centre = local_backward(
            False, scalars, rows, group_rows, q, k, v, do, o, line, None, None, None, None
        )
    else:
        sum_first, last, message, rest, z_head = dws
        dqt, dk, dv, centre, everyone, sum_second, rest = local_backward(
            True, scalars, rows, group_rows, q, k, v, do, o, line, message, rest, last, dwo
        )
        z_head, rest = lax.optimization_barrier((z_head, rest))
        halo_z = from_behind(z_head, "seq", -1)
    dq, dk, dv, dqkv, dgh, dnorm_global = slot_backward(
        grid_of,
        scalars,
        rows,
        group_rows,
        q,
        k,
        v,
        do,
        line,
        centre,
        dqt,
        dk,
        dv,
        gq,
        gk,
        gv,
        everyone,
        all_states,
        gh,
        h,
        wq,
        wk,
        wv,
    )
    if grid_of is None:
        dx, dnorm = project_back(x, dy, dq, dk, dv, wq, wk, wv, norms[0])
        back_z, back_grad = from_behind((z[:HALF], dx[:HALF].astype(bf16)), "seq", -1)
        layer_out = jnp.concatenate([z[HALF:], back_z], 0)
        token_grad = jnp.concatenate([dx[HALF:], back_grad.astype(f32)], 0)
        small = jnp.concatenate([db1, db2, dnorm[:2], dnorm_global[:2], dgain2, doffset2], 0)
        dgh = lax.psum_scatter(dgh, "seq", scatter_dimension=0, tiled=True).astype(f32)
        gunit, gscale = normalize_rows(global_states[0].astype(f32))
        global_grad = gdy + norm_back(gunit, gscale, norms[2], dgh)
        small = lax.psum(small, ("batch", "seq"))
        dw1, dw2 = dws
        weights = [scatter_sum(value) for value in (dqkv[0], dqkv[1], dqkv[2], dwo, dw1, dw2)]
    else:
        sum_third, small, global_grad, dx, halo_dx = finish_all(
            rest,
            x,
            dy,
            dq,
            dk,
            dv,
            dqkv,
            dgh,
            wq,
            wk,
            wv,
            (db1, db2, dnorm_global, dgain2, doffset2),
            global_states[0],
            gdy,
            norm_params,
        )
        results = unpack(
            z,
            halo_z,
            dx,
            halo_dx,
            gz,
            global_grad,
            sum_first,
            sum_second,
            sum_third,
            small,
            width // seq_count,
            w1.shape[1],
        )
        weights = [value.T for value in results[4:10]]
        biases = [value.reshape(-1) for value in results[10:12]]
        return (*results[:4], *weights, *biases, results[12])
    hidden_rows = w1.shape[1] // width
    return (
        layer_out[None],
        gz[None],
        token_grad[None],
        global_grad[None],
        *weights,
        small[:hidden_rows].reshape(-1),
        small[hidden_rows],
        small[hidden_rows + 1 : hidden_rows + 7],
    )


def solution(mesh):
    split = P("batch", "seq", None)
    return jax.shard_map(
        on_device,
        mesh=mesh,
        in_specs=(split, split) + (P(),) * 11 + (split, split),
        out_specs=(split,) * 4 + (P("batch", "seq"),) * 6 + (P(),) * 3,
        check_vma=False,
    )
```
